32 devices in a mesh: shard: 8 (over z, x), rep: 4 (over y, core).
Axes of the slice: x: 2, y: 2, z: 4, core: 2. Of those that a mesh axis runs over, the one named last changes fastest.
Arguments:
- tokens: bfloat16 [32, 256, 2048], P(('shard', 'rep')), may hold values from -6 to 6
- segments: int32 [32, 256], P(('shard', 'rep')), may hold values from 0 to 3, never falling along the last dimension, each value on 1 to 128 neighbouring positions
- norm_attn: bfloat16 [2048], P('shard'), may hold values from 0.099609375 to 1.8984375
- w_query: bfloat16 [2048, 2048], P('shard'), may hold values from -0.125 to 0.125
- key_weight: bfloat16 [2048, 512], P('shard'), may hold values from -0.125 to 0.125
- value_weight: bfloat16 [2048, 512], P('shard'), may hold values from -0.125 to 0.125
- w_out: bfloat16 [2048, 2048], P('shard'), may hold values from -0.75 to 0.75
- norm_mlp: bfloat16 [2048], P('shard'), may hold values from 0.099609375 to 1.8984375
- w_gate: bfloat16 [2048, 8192], P('shard'), may hold values from -0.125 to 0.125
- w_up: bfloat16 [2048, 8192], P('shard'), may hold values from -0.125 to 0.125
- w_down: bfloat16 [8192, 2048], P('shard'), may hold values from -0.0625 to 0.0625
- cotangent: float32 [32, 256, 2048], P(('shard', 'rep')), may hold values from -6 to 6
Outputs:
- activations: float32 [32, 256, 2048], P(('shard', 'rep'))
- input_grad: float32 [32, 256, 2048], P(('shard', 'rep'))
- grad_norm_attn: float32 [2048], P('shard')
- grad_query: float32 [2048, 2048], P('shard')
- grad_key: float32 [2048, 512], P('shard')
- grad_value: float32 [2048, 512], P('shard')
- grad_out: float32 [2048, 2048], P('shard')
- grad_norm_mlp: float32 [2048], P('shard')
- grad_gate: float32 [2048, 8192], P('shard')
- grad_up: float32 [2048, 8192], P('shard')
- grad_down: float32 [8192, 2048], P('shard')
The draws below stay inside these ranges and needn't reach their ends.
Inputs may be any that keep to these rules, and one draw needn't show every extreme that they name: `segments`: segment numbers never fall along a sequence; a document holds 1 to 128 tokens, and one holds exactly 128.
All inputs are finite; a program needn't handle non-finite values.
Results may differ from the reference program's by a relative error of at most 0.02.
Values may be sent and summed in bfloat16 or wider, within the bound.
A program may use at most 512 MiB of HBM per device.

```python
import math
import jax
import jax.numpy as jnp
import numpy as np
from jax import lax

MODEL_WIDTH = 2048
QUERY_HEADS = 32
KEY_VALUE_HEADS = 8
HEAD_SIZE = 64
FF = 8192
SEQ = 256
SEQS = 32


def block_levels(rng, extent, split, low, largest):
    loudness, own = 1.0, jax.random.fold_in(rng, 6)
    for axis_at, parts in split:
        draws = jnp.exp(jax.random.uniform(jax.random.fold_in(own, axis_at), (parts,), jnp.float32, low / len(split), largest / len(split)))
        loudness = loudness * jnp.repeat(draws, extent[axis_at] // parts).reshape([-1 if axis == axis_at else 1 for axis in range(len(extent))])
    return loudness


def length_profile(count, total, bound, skew):
    weights = [(1 << 20) // math.isqrt(standing ** skew) + 1 for standing in range(2, count + 1)]
    surplus, holding = total - bound - (count - 1), [1] * (count - 1)
    while surplus > 0:
        candidates = [i for i in range(count - 1) if holding[i] < bound]
        whole, remaining = sum([weights[i] for i in candidates]), surplus
        for i in candidates:
            addition = min(bound - holding[i], max(1, remaining * weights[i] // whole), surplus)
            holding[i] = holding[i] + addition
            surplus = surplus - addition
    return np.array([bound] + holding)


def ragged_sizes(own_key, count, total, limit, skew):
    if count == 2:
        one = jax.random.randint(own_key, (), max(1, total - limit), min(limit, total - 1) + 1)
        return jnp.stack([one, total - one])
    sizes = jnp.asarray(length_profile(count, total, limit, skew), jnp.int32)
    pairs = (count - 1) // 2
    donor, sink = sizes[1:1 + 2 * pairs:2], sizes[2:2 + 2 * pairs:2]
    margin = jnp.minimum(donor - 1, limit - sink)
    passed = jax.random.randint(jax.random.fold_in(own_key, 1), (pairs,), 0, 1 << 20) % (margin + 1)
    sizes = sizes.at[1:1 + 2 * pairs:2].set(donor - passed).at[2:2 + 2 * pairs:2].set(sink + passed)
    return sizes[jax.random.permutation(jax.random.fold_in(own_key, 2), count)]


def normal_values(stream_key, extent, scale, bound, cuts=(), kind=jnp.bfloat16):
    factor_of = block_levels(stream_key, extent, cuts, -0.22, 0.18) if cuts else 1.0
    drawn = jax.random.normal(stream_key, extent, jnp.float32) * scale * factor_of
    return jnp.minimum(jnp.maximum(drawn, -bound), bound).astype(kind)


def setup_inputs(seed: int = 0) -> dict:
    keys = jax.random.split(jax.random.key(seed), 13)
    tokens = normal_values(keys[0], (SEQS, SEQ, MODEL_WIDTH), 1.0, 6.0, ((0, 32),))
    segments = jax.vmap(lambda own: jnp.searchsorted(jnp.cumsum(ragged_sizes(own, 4, SEQ, SEQ // 2, 1)), jnp.arange(SEQ), side="right"))(jax.random.split(keys[1], SEQS)).reshape((SEQS, SEQ)).astype(jnp.int32)
    norm_attn = jnp.clip(1.0 + 0.18 * jax.random.normal(keys[2], (MODEL_WIDTH,), jnp.float32), 0.099609375, 1.8984375).astype(jnp.bfloat16)
    w_query = normal_values(keys[3], (MODEL_WIDTH, QUERY_HEADS * HEAD_SIZE), MODEL_WIDTH ** -0.5, 0.125, ((0, 8),))
    key_weight = normal_values(keys[4], (MODEL_WIDTH, KEY_VALUE_HEADS * HEAD_SIZE), MODEL_WIDTH ** -0.5, 0.125, ((0, 8),))
    value_weight = normal_values(keys[5], (MODEL_WIDTH, KEY_VALUE_HEADS * HEAD_SIZE), MODEL_WIDTH ** -0.5, 0.125, ((0, 8),))
    w_out = normal_values(keys[6], (QUERY_HEADS * HEAD_SIZE, MODEL_WIDTH), (MODEL_WIDTH // 32) ** -0.5, 0.75, ((0, 8),))
    norm_mlp = jnp.clip(1.0 + 0.18 * jax.random.normal(keys[7], (MODEL_WIDTH,), jnp.float32), 0.099609375, 1.8984375).astype(jnp.bfloat16)
    w_gate = normal_values(keys[8], (MODEL_WIDTH, FF), MODEL_WIDTH ** -0.5, 0.125, ((0, 8),))
    w_up = normal_values(keys[9], (MODEL_WIDTH, FF), MODEL_WIDTH ** -0.5, 0.125, ((0, 8),))
    w_down = normal_values(keys[10], (FF, MODEL_WIDTH), FF ** -0.5, 0.0625, ((0, 8),))
    cotangent = normal_values(keys[11], (SEQS, SEQ, MODEL_WIDTH), 1.0, 6.0, ((0, 32),), jnp.float32)
    return {"tokens": tokens, "segments": segments, "norm_attn": norm_attn, "w_query": w_query, "key_weight": key_weight, "value_weight": value_weight, "w_out": w_out, "norm_mlp": norm_mlp, "w_gate": w_gate, "w_up": w_up, "w_down": w_down, "cotangent": cotangent}


epsilon = 1e-05
masked_score = -1000000000.0
rope_base = 500000.0

@jax.custom_vjp
def lower_shard(v):
    return lax.optimization_barrier(v.astype(jnp.bfloat16)).astype(jnp.float32)

@jax.custom_vjp
def lower_shard_backward(v):
    return v

def low_keep(v):
    return (lower_shard(v), None)

def low_pass(kept, grad):
    return (grad,)

def back_keep(v):
    return (v, None)

def back_low(kept, grad):
    return (lower_shard(grad),)
lower_shard.defvjp(low_keep, low_pass)
lower_shard_backward.defvjp(back_keep, back_low)

def positions(segment_ids):
    index = lax.broadcasted_iota(jnp.int32, segment_ids.shape, 1)
    first = jnp.concatenate([jnp.ones_like(segment_ids[:, :1]), (segment_ids[:, 1:] != segment_ids[:, :-1]).astype(jnp.int32)], 1)
    starts = lax.cummax(jnp.where(first > 0, index, 0), axis=1)
    return (index - starts).astype(jnp.float32)

def rope_tables(segment_ids):
    half = HEAD_SIZE // 2
    inverse = rope_base ** (-(2.0 * jnp.arange(half, dtype=jnp.float32)) / HEAD_SIZE)
    angle = positions(segment_ids)[..., None] * inverse
    return (jnp.cos(angle), jnp.sin(angle))

def apply_rotary(value_rows, cosine_table, sine_table):
    half = value_rows.shape[-1] // 2
    first = value_rows[..., :half]
    second = value_rows[..., half:]
    cosine_table = cosine_table[:, :, None, :]
    sine_table = sine_table[:, :, None, :]
    return jnp.concatenate([first * cosine_table - second * sine_table, second * cosine_table + first * sine_table], -1)

def allowed_pairs(segment_ids):
    sequence_length = segment_ids.shape[1]
    same = segment_ids[:, :, None] == segment_ids[:, None, :]
    causal = lax.broadcasted_iota(jnp.int32, (sequence_length, sequence_length), 0) >= lax.broadcasted_iota(jnp.int32, (sequence_length, sequence_length), 1)
    return (same & causal[None])[:, None, None]

def apply_projection(left, right):
    return jnp.dot(left, right, precision=lax.Precision.HIGHEST)

def unit_rows(value_rows):
    return value_rows * lax.rsqrt(lax.optimization_barrier(jnp.mean(value_rows * value_rows, -1, keepdims=True)) + epsilon)

def block_forward(resid, weights, cosine_table, sine_table, allowed):
    gain_one, w_query, key_weight, value_weight, w_out, gain_two, w_gate, w_up, w_down = weights
    batch_input, sequence_length, width = resid.shape
    query_groups = QUERY_HEADS // KEY_VALUE_HEADS
    first_normed = lower_shard(unit_rows(resid) * gain_one)
    query_linear = lower_shard_backward(apply_projection(first_normed, w_query)).reshape(batch_input, sequence_length, QUERY_HEADS, HEAD_SIZE)
    key_linear = lower_shard_backward(apply_projection(first_normed, key_weight)).reshape(batch_input, sequence_length, KEY_VALUE_HEADS, HEAD_SIZE)
    value_linear = lower_shard_backward(apply_projection(first_normed, value_weight)).reshape(batch_input, sequence_length, KEY_VALUE_HEADS, HEAD_SIZE)
    query_rows = lower_shard(apply_rotary(query_linear, cosine_table, sine_table)).reshape(batch_input, sequence_length, KEY_VALUE_HEADS, query_groups, HEAD_SIZE)
    key_rows = lower_shard(apply_rotary(key_linear, cosine_table, sine_table))
    value_rows = lower_shard(value_linear)
    scores = lower_shard_backward(jnp.einsum('bqhgd,bkhd->bhgqk', query_rows, key_rows, precision=lax.Precision.HIGHEST) * HEAD_SIZE ** (-0.5))
    scores = jnp.where(allowed, scores, masked_score)
    probs = lower_shard(jax.nn.softmax(scores, axis=-1))
    attended = jnp.einsum('bhgqk,bkhd->bqhgd', probs, value_rows, precision=lax.Precision.HIGHEST).reshape(batch_input, sequence_length, QUERY_HEADS * HEAD_SIZE)
    attended = lower_shard_backward(lower_shard(attended))
    middle = resid + lower_shard_backward(apply_projection(attended, w_out))
    normed_two = lower_shard(unit_rows(middle) * gain_two)
    gate = lower_shard_backward(apply_projection(normed_two, w_gate))
    up_proj = lower_shard_backward(apply_projection(normed_two, w_up))
    hidden = lower_shard(jax.nn.silu(gate) * up_proj)
    return middle + lower_shard_backward(apply_projection(hidden, w_down))

def reference(tokens, segments, norm_attn, w_query, key_weight, value_weight, w_out, norm_mlp, w_gate, w_up, w_down, cotangent):
    params = tuple((weight.astype(jnp.float32) for weight in (norm_attn, w_query, key_weight, value_weight, w_out, norm_mlp, w_gate, w_up, w_down)))
    per_step = math.gcd(SEQS, max(1, 4096 // SEQ))
    count_steps = SEQS // per_step
    inputs = tokens.astype(jnp.float32).reshape(count_steps, per_step, SEQ, MODEL_WIDTH)
    seg_steps = segments.reshape(count_steps, per_step, SEQ)
    grad_steps = cotangent.astype(jnp.float32).reshape(count_steps, per_step, SEQ, MODEL_WIDTH)

    def one_step(grad_sums, step_data):
        resid, segment_ids, grad_output = step_data
        cosine_table, sine_table = rope_tables(segment_ids)
        allowed = allowed_pairs(segment_ids)

        def forward_fn(values_in, *weights):
            return block_forward(values_in, weights, cosine_table, sine_table, allowed)
        output, pullback = jax.vjp(forward_fn, resid, *params)
        grads = pullback(grad_output)
        return (tuple((earlier + new_grad for earlier, new_grad in zip(grad_sums, grads[1:]))), (output, grads[0]))
    init = tuple((jnp.zeros_like(weight) for weight in params))
    grad_sums, (outputs, grad_inputs) = lax.scan(one_step, init, (inputs, seg_steps, grad_steps))
    return (outputs.reshape(SEQS, SEQ, MODEL_WIDTH), grad_inputs.reshape(SEQS, SEQ, MODEL_WIDTH), grad_sums[0], grad_sums[1], grad_sums[2], grad_sums[3], grad_sums[4], grad_sums[5], grad_sums[6], grad_sums[7], grad_sums[8])
```

```python
import functools

import jax
import jax.numpy as jnp
from jax import lax
from jax.experimental import pallas as pl
from jax.experimental.pallas import tpu as pltpu
from jax.sharding import PartitionSpec as P

QUERY_HEADS = 32
KEY_VALUE_HEADS = 8
HEAD_SIZE = 64
GROUP = QUERY_HEADS // KEY_VALUE_HEADS

epsilon = 1e-05
masked_score = -1000000000.0
rope_base = 500000.0
BF = jnp.bfloat16
F32 = jnp.float32


def dot(left, right):
    return jnp.dot(left, right, preferred_element_type=F32)


def contract_last(left, right):
    return lax.dot_general(left, right, (((1,), (1,)), ((), ())), preferred_element_type=F32)


def contract_first(left, right):
    return lax.dot_general(left, right, (((0,), (0,)), ((), ())), preferred_element_type=F32)


def positions(segment_ids):
    index = lax.broadcasted_iota(jnp.int32, segment_ids.shape, 1)
    first = jnp.concatenate(
        [
            jnp.ones_like(segment_ids[:, :1]),
            (segment_ids[:, 1:] != segment_ids[:, :-1]).astype(jnp.int32),
        ],
        1,
    )
    starts = lax.cummax(jnp.where(first > 0, index, 0), axis=1)
    return (index - starts).astype(F32)


def rope_tables(segment_ids):
    half = HEAD_SIZE // 2
    inverse = rope_base ** (-(2.0 * jnp.arange(half, dtype=F32)) / HEAD_SIZE)
    angle = positions(segment_ids)[0, :, None] * inverse
    cosine, sine = jnp.cos(angle), jnp.sin(angle)
    return jnp.concatenate([cosine] * 4, 1), jnp.concatenate([-sine, sine] * 2, 1)


def normalize(rows):
    scale_row = lax.rsqrt(jnp.mean(rows * rows, -1, keepdims=True) + epsilon)
    return rows * scale_row, scale_row


def norm_back(grad_unit, unit, scale_row):
    return scale_row * (grad_unit - unit * jnp.mean(grad_unit * unit, -1, keepdims=True))


def rotate(block, cosine, sine):
    lane = lax.broadcasted_iota(jnp.int32, cosine.shape, 1)
    lower = lane % HEAD_SIZE < HEAD_SIZE // 2
    parts = []
    for at in range(0, block.shape[1], 128):
        part = block[:, at : at + 128]
        other = jnp.where(
            lower, pltpu.roll(part, 128 - HEAD_SIZE // 2, 1), pltpu.roll(part, HEAD_SIZE // 2, 1)
        )
        parts.append(part * cosine + other * sine)
    return parts[0] if len(parts) == 1 else jnp.concatenate(parts, 1)


def stack_heads(block, key_head):
    first = key_head * GROUP
    return jnp.concatenate(
        [block[:, (first + i) * HEAD_SIZE : (first + i + 1) * HEAD_SIZE] for i in range(GROUP)], 0
    )


def unstack_heads(rows):
    count = rows.shape[0] // GROUP
    return [rows[i * count : (i + 1) * count] for i in range(GROUP)]


def softmax_rows(query, key, allowed):
    raw = contract_last(query, key) * HEAD_SIZE ** (-0.5)
    scores = jnp.where(allowed, raw, masked_score)
    exponent = jnp.exp(scores - jnp.max(scores, -1, keepdims=True))
    return exponent / jnp.sum(exponent, -1, keepdims=True)


def allowed_rows(seg_column, seg_row):
    count = seg_row.shape[1]
    shape = (count, count)
    causal = lax.broadcasted_iota(jnp.int32, shape, 0) >= lax.broadcasted_iota(jnp.int32, shape, 1)
    one = ((seg_column == seg_row) & causal).astype(jnp.int32)
    return jnp.concatenate([one] * GROUP, 0) > 0


def attend_kernel(q_ref, k_ref, v_ref, cos_ref, sin_ref, segc_ref, segr_ref, qo, ko, vo, ao):
    cosine, sine = cos_ref[...], sin_ref[...]
    allowed = allowed_rows(segc_ref[...], segr_ref[...])
    query = rotate(q_ref[...], cosine, sine).astype(BF)
    key = rotate(k_ref[...], cosine, sine).astype(BF)
    value = v_ref[...].astype(BF)
    qo[...] = query
    ko[...] = key
    vo[...] = value
    heads = []
    for j in range(2):
        cols = slice(j * HEAD_SIZE, (j + 1) * HEAD_SIZE)
        probs = softmax_rows(stack_heads(query, j), key[:, cols], allowed).astype(BF)
        heads += unstack_heads(dot(probs, value[:, cols]).astype(BF))
    ao[...] = jnp.concatenate(heads, 1)


def attend_back_kernel(q_ref, k_ref, v_ref, g_ref, cos_ref, sin_ref, segc_ref, segr_ref, gq, gk, gv):
    cosine, sine = cos_ref[...], -sin_ref[...]
    allowed = allowed_rows(segc_ref[...], segr_ref[...])
    query, key, value, grad = q_ref[...], k_ref[...], v_ref[...], g_ref[...]
    heads, keys, values = [], [], []
    for j in range(2):
        cols = slice(j * HEAD_SIZE, (j + 1) * HEAD_SIZE)
        rows, grad_rows = stack_heads(query, j), stack_heads(grad, j)
        probs = softmax_rows(rows, key[:, cols], allowed)
        grad_probs = contract_last(grad_rows, value[:, cols])
        grad_scores = (
            probs * (grad_probs - jnp.sum(probs * grad_probs, -1, keepdims=True))
        ).astype(BF)
        heads += unstack_heads(dot(grad_scores, key[:, cols]) * HEAD_SIZE ** (-0.5))
        keys.append(contract_first(grad_scores, rows) * HEAD_SIZE ** (-0.5))
        values.append(contract_first(probs.astype(BF), grad_rows))
    gq[...] = rotate(jnp.concatenate(heads, 1), cosine, sine).astype(BF)
    gk[...] = rotate(jnp.concatenate(keys, 1), cosine, sine).astype(BF)
    gv[...] = jnp.concatenate(values, 1).astype(BF)


def attention_specs(count):
    wide = pl.BlockSpec((count, 2 * GROUP * HEAD_SIZE), lambda i: (0, i))
    thin = pl.BlockSpec((count, 2 * HEAD_SIZE), lambda i: (0, i))
    whole = lambda shape: pl.BlockSpec(shape, lambda i: (0, 0))
    fixed = [whole((count, 128)), whole((count, 128)), whole((count, 1)), whole((1, count))]
    return wide, thin, fixed


def attend(query_lin, key_lin, value_lin, tables):
    count = query_lin.shape[0]
    wide, thin, fixed = attention_specs(count)
    kinds = [jax.ShapeDtypeStruct(a.shape, BF) for a in (query_lin, key_lin, value_lin, query_lin)]
    return pl.pallas_call(
        attend_kernel,
        grid=(KEY_VALUE_HEADS // 2,),
        in_specs=[wide, thin, thin] + fixed,
        out_specs=[wide, thin, thin, wide],
        out_shape=kinds,
        compiler_params=pltpu.CompilerParams(vmem_limit_bytes=48 * 2**20),
        cost_estimate=pl.CostEstimate(
            flops=2 * 10**9, bytes_accessed=6 * 10**6, transcendentals=2 * 10**6
        ),
    )(query_lin, key_lin, value_lin, *tables)


def attend_back(query, key, value, grad, tables):
    count = query.shape[0]
    wide, thin, fixed = attention_specs(count)
    kinds = [jax.ShapeDtypeStruct(a.shape, BF) for a in (query, key, value)]
    return pl.pallas_call(
        attend_back_kernel,
        grid=(KEY_VALUE_HEADS // 2,),
        in_specs=[wide, thin, thin, wide] + fixed,
        out_specs=[wide, thin, thin],
        out_shape=kinds,
        compiler_params=pltpu.CompilerParams(vmem_limit_bytes=48 * 2**20),
        cost_estimate=pl.CostEstimate(
            flops=4 * 10**9, bytes_accessed=6 * 10**6, transcendentals=2 * 10**6
        ),
    )(query, key, value, grad, *tables)


def ring_order(count):
    return list(range(0, count, 2)) + list(range(count - 1, 0, -2)) if count % 2 == 0 else list(range(count))


class Ring:
    def __init__(self, count):
        self.count = count
        self.half = count // 2
        self.order = ring_order(count)
        inverse = [self.order.index(i) for i in range(count)]
        self.table = jnp.asarray(self.order, jnp.int32)
        self.place = jnp.asarray(inverse, jnp.int32)[lax.axis_index("shard")]

    def at(self, offset):
        return self.table[(self.place + offset + self.count) % self.count]

    def send(self, array, offset):
        n, order = self.count, self.order
        pairs = [(order[i], order[(i + offset) % n]) for i in range(n)]
        return lax.ppermute(array, "shard", pairs)

    def gather(self, array):
        cut = array.shape[0] // 2
        ahead = back = array
        out = {0: array}
        for k in range(1, self.half):
            ahead, back = self.send(ahead, 1), self.send(back, -1)
            out[k], out[-k] = ahead, back
        out[self.half] = jnp.concatenate([self.send(ahead[:cut], 1), self.send(back[cut:], -1)], 0)
        return out

    def scatter(self, part):
        far = part(self.half).astype(BF)
        cut = far.shape[0] // 2
        ahead, back = self.send(far[:cut], 1), self.send(far[cut:], -1)
        for k in range(self.half - 1, 0, -1):
            up, down = part(k), part(-k)
            if k == self.half - 1:
                up = jnp.concatenate([up[:cut] + ahead.astype(F32), up[cut:]], 0)
                down = jnp.concatenate([down[:cut], down[cut:] + back.astype(F32)], 0)
            else:
                up, down = up + ahead.astype(F32), down + back.astype(F32)
            ahead, back = self.send(up.astype(BF), 1), self.send(down.astype(BF), -1)
        return part(0) + ahead.astype(F32) + back.astype(F32)


def swap(array, bit):
    return lax.ppermute(array, "rep", [(i, i ^ bit) for i in range(4)])


def cols(array, start, width):
    return lax.dynamic_slice_in_dim(array, start, width, 1)


def rows_of(array, start, height):
    return lax.dynamic_slice_in_dim(array, start, height, 0)


def put(array, piece, start, axis):
    return lax.dynamic_update_slice_in_dim(array, piece, start, axis)


def on_device(
    count,
    tokens,
    segments,
    norm_attn,
    w_query,
    key_weight,
    value_weight,
    w_out,
    norm_mlp,
    w_gate,
    w_up,
    w_down,
    cotangent,
):
    ring = Ring(count)
    rep = lax.axis_index("rep")
    core = rep % 2
    sequence, width = tokens.shape[1], tokens.shape[2]
    own_rows = w_query.shape[0]
    ff = w_gate.shape[1]
    ff_own = ff // count
    wide_q, wide_k = w_query.shape[1], key_weight.shape[1]

    def halves(*arrays):
        return tuple(
            jnp.concatenate([cols(a, c * (a.shape[1] // 2), a.shape[1] // 2) for a in arrays], 1)
            for c in (core, 1 - core)
        )

    def order_halves(mine, other):
        first = core == 0
        return jnp.where(first, mine, other), jnp.where(first, other, mine)

    def split_halves(mine, other, widths):
        low, high = order_halves(mine, other)
        out, at = [], 0
        for w in widths:
            out.append(jnp.concatenate([low[:, at : at + w // 2], high[:, at : at + w // 2]], 1))
            at += w // 2
        return out

    def gather_weights(mine):
        parts = ring.gather(mine)
        full = [jnp.zeros((count * own_rows, mine.shape[1]), BF)] * 2
        for k in [0] + [s * j for j in range(1, ring.half) for s in (1, -1)] + [ring.half]:
            other = swap(parts[k], 1)
            start = ring.at(-k) * own_rows
            full = [put(full[0], parts[k], start, 0), put(full[1], other, start, 0)]
        return full

    gains_own = jnp.concatenate([norm_attn[None], norm_mlp[None]], 0)
    gains = jnp.zeros((2, width), BF)
    for k in range(count):
        piece = ring.send(gains_own, k) if k else gains_own
        gains = put(gains, piece, ring.at(-k) * own_rows, 1)
    gains = gains.astype(F32)
    gain_one, gain_two = gains[:1], gains[1:]

    qkv_half, _ = halves(w_query, key_weight, value_weight)
    qkv_mine, qkv_other = gather_weights(qkv_half)
    out_half, _ = halves(w_out)
    out_mine, out_other = gather_weights(out_half)

    quarter = own_rows // 4
    gate_rows = rows_of(w_gate, rep * quarter, quarter)
    up_rows = rows_of(w_up, rep * quarter, quarter)
    fetched = jnp.zeros((count, quarter, 2 * ff_own), BF)
    for k in range(count):
        dest = ring.at(k) * ff_own
        piece = jnp.concatenate([cols(gate_rows, dest, ff_own), cols(up_rows, dest, ff_own)], 1)
        piece = ring.send(piece, k) if k else piece
        fetched = put(fetched, piece[None], ring.at(-k), 0)
    pieces = [fetched, swap(fetched, 2)]
    pieces += [swap(piece, 1) for piece in pieces]
    w_both = jnp.zeros((count, 4, quarter, 2 * ff_own), BF)
    for bits, piece in zip((0, 2, 1, 3), pieces):
        w_both = put(w_both, piece[:, None], rep ^ bits, 1)
    w_both = w_both.reshape(width, 2 * ff_own)

    grad_output = cotangent.reshape(sequence, width)
    grad_low_all = ring.gather(grad_output.astype(BF))

    cosine, sine = rope_tables(segments)
    seg_row = segments.reshape(1, sequence)
    tables = (cosine, sine, seg_row.reshape(sequence, 1), seg_row)
    resid = tokens.astype(F32).reshape(sequence, width)
    unit_one, scale_one = normalize(resid)
    normed_one = (unit_one * gain_one).astype(BF)
    query_lin, key_lin, value_lin = split_halves(
        dot(normed_one, qkv_mine), dot(normed_one, qkv_other), (wide_q, wide_k, wide_k)
    )
    query, key, value, attended = attend(query_lin, key_lin, value_lin, tables)
    (branch,) = split_halves(dot(attended, out_mine), dot(attended, out_other), (width,))
    middle = resid + branch
    unit_two, scale_two = normalize(middle)
    normed_two = (unit_two * gain_two).astype(BF)

    normed_all = ring.gather(normed_two)
    hidden, grad_both, low = {}, {}, {}
    for k in normed_all:
        both = dot(normed_all[k], w_both)
        gate, up = both[:, :ff_own], both[:, ff_own:]
        grad_hidden = contract_last(grad_low_all[k], w_down)
        sigmoid = jax.nn.sigmoid(gate)
        silu = gate * sigmoid
        hidden[k] = (silu * up).astype(BF)
        grad_gate = (grad_hidden * up * sigmoid * (1.0 + gate * (1.0 - sigmoid))).astype(BF)
        grad_up = (grad_hidden * silu).astype(BF)
        grad_both[k] = jnp.concatenate([grad_gate, grad_up], 1)

    back = lambda k: k if k == ring.half else -k
    grad_normed_two = ring.scatter(lambda k: contract_last(grad_both[back(k)], w_both))
    output = middle + ring.scatter(lambda k: dot(hidden[back(k)], w_down))

    grad_gain_two = jnp.sum(grad_normed_two * unit_two, 0)
    grad_middle = grad_output + norm_back(grad_normed_two * gain_two, unit_two, scale_two)
    grad_mid_low = grad_middle.astype(BF)

    keys = list(normed_all)
    together = lambda parts: jnp.concatenate([parts[k] for k in keys], 0)
    normed_full, grad_both_full = together(normed_all), together(grad_both)
    hidden_full, low_full = together(hidden), together(grad_low_all)

    def sum_cores(array, half_of):
        keep, pass_on = half_of(array, core), half_of(array, 1 - core)
        return keep + swap(pass_on.astype(BF), 1).astype(F32)

    down_term = contract_first(hidden_full, low_full)
    down_half = sum_cores(
        down_term, lambda a, c: rows_of(a, c * (a.shape[0] // 2), a.shape[0] // 2)
    ).astype(BF)
    down_half = (down_half.astype(F32) + swap(down_half, 2).astype(F32)).astype(BF)
    down_grad = jnp.concatenate(order_halves(down_half, swap(down_half, 1)), 0).astype(F32)

    both_term = contract_first(normed_full, grad_both_full)
    both_term = both_term.reshape(count, 2, 2, quarter, 2 * ff_own)
    both_half = sum_cores(
        both_term, lambda a, c: lax.dynamic_index_in_dim(a, c, 2, keepdims=False)
    )
    chip = rep // 2
    keep = lax.dynamic_index_in_dim(both_half, chip, 1, keepdims=False)
    pass_on = lax.dynamic_index_in_dim(both_half, 1 - chip, 1, keepdims=False)
    both_quarter = (keep + swap(pass_on.astype(BF), 2).astype(F32)).astype(BF)
    gate_quarter = jnp.zeros((quarter, ff), BF)
    up_quarter = jnp.zeros((quarter, ff), BF)
    for k in range(count):
        piece = lax.dynamic_index_in_dim(both_quarter, ring.at(k), 0, keepdims=False)
        piece = ring.send(piece, k) if k else piece
        start = ring.at(-k) * ff_own
        gate_quarter = put(gate_quarter, piece[:, :ff_own], start, 1)
        up_quarter = put(up_quarter, piece[:, ff_own:], start, 1)

    def collect(quarter_rows):
        parts = [quarter_rows, swap(quarter_rows, 2)]
        parts += [swap(part, 1) for part in parts]
        full = jnp.zeros((4 * quarter, ff), F32)
        for bits, part in zip((0, 2, 1, 3), parts):
            full = put(full, part.astype(F32), (rep ^ bits) * quarter, 0)
        return full

    gate_grad, up_grad = collect(gate_quarter), collect(up_quarter)

    def part_sums(left, grads_mine, grads_other):
        def part(k):
            block = cols(left, ring.at(k) * own_rows, own_rows)
            other = contract_first(block, grads_other).astype(BF)
            return contract_first(block, grads_mine) + swap(other, 1).astype(F32)

        mine = ring.scatter(part).astype(BF)
        mine = (mine.astype(F32) + swap(mine, 2).astype(F32)).astype(BF)
        return mine.astype(F32), swap(mine, 1).astype(F32)

    mid_mine, mid_other = halves(grad_mid_low)
    (out_grad,) = split_halves(*part_sums(attended, mid_mine, mid_other), (width,))
    grad_attended = (
        contract_last(mid_mine, out_mine) + contract_last(mid_other, out_other)
    ).astype(BF)
    grads = attend_back(query, key, value, grad_attended, tables)
    grad_mine, grad_other = halves(*grads)
    query_grad, key_grad, value_grad = split_halves(
        *part_sums(normed_one, grad_mine, grad_other), (wide_q, wide_k, wide_k)
    )
    grad_normed_one = contract_last(grad_mine, qkv_mine) + contract_last(grad_other, qkv_other)
    grad_gain_one = jnp.sum(grad_normed_one * unit_one, 0)
    grad_input = grad_middle + norm_back(grad_normed_one * gain_one, unit_one, scale_one)

    gain_terms = jnp.concatenate([grad_gain_one[None], grad_gain_two[None]], 0)
    gain_sums = cols(gain_terms, ring.at(0) * own_rows, own_rows)
    for k in range(1, count):
        gain_sums = gain_sums + ring.send(cols(gain_terms, ring.at(k) * own_rows, own_rows), k)
    gain_sums = gain_sums + swap(gain_sums, 1)
    gain_sums = gain_sums + swap(gain_sums, 2)

    return (
        output.reshape(tokens.shape),
        grad_input.reshape(tokens.shape),
        gain_sums[0],
        query_grad,
        key_grad,
        value_grad,
        out_grad,
        gain_sums[1],
        gate_grad,
        up_grad,
        down_grad,
    )


def solution(mesh):
    row, vector, matrix = P(("shard", "rep"), None, None), P("shard"), P("shard", None)
    in_specs = (row, P(("shard", "rep"), None), vector, matrix, matrix, matrix, matrix, vector)
    in_specs += (matrix, matrix, matrix, row)
    out_specs = (row, row, vector, matrix, matrix, matrix, matrix, vector, matrix, matrix, matrix)
    return jax.shard_map(
        functools.partial(on_device, mesh.shape["shard"]),
        mesh=mesh,
        in_specs=in_specs,
        out_specs=out_specs,
        check_vma=False,
    )
```

```python
import functools

import jax
import jax.numpy as jnp
from jax import lax
from jax.experimental import pallas as pl
from jax.experimental.pallas import tpu as pltpu
from jax.sharding import PartitionSpec as P

QUERY_HEADS = 32
KEY_VALUE_HEADS = 8
HEAD_SIZE = 64
GROUP = QUERY_HEADS // KEY_VALUE_HEADS

epsilon = 1e-05
masked_score = -1000000000.0
rope_base = 500000.0
WINDOW = 2
TILE = 256
VMEM_BYTES = 62 * 2**20
BF = jnp.bfloat16
F32 = jnp.float32


def dot(left, right):
    return jnp.dot(left, right, preferred_element_type=F32)


def contract_last(left, right):
    return lax.dot_general(left, right, (((1,), (1,)), ((), ())), preferred_element_type=F32)


def contract_first(left, right):
    return lax.dot_general(left, right, (((0,), (0,)), ((), ())), preferred_element_type=F32)


def positions(segment_ids):
    index = lax.broadcasted_iota(jnp.int32, segment_ids.shape, 1)
    first = jnp.concatenate(
        [
            jnp.ones_like(segment_ids[:, :1]),
            (segment_ids[:, 1:] != segment_ids[:, :-1]).astype(jnp.int32),
        ],
        1,
    )
    starts = lax.cummax(jnp.where(first > 0, index, 0), axis=1)
    return (index - starts).astype(F32)


def rope_tables(segment_ids):
    half = HEAD_SIZE // 2
    inverse = rope_base ** (-(2.0 * jnp.arange(half, dtype=F32)) / HEAD_SIZE)
    angle = positions(segment_ids)[0, :, None] * inverse
    cosine, sine = jnp.cos(angle), jnp.sin(angle)
    return jnp.concatenate([cosine] * 4, 1), jnp.concatenate([-sine, sine] * 2, 1)


def normalize(rows):
    scale_row = lax.rsqrt(jnp.mean(rows * rows, -1, keepdims=True) + epsilon)
    return rows * scale_row, scale_row


def norm_back(grad_unit, unit, scale_row):
    return scale_row * (grad_unit - unit * jnp.mean(grad_unit * unit, -1, keepdims=True))


def rotate(block, cosine, sine):
    lane = lax.broadcasted_iota(jnp.int32, cosine.shape, 1)
    lower = lane % HEAD_SIZE < HEAD_SIZE // 2
    parts = []
    for at in range(0, block.shape[1], 128):
        part = block[:, at : at + 128]
        other = jnp.where(
            lower, pltpu.roll(part, 128 - HEAD_SIZE // 2, 1), pltpu.roll(part, HEAD_SIZE // 2, 1)
        )
        parts.append(part * cosine + other * sine)
    return parts[0] if len(parts) == 1 else jnp.concatenate(parts, 1)


def stack_heads(block, key_head):
    first = key_head * GROUP
    return jnp.concatenate(
        [block[:, (first + i) * HEAD_SIZE : (first + i + 1) * HEAD_SIZE] for i in range(GROUP)], 0
    )


def unstack_heads(rows):
    count = rows.shape[0] // GROUP
    return [rows[i * count : (i + 1) * count] for i in range(GROUP)]


def softmax_rows(query, key, allowed):
    raw = contract_last(query, key) * HEAD_SIZE ** (-0.5)
    scores = jnp.where(allowed, raw, masked_score)
    exponent = jnp.exp(scores - jnp.max(scores, -1, keepdims=True))
    return exponent / jnp.sum(exponent, -1, keepdims=True)


def allowed_rows(seg_column, seg_row):
    count = seg_row.shape[1]
    shape = (count, count)
    causal = lax.broadcasted_iota(jnp.int32, shape, 0) >= lax.broadcasted_iota(jnp.int32, shape, 1)
    one = ((seg_column == seg_row) & causal).astype(jnp.int32)
    return jnp.concatenate([one] * GROUP, 0) > 0


def attend_kernel(q_ref, k_ref, v_ref, cos_ref, sin_ref, segc_ref, segr_ref, qo, ko, vo, ao):
    cosine, sine = cos_ref[...], sin_ref[...]
    allowed = allowed_rows(segc_ref[...], segr_ref[...])
    query = rotate(q_ref[...], cosine, sine).astype(BF)
    key = rotate(k_ref[...], cosine, sine).astype(BF)
    value = v_ref[...].astype(BF)
    qo[...] = query
    ko[...] = key
    vo[...] = value
    heads = []
    for j in range(2):
        cols = slice(j * HEAD_SIZE, (j + 1) * HEAD_SIZE)
        probs = softmax_rows(stack_heads(query, j), key[:, cols], allowed).astype(BF)
        heads += unstack_heads(dot(probs, value[:, cols]).astype(BF))
    ao[...] = jnp.concatenate(heads, 1)


def attend_back_kernel(q_ref, k_ref, v_ref, g_ref, cos_ref, sin_ref, segc_ref, segr_ref, gq, gk, gv):
    cosine, sine = cos_ref[...], -sin_ref[...]
    allowed = allowed_rows(segc_ref[...], segr_ref[...])
    query, key, value, grad = q_ref[...], k_ref[...], v_ref[...], g_ref[...]
    heads, keys, values = [], [], []
    for j in range(2):
        cols = slice(j * HEAD_SIZE, (j + 1) * HEAD_SIZE)
        rows, grad_rows = stack_heads(query, j), stack_heads(grad, j)
        probs = softmax_rows(rows, key[:, cols], allowed)
        grad_probs = contract_last(grad_rows, value[:, cols])
        grad_scores = (
            probs * (grad_probs - jnp.sum(probs * grad_probs, -1, keepdims=True))
        ).astype(BF)
        heads += unstack_heads(dot(grad_scores, key[:, cols]) * HEAD_SIZE ** (-0.5))
        keys.append(contract_first(grad_scores, rows) * HEAD_SIZE ** (-0.5))
        values.append(contract_first(probs.astype(BF), grad_rows))
    gq[...] = rotate(jnp.concatenate(heads, 1), cosine, sine).astype(BF)
    gk[...] = rotate(jnp.concatenate(keys, 1), cosine, sine).astype(BF)
    gv[...] = jnp.concatenate(values, 1).astype(BF)


def attention_specs(count):
    wide = pl.BlockSpec((count, 2 * GROUP * HEAD_SIZE), lambda i: (0, i))
    thin = pl.BlockSpec((count, 2 * HEAD_SIZE), lambda i: (0, i))
    whole = lambda shape: pl.BlockSpec(shape, lambda i: (0, 0))
    fixed = [whole((count, 128)), whole((count, 128)), whole((count, 1)), whole((1, count))]
    return wide, thin, fixed


def attend(query_lin, key_lin, value_lin, tables):
    count = query_lin.shape[0]
    wide, thin, fixed = attention_specs(count)
    kinds = [jax.ShapeDtypeStruct(a.shape, BF) for a in (query_lin, key_lin, value_lin, query_lin)]
    return pl.pallas_call(
        attend_kernel,
        grid=(KEY_VALUE_HEADS // 2,),
        in_specs=[wide, thin, thin] + fixed,
        out_specs=[wide, thin, thin, wide],
        out_shape=kinds,
        compiler_params=pltpu.CompilerParams(vmem_limit_bytes=48 * 2**20),
        cost_estimate=pl.CostEstimate(
            flops=2 * 10**9, bytes_accessed=6 * 10**6, transcendentals=2 * 10**6
        ),
    )(query_lin, key_lin, value_lin, *tables)


def attend_back(query, key, value, grad, tables):
    count = query.shape[0]
    wide, thin, fixed = attention_specs(count)
    kinds = [jax.ShapeDtypeStruct(a.shape, BF) for a in (query, key, value)]
    return pl.pallas_call(
        attend_back_kernel,
        grid=(KEY_VALUE_HEADS // 2,),
        in_specs=[wide, thin, thin, wide] + fixed,
        out_specs=[wide, thin, thin],
        out_shape=kinds,
        compiler_params=pltpu.CompilerParams(vmem_limit_bytes=48 * 2**20),
        cost_estimate=pl.CostEstimate(
            flops=4 * 10**9, bytes_accessed=6 * 10**6, transcendentals=2 * 10**6
        ),
    )(query, key, value, grad, *tables)


def ring_order(count):
    return list(range(0, count, 2)) + list(range(count - 1, 0, -2)) if count % 2 == 0 else list(range(count))


class Ring:
    def __init__(self, count):
        self.count = count
        self.half = count // 2
        self.order = ring_order(count)
        inverse = [self.order.index(i) for i in range(count)]
        self.table = jnp.asarray(self.order, jnp.int32)
        self.turns = []
        self.place = jnp.asarray(inverse, jnp.int32)[lax.axis_index("shard")]

    def at(self, offset):
        return self.table[(self.place + offset + self.count) % self.count]

    def send(self, array, offset):
        n, order = self.count, self.order
        pairs = [(order[i], order[(i + offset) % n]) for i in range(n)]
        return lax.ppermute(array, "shard", pairs)

    def queue(self, *sends):
        arrays = [array for array, _ in sends]
        if len(self.turns) >= WINDOW:
            arrays, _ = lax.optimization_barrier((arrays, self.turns[-WINDOW]))
        got = [self.send(array, offset) for array, (_, offset) in zip(arrays, sends)]
        self.turns.append(got[:2])
        return got

    def gather(self, array):
        cut = array.shape[0] // 2
        ahead = back = array
        out = {0: array}
        for k in range(1, self.half):
            ahead, back = self.queue((ahead, 1), (back, -1))
            out[k], out[-k] = ahead, back
            yield out
        out[self.half] = jnp.concatenate(self.queue((ahead[:cut], 1), (back[cut:], -1)), 0)
        yield out

    def scatter(self, terms):
        (far,) = terms((self.half,))
        far = far.astype(BF)
        cut = far.shape[0] // 2
        ahead, back = self.queue((far[:cut], 1), (far[cut:], -1))
        yield None
        for k in range(self.half - 1, 0, -1):
            up, down = terms((k, -k))
            if k == self.half - 1:
                up = jnp.concatenate([up[:cut] + ahead.astype(F32), up[cut:]], 0)
                down = jnp.concatenate([down[:cut], down[cut:] + back.astype(F32)], 0)
            else:
                up, down = up + ahead.astype(F32), down + back.astype(F32)
            ahead, back = self.queue((up.astype(BF), 1), (down.astype(BF), -1))
            if k > 1:
                yield None
        (own,) = terms((0,))
        yield own + ahead.astype(F32) + back.astype(F32)


def run(*flows):
    flows = list(flows)
    last = [None] * len(flows)
    live = list(range(len(flows)))
    while live:
        for i in list(live):
            try:
                last[i] = next(flows[i])
            except StopIteration:
                live.remove(i)
    return last


def ring_neighbours(count):
    me = lax.axis_index("shard")
    even = me % 2 == 0
    ahead = jnp.where(
        even,
        jnp.where(me == count - 2, count - 1, me + 2),
        jnp.where(me == 1, 0, me - 2),
    )
    back = jnp.where(
        even,
        jnp.where(me == 0, 1, me - 2),
        jnp.where(me == count - 1, count - 2, me + 2),
    )
    return ahead, back


def feed_forward_kernel(
    count,
    normed_ref,
    low_ref,
    both_ref,
    down_ref,
    grad_ref,
    branch_ref,
    weight_grads_ref,
    normed,
    low,
    hidden,
    grads,
    w_both,
    w_down,
    turned,
    staged,
    outgoing,
    incoming,
    local_sem,
    gather_send,
    gather_recv,
    scatter_send,
    scatter_recv,
    credit,
    staged_sem,
):
    half = count // 2
    rows = normed_ref.shape[0]
    cut = rows // 2
    width = normed_ref.shape[1]
    ff = down_ref.shape[0]
    neighbours = ring_neighbours(count)
    everywhere = pl.ds(0, rows)
    halves = (pl.ds(0, cut), pl.ds(cut, cut))

    def at(slot, part=None):
        start, size = (0, rows) if part is None else (part * cut, cut)
        return pl.ds(pl.multiple_of(slot * rows + start, cut), size)

    def tile(j):
        return pl.ds(pl.multiple_of(j * TILE, TILE), TILE)

    def remote(src, dst, send, recv, direction):
        return pltpu.make_async_remote_copy(
            src_ref=src,
            dst_ref=dst,
            send_sem=send,
            recv_sem=recv,
            device_id={"shard": neighbours[direction]},
            device_id_type=pl.DeviceIdType.MESH,
        )

    loads = [
        pltpu.make_async_copy(low_ref, low.at[at(0)], local_sem.at[0]),
        pltpu.make_async_copy(normed_ref, normed.at[at(0)], local_sem.at[1]),
        pltpu.make_async_copy(both_ref, w_both, local_sem.at[2]),
        pltpu.make_async_copy(down_ref, w_down, local_sem.at[3]),
    ]
    for load in loads:
        load.start()

    for chain in range(2):
        for direction in range(2):
            blank = halves[1 - direction]
            incoming[chain, direction, 0, blank] = jnp.zeros((cut, width), BF)

    barrier = pltpu.get_barrier_semaphore()
    for neighbour in neighbours:
        pl.semaphore_signal(
            barrier,
            inc=1,
            device_id={"shard": neighbour},
            device_id_type=pl.DeviceIdType.MESH,
        )
    pl.semaphore_wait(barrier, 2)

    buffers = (low, normed)

    def gathered(which, direction, step):
        base = 0 if direction == 0 else half
        if isinstance(step, int) and step == 1:
            source = 0
        else:
            source = jnp.where(step == 1, 0, base + step - 1)
        return remote(
            buffers[which].at[at(source)],
            buffers[which].at[at(base + step)],
            gather_send.at[which, direction, step - 1],
            gather_recv.at[which, direction, step - 1],
            direction,
        )

    def gathered_last(which, direction):
        source = half - 1 if direction == 0 else 2 * half - 1
        return remote(
            buffers[which].at[at(source, direction)],
            buffers[which].at[at(half, direction)],
            gather_send.at[which, direction, half - 1],
            gather_recv.at[which, direction, half - 1],
            direction,
        )

    def products(slot):
        mine = at(slot)

        def body(j, carry):
            gate_at, up_at = tile(j), tile(j + ff // TILE)
            own = normed[mine, :]
            gate = dot(own, w_both[:, gate_at])
            up = dot(own, w_both[:, up_at])
            grad_hidden = contract_last(low[mine, :], w_down[gate_at, :])
            sigmoid = jax.nn.sigmoid(gate)
            silu = gate * sigmoid
            hidden[mine, gate_at] = (silu * up).astype(BF)
            grads[mine, gate_at] = (
                grad_hidden * up * sigmoid * (1.0 + gate * (1.0 - sigmoid))
            ).astype(BF)
            grads[mine, up_at] = (grad_hidden * silu).astype(BF)
            return carry

        lax.fori_loop(0, ff // TILE, body, 0)

    both_ways = ((0, 0), (0, 1), (1, 0), (1, 1))
    for which in range(2):
        loads[which].wait()
        for direction in range(2):
            gathered(which, direction, 1).start()
    loads[2].wait()
    loads[3].wait()
    products(0)

    def gather_step(step, carry):
        for which in range(2):
            for direction in range(2):
                gathered(which, direction, step).wait_recv()

                @pl.when(step < half - 1)
                def _():
                    gathered(which, direction, step + 1).start()

                @pl.when(step == half - 1)
                def _():
                    gathered_last(which, direction).start()

        products(step)
        products(half + step)
        return carry

    lax.fori_loop(1, half, gather_step, 0)
    for which, direction in both_ways:
        gathered_last(which, direction).wait_recv()
    products(half)

    def term(chain, rows_at, j):
        if chain == 0:
            return contract_last(grads[rows_at, :], w_both[tile(j), :])
        return dot(hidden[rows_at, :], w_down[:, tile(j)])

    def scattered(chain, direction, step):
        if isinstance(step, int) and step == 0:
            own, there = halves[direction], 0
        else:
            own, there = everywhere, step % 2
        return remote(
            outgoing.at[chain, direction, own],
            incoming.at[chain, direction, there, own],
            scatter_send.at[chain, direction, step],
            scatter_recv.at[chain, direction, step],
            direction,
        )

    def weight_unit(unit):
        spot = unit % 2
        target = weight_grads_ref.at[pl.ds(pl.multiple_of(unit * TILE, TILE), TILE)]
        stage = pltpu.make_async_copy(staged.at[spot], target, staged_sem.at[spot])

        @pl.when(unit >= 2)
        def _():
            stage.wait()

        def from_arrays(left, right, block):
            def turn(c, carry):
                turned[:, at(c)] = left[at(c), tile(block)].T
                return carry

            lax.fori_loop(0, count, turn, 0)

            def body(j, carry):
                staged[spot, :, tile(j)] = dot(turned[...], right[:, tile(j)]).astype(BF)
                return carry

            lax.fori_loop(0, width // TILE, body, 0)

        @pl.when(unit < width // TILE)
        def _():
            from_arrays(normed, grads, unit)

        @pl.when(unit >= width // TILE)
        def _():
            from_arrays(hidden, low, unit - width // TILE)

        stage.start()

    units = (width + ff) // TILE
    per_step = -(-units // (half - 1))

    for chain in range(2):

        def first(j, carry):
            value = term(chain, at(half), j).astype(BF)
            outgoing[chain, 0, halves[0], tile(j)] = value[:cut]
            outgoing[chain, 1, halves[1], tile(j)] = value[cut:]
            return carry

        lax.fori_loop(0, width // TILE, first, 0)
        for direction in range(2):
            scattered(chain, direction, 0).start()

    def scatter_step(step, carry):
        k = half - step
        for chain in range(2):
            for direction in range(2):
                slot = half + k if direction == 0 else k

                @pl.when(step == 1)
                def _():
                    scattered(chain, direction, 0).wait()

                @pl.when(step > 1)
                def _():
                    scattered(chain, direction, step - 1).wait()
                    pl.semaphore_wait(credit.at[chain, direction], 1)

                def add(j, carry):
                    value = term(chain, at(slot), j)
                    value += incoming[chain, direction, (step - 1) % 2, :, tile(j)].astype(F32)
                    outgoing[chain, direction, :, tile(j)] = value.astype(BF)
                    return carry

                lax.fori_loop(0, width // TILE, add, 0)
                scattered(chain, direction, step).start()

                @pl.when(step < half - 1)
                def _():
                    pl.semaphore_signal(
                        credit.at[chain, direction],
                        inc=1,
                        device_id={"shard": neighbours[1 - direction]},
                        device_id_type=pl.DeviceIdType.MESH,
                    )

        lax.fori_loop(
            (step - 1) * per_step,
            jnp.minimum(step * per_step, units),
            lambda unit, c: (weight_unit(unit), c)[1],
            0,
        )
        return carry

    lax.fori_loop(1, half, scatter_step, 0)

    for chain, result in enumerate((grad_ref, branch_ref)):
        for direction in range(2):
            scattered(chain, direction, half - 1).wait()

        def last(j, carry):
            value = term(chain, at(0), j)
            for direction in range(2):
                value += incoming[chain, direction, (half - 1) % 2, :, tile(j)].astype(F32)
            result[:, tile(j)] = value
            return carry

        lax.fori_loop(0, width // TILE, last, 0)

    for unit in (units - 2, units - 1):
        target = weight_grads_ref.at[pl.ds(unit * TILE, TILE)]
        pltpu.make_async_copy(staged.at[unit % 2], target, staged_sem.at[unit % 2]).wait()
    for which, direction in both_ways:
        lax.fori_loop(
            1,
            half,
            lambda step, c: (gathered(which, direction, step).wait_send(), c)[1],
            0,
        )
        gathered_last(which, direction).wait_send()


def feed_forward_bytes(count, rows, width, ff):
    tokens = count * rows
    return 2 * (
        tokens * (2 * width + 3 * ff)
        + 3 * width * ff
        + TILE * tokens
        + 2 * TILE * width
        + 12 * rows * width
        + 4 * rows * width
    )


def feed_forward(count, normed, low, w_both, w_down):
    rows, width = normed.shape
    ff = w_down.shape[0]
    tokens = count * rows
    half = count // 2
    here = pl.BlockSpec(memory_space=pl.ANY)
    inside = pl.BlockSpec(memory_space=pltpu.VMEM)
    return pl.pallas_call(
        functools.partial(feed_forward_kernel, count),
        in_specs=[here] * 4,
        out_specs=[inside, inside, here],
        out_shape=[
            jax.ShapeDtypeStruct((rows, width), F32),
            jax.ShapeDtypeStruct((rows, width), F32),
            jax.ShapeDtypeStruct((width + ff, width), BF),
        ],
        scratch_shapes=[
            pltpu.VMEM((tokens, width), BF),
            pltpu.VMEM((tokens, width), BF),
            pltpu.VMEM((tokens, ff), BF),
            pltpu.VMEM((tokens, 2 * ff), BF),
            pltpu.VMEM((width, 2 * ff), BF),
            pltpu.VMEM((ff, width), BF),
            pltpu.VMEM((TILE, tokens), BF),
            pltpu.VMEM((2, TILE, width), BF),
            pltpu.VMEM((2, 2, rows, width), BF),
            pltpu.VMEM((2, 2, 2, rows, width), BF),
            pltpu.SemaphoreType.DMA((4,)),
            pltpu.SemaphoreType.DMA((2, 2, half)),
            pltpu.SemaphoreType.DMA((2, 2, half)),
            pltpu.SemaphoreType.DMA((2, 2, half)),
            pltpu.SemaphoreType.DMA((2, 2, half)),
            pltpu.SemaphoreType.REGULAR((2, 2)),
            pltpu.SemaphoreType.DMA((2,)),
        ],
        compiler_params=pltpu.CompilerParams(
            collective_id=0, has_side_effects=True, vmem_limit_bytes=VMEM_BYTES
        ),
        cost_estimate=pl.CostEstimate(
            flops=18 * tokens * width * ff, bytes_accessed=50 * 10**6, transcendentals=tokens * ff
        ),
    )(normed, low, w_both, w_down)


def feed_forward_parts(ring, normed_two, grad_low, w_both, w_down):
    sequence, ff_own = normed_two.shape[0], w_down.shape[0]
    low_all, normed_all = run(ring.gather(grad_low), ring.gather(normed_two))
    hidden, grad_both = {}, {}
    for k in normed_all:
        both = dot(normed_all[k], w_both)
        gate, up = both[:, :ff_own], both[:, ff_own:]
        grad_hidden = contract_last(low_all[k], w_down)
        sigmoid = jax.nn.sigmoid(gate)
        silu = gate * sigmoid
        hidden[k] = (silu * up).astype(BF)
        grad_gate = (grad_hidden * up * sigmoid * (1.0 + gate * (1.0 - sigmoid))).astype(BF)
        grad_up = (grad_hidden * silu).astype(BF)
        grad_both[k] = jnp.concatenate([grad_gate, grad_up], 1)

    def terms_of(chunks, product):
        def terms(ks):
            sources = [k if k == ring.half else -k for k in ks]
            whole = product(jnp.concatenate([chunks[k] for k in sources], 0))
            return [whole[i * sequence : (i + 1) * sequence] for i in range(len(ks))]

        return terms

    (grad_normed_two,) = run(ring.scatter(terms_of(grad_both, lambda a: contract_last(a, w_both))))
    (branch_two,) = run(ring.scatter(terms_of(hidden, lambda a: dot(a, w_down))))
    keys = list(normed_all)
    together = lambda parts: jnp.concatenate([parts[k] for k in keys], 0)
    both_term = contract_first(together(normed_all), together(grad_both))
    down_term = contract_first(together(hidden), together(low_all))
    return grad_normed_two, branch_two, both_term, down_term


def swap(array, bit):
    return lax.ppermute(array, "rep", [(i, i ^ bit) for i in range(4)])


def cols(array, start, width):
    return lax.dynamic_slice_in_dim(array, start, width, 1)


def rows_of(array, start, height):
    return lax.dynamic_slice_in_dim(array, start, height, 0)


def put(array, piece, start, axis):
    return lax.dynamic_update_slice_in_dim(array, piece, start, axis)


def on_device(
    count,
    tokens,
    segments,
    norm_attn,
    w_query,
    key_weight,
    value_weight,
    w_out,
    norm_mlp,
    w_gate,
    w_up,
    w_down,
    cotangent,
):
    ring = Ring(count)
    rep = lax.axis_index("rep")
    core = rep % 2
    sequence, width = tokens.shape[1], tokens.shape[2]
    own_rows = w_query.shape[0]
    ff = w_gate.shape[1]
    ff_own = ff // count
    wide_q, wide_k = w_query.shape[1], key_weight.shape[1]

    def halves(*arrays):
        return tuple(
            jnp.concatenate([cols(a, c * (a.shape[1] // 2), a.shape[1] // 2) for a in arrays], 1)
            for c in (core, 1 - core)
        )

    def order_halves(mine, other):
        first = core == 0
        return jnp.where(first, mine, other), jnp.where(first, other, mine)

    def split_halves(mine, other, widths):
        low, high = order_halves(mine, other)
        out, at = [], 0
        for w in widths:
            out.append(jnp.concatenate([low[:, at : at + w // 2], high[:, at : at + w // 2]], 1))
            at += w // 2
        return out

    def gather_weights(mine):
        full = [jnp.zeros((count * own_rows, mine.shape[1]), BF)] * 2
        seen = set()
        for parts in ring.gather(mine):
            for k in parts:
                if k not in seen:
                    other = swap(parts[k], 1)
                    start = ring.at(-k) * own_rows
                    full = [put(full[0], parts[k], start, 0), put(full[1], other, start, 0)]
                    seen.add(k)
            yield full

    gains_own = jnp.concatenate([norm_attn[None], norm_mlp[None]], 0)
    gains = jnp.zeros((2, width), BF)
    for k in range(count):
        piece = ring.send(gains_own, k) if k else gains_own
        gains = put(gains, piece, ring.at(-k) * own_rows, 1)
    gains = gains.astype(F32)
    gain_one, gain_two = gains[:1], gains[1:]

    qkv_half, _ = halves(w_query, key_weight, value_weight)
    ((qkv_mine, qkv_other),) = run(gather_weights(qkv_half))
    out_half, _ = halves(w_out)
    ((out_mine, out_other),) = run(gather_weights(out_half))

    quarter = own_rows // 4
    gate_rows = rows_of(w_gate, rep * quarter, quarter)
    up_rows = rows_of(w_up, rep * quarter, quarter)
    sends = []
    for k in range(count):
        dest = ring.at(k) * ff_own
        piece = jnp.concatenate([cols(gate_rows, dest, ff_own), cols(up_rows, dest, ff_own)], 1)
        sends.append((piece, k))
    fetched = jnp.zeros((count, quarter, 2 * ff_own), BF)
    for k, piece in enumerate([sends[0][0]] + ring.queue(*sends[1:])):
        fetched = put(fetched, piece[None], ring.at(-k), 0)
    pieces = [fetched, swap(fetched, 2)]
    pieces += [swap(piece, 1) for piece in pieces]
    w_both = jnp.zeros((count, 4, quarter, 2 * ff_own), BF)
    for bits, piece in zip((0, 2, 1, 3), pieces):
        w_both = put(w_both, piece[:, None], rep ^ bits, 1)
    w_both = w_both.reshape(width, 2 * ff_own)

    grad_output = cotangent.reshape(sequence, width)

    cosine, sine = rope_tables(segments)
    seg_row = segments.reshape(1, sequence)
    tables = (cosine, sine, seg_row.reshape(sequence, 1), seg_row)
    resid = tokens.astype(F32).reshape(sequence, width)
    unit_one, scale_one = normalize(resid)
    normed_one = (unit_one * gain_one).astype(BF)
    query_lin, key_lin, value_lin = split_halves(
        dot(normed_one, qkv_mine), dot(normed_one, qkv_other), (wide_q, wide_k, wide_k)
    )
    query, key, value, attended = attend(query_lin, key_lin, value_lin, tables)
    (branch,) = split_halves(dot(attended, out_mine), dot(attended, out_other), (width,))
    middle = resid + branch
    unit_two, scale_two = normalize(middle)
    normed_two = (unit_two * gain_two).astype(BF)

    grad_low = grad_output.astype(BF)
    if feed_forward_bytes(count, sequence, width, ff_own) <= VMEM_BYTES:
        grad_normed_two, branch_two, weight_terms = feed_forward(
            count, normed_two, grad_low, w_both, w_down
        )
        both_term, down_term = weight_terms[:width], weight_terms[width:]
    else:
        grad_normed_two, branch_two, both_term, down_term = feed_forward_parts(
            ring, normed_two, grad_low, w_both, w_down
        )
    output = middle + branch_two

    grad_gain_two = jnp.sum(grad_normed_two * unit_two, 0)
    grad_middle = grad_output + norm_back(grad_normed_two * gain_two, unit_two, scale_two)
    grad_mid_low = grad_middle.astype(BF)

    def sum_cores(array, half_of):
        keep, pass_on = half_of(array, core), half_of(array, 1 - core)
        return keep.astype(F32) + swap(pass_on.astype(BF), 1).astype(F32)

    both_term = both_term.reshape(count, 2, 2, quarter, 2 * ff_own)
    both_half = sum_cores(
        both_term, lambda a, c: lax.dynamic_index_in_dim(a, c, 2, keepdims=False)
    )
    chip = rep // 2
    keep = lax.dynamic_index_in_dim(both_half, chip, 1, keepdims=False)
    pass_on = lax.dynamic_index_in_dim(both_half, 1 - chip, 1, keepdims=False)
    both_quarter = (keep + swap(pass_on.astype(BF), 2).astype(F32)).astype(BF)
    gate_quarter = jnp.zeros((quarter, ff), BF)
    up_quarter = jnp.zeros((quarter, ff), BF)
    sends = [
        (lax.dynamic_index_in_dim(both_quarter, ring.at(k), 0, keepdims=False), k)
        for k in range(count)
    ]
    for k, piece in enumerate([sends[0][0]] + ring.queue(*sends[1:])):
        start = ring.at(-k) * ff_own
        gate_quarter = put(gate_quarter, piece[:, :ff_own], start, 1)
        up_quarter = put(up_quarter, piece[:, ff_own:], start, 1)

    def collect(quarter_rows):
        parts = [quarter_rows, swap(quarter_rows, 2)]
        parts += [swap(part, 1) for part in parts]
        full = jnp.zeros((4 * quarter, ff), F32)
        for bits, part in zip((0, 2, 1, 3), parts):
            full = put(full, part.astype(F32), (rep ^ bits) * quarter, 0)
        return full

    gate_grad, up_grad = collect(gate_quarter), collect(up_quarter)

    down_half = sum_cores(
        down_term, lambda a, c: rows_of(a, c * (a.shape[0] // 2), a.shape[0] // 2)
    ).astype(BF)
    down_half = (down_half.astype(F32) + swap(down_half, 2).astype(F32)).astype(BF)
    down_grad = jnp.concatenate(order_halves(down_half, swap(down_half, 1)), 0).astype(F32)

    def part_sums(left, grads_mine, grads_other):
        def terms(ks):
            blocks = [cols(left, ring.at(k) * own_rows, own_rows) for k in ks]
            block = blocks[0] if len(ks) == 1 else jnp.concatenate(blocks, 1)
            other = swap(contract_first(block, grads_other).astype(BF), 1)
            whole = contract_first(block, grads_mine) + other.astype(F32)
            return [whole[i * own_rows : (i + 1) * own_rows] for i in range(len(ks))]

        mine = run(ring.scatter(terms))[0].astype(BF)
        mine = (mine.astype(F32) + swap(mine, 2).astype(F32)).astype(BF)
        return mine.astype(F32), swap(mine, 1).astype(F32)

    mid_mine, mid_other = halves(grad_mid_low)
    (out_grad,) = split_halves(*part_sums(attended, mid_mine, mid_other), (width,))
    grad_attended = (
        contract_last(mid_mine, out_mine) + contract_last(mid_other, out_other)
    ).astype(BF)
    grads = attend_back(query, key, value, grad_attended, tables)
    grad_mine, grad_other = halves(*grads)
    query_grad, key_grad, value_grad = split_halves(
        *part_sums(normed_one, grad_mine, grad_other), (wide_q, wide_k, wide_k)
    )
    grad_normed_one = contract_last(grad_mine, qkv_mine) + contract_last(grad_other, qkv_other)
    grad_gain_one = jnp.sum(grad_normed_one * unit_one, 0)
    grad_input = grad_middle + norm_back(grad_normed_one * gain_one, unit_one, scale_one)

    gain_terms = jnp.concatenate([grad_gain_one[None], grad_gain_two[None]], 0)
    gain_sums = cols(gain_terms, ring.at(0) * own_rows, own_rows)
    for k in range(1, count):
        gain_sums = gain_sums + ring.send(cols(gain_terms, ring.at(k) * own_rows, own_rows), k)
    gain_sums = gain_sums + swap(gain_sums, 1)
    gain_sums = gain_sums + swap(gain_sums, 2)

    return (
        output.reshape(tokens.shape),
        grad_input.reshape(tokens.shape),
        gain_sums[0],
        query_grad,
        key_grad,
        value_grad,
        out_grad,
        gain_sums[1],
        gate_grad,
        up_grad,
        down_grad,
    )


def solution(mesh):
    row, vector, matrix = P(("shard", "rep"), None, None), P("shard"), P("shard", None)
    in_specs = (row, P(("shard", "rep"), None), vector, matrix, matrix, matrix, matrix, vector)
    in_specs += (matrix, matrix, matrix, row)
    out_specs = (row, row, vector, matrix, matrix, matrix, matrix, vector, matrix, matrix, matrix)
    return jax.shard_map(
        functools.partial(on_device, mesh.shape["shard"]),
        mesh=mesh,
        in_specs=in_specs,
        out_specs=out_specs,
        check_vma=False,
    )
```

```python
import functools

import jax
import jax.numpy as jnp
from jax import lax
from jax.experimental import pallas as pl
from jax.experimental.pallas import tpu as pltpu
from jax.sharding import PartitionSpec as P

QUERY_HEADS = 32
KEY_VALUE_HEADS = 8
HEAD_SIZE = 64
GROUP = QUERY_HEADS // KEY_VALUE_HEADS

epsilon = 1e-05
masked_score = -1000000000.0
rope_base = 500000.0
WINDOW = 2
TILE = 256
WIDE_TILE = 512
VMEM_BYTES = 62 * 2**20
BF = jnp.bfloat16
F32 = jnp.float32


def dot(left, right):
    return jnp.dot(left, right, preferred_element_type=F32)


def contract_last(left, right):
    return lax.dot_general(left, right, (((1,), (1,)), ((), ())), preferred_element_type=F32)


def contract_first(left, right):
    return lax.dot_general(left, right, (((0,), (0,)), ((), ())), preferred_element_type=F32)


def positions(segment_ids):
    index = lax.broadcasted_iota(jnp.int32, segment_ids.shape, 1)
    first = jnp.concatenate(
        [
            jnp.ones_like(segment_ids[:, :1]),
            (segment_ids[:, 1:] != segment_ids[:, :-1]).astype(jnp.int32),
        ],
        1,
    )
    starts = lax.cummax(jnp.where(first > 0, index, 0), axis=1)
    return (index - starts).astype(F32)


def rope_tables(segment_ids):
    half = HEAD_SIZE // 2
    inverse = rope_base ** (-(2.0 * jnp.arange(half, dtype=F32)) / HEAD_SIZE)
    angle = positions(segment_ids)[0, :, None] * inverse
    cosine, sine = jnp.cos(angle), jnp.sin(angle)
    return jnp.concatenate([cosine] * 4, 1), jnp.concatenate([-sine, sine] * 2, 1)


def normalize(rows):
    scale_row = lax.rsqrt(jnp.mean(rows * rows, -1, keepdims=True) + epsilon)
    return rows * scale_row, scale_row


def norm_back(grad_unit, unit, scale_row):
    return scale_row * (grad_unit - unit * jnp.mean(grad_unit * unit, -1, keepdims=True))


def rotate(block, cosine, sine):
    lane = lax.broadcasted_iota(jnp.int32, cosine.shape, 1)
    lower = lane % HEAD_SIZE < HEAD_SIZE // 2
    parts = []
    for at in range(0, block.shape[1], 128):
        part = block[:, at : at + 128]
        other = jnp.where(
            lower, pltpu.roll(part, 128 - HEAD_SIZE // 2, 1), pltpu.roll(part, HEAD_SIZE // 2, 1)
        )
        parts.append(part * cosine + other * sine)
    return parts[0] if len(parts) == 1 else jnp.concatenate(parts, 1)


def stack_heads(block, key_head):
    first = key_head * GROUP
    return jnp.concatenate(
        [block[:, (first + i) * HEAD_SIZE : (first + i + 1) * HEAD_SIZE] for i in range(GROUP)], 0
    )


def unstack_heads(rows):
    count = rows.shape[0] // GROUP
    return [rows[i * count : (i + 1) * count] for i in range(GROUP)]


def softmax_rows(query, key, allowed):
    raw = contract_last(query, key) * HEAD_SIZE ** (-0.5)
    scores = jnp.where(allowed, raw, masked_score)
    exponent = jnp.exp(scores - jnp.max(scores, -1, keepdims=True))
    return exponent / jnp.sum(exponent, -1, keepdims=True)


def allowed_rows(seg_column, seg_row):
    count = seg_row.shape[1]
    shape = (count, count)
    causal = lax.broadcasted_iota(jnp.int32, shape, 0) >= lax.broadcasted_iota(jnp.int32, shape, 1)
    one = ((seg_column == seg_row) & causal).astype(jnp.int32)
    return jnp.concatenate([one] * GROUP, 0) > 0


def attend_kernel(q_ref, k_ref, v_ref, cos_ref, sin_ref, segc_ref, segr_ref, qo, ko, vo, ao):
    cosine, sine = cos_ref[...], sin_ref[...]
    allowed = allowed_rows(segc_ref[...], segr_ref[...])
    query = rotate(q_ref[...], cosine, sine).astype(BF)
    key = rotate(k_ref[...], cosine, sine).astype(BF)
    value = v_ref[...].astype(BF)
    qo[...] = query
    ko[...] = key
    vo[...] = value
    heads = []
    for j in range(2):
        cols = slice(j * HEAD_SIZE, (j + 1) * HEAD_SIZE)
        probs = softmax_rows(stack_heads(query, j), key[:, cols], allowed).astype(BF)
        heads += unstack_heads(dot(probs, value[:, cols]).astype(BF))
    ao[...] = jnp.concatenate(heads, 1)


def attend_back_kernel(q_ref, k_ref, v_ref, g_ref, cos_ref, sin_ref, segc_ref, segr_ref, gq, gk, gv):
    cosine, sine = cos_ref[...], -sin_ref[...]
    allowed = allowed_rows(segc_ref[...], segr_ref[...])
    query, key, value, grad = q_ref[...], k_ref[...], v_ref[...], g_ref[...]
    heads, keys, values = [], [], []
    for j in range(2):
        cols = slice(j * HEAD_SIZE, (j + 1) * HEAD_SIZE)
        rows, grad_rows = stack_heads(query, j), stack_heads(grad, j)
        probs = softmax_rows(rows, key[:, cols], allowed)
        grad_probs = contract_last(grad_rows, value[:, cols])
        grad_scores = (
            probs * (grad_probs - jnp.sum(probs * grad_probs, -1, keepdims=True))
        ).astype(BF)
        heads += unstack_heads(dot(grad_scores, key[:, cols]) * HEAD_SIZE ** (-0.5))
        keys.append(contract_first(grad_scores, rows) * HEAD_SIZE ** (-0.5))
        values.append(contract_first(probs.astype(BF), grad_rows))
    gq[...] = rotate(jnp.concatenate(heads, 1), cosine, sine).astype(BF)
    gk[...] = rotate(jnp.concatenate(keys, 1), cosine, sine).astype(BF)
    gv[...] = jnp.concatenate(values, 1).astype(BF)


def attention_specs(count):
    wide = pl.BlockSpec((count, 2 * GROUP * HEAD_SIZE), lambda i: (0, i))
    thin = pl.BlockSpec((count, 2 * HEAD_SIZE), lambda i: (0, i))
    whole = lambda shape: pl.BlockSpec(shape, lambda i: (0, 0))
    fixed = [whole((count, 128)), whole((count, 128)), whole((count, 1)), whole((1, count))]
    return wide, thin, fixed


def attend(query_lin, key_lin, value_lin, tables):
    count = query_lin.shape[0]
    wide, thin, fixed = attention_specs(count)
    kinds = [jax.ShapeDtypeStruct(a.shape, BF) for a in (query_lin, key_lin, value_lin, query_lin)]
    return pl.pallas_call(
        attend_kernel,
        grid=(KEY_VALUE_HEADS // 2,),
        in_specs=[wide, thin, thin] + fixed,
        out_specs=[wide, thin, thin, wide],
        out_shape=kinds,
        compiler_params=pltpu.CompilerParams(vmem_limit_bytes=48 * 2**20),
        cost_estimate=pl.CostEstimate(
            flops=2 * 10**9, bytes_accessed=6 * 10**6, transcendentals=2 * 10**6
        ),
    )(query_lin, key_lin, value_lin, *tables)


def attend_back(query, key, value, grad, tables):
    count = query.shape[0]
    wide, thin, fixed = attention_specs(count)
    kinds = [jax.ShapeDtypeStruct(a.shape, BF) for a in (query, key, value)]
    return pl.pallas_call(
        attend_back_kernel,
        grid=(KEY_VALUE_HEADS // 2,),
        in_specs=[wide, thin, thin, wide] + fixed,
        out_specs=[wide, thin, thin],
        out_shape=kinds,
        compiler_params=pltpu.CompilerParams(vmem_limit_bytes=48 * 2**20),
        cost_estimate=pl.CostEstimate(
            flops=4 * 10**9, bytes_accessed=6 * 10**6, transcendentals=2 * 10**6
        ),
    )(query, key, value, grad, *tables)


def ring_order(count):
    return list(range(0, count, 2)) + list(range(count - 1, 0, -2)) if count % 2 == 0 else list(range(count))


class Ring:
    def __init__(self, count):
        self.count = count
        self.half = count // 2
        self.order = ring_order(count)
        inverse = [self.order.index(i) for i in range(count)]
        self.table = jnp.asarray(self.order, jnp.int32)
        self.turns = []
        self.place = jnp.asarray(inverse, jnp.int32)[lax.axis_index("shard")]

    def at(self, offset):
        return self.table[(self.place + offset + self.count) % self.count]

    def send(self, array, offset):
        n, order = self.count, self.order
        pairs = [(order[i], order[(i + offset) % n]) for i in range(n)]
        return lax.ppermute(array, "shard", pairs)

    def queue(self, *sends):
        arrays = [array for array, _ in sends]
        if len(self.turns) >= WINDOW:
            arrays, _ = lax.optimization_barrier((arrays, self.turns[-WINDOW]))
        got = [self.send(array, offset) for array, (_, offset) in zip(arrays, sends)]
        self.turns.append(got[:2])
        return got

    def gather(self, array):
        cut = array.shape[0] // 2
        ahead = back = array
        out = {0: array}
        for k in range(1, self.half):
            ahead, back = self.queue((ahead, 1), (back, -1))
            out[k], out[-k] = ahead, back
            yield out
        out[self.half] = jnp.concatenate(self.queue((ahead[:cut], 1), (back[cut:], -1)), 0)
        yield out

    def scatter(self, terms):
        (far,) = terms((self.half,))
        far = far.astype(BF)
        cut = far.shape[0] // 2
        ahead, back = self.queue((far[:cut], 1), (far[cut:], -1))
        yield None
        for k in range(self.half - 1, 0, -1):
            up, down = terms((k, -k))
            if k == self.half - 1:
                up = jnp.concatenate([up[:cut] + ahead.astype(F32), up[cut:]], 0)
                down = jnp.concatenate([down[:cut], down[cut:] + back.astype(F32)], 0)
            else:
                up, down = up + ahead.astype(F32), down + back.astype(F32)
            ahead, back = self.queue((up.astype(BF), 1), (down.astype(BF), -1))
            if k > 1:
                yield None
        (own,) = terms((0,))
        yield own + ahead.astype(F32) + back.astype(F32)


def run(*flows):
    flows = list(flows)
    last = [None] * len(flows)
    live = list(range(len(flows)))
    while live:
        for i in list(live):
            try:
                last[i] = next(flows[i])
            except StopIteration:
                live.remove(i)
    return last


def ring_place(count, shard):
    return jnp.where(shard % 2 == 0, shard // 2, count - 1 - shard // 2)


def ring_shard(count, place):
    place = (place + count) % count
    return jnp.where(place < count // 2, 2 * place, 2 * (count - 1 - place) + 1)


def core_partner(rep):
    return rep + 1 - 2 * (rep % 2)


def chip_partner(rep):
    return (rep + 2) % 4


def greet(devices):
    barrier = pltpu.get_barrier_semaphore()
    for device in devices:
        pl.semaphore_signal(
            barrier, inc=1, device_id=device, device_id_type=pl.DeviceIdType.MESH
        )
    pl.semaphore_wait(barrier, len(devices))


def remote_copy(src, dst, send, recv, device):
    return pltpu.make_async_remote_copy(
        src_ref=src,
        dst_ref=dst,
        send_sem=send,
        recv_sem=recv,
        device_id=device,
        device_id_type=pl.DeviceIdType.MESH,
    )


def front_kernel(
    count,
    tokens_ref,
    gains_ref,
    cos_ref,
    sin_ref,
    segc_ref,
    segr_ref,
    qkv_own_ref,
    out_own_ref,
    gate_ref,
    up_ref,
    qkv_all_ref,
    out_all_ref,
    both_ref,
    gains_all_ref,
    query_ref,
    key_ref,
    value_ref,
    attended_ref,
    middle_ref,
    normed_two_ref,
    qkv_all,
    out_all,
    normed,
    linear,
    own_sem,
    load_sem,
    gain_send,
    gain_recv,
    ring_send,
    ring_recv,
    core_send,
    core_recv,
    across_send,
    across_recv,
    group_send,
    group_recv,
):
    half = count // 2
    me, rep = lax.axis_index("shard"), lax.axis_index("rep")
    core = rep % 2
    place = ring_place(count, me)
    others = [ring_shard(count, place + k) for k in range(1, count)]
    near = ({"shard": ring_shard(count, place + 1)}, {"shard": ring_shard(count, place - 1)})
    other_core, other_chip = {"rep": core_partner(rep)}, {"rep": chip_partner(rep)}
    own_rows = qkv_own_ref.shape[0]
    strip = own_rows // 2
    cut = strip // 2
    quarter = own_rows // 4
    ff_own = gate_ref.shape[1] // count
    rows, width = tokens_ref.shape
    full_refs = (qkv_all_ref, out_all_ref)
    own_refs = (qkv_own_ref, out_own_ref)
    inside = (qkv_all, out_all)

    def rows_at(start, size):
        return pl.ds(pl.multiple_of(start, cut), size)

    def shard_rows(shard):
        return rows_at(shard * own_rows, own_rows)

    def strip_of(shard, which_core, part=None):
        start = shard * own_rows + which_core * strip
        if part is None:
            return rows_at(start, strip)
        return rows_at(start + part * cut, cut)

    keep = [
        pltpu.make_async_copy(own_refs[i], full_refs[i].at[shard_rows(me)], own_sem.at[i])
        for i in range(2)
    ]
    for i, (ref, at) in enumerate(((gate_ref, 0), (up_ref, ff_own))):
        keep.append(
            pltpu.make_async_copy(
                ref.at[rows_at(rep * quarter, quarter), pl.ds(pl.multiple_of(me * ff_own, 128), ff_own)],
                both_ref.at[me, rep, :, pl.ds(at, ff_own)],
                own_sem.at[2 + i],
            )
        )
    for copy in keep:
        copy.start()
    gains_all_ref[:, pl.ds(pl.multiple_of(me * own_rows, 128), own_rows)] = gains_ref[...]

    greet([{"shard": shard} for shard in others] + [other_core, other_chip])

    def gain_copy(k):
        columns = pl.ds(pl.multiple_of(me * own_rows, 128), own_rows)
        return remote_copy(
            gains_ref,
            gains_all_ref.at[:, columns],
            gain_send.at[k - 1],
            gain_recv.at[k - 1],
            {"shard": others[k - 1]},
        )

    def across(k, which):
        ref = (gate_ref, up_ref)[which]
        there = others[k - 1]
        columns = pl.ds(pl.multiple_of(there * ff_own, 128), ff_own)
        return remote_copy(
            ref.at[rows_at(rep * quarter, quarter), columns],
            both_ref.at[me, rep, :, pl.ds(which * ff_own, ff_own)],
            across_send.at[which, k - 1],
            across_recv.at[which, k - 1],
            {"shard": there},
        )

    def ring_copy(i, direction, step):
        sign = 1 if direction == 0 else -1
        shard = ring_shard(count, place - sign * (step - 1))
        if step < half:
            at = strip_of(shard, core)
        else:
            at = strip_of(shard, core, direction)
        src = full_refs[i].at[at]
        if step == 1:
            src = own_refs[i].at[rows_at(core * strip, strip)]
        return remote_copy(
            src,
            full_refs[i].at[at],
            ring_send.at[i, direction, step - 1],
            ring_recv.at[i, direction, step - 1],
            near[direction],
        )

    def core_copy(i, k):
        at = strip_of(ring_shard(count, place - k), core)
        slot = k + half - 1
        return remote_copy(
            full_refs[i].at[at],
            full_refs[i].at[at],
            core_send.at[i, slot],
            core_recv.at[i, slot],
            other_core,
        )

    def load(i, k):
        at = shard_rows(ring_shard(count, place - k))
        return pltpu.make_async_copy(
            full_refs[i].at[at], inside[i].at[at], load_sem.at[i, k + half - 1]
        )

    def start_step(i, step):
        for direction in range(2):
            ring_copy(i, direction, step).start()

    def finish_step(i, step):
        for direction in range(2):
            ring_copy(i, direction, step).wait_recv()
        if step < half:
            start_step(i, step + 1)
            core_copy(i, step).start()
            core_copy(i, -step).start()
        else:
            core_copy(i, half).start()

    def load_step(i, step):
        for k in (step, -step) if step < half else (half,):
            core_copy(i, k).wait_recv()
            load(i, k).start()

    for k in range(1, count):
        gain_copy(k).start()
    for k in range(1, count):
        for which in range(2):
            across(k, which).start()
    start_step(0, 1)
    for copy in keep:
        copy.wait()
    for i in range(2):
        load(i, 0).start()
    resid = tokens_ref[...].astype(F32)
    unit, _ = normalize(resid)
    for k in range(1, count):
        gain_copy(k).wait_recv()
    normed[...] = (unit * gains_all_ref[0:1, :]).astype(BF)

    for step in range(1, half + 1):
        finish_step(0, step)
        if step > 1:
            load_step(0, step - 1)
    start_step(1, 1)

    def group_copy(index, quarter_at, device):
        at = both_ref.at[:, quarter_at]
        return remote_copy(at, at, group_send.at[index], group_recv.at[index], device)

    chip_copies = [group_copy(0, rep, other_chip)]
    core_copies = [
        group_copy(1, rep, other_core),
        group_copy(2, chip_partner(rep), other_core),
    ]
    for k in range(1, count):
        for which in range(2):
            across(k, which).wait_recv()
    chip_copies[0].start()
    core_copies[0].start()

    load_step(0, half)
    for k in range(-(half - 1), half + 1):
        load(0, k).wait()

    def linear_tile(j, carry):
        at = pl.ds(pl.multiple_of(j * TILE, TILE), TILE)
        linear[:, at] = dot(normed[...], qkv_all[:, at])
        return carry

    lax.fori_loop(0, linear.shape[1] // TILE, linear_tile, 0)

    cosine, sine = cos_ref[...], sin_ref[...]
    wide, thin = 2 * GROUP * HEAD_SIZE, 2 * HEAD_SIZE
    key_at, value_at = width, width + key_ref.shape[1]

    def heads_pair(pair):
        allowed = allowed_rows(segc_ref[...], segr_ref[...])
        wide_at = pl.ds(pair * wide, wide)
        thin_at = pl.ds(pair * thin, thin)
        query = rotate(linear[:, wide_at], cosine, sine).astype(BF)
        key = rotate(linear[:, pl.ds(key_at + pair * thin, thin)], cosine, sine).astype(BF)
        value = linear[:, pl.ds(value_at + pair * thin, thin)].astype(BF)
        query_ref[:, wide_at] = query
        key_ref[:, thin_at] = key
        value_ref[:, thin_at] = value
        heads = []
        for j in range(2):
            cols = slice(j * HEAD_SIZE, (j + 1) * HEAD_SIZE)
            probs = softmax_rows(stack_heads(query, j), key[:, cols], allowed).astype(BF)
            heads += unstack_heads(dot(probs, value[:, cols]).astype(BF))
        attended_ref[:, wide_at] = jnp.concatenate(heads, 1)

    pairs = KEY_VALUE_HEADS // 2
    for pair in range(max(pairs, half)):
        if pair < pairs:
            heads_pair(pair)
        if pair < half:
            finish_step(1, pair + 1)
            if pair > 0:
                load_step(1, pair)
        if pair == 1:
            chip_copies[0].wait_recv()
            core_copies[1].start()
    load_step(1, half)
    for k in range(-(half - 1), half + 1):
        load(1, k).wait()

    def branch_tile(j, carry):
        at = pl.ds(pl.multiple_of(j * TILE, TILE), TILE)
        branch = dot(attended_ref[...], out_all[:, at])
        middle_ref[:, at] = tokens_ref[:, at].astype(F32) + branch
        return carry

    lax.fori_loop(0, width // TILE, branch_tile, 0)
    unit, _ = normalize(middle_ref[...])
    normed_two_ref[...] = (unit * gains_all_ref[1:2, :]).astype(BF)

    for copy in core_copies:
        copy.wait_recv()
    for copy in chip_copies + core_copies:
        copy.wait_send()
    for i in range(2):
        for step in range(1, half + 1):
            for direction in range(2):
                ring_copy(i, direction, step).wait_send()
            for k in (step, -step) if step < half else (half,):
                core_copy(i, k).wait_send()
    for k in range(1, count):
        gain_copy(k).wait_send()
        for which in range(2):
            across(k, which).wait_send()


def front(count, tokens, gains, tables, qkv_own, out_own, gate_own, up_own, wide_k):
    rows, width = tokens.shape
    own_rows, qkv_width = qkv_own.shape
    ff_own = gate_own.shape[1] // count
    half = count // 2
    here = pl.BlockSpec(memory_space=pl.ANY)
    inside = pl.BlockSpec(memory_space=pltpu.VMEM)
    kind = jax.ShapeDtypeStruct
    dma = pltpu.SemaphoreType.DMA
    return pl.pallas_call(
        functools.partial(front_kernel, count),
        in_specs=[inside] * 6 + [here] * 4,
        out_specs=[here] * 3 + [inside] * 7,
        out_shape=[
            kind((count * own_rows, qkv_width), BF),
            kind((count * own_rows, width), BF),
            kind((count, 4, own_rows // 4, 2 * ff_own), BF),
            kind((gains.shape[0], width), F32),
            kind((rows, width), BF),
            kind((rows, wide_k), BF),
            kind((rows, wide_k), BF),
            kind((rows, width), BF),
            kind((rows, width), F32),
            kind((rows, width), BF),
        ],
        scratch_shapes=[
            pltpu.VMEM((count * own_rows, qkv_width), BF),
            pltpu.VMEM((count * own_rows, width), BF),
            pltpu.VMEM((rows, width), BF),
            pltpu.VMEM((rows, qkv_width), F32),
            dma((4,)),
            dma((2, count)),
            dma((count - 1,)),
            dma((count - 1,)),
            dma((2, 2, half)),
            dma((2, 2, half)),
            dma((2, count)),
            dma((2, count)),
            dma((2, count - 1)),
            dma((2, count - 1)),
            dma((3,)),
            dma((3,)),
        ],
        compiler_params=pltpu.CompilerParams(
            collective_id=1, has_side_effects=True, vmem_limit_bytes=VMEM_BYTES
        ),
        cost_estimate=pl.CostEstimate(
            flops=2 * rows * width * (qkv_width + width) + 2 * 10**9,
            bytes_accessed=60 * 10**6,
            transcendentals=2 * 10**6,
        ),
    )(tokens, gains, *tables, qkv_own, out_own, gate_own, up_own)


def feed_forward_kernel(
    count,
    normed_ref,
    low_ref,
    both_ref,
    down_ref,
    grad_ref,
    branch_ref,
    sums_ref,
    normed,
    low,
    hidden,
    grads,
    w_both,
    w_down,
    turned,
    staged,
    from_core,
    core_sums,
    from_chip,
    group_sums,
    result_tile,
    outgoing,
    incoming,
    local_sem,
    gather_send,
    gather_recv,
    scatter_send,
    scatter_recv,
    credit,
    core_send,
    core_recv,
    chip_send,
    chip_recv,
    group_credit,
    sums_sem,
    result_sem,
):
    half = count // 2
    rows = normed_ref.shape[0]
    cut = rows // 2
    width = normed_ref.shape[1]
    ff = down_ref.shape[0]
    place = ring_place(count, lax.axis_index("shard"))
    neighbours = (ring_shard(count, place + 1), ring_shard(count, place - 1))
    rep = lax.axis_index("rep")
    core, chip = rep % 2, rep // 2
    other_core, other_chip = {"rep": core_partner(rep)}, {"rep": chip_partner(rep)}
    everywhere = pl.ds(0, rows)
    halves = (pl.ds(0, cut), pl.ds(cut, cut))

    def at(slot, part=None):
        start, size = (0, rows) if part is None else (part * cut, cut)
        return pl.ds(pl.multiple_of(slot * rows + start, cut), size)

    def tile(j):
        return pl.ds(pl.multiple_of(j * TILE, TILE), TILE)

    def remote(src, dst, send, recv, direction):
        return remote_copy(src, dst, send, recv, {"shard": neighbours[direction]})

    loads = [
        pltpu.make_async_copy(low_ref, low.at[at(0)], local_sem.at[0]),
        pltpu.make_async_copy(normed_ref, normed.at[at(0)], local_sem.at[1]),
        pltpu.make_async_copy(both_ref, w_both, local_sem.at[2]),
        pltpu.make_async_copy(down_ref, w_down, local_sem.at[3]),
    ]
    for load in loads:
        load.start()

    for chain in range(2):
        for direction in range(2):
            blank = halves[1 - direction]
            incoming[chain, direction, 0, blank] = jnp.zeros((cut, width), BF)

    greet([{"shard": neighbour} for neighbour in neighbours] + [other_core, other_chip])

    buffers = (low, normed)

    def gathered(which, direction, step):
        base = 0 if direction == 0 else half
        if isinstance(step, int) and step == 1:
            source = 0
        else:
            source = jnp.where(step == 1, 0, base + step - 1)
        return remote(
            buffers[which].at[at(source)],
            buffers[which].at[at(base + step)],
            gather_send.at[which, direction, step - 1],
            gather_recv.at[which, direction, step - 1],
            direction,
        )

    def gathered_last(which, direction):
        source = half - 1 if direction == 0 else 2 * half - 1
        return remote(
            buffers[which].at[at(source, direction)],
            buffers[which].at[at(half, direction)],
            gather_send.at[which, direction, half - 1],
            gather_recv.at[which, direction, half - 1],
            direction,
        )

    def products(slot):
        mine = at(slot)

        def body(j, carry):
            gate_at, up_at = tile(j), tile(j + ff // TILE)
            own = normed[mine, :]
            gate = dot(own, w_both[:, gate_at])
            up = dot(own, w_both[:, up_at])
            grad_hidden = contract_last(low[mine, :], w_down[gate_at, :])
            sigmoid = jax.nn.sigmoid(gate)
            silu = gate * sigmoid
            hidden[mine, gate_at] = (silu * up).astype(BF)
            grads[mine, gate_at] = (
                grad_hidden * up * sigmoid * (1.0 + gate * (1.0 - sigmoid))
            ).astype(BF)
            grads[mine, up_at] = (grad_hidden * silu).astype(BF)
            return carry

        lax.fori_loop(0, ff // TILE, body, 0)

    both_ways = ((0, 0), (0, 1), (1, 0), (1, 1))
    for which in range(2):
        loads[which].wait()
        for direction in range(2):
            gathered(which, direction, 1).start()
    loads[2].wait()
    loads[3].wait()
    products(0)

    def gather_step(step, carry):
        for which in range(2):
            for direction in range(2):
                gathered(which, direction, step).wait_recv()

                @pl.when(step < half - 1)
                def _():
                    gathered(which, direction, step + 1).start()

                @pl.when(step == half - 1)
                def _():
                    gathered_last(which, direction).start()

        products(step)
        products(half + step)
        return carry

    lax.fori_loop(1, half, gather_step, 0)
    for which, direction in both_ways:
        gathered_last(which, direction).wait_recv()
    products(half)

    def term(chain, rows_at, j):
        if chain == 0:
            return contract_last(grads[rows_at, :], w_both[tile(j), :])
        return dot(hidden[rows_at, :], w_down[:, tile(j)])

    def scattered(chain, direction, step):
        if isinstance(step, int) and step == 0:
            own, there = halves[direction], 0
        else:
            own, there = everywhere, step % 2
        return remote(
            outgoing.at[chain, direction, own],
            incoming.at[chain, direction, there, own],
            scatter_send.at[chain, direction, step],
            scatter_recv.at[chain, direction, step],
            direction,
        )

    units = (width + ff) // TILE
    per_step = -(-(units + 2) // (half - 1))
    quarter = TILE // 4

    def core_copy(unit):
        spot = unit % 2
        return remote_copy(
            staged.at[spot, :, 1 - core],
            from_core.at[spot],
            core_send.at[spot],
            core_recv.at[spot],
            other_core,
        )

    def chip_copy(unit):
        spot = unit % 2
        return remote_copy(
            core_sums.at[spot, 1 - chip],
            from_chip.at[spot],
            chip_send.at[spot],
            chip_recv.at[spot],
            other_chip,
        )

    def sums_copy(unit):
        spot = unit % 2
        return pltpu.make_async_copy(group_sums.at[spot], sums_ref.at[unit], sums_sem.at[spot])

    def give_credit(which, device):
        pl.semaphore_signal(
            group_credit.at[which], inc=1, device_id=device, device_id_type=pl.DeviceIdType.MESH
        )

    def weight_unit(unit):
        spot = unit % 2

        def from_arrays(left, right, block):
            def turn(c, carry):
                turned[:, at(c)] = left[at(c), tile(block)].T
                return carry

            lax.fori_loop(0, count, turn, 0)

            def body(j, carry):
                value = dot(turned[...], right[:, tile(j)]).astype(BF)
                staged[spot, :, :, :, tile(j)] = value.reshape(2, 2, quarter, TILE)
                return carry

            lax.fori_loop(0, width // TILE, body, 0)

        @pl.when(unit < width // TILE)
        def _():
            from_arrays(normed, grads, unit)

        @pl.when(unit >= width // TILE)
        def _():
            from_arrays(hidden, low, unit - width // TILE)

        @pl.when(unit >= 2)
        def _():
            pl.semaphore_wait(group_credit.at[0], 1)

        core_copy(unit).start()

    def sum_over_cores(unit):
        spot = unit % 2
        core_copy(unit).wait()
        for y in range(2):
            total = staged[spot, y, core].astype(F32) + from_core[spot, y].astype(F32)
            core_sums[spot, y] = total.astype(BF)

        @pl.when(unit < units - 2)
        def _():
            give_credit(0, other_core)

        @pl.when(unit >= 2)
        def _():
            pl.semaphore_wait(group_credit.at[1], 1)

        chip_copy(unit).start()

    def sum_over_chips(unit):
        spot = unit % 2
        chip_copy(unit).wait()

        @pl.when(unit >= 2)
        def _():
            sums_copy(unit - 2).wait()

        total = core_sums[spot, chip].astype(F32) + from_chip[spot].astype(F32)
        group_sums[spot] = total.astype(BF)

        @pl.when(unit < units - 2)
        def _():
            give_credit(1, other_chip)

        sums_copy(unit).start()

    def weight_step(turn):
        @pl.when(turn < units)
        def _():
            weight_unit(turn)

        @pl.when((turn >= 1) & (turn <= units))
        def _():
            sum_over_cores(turn - 1)

        @pl.when(turn >= 2)
        def _():
            sum_over_chips(turn - 2)

    for chain in range(2):

        def first(j, carry):
            value = term(chain, at(half), j).astype(BF)
            outgoing[chain, 0, halves[0], tile(j)] = value[:cut]
            outgoing[chain, 1, halves[1], tile(j)] = value[cut:]
            return carry

        lax.fori_loop(0, width // TILE, first, 0)
        for direction in range(2):
            scattered(chain, direction, 0).start()

    def scatter_step(step, carry):
        k = half - step
        for chain in range(2):
            for direction in range(2):
                slot = half + k if direction == 0 else k

                @pl.when(step == 1)
                def _():
                    scattered(chain, direction, 0).wait()

                @pl.when(step > 1)
                def _():
                    scattered(chain, direction, step - 1).wait()
                    pl.semaphore_wait(credit.at[chain, direction], 1)

                def add(j, carry):
                    value = term(chain, at(slot), j)
                    value += incoming[chain, direction, (step - 1) % 2, :, tile(j)].astype(F32)
                    outgoing[chain, direction, :, tile(j)] = value.astype(BF)
                    return carry

                lax.fori_loop(0, width // TILE, add, 0)
                scattered(chain, direction, step).start()

                @pl.when(step < half - 1)
                def _():
                    pl.semaphore_signal(
                        credit.at[chain, direction],
                        inc=1,
                        device_id={"shard": neighbours[1 - direction]},
                        device_id_type=pl.DeviceIdType.MESH,
                    )

        lax.fori_loop(
            (step - 1) * per_step,
            jnp.minimum(step * per_step, units + 2),
            lambda turn, c: (weight_step(turn), c)[1],
            0,
        )
        return carry

    lax.fori_loop(1, half, scatter_step, 0)

    for chain, result in enumerate((grad_ref, branch_ref)):
        for direction in range(2):
            scattered(chain, direction, half - 1).wait()

        def result_copy(j):
            return pltpu.make_async_copy(
                result_tile.at[j % 2], result.at[:, tile(j)], result_sem.at[j % 2]
            )

        def last(j, carry):
            @pl.when(j >= 2)
            def _():
                result_copy(j - 2).wait()

            value = term(chain, at(0), j)
            for direction in range(2):
                value += incoming[chain, direction, (half - 1) % 2, :, tile(j)].astype(F32)
            result_tile[j % 2] = value
            result_copy(j).start()
            return carry

        lax.fori_loop(0, width // TILE, last, 0)
        for j in (width // TILE - 2, width // TILE - 1):
            result_copy(j).wait()

    for unit in (units - 2, units - 1):
        sums_copy(unit).wait()
    for which, direction in both_ways:
        lax.fori_loop(
            1,
            half,
            lambda step, c: (gathered(which, direction, step).wait_send(), c)[1],
            0,
        )
        gathered_last(which, direction).wait_send()


def feed_forward_bytes(count, rows, width, ff):
    tokens = count * rows
    return 2 * (
        tokens * (2 * width + 3 * ff)
        + 3 * width * ff
        + TILE * tokens
        + 5 * TILE * width
        + 12 * rows * width
        + 4 * TILE * rows
    )


def feed_forward(count, normed, low, w_both, w_down):
    rows, width = normed.shape
    ff = w_down.shape[0]
    tokens = count * rows
    half = count // 2
    quarter = TILE // 4
    here = pl.BlockSpec(memory_space=pl.ANY)
    dma = pltpu.SemaphoreType.DMA
    return pl.pallas_call(
        functools.partial(feed_forward_kernel, count),
        in_specs=[here] * 4,
        out_specs=[here] * 3,
        out_shape=[
            jax.ShapeDtypeStruct((rows, width), F32),
            jax.ShapeDtypeStruct((rows, width), F32),
            jax.ShapeDtypeStruct(((width + ff) // TILE, quarter, width), BF),
        ],
        scratch_shapes=[
            pltpu.VMEM((tokens, width), BF),
            pltpu.VMEM((tokens, width), BF),
            pltpu.VMEM((tokens, ff), BF),
            pltpu.VMEM((tokens, 2 * ff), BF),
            pltpu.VMEM((width, 2 * ff), BF),
            pltpu.VMEM((ff, width), BF),
            pltpu.VMEM((TILE, tokens), BF),
            pltpu.VMEM((2, 2, 2, quarter, width), BF),
            pltpu.VMEM((2, 2, quarter, width), BF),
            pltpu.VMEM((2, 2, quarter, width), BF),
            pltpu.VMEM((2, quarter, width), BF),
            pltpu.VMEM((2, quarter, width), BF),
            pltpu.VMEM((2, rows, TILE), F32),
            pltpu.VMEM((2, 2, rows, width), BF),
            pltpu.VMEM((2, 2, 2, rows, width), BF),
            dma((4,)),
            dma((2, 2, half)),
            dma((2, 2, half)),
            dma((2, 2, half)),
            dma((2, 2, half)),
            pltpu.SemaphoreType.REGULAR((2, 2)),
            dma((2,)),
            dma((2,)),
            dma((2,)),
            dma((2,)),
            pltpu.SemaphoreType.REGULAR((2,)),
            dma((2,)),
            dma((2,)),
        ],
        compiler_params=pltpu.CompilerParams(
            collective_id=0, has_side_effects=True, vmem_limit_bytes=VMEM_BYTES
        ),
        cost_estimate=pl.CostEstimate(
            flops=18 * tokens * width * ff, bytes_accessed=50 * 10**6, transcendentals=tokens * ff
        ),
    )(normed, low, w_both, w_down)


def back_kernel(
    count,
    sums_ref,
    mid_low_ref,
    grad_middle_ref,
    gain_two_ref,
    attended_ref,
    query_ref,
    key_ref,
    value_ref,
    tokens_ref,
    gains_ref,
    cos_ref,
    sin_ref,
    segc_ref,
    segr_ref,
    qkv_all_ref,
    out_all_ref,
    gate_grad_ref,
    up_grad_ref,
    down_grad_ref,
    out_grad_ref,
    qkv_grad_ref,
    grad_input_ref,
    gain_grad_ref,
    turned,
    grad_attended,
    grads,
    weight_tile,
    to_core,
    from_core_out,
    from_core_qkv,
    outgoing,
    incoming_out,
    incoming_qkv,
    summed,
    from_chip,
    finished,
    gain_terms,
    gains_in,
    gain_parts,
    gain_swaps,
    own_sem,
    tile_sem,
    across_send,
    across_recv,
    group_send,
    group_recv,
    core_send,
    core_recv,
    ring_send,
    ring_recv,
    chip_send,
    chip_recv,
    last_send,
    last_recv,
    gain_send,
    gain_recv,
    swap_send,
    swap_recv,
):
    half = count // 2
    me, rep = lax.axis_index("shard"), lax.axis_index("rep")
    core = rep % 2
    place = ring_place(count, me)
    others = [ring_shard(count, place + k) for k in range(1, count)]
    near = ({"shard": ring_shard(count, place + 1)}, {"shard": ring_shard(count, place - 1)})
    other_core, other_chip = {"rep": core_partner(rep)}, {"rep": chip_partner(rep)}
    rows, width = tokens_ref.shape
    own_rows = width // count
    strip = own_rows // 2
    cut = strip // 2
    ff_own = gate_grad_ref.shape[2] // count
    wides = (width, grads.shape[1])
    from_core = (from_core_out, from_core_qkv)
    incoming = (incoming_out, incoming_qkv)
    result_refs = (out_grad_ref, qkv_grad_ref)
    right = (mid_low_ref, grads)

    def tile(j, size=TILE):
        return pl.ds(pl.multiple_of(j * size, size), size)

    gate_up = (gate_grad_ref, up_grad_ref)

    def own_columns(shard):
        return pl.ds(pl.multiple_of(shard * ff_own, 128), ff_own)

    def across(k, which):
        there = others[k - 1]
        return remote_copy(
            sums_ref.at[there, :, pl.ds(which * ff_own, ff_own)],
            gate_up[which].at[rep, :, own_columns(me)],
            across_send.at[which, k - 1],
            across_recv.at[which, k - 1],
            {"shard": there},
        )

    down_own = sums_ref.at[pl.ds(count, down_grad_ref.shape[0])]
    keep = [
        pltpu.make_async_copy(
            sums_ref.at[me, :, pl.ds(which * ff_own, ff_own)],
            gate_up[which].at[rep, :, own_columns(me)],
            own_sem.at[which],
        )
        for which in range(2)
    ]
    keep.append(pltpu.make_async_copy(down_own, down_grad_ref.at[:, rep], own_sem.at[2]))

    def group_copy(which, index):
        quarter = chip_partner(rep) if index == 2 else rep
        if which == 2:
            dst = down_grad_ref.at[:, quarter]
            src = dst if index == 2 else down_own
        else:
            dst = src = gate_up[which].at[quarter]
        return remote_copy(
            src,
            dst,
            group_send.at[which, index],
            group_recv.at[which, index],
            other_chip if index == 0 else other_core,
        )

    def shard_of(k):
        return ring_shard(count, place + k)

    def core_copy(i, k):
        slot = k + half - 1
        return remote_copy(
            to_core.at[slot, :, pl.ds(0, wides[i])],
            from_core[i].at[slot],
            core_send.at[i, slot],
            core_recv.at[i, slot],
            other_core,
        )

    def left_rows(k, which_core):
        start = shard_of(k) * own_rows + which_core * strip
        return turned[pl.ds(pl.multiple_of(start, strip), strip), :]

    def for_other_core(i):
        for k in [half] + [s * j for j in range(half - 1, 0, -1) for s in (1, -1)] + [0]:
            slot = k + half - 1
            if i == 1:
                core_copy(0, k).wait_send()

            def body(j, carry):
                value = dot(left_rows(k, 1 - core), right[i][:, tile(j, WIDE_TILE)])
                to_core[slot, :, tile(j, WIDE_TILE)] = value.astype(BF)
                return carry

            lax.fori_loop(0, wides[i] // WIDE_TILE, body, 0)
            core_copy(i, k).start()

    def strip_sum(i, k, extra, store):
        core_copy(i, k).wait_recv()

        def body(j, carry):
            at = tile(j, WIDE_TILE)
            value = dot(left_rows(k, core), right[i][:, at])
            value += from_core[i][k + half - 1, :, at].astype(F32)
            for direction, step in extra:
                value += incoming[i][direction, step, :, at].astype(F32)
            store(at, value.astype(BF))
            return carry

        lax.fori_loop(0, wides[i] // WIDE_TILE, body, 0)

    def ring_copy(i, direction, step):
        at = pl.ds(direction * cut, cut) if step == 0 else pl.ds(0, strip)
        return remote_copy(
            outgoing.at[i, direction, at, pl.ds(0, wides[i])],
            incoming[i].at[direction, step, at],
            ring_send.at[i, direction, step],
            ring_recv.at[i, direction, step],
            near[direction],
        )

    def ring_step(i, step):
        if step == 0:

            def store(at, value):
                outgoing[i, 0, pl.ds(0, cut), at] = value[:cut]
                outgoing[i, 1, pl.ds(cut, cut), at] = value[cut:]

            strip_sum(i, half, (), store)
            for direction in range(2):
                ring_copy(i, direction, 0).start()
            return
        for direction in range(2):
            ring_copy(i, direction, step - 1).wait()

            def store(at, value):
                outgoing[i, direction, :, at] = value

            k = half - step if direction == 0 else step - half
            strip_sum(i, k, ((direction, step - 1),), store)
            ring_copy(i, direction, step).start()

    def chip_copy(i):
        return remote_copy(
            summed.at[i, :, pl.ds(0, wides[i])],
            from_chip.at[i, :, pl.ds(0, wides[i])],
            chip_send.at[i],
            chip_recv.at[i],
            other_chip,
        )

    def ring_end(i):
        for direction in range(2):
            ring_copy(i, direction, half - 1).wait()

        def store(at, value):
            summed[i, :, at] = value

        strip_sum(i, 0, tuple((d, half - 1) for d in range(2)), store)
        chip_copy(i).start()

    own_strip = pl.ds(pl.multiple_of(core * strip, strip), strip)

    def last_copies(i):
        src = finished.at[i, :, pl.ds(0, wides[i])]
        dst = result_refs[i].at[own_strip]
        return (
            pltpu.make_async_copy(src, dst, own_sem.at[3 + i]),
            remote_copy(src, dst, last_send.at[i], last_recv.at[i], other_core),
        )

    def group_end(i):
        chip_copy(i).wait()
        at = pl.ds(0, wides[i])
        total = summed[i, :, at].astype(F32) + from_chip[i, :, at].astype(F32)
        finished[i, :, at] = total.astype(BF)
        for copy in last_copies(i):
            copy.start()

    def gain_copy(k):
        return remote_copy(
            gain_terms.at[:, tile(others[k - 1], own_rows)],
            gains_in.at[k],
            gain_send.at[k - 1],
            gain_recv.at[k - 1],
            {"shard": others[k - 1]},
        )

    def gain_swap(index):
        return remote_copy(
            gain_parts.at[index],
            gain_swaps.at[index],
            swap_send.at[index],
            swap_recv.at[index],
            (other_core, other_chip)[index],
        )

    def weight_load(ref, j, wide):
        return pltpu.make_async_copy(
            ref.at[tile(j)], weight_tile.at[j % 2, :, pl.ds(0, wide)], tile_sem.at[j % 2]
        )

    def times_transposed(left, ref, wide, store):
        blocks = width // TILE

        def body(j, carry):
            @pl.when(j + 1 < blocks)
            def _():
                weight_load(ref, j + 1, wide).start()

            weight_load(ref, j, wide).wait()
            store(tile(j), contract_last(left[...], weight_tile[j % 2, :, pl.ds(0, wide)]))
            return carry

        lax.fori_loop(0, blocks, body, 0)

    def turn(array):
        def body(j, carry):
            turned[tile(j), :] = array[:, tile(j)].T
            return carry

        lax.fori_loop(0, width // TILE, body, 0)

    cosine, sine = cos_ref[...], -sin_ref[...]
    wide, thin = 2 * GROUP * HEAD_SIZE, 2 * HEAD_SIZE
    key_at, value_at = width, width + key_ref.shape[1]

    def heads_pair(pair):
        allowed = allowed_rows(segc_ref[...], segr_ref[...])
        wide_at, thin_at = pl.ds(pair * wide, wide), pl.ds(pair * thin, thin)
        query, grad = query_ref[:, wide_at], grad_attended[:, wide_at]
        key, value = key_ref[:, thin_at], value_ref[:, thin_at]
        heads, keys, values = [], [], []
        for j in range(2):
            cols = slice(j * HEAD_SIZE, (j + 1) * HEAD_SIZE)
            query_rows, grad_rows = stack_heads(query, j), stack_heads(grad, j)
            probs = softmax_rows(query_rows, key[:, cols], allowed)
            grad_probs = contract_last(grad_rows, value[:, cols])
            grad_scores = (
                probs * (grad_probs - jnp.sum(probs * grad_probs, -1, keepdims=True))
            ).astype(BF)
            heads += unstack_heads(dot(grad_scores, key[:, cols]) * HEAD_SIZE ** (-0.5))
            keys.append(contract_first(grad_scores, query_rows) * HEAD_SIZE ** (-0.5))
            values.append(contract_first(probs.astype(BF), grad_rows))
        grads[:, wide_at] = rotate(jnp.concatenate(heads, 1), cosine, sine).astype(BF)
        grads[:, pl.ds(key_at + pair * thin, thin)] = rotate(
            jnp.concatenate(keys, 1), cosine, sine
        ).astype(BF)
        grads[:, pl.ds(value_at + pair * thin, thin)] = jnp.concatenate(values, 1).astype(BF)

    for copy in keep:
        copy.start()
    for i in range(2):
        for direction in range(2):
            blank = pl.ds((1 - direction) * cut, cut)
            incoming[i][direction, 0, blank] = jnp.zeros((cut, wides[i]), BF)

    greet([{"shard": shard} for shard in others] + [other_core, other_chip])

    for k in range(1, count):
        for which in range(2):
            across(k, which).start()
    group_copy(2, 0).start()
    group_copy(2, 1).start()
    weight_load(out_all_ref, 0, width).start()
    turn(attended_ref)
    for_other_core(0)
    ring_step(0, 0)

    def store_attended(at, value):
        grad_attended[:, at] = value.astype(BF)

    times_transposed(mid_low_ref, out_all_ref, width, store_attended)
    weight_load(qkv_all_ref, 0, wides[1]).start()
    ring_step(0, 1)
    pairs = KEY_VALUE_HEADS // 2
    for pair in range(max(pairs, half - 1)):
        if pair < pairs:
            heads_pair(pair)
        if pair + 2 < half:
            ring_step(0, pair + 2)
        elif pair + 2 == half:
            ring_end(0)

    unit, scale_row = normalize(tokens_ref[...].astype(F32))
    gain = gains_ref[0:1, :]
    grad_attended[...] = (unit * gain).astype(BF)
    turn(grad_attended)
    for_other_core(1)
    ring_step(1, 0)

    for copy in keep:
        copy.wait()
    for k in range(1, count):
        for which in range(2):
            across(k, which).wait_recv()
    for which in range(2):
        for index in range(2):
            group_copy(which, index).start()
    group_copy(2, 0).wait_recv()
    group_copy(2, 2).start()
    group_end(0)

    ring_step(1, 1)

    def store_input(at, value):
        grad_input_ref[:, at] = value

    times_transposed(grads, qkv_all_ref, wides[1], store_input)
    if half > 2:
        ring_step(1, 2)
    unit, scale_row = normalize(tokens_ref[...].astype(F32))
    grad_normed = grad_input_ref[...]
    gain_terms[...] = jnp.zeros_like(gain_terms)
    gain_terms[0:1, :] = jnp.sum(grad_normed * unit, 0, keepdims=True)
    gain_terms[1:2, :] = gain_two_ref[...]
    for k in range(1, count):
        gain_copy(k).start()
    grad_input_ref[...] = grad_middle_ref[...] + norm_back(grad_normed * gain, unit, scale_row)
    for step in range(3, half):
        ring_step(1, step)
    for which in range(2):
        group_copy(which, 0).wait_recv()
        group_copy(which, 2).start()
    total = gain_terms[:, tile(me, own_rows)]
    for k in range(1, count):
        gain_copy(k).wait_recv()
        total += gains_in[k]
    gain_parts[0] = total
    gain_swap(0).start()
    ring_end(1)
    gain_swap(0).wait()
    gain_parts[1] = gain_parts[0] + gain_swaps[0]
    gain_swap(1).start()
    group_end(1)
    gain_swap(1).wait()
    gain_grad_ref[...] = gain_parts[1] + gain_swaps[1]

    for i in range(2):
        kept, passed = last_copies(i)
        kept.wait()
        passed.wait()
        for k in range(-(half - 1), half + 1):
            if i == 1:
                core_copy(i, k).wait_send()
    for which in range(3):
        for index in range(3):
            if index > 0:
                group_copy(which, index).wait_recv()
            group_copy(which, index).wait_send()
    for k in range(1, count):
        gain_copy(k).wait_send()
        for which in range(2):
            across(k, which).wait_send()


def back(
    count,
    sums,
    mid_low,
    grad_middle,
    gain_two_term,
    attended,
    query,
    key,
    value,
    tokens,
    gains,
    tables,
    qkv_all,
    out_all,
):
    rows, width = tokens.shape
    qkv_width = qkv_all.shape[1]
    own_rows = width // count
    strip, quarter = own_rows // 2, own_rows // 4
    ff_own = sums.shape[2] // 2
    half = count // 2
    here = pl.BlockSpec(memory_space=pl.ANY)
    inside = pl.BlockSpec(memory_space=pltpu.VMEM)
    kind = jax.ShapeDtypeStruct
    dma = pltpu.SemaphoreType.DMA
    vmem = pltpu.VMEM
    return pl.pallas_call(
        functools.partial(back_kernel, count),
        in_specs=[here] + [inside] * 13 + [here] * 2,
        out_specs=[here] * 5 + [inside] * 2,
        out_shape=[
            kind((4, quarter, count * ff_own), BF),
            kind((4, quarter, count * ff_own), BF),
            kind((ff_own // own_rows, 4, quarter, width), BF),
            kind((own_rows, width), BF),
            kind((own_rows, qkv_width), BF),
            kind((rows, width), F32),
            kind((8, own_rows), F32),
        ],
        scratch_shapes=[
            vmem((width, rows), BF),
            vmem((rows, width), BF),
            vmem((rows, qkv_width), BF),
            vmem((2, TILE, qkv_width), BF),
            vmem((count, strip, qkv_width), BF),
            vmem((count, strip, width), BF),
            vmem((count, strip, qkv_width), BF),
            vmem((2, 2, strip, qkv_width), BF),
            vmem((2, half, strip, width), BF),
            vmem((2, half, strip, qkv_width), BF),
            vmem((2, strip, qkv_width), BF),
            vmem((2, strip, qkv_width), BF),
            vmem((2, strip, qkv_width), BF),
            vmem((8, width), F32),
            vmem((count, 8, own_rows), F32),
            vmem((2, 8, own_rows), F32),
            vmem((2, 8, own_rows), F32),
            dma((5,)),
            dma((2,)),
            dma((2, count - 1)),
            dma((2, count - 1)),
            dma((3, 3)),
            dma((3, 3)),
            dma((2, count)),
            dma((2, count)),
            dma((2, 2, half)),
            dma((2, 2, half)),
            dma((2,)),
            dma((2,)),
            dma((2,)),
            dma((2,)),
            dma((count - 1,)),
            dma((count - 1,)),
            dma((2,)),
            dma((2,)),
        ],
        compiler_params=pltpu.CompilerParams(
            collective_id=2, has_side_effects=True, vmem_limit_bytes=VMEM_BYTES
        ),
        cost_estimate=pl.CostEstimate(
            flops=4 * rows * width * (qkv_width + width) + 4 * 10**9,
            bytes_accessed=60 * 10**6,
            transcendentals=2 * 10**6,
        ),
    )(
        sums,
        mid_low,
        grad_middle,
        gain_two_term,
        attended,
        query,
        key,
        value,
        tokens,
        gains,
        *tables,
        qkv_all,
        out_all,
    )


def feed_forward_parts(ring, normed_two, grad_low, w_both, w_down):
    sequence, ff_own = normed_two.shape[0], w_down.shape[0]
    low_all, normed_all = run(ring.gather(grad_low), ring.gather(normed_two))
    hidden, grad_both = {}, {}
    for k in normed_all:
        both = dot(normed_all[k], w_both)
        gate, up = both[:, :ff_own], both[:, ff_own:]
        grad_hidden = contract_last(low_all[k], w_down)
        sigmoid = jax.nn.sigmoid(gate)
        silu = gate * sigmoid
        hidden[k] = (silu * up).astype(BF)
        grad_gate = (grad_hidden * up * sigmoid * (1.0 + gate * (1.0 - sigmoid))).astype(BF)
        grad_up = (grad_hidden * silu).astype(BF)
        grad_both[k] = jnp.concatenate([grad_gate, grad_up], 1)

    def terms_of(chunks, product):
        def terms(ks):
            sources = [k if k == ring.half else -k for k in ks]
            whole = product(jnp.concatenate([chunks[k] for k in sources], 0))
            return [whole[i * sequence : (i + 1) * sequence] for i in range(len(ks))]

        return terms

    (grad_normed_two,) = run(ring.scatter(terms_of(grad_both, lambda a: contract_last(a, w_both))))
    (branch_two,) = run(ring.scatter(terms_of(hidden, lambda a: dot(a, w_down))))
    keys = list(normed_all)
    together = lambda parts: jnp.concatenate([parts[k] for k in keys], 0)
    both_term = contract_first(together(normed_all), together(grad_both))
    down_term = contract_first(together(hidden), together(low_all))
    return grad_normed_two, branch_two, both_term, down_term


def swap(array, bit):
    return lax.ppermute(array, "rep", [(i, i ^ bit) for i in range(4)])


def cols(array, start, width):
    return lax.dynamic_slice_in_dim(array, start, width, 1)


def rows_of(array, start, height):
    return lax.dynamic_slice_in_dim(array, start, height, 0)


def put(array, piece, start, axis):
    return lax.dynamic_update_slice_in_dim(array, piece, start, axis)


def gather_rows(ring, array):
    rows = array.shape[0]
    (parts,) = run(ring.gather(array))
    full = jnp.zeros((ring.count * rows, array.shape[1]), array.dtype)
    for k, part in parts.items():
        full = put(full, part, ring.at(-k) * rows, 0)
    return full


def front_parts(ring, tokens, gains_own, tables, qkv_own, w_out, w_gate, w_up, wide_k):
    count, own_rows = ring.count, qkv_own.shape[0]
    rep = lax.axis_index("rep")
    ff_own = w_gate.shape[1] // count
    width = tokens.shape[1]
    gains = jnp.zeros((gains_own.shape[0], width), F32)
    for k in range(count):
        piece = ring.send(gains_own, k) if k else gains_own
        gains = put(gains, piece, ring.at(-k) * own_rows, 1)
    qkv_all, out_all = gather_rows(ring, qkv_own), gather_rows(ring, w_out)
    quarter = own_rows // 4
    gate_rows = rows_of(w_gate, rep * quarter, quarter)
    up_rows = rows_of(w_up, rep * quarter, quarter)
    sends = []
    for k in range(count):
        dest = ring.at(k) * ff_own
        piece = jnp.concatenate([cols(gate_rows, dest, ff_own), cols(up_rows, dest, ff_own)], 1)
        sends.append((piece, k))
    fetched = jnp.zeros((count, quarter, 2 * ff_own), BF)
    for k, piece in enumerate([sends[0][0]] + ring.queue(*sends[1:])):
        fetched = put(fetched, piece[None], ring.at(-k), 0)
    pieces = [fetched, swap(fetched, 2)]
    pieces += [swap(piece, 1) for piece in pieces]
    w_both = jnp.zeros((count, 4, quarter, 2 * ff_own), BF)
    for bits, piece in zip((0, 2, 1, 3), pieces):
        w_both = put(w_both, piece[:, None], rep ^ bits, 1)
    resid = tokens.astype(F32)
    unit, _ = normalize(resid)
    linear = dot((unit * gains[:1]).astype(BF), qkv_all)
    query, key, value, attended = attend(
        linear[:, :width], linear[:, width : width + wide_k], linear[:, width + wide_k :], tables
    )
    middle = resid + dot(attended, out_all)
    unit, _ = normalize(middle)
    normed_two = (unit * gains[1:2]).astype(BF)
    return qkv_all, out_all, w_both, gains, query, key, value, attended, middle, normed_two


def back_parts(
    ring,
    both_term,
    down_term,
    mid_low,
    grad_middle,
    gain_two_term,
    attended,
    query,
    key,
    value,
    tokens,
    gains,
    tables,
    qkv_all,
    out_all,
):
    count = ring.count
    rep = lax.axis_index("rep")
    core, chip = rep % 2, rep // 2
    width = tokens.shape[1]
    own_rows = width // count
    quarter = own_rows // 4
    ff_own = both_term.shape[1] // 2
    ff = ff_own * count

    def order_halves(mine, other):
        first = core == 0
        return jnp.where(first, mine, other), jnp.where(first, other, mine)

    def sum_cores(array, half_of):
        keep, pass_on = half_of(array, core), half_of(array, 1 - core)
        return keep.astype(F32) + swap(pass_on.astype(BF), 1).astype(F32)

    both_term = both_term.reshape(count, 2, 2, quarter, 2 * ff_own)
    both_half = sum_cores(
        both_term, lambda a, c: lax.dynamic_index_in_dim(a, c, 2, keepdims=False)
    )
    keep = lax.dynamic_index_in_dim(both_half, chip, 1, keepdims=False)
    pass_on = lax.dynamic_index_in_dim(both_half, 1 - chip, 1, keepdims=False)
    both_quarter = (keep + swap(pass_on.astype(BF), 2).astype(F32)).astype(BF)
    gate_quarter = jnp.zeros((quarter, ff), BF)
    up_quarter = jnp.zeros((quarter, ff), BF)
    sends = [
        (lax.dynamic_index_in_dim(both_quarter, ring.at(k), 0, keepdims=False), k)
        for k in range(count)
    ]
    for k, piece in enumerate([sends[0][0]] + ring.queue(*sends[1:])):
        start = ring.at(-k) * ff_own
        gate_quarter = put(gate_quarter, piece[:, :ff_own], start, 1)
        up_quarter = put(up_quarter, piece[:, ff_own:], start, 1)

    def collect(quarter_rows):
        parts = [quarter_rows, swap(quarter_rows, 2)]
        parts += [swap(part, 1) for part in parts]
        full = jnp.zeros((4 * quarter, ff), BF)
        for bits, part in zip((0, 2, 1, 3), parts):
            full = put(full, part, (rep ^ bits) * quarter, 0)
        return full

    gate_grad, up_grad = collect(gate_quarter), collect(up_quarter)

    down_half = sum_cores(
        down_term, lambda a, c: rows_of(a, c * (a.shape[0] // 2), a.shape[0] // 2)
    ).astype(BF)
    down_half = (down_half.astype(F32) + swap(down_half, 2).astype(F32)).astype(BF)
    down_grad = jnp.concatenate(order_halves(down_half, swap(down_half, 1)), 0)

    def part_sums(left, grads):
        wide = grads.shape[1] // 2
        grads_mine, grads_other = cols(grads, core * wide, wide), cols(grads, (1 - core) * wide, wide)

        def terms(ks):
            blocks = [cols(left, ring.at(k) * own_rows, own_rows) for k in ks]
            block = blocks[0] if len(ks) == 1 else jnp.concatenate(blocks, 1)
            other = swap(contract_first(block, grads_other).astype(BF), 1)
            whole = contract_first(block, grads_mine) + other.astype(F32)
            return [whole[i * own_rows : (i + 1) * own_rows] for i in range(len(ks))]

        mine = run(ring.scatter(terms))[0].astype(BF)
        mine = (mine.astype(F32) + swap(mine, 2).astype(F32)).astype(BF)
        return jnp.concatenate(order_halves(mine, swap(mine, 1)), 1)

    out_grad = part_sums(attended, mid_low)
    grad_attended = contract_last(mid_low, out_all).astype(BF)
    grads = jnp.concatenate(attend_back(query, key, value, grad_attended, tables), 1)
    unit_one, scale_one = normalize(tokens.astype(F32))
    gain_one = gains[:1]
    qkv_grad = part_sums((unit_one * gain_one).astype(BF), grads)
    grad_normed_one = contract_last(grads, qkv_all)
    gain_one_term = jnp.sum(grad_normed_one * unit_one, 0, keepdims=True)
    grad_input = grad_middle + norm_back(grad_normed_one * gain_one, unit_one, scale_one)

    gain_terms = jnp.concatenate([gain_one_term, gain_two_term], 0)
    gain_sums = cols(gain_terms, ring.at(0) * own_rows, own_rows)
    for k in range(1, count):
        gain_sums = gain_sums + ring.send(cols(gain_terms, ring.at(k) * own_rows, own_rows), k)
    gain_sums = gain_sums + swap(gain_sums, 1)
    gain_sums = gain_sums + swap(gain_sums, 2)
    return gate_grad, up_grad, down_grad, out_grad, qkv_grad, grad_input, gain_sums


def on_device(
    count,
    tokens,
    segments,
    norm_attn,
    w_query,
    key_weight,
    value_weight,
    w_out,
    norm_mlp,
    w_gate,
    w_up,
    w_down,
    cotangent,
):
    ring = Ring(count)
    sequence, width = tokens.shape[1], tokens.shape[2]
    own_rows = w_query.shape[0]
    ff = w_gate.shape[1]
    ff_own = ff // count
    wide_k = key_weight.shape[1]
    fits = feed_forward_bytes(count, sequence, width, ff_own) <= VMEM_BYTES
    kernels = fits and sequence == own_rows == TILE

    grad_output = cotangent.reshape(sequence, width)
    grad_low = grad_output.astype(BF)
    cosine, sine = rope_tables(segments)
    seg_row = segments.reshape(1, sequence)
    tables = (cosine, sine, seg_row.reshape(sequence, 1), seg_row)
    own = tokens.reshape(sequence, width)
    qkv_own = jnp.concatenate([w_query, key_weight, value_weight], 1)
    gains_own = jnp.zeros((8, own_rows), F32)
    gains_own = gains_own.at[0].set(norm_attn.astype(F32)).at[1].set(norm_mlp.astype(F32))
    bring = functools.partial(front, count) if kernels else functools.partial(front_parts, ring)
    qkv_all, out_all, w_both, gains, query, key, value, attended, middle, normed_two = bring(
        own, gains_own, tables, qkv_own, w_out, w_gate, w_up, wide_k
    )
    w_both = w_both.reshape(width, 2 * ff_own)
    gain_one, gain_two = gains[:1], gains[1:2]

    if kernels:
        grad_normed_two, branch_two, sums = feed_forward(count, normed_two, grad_low, w_both, w_down)
    else:
        grad_normed_two, branch_two, both_term, down_term = feed_forward_parts(
            ring, normed_two, grad_low, w_both, w_down
        )
    output = middle + branch_two

    unit_two, scale_two = normalize(middle)
    gain_two_term = jnp.sum(grad_normed_two * unit_two, 0, keepdims=True)
    grad_middle = grad_output + norm_back(grad_normed_two * gain_two, unit_two, scale_two)
    grad_mid_low = grad_middle.astype(BF)

    if kernels:
        gate_grad, up_grad, down_grad, out_grad, qkv_grad, grad_input, gain_sums = back(
            count,
            sums,
            grad_mid_low,
            grad_middle,
            gain_two_term,
            attended,
            query,
            key,
            value,
            own,
            gains,
            tables,
            qkv_all,
            out_all,
        )
    else:
        gate_grad, up_grad, down_grad, out_grad, qkv_grad, grad_input, gain_sums = back_parts(
            ring,
            both_term,
            down_term,
            grad_mid_low,
            grad_middle,
            gain_two_term,
            attended,
            query,
            key,
            value,
            own,
            gains,
            tables,
            qkv_all,
            out_all,
        )
    qkv_grad = qkv_grad.astype(F32)

    return (
        output.reshape(tokens.shape),
        grad_input.reshape(tokens.shape),
        gain_sums[0],
        qkv_grad[:, :width],
        qkv_grad[:, width : width + wide_k],
        qkv_grad[:, width + wide_k :],
        out_grad.astype(F32),
        gain_sums[1],
        gate_grad.reshape(own_rows, ff).astype(F32),
        up_grad.reshape(own_rows, ff).astype(F32),
        down_grad.reshape(ff_own, width).astype(F32),
    )


def solution(mesh):
    row, vector, matrix = P(("shard", "rep"), None, None), P("shard"), P("shard", None)
    in_specs = (row, P(("shard", "rep"), None), vector, matrix, matrix, matrix, matrix, vector)
    in_specs += (matrix, matrix, matrix, row)
    out_specs = (row, row, vector, matrix, matrix, matrix, matrix, vector, matrix, matrix, matrix)
    return jax.shard_map(
        functools.partial(on_device, mesh.shape["shard"]),
        mesh=mesh,
        in_specs=in_specs,
        out_specs=out_specs,
        check_vma=False,
    )
```

```python
import functools

import jax
import jax.numpy as jnp
from jax import lax
from jax.experimental import pallas as pl
from jax.experimental.pallas import tpu as pltpu
from jax.sharding import PartitionSpec as P

QUERY_HEADS = 32
KEY_VALUE_HEADS = 8
HEAD_SIZE = 64
GROUP = QUERY_HEADS // KEY_VALUE_HEADS

epsilon = 1e-05
masked_score = -1000000000.0
rope_base = 500000.0
WINDOW = 2
TILE = 256
WIDE_TILE = 512
LOAD_TILE = 128
VMEM_BYTES = 62 * 2**20
BF = jnp.bfloat16
F32 = jnp.float32


def dot(left, right):
    return jnp.dot(left, right, preferred_element_type=F32)


def contract_last(left, right):
    return lax.dot_general(left, right, (((1,), (1,)), ((), ())), preferred_element_type=F32)


def contract_first(left, right):
    return lax.dot_general(left, right, (((0,), (0,)), ((), ())), preferred_element_type=F32)


def positions(segment_ids):
    index = lax.broadcasted_iota(jnp.int32, segment_ids.shape, 1)
    first = jnp.concatenate(
        [
            jnp.ones_like(segment_ids[:, :1]),
            (segment_ids[:, 1:] != segment_ids[:, :-1]).astype(jnp.int32),
        ],
        1,
    )
    starts = lax.cummax(jnp.where(first > 0, index, 0), axis=1)
    return (index - starts).astype(F32)


def rope_tables(segment_ids):
    half = HEAD_SIZE // 2
    inverse = rope_base ** (-(2.0 * jnp.arange(half, dtype=F32)) / HEAD_SIZE)
    angle = positions(segment_ids)[0, :, None] * inverse
    cosine, sine = jnp.cos(angle), jnp.sin(angle)
    return jnp.concatenate([cosine] * 4, 1), jnp.concatenate([-sine, sine] * 2, 1)


def normalize(rows):
    scale_row = lax.rsqrt(jnp.mean(rows * rows, -1, keepdims=True) + epsilon)
    return rows * scale_row, scale_row


def norm_back(grad_unit, unit, scale_row):
    return scale_row * (grad_unit - unit * jnp.mean(grad_unit * unit, -1, keepdims=True))


def rotate(block, cosine, sine):
    lane = lax.broadcasted_iota(jnp.int32, cosine.shape, 1)
    lower = lane % HEAD_SIZE < HEAD_SIZE // 2
    parts = []
    for at in range(0, block.shape[1], 128):
        part = block[:, at : at + 128]
        other = jnp.where(
            lower, pltpu.roll(part, 128 - HEAD_SIZE // 2, 1), pltpu.roll(part, HEAD_SIZE // 2, 1)
        )
        parts.append(part * cosine + other * sine)
    return parts[0] if len(parts) == 1 else jnp.concatenate(parts, 1)


def stack_heads(block, key_head):
    first = key_head * GROUP
    return jnp.concatenate(
        [block[:, (first + i) * HEAD_SIZE : (first + i + 1) * HEAD_SIZE] for i in range(GROUP)], 0
    )


def unstack_heads(rows):
    count = rows.shape[0] // GROUP
    return [rows[i * count : (i + 1) * count] for i in range(GROUP)]


def softmax_rows(query, key, allowed):
    raw = contract_last(query, key) * HEAD_SIZE ** (-0.5)
    scores = jnp.where(allowed, raw, masked_score)
    exponent = jnp.exp(scores - jnp.max(scores, -1, keepdims=True))
    return exponent / jnp.sum(exponent, -1, keepdims=True)


def allowed_rows(seg_column, seg_row):
    count = seg_row.shape[1]
    shape = (count, count)
    causal = lax.broadcasted_iota(jnp.int32, shape, 0) >= lax.broadcasted_iota(jnp.int32, shape, 1)
    one = ((seg_column == seg_row) & causal).astype(jnp.int32)
    return jnp.concatenate([one] * GROUP, 0) > 0


def attend_kernel(q_ref, k_ref, v_ref, cos_ref, sin_ref, segc_ref, segr_ref, qo, ko, vo, ao):
    cosine, sine = cos_ref[...], sin_ref[...]
    allowed = allowed_rows(segc_ref[...], segr_ref[...])
    query = rotate(q_ref[...], cosine, sine).astype(BF)
    key = rotate(k_ref[...], cosine, sine).astype(BF)
    value = v_ref[...].astype(BF)
    qo[...] = query
    ko[...] = key
    vo[...] = value
    heads = []
    for j in range(2):
        cols = slice(j * HEAD_SIZE, (j + 1) * HEAD_SIZE)
        probs = softmax_rows(stack_heads(query, j), key[:, cols], allowed).astype(BF)
        heads += unstack_heads(dot(probs, value[:, cols]).astype(BF))
    ao[...] = jnp.concatenate(heads, 1)


def attend_back_kernel(q_ref, k_ref, v_ref, g_ref, cos_ref, sin_ref, segc_ref, segr_ref, gq, gk, gv):
    cosine, sine = cos_ref[...], -sin_ref[...]
    allowed = allowed_rows(segc_ref[...], segr_ref[...])
    query, key, value, grad = q_ref[...], k_ref[...], v_ref[...], g_ref[...]
    heads, keys, values = [], [], []
    for j in range(2):
        cols = slice(j * HEAD_SIZE, (j + 1) * HEAD_SIZE)
        rows, grad_rows = stack_heads(query, j), stack_heads(grad, j)
        probs = softmax_rows(rows, key[:, cols], allowed)
        grad_probs = contract_last(grad_rows, value[:, cols])
        grad_scores = (
            probs * (grad_probs - jnp.sum(probs * grad_probs, -1, keepdims=True))
        ).astype(BF)
        heads += unstack_heads(dot(grad_scores, key[:, cols]) * HEAD_SIZE ** (-0.5))
        keys.append(contract_first(grad_scores, rows) * HEAD_SIZE ** (-0.5))
        values.append(contract_first(probs.astype(BF), grad_rows))
    gq[...] = rotate(jnp.concatenate(heads, 1), cosine, sine).astype(BF)
    gk[...] = rotate(jnp.concatenate(keys, 1), cosine, sine).astype(BF)
    gv[...] = jnp.concatenate(values, 1).astype(BF)


def attention_specs(count):
    wide = pl.BlockSpec((count, 2 * GROUP * HEAD_SIZE), lambda i: (0, i))
    thin = pl.BlockSpec((count, 2 * HEAD_SIZE), lambda i: (0, i))
    whole = lambda shape: pl.BlockSpec(shape, lambda i: (0, 0))
    fixed = [whole((count, 128)), whole((count, 128)), whole((count, 1)), whole((1, count))]
    return wide, thin, fixed


def attend(query_lin, key_lin, value_lin, tables):
    count = query_lin.shape[0]
    wide, thin, fixed = attention_specs(count)
    kinds = [jax.ShapeDtypeStruct(a.shape, BF) for a in (query_lin, key_lin, value_lin, query_lin)]
    return pl.pallas_call(
        attend_kernel,
        grid=(KEY_VALUE_HEADS // 2,),
        in_specs=[wide, thin, thin] + fixed,
        out_specs=[wide, thin, thin, wide],
        out_shape=kinds,
        compiler_params=pltpu.CompilerParams(vmem_limit_bytes=48 * 2**20),
        cost_estimate=pl.CostEstimate(
            flops=2 * 10**9, bytes_accessed=6 * 10**6, transcendentals=2 * 10**6
        ),
    )(query_lin, key_lin, value_lin, *tables)


def attend_back(query, key, value, grad, tables):
    count = query.shape[0]
    wide, thin, fixed = attention_specs(count)
    kinds = [jax.ShapeDtypeStruct(a.shape, BF) for a in (query, key, value)]
    return pl.pallas_call(
        attend_back_kernel,
        grid=(KEY_VALUE_HEADS // 2,),
        in_specs=[wide, thin, thin, wide] + fixed,
        out_specs=[wide, thin, thin],
        out_shape=kinds,
        compiler_params=pltpu.CompilerParams(vmem_limit_bytes=48 * 2**20),
        cost_estimate=pl.CostEstimate(
            flops=4 * 10**9, bytes_accessed=6 * 10**6, transcendentals=2 * 10**6
        ),
    )(query, key, value, grad, *tables)


def ring_order(count):
    return list(range(0, count, 2)) + list(range(count - 1, 0, -2)) if count % 2 == 0 else list(range(count))


class Ring:
    def __init__(self, count):
        self.count = count
        self.half = count // 2
        self.order = ring_order(count)
        inverse = [self.order.index(i) for i in range(count)]
        self.table = jnp.asarray(self.order, jnp.int32)
        self.turns = []
        self.place = jnp.asarray(inverse, jnp.int32)[lax.axis_index("shard")]

    def at(self, offset):
        return self.table[(self.place + offset + self.count) % self.count]

    def send(self, array, offset):
        n, order = self.count, self.order
        pairs = [(order[i], order[(i + offset) % n]) for i in range(n)]
        return lax.ppermute(array, "shard", pairs)

    def queue(self, *sends):
        arrays = [array for array, _ in sends]
        if len(self.turns) >= WINDOW:
            arrays, _ = lax.optimization_barrier((arrays, self.turns[-WINDOW]))
        got = [self.send(array, offset) for array, (_, offset) in zip(arrays, sends)]
        self.turns.append(got[:2])
        return got

    def gather(self, array):
        cut = array.shape[0] // 2
        ahead = back = array
        out = {0: array}
        for k in range(1, self.half):
            ahead, back = self.queue((ahead, 1), (back, -1))
            out[k], out[-k] = ahead, back
            yield out
        out[self.half] = jnp.concatenate(self.queue((ahead[:cut], 1), (back[cut:], -1)), 0)
        yield out

    def scatter(self, terms):
        (far,) = terms((self.half,))
        far = far.astype(BF)
        cut = far.shape[0] // 2
        ahead, back = self.queue((far[:cut], 1), (far[cut:], -1))
        yield None
        for k in range(self.half - 1, 0, -1):
            up, down = terms((k, -k))
            if k == self.half - 1:
                up = jnp.concatenate([up[:cut] + ahead.astype(F32), up[cut:]], 0)
                down = jnp.concatenate([down[:cut], down[cut:] + back.astype(F32)], 0)
            else:
                up, down = up + ahead.astype(F32), down + back.astype(F32)
            ahead, back = self.queue((up.astype(BF), 1), (down.astype(BF), -1))
            if k > 1:
                yield None
        (own,) = terms((0,))
        yield own + ahead.astype(F32) + back.astype(F32)


def run(*flows):
    flows = list(flows)
    last = [None] * len(flows)
    live = list(range(len(flows)))
    while live:
        for i in list(live):
            try:
                last[i] = next(flows[i])
            except StopIteration:
                live.remove(i)
    return last


def ring_place(count, shard):
    return jnp.where(shard % 2 == 0, shard // 2, count - 1 - shard // 2)


def ring_shard(count, place):
    place = (place + count) % count
    return jnp.where(place < count // 2, 2 * place, 2 * (count - 1 - place) + 1)


def core_partner(rep):
    return rep + 1 - 2 * (rep % 2)


def chip_partner(rep):
    return (rep + 2) % 4


def greet(devices):
    barrier = pltpu.get_barrier_semaphore()
    for device in devices:
        pl.semaphore_signal(
            barrier, inc=1, device_id=device, device_id_type=pl.DeviceIdType.MESH
        )
    pl.semaphore_wait(barrier, len(devices))


def remote_copy(src, dst, send, recv, device):
    return pltpu.make_async_remote_copy(
        src_ref=src,
        dst_ref=dst,
        send_sem=send,
        recv_sem=recv,
        device_id=device,
        device_id_type=pl.DeviceIdType.MESH,
    )


def front_kernel(
    count,
    tokens_ref,
    gains_ref,
    cotangent_ref,
    cos_ref,
    sin_ref,
    segc_ref,
    segr_ref,
    qkv_own_ref,
    out_own_ref,
    gate_ref,
    up_ref,
    qkv_all_ref,
    out_all_ref,
    both_ref,
    low_all_ref,
    gains_all_ref,
    query_ref,
    key_ref,
    value_ref,
    attended_ref,
    middle_ref,
    normed_two_ref,
    low_own,
    both_own,
    qkv_all,
    out_all,
    normed,
    linear,
    own_sem,
    load_sem,
    gain_send,
    gain_recv,
    ring_send,
    ring_recv,
    core_send,
    core_recv,
    chip_send,
    chip_recv,
    across_send,
    across_recv,
    group_send,
    group_recv,
    low_send,
    low_recv,
):
    half = count // 2
    me, rep = lax.axis_index("shard"), lax.axis_index("rep")
    core, chip = rep % 2, rep // 2
    place = ring_place(count, me)
    others = [ring_shard(count, place + k) for k in range(1, count)]
    near = ({"shard": ring_shard(count, place + 1)}, {"shard": ring_shard(count, place - 1)})
    other_core, other_chip = {"rep": core_partner(rep)}, {"rep": chip_partner(rep)}
    own_rows = qkv_own_ref.shape[0]
    quarter = own_rows // 4
    cut = quarter // 2
    ff_own = gate_ref.shape[1] // count
    rows, width = tokens_ref.shape
    full_refs = (qkv_all_ref, out_all_ref)
    own_refs = (qkv_own_ref, out_own_ref)
    inside = (qkv_all, out_all)

    def rows_at(start, size):
        return pl.ds(pl.multiple_of(start, cut), size)

    def shard_rows(shard):
        return rows_at(shard * own_rows, own_rows)

    def piece_of(shard, which_core, which_chip, part=None):
        start = shard * own_rows + (2 * which_core + which_chip) * quarter
        if part is None:
            return rows_at(start, quarter)
        return rows_at(start + part * cut, cut)

    own_loads = [
        pltpu.make_async_copy(own_refs[i], inside[i].at[shard_rows(me)], load_sem.at[i, half - 1])
        for i in range(2)
    ]
    keep = [
        pltpu.make_async_copy(
            inside[i].at[shard_rows(me)], full_refs[i].at[shard_rows(me)], own_sem.at[i]
        )
        for i in range(2)
    ]
    for i, ref in enumerate((gate_ref, up_ref)):
        block = (rows_at(rep * quarter, quarter), pl.ds(pl.multiple_of(me * ff_own, 128), ff_own))
        own_loads.append(
            pltpu.make_async_copy(
                ref.at[block], both_own.at[:, pl.ds(i * ff_own, ff_own)], own_sem.at[2 + i]
            )
        )
    for copy in own_loads:
        copy.start()
    gains_all_ref[:, pl.ds(pl.multiple_of(me * own_rows, 128), own_rows)] = gains_ref[...]
    low_own[...] = cotangent_ref[...].astype(BF)
    for copy in own_loads:
        copy.wait()
    keep.append(pltpu.make_async_copy(low_own, low_all_ref.at[pl.ds(0, rows)], own_sem.at[4]))
    keep.append(pltpu.make_async_copy(both_own, both_ref.at[me, rep], own_sem.at[5]))
    for copy in keep:
        copy.start()

    greet([{"shard": shard} for shard in others] + [other_core, other_chip])

    def gain_copy(k):
        columns = pl.ds(pl.multiple_of(me * own_rows, 128), own_rows)
        return remote_copy(
            gains_ref,
            gains_all_ref.at[:, columns],
            gain_send.at[k - 1],
            gain_recv.at[k - 1],
            {"shard": others[k - 1]},
        )

    def across(k, which):
        ref = (gate_ref, up_ref)[which]
        there = others[k - 1]
        columns = pl.ds(pl.multiple_of(there * ff_own, 128), ff_own)
        return remote_copy(
            ref.at[rows_at(rep * quarter, quarter), columns],
            both_ref.at[me, rep, :, pl.ds(which * ff_own, ff_own)],
            across_send.at[which, k - 1],
            across_recv.at[which, k - 1],
            {"shard": there},
        )

    def ring_copy(i, direction, step):
        sign = 1 if direction == 0 else -1
        shard = ring_shard(count, place - sign * (step - 1))
        if step < half:
            at = piece_of(shard, core, chip)
        else:
            at = piece_of(shard, core, chip, direction)
        src = full_refs[i].at[at]
        if step == 1:
            src = own_refs[i].at[piece_of(0, core, chip)]
        return remote_copy(
            src,
            full_refs[i].at[at],
            ring_send.at[i, direction, step - 1],
            ring_recv.at[i, direction, step - 1],
            near[direction],
        )

    def chip_copy(i, k):
        at = piece_of(ring_shard(count, place - k), core, chip)
        slot = k + half - 1
        return remote_copy(
            full_refs[i].at[at],
            full_refs[i].at[at],
            chip_send.at[i, slot],
            chip_recv.at[i, slot],
            other_chip,
        )

    def core_copy(i, k, which):
        from_chip = chip if which == 0 else 1 - chip
        at = piece_of(ring_shard(count, place - k), core, from_chip)
        slot = k + half - 1
        return remote_copy(
            full_refs[i].at[at],
            full_refs[i].at[at],
            core_send.at[i, which, slot],
            core_recv.at[i, which, slot],
            other_core,
        )

    def load(i, k):
        at = shard_rows(ring_shard(count, place - k))
        return pltpu.make_async_copy(
            full_refs[i].at[at], inside[i].at[at], load_sem.at[i, k + half - 1]
        )

    def low_copy(direction, step):
        base = 0 if direction == 0 else half
        to, size = (base + step) * rows, rows
        source = to - rows
        if step == half:
            size = rows // 2
            to = half * rows + direction * size
            source = (base + half - 1) * rows + direction * size
        src = low_all_ref.at[pl.ds(source, size)] if step > 1 else low_own
        return remote_copy(
            src,
            low_all_ref.at[pl.ds(to, size)],
            low_send.at[direction, step - 1],
            low_recv.at[direction, step - 1],
            near[direction],
        )

    def start_low(step):
        for direction in range(2):
            low_copy(direction, step).start()

    def finish_low(step):
        for direction in range(2):
            low_copy(direction, step).wait_recv()
        if step < half:
            start_low(step + 1)

    def start_step(i, step):
        for direction in range(2):
            ring_copy(i, direction, step).start()

    def places(step):
        return (step, -step) if step < half else (half,)

    def finish_step(i, step):
        for direction in range(2):
            ring_copy(i, direction, step).wait_recv()
        if step < half:
            start_step(i, step + 1)
        for k in places(step):
            core_copy(i, k, 0).start()

    def start_chip(i, step):
        for k in places(step):
            chip_copy(i, k).start()

    def pass_step(i, step):
        for k in places(step):
            chip_copy(i, k).wait_recv()
            core_copy(i, k, 1).start()

    def load_step(i, step):
        for k in places(step):
            for which in range(2):
                core_copy(i, k, which).wait_recv()
            load(i, k).start()

    for k in range(1, count):
        gain_copy(k).start()
    start_step(0, 1)
    resid = tokens_ref[...].astype(F32)
    unit, _ = normalize(resid)
    for k in range(1, count):
        gain_copy(k).wait_recv()
    normed[...] = (unit * gains_all_ref[0:1, :]).astype(BF)

    for step in range(1, half + 1):
        finish_step(0, step)
        start_chip(0, step)
        if step == half - 1:
            for k in range(1, count):
                for which in range(2):
                    across(k, which).start()
    start_step(1, 1)
    for step in range(1, half + 1):
        pass_step(0, step)
        if step > 1:
            load_step(0, step - 1)

    def group_copy(index, quarter_at, device):
        at = both_ref.at[:, quarter_at]
        return remote_copy(at, at, group_send.at[index], group_recv.at[index], device)

    chip_copies = [group_copy(0, rep, other_chip)]
    core_copies = [
        group_copy(1, rep, other_core),
        group_copy(2, chip_partner(rep), other_core),
    ]
    load_step(0, half)
    for k in range(-(half - 1), half + 1):
        if k:
            load(0, k).wait()

    def linear_tile(j, carry):
        at = pl.ds(pl.multiple_of(j * TILE, TILE), TILE)
        linear[:, at] = dot(normed[...], qkv_all[:, at])
        return carry

    lax.fori_loop(0, linear.shape[1] // TILE, linear_tile, 0)

    cosine, sine = cos_ref[...], sin_ref[...]
    wide, thin = 2 * GROUP * HEAD_SIZE, 2 * HEAD_SIZE
    key_at, value_at = width, width + key_ref.shape[1]

    def heads_pair(pair):
        allowed = allowed_rows(segc_ref[...], segr_ref[...])
        wide_at = pl.ds(pair * wide, wide)
        thin_at = pl.ds(pair * thin, thin)
        query = rotate(linear[:, wide_at], cosine, sine).astype(BF)
        key = rotate(linear[:, pl.ds(key_at + pair * thin, thin)], cosine, sine).astype(BF)
        value = linear[:, pl.ds(value_at + pair * thin, thin)].astype(BF)
        query_ref[:, wide_at] = query
        key_ref[:, thin_at] = key
        value_ref[:, thin_at] = value
        heads = []
        for j in range(2):
            cols = slice(j * HEAD_SIZE, (j + 1) * HEAD_SIZE)
            probs = softmax_rows(stack_heads(query, j), key[:, cols], allowed).astype(BF)
            heads += unstack_heads(dot(probs, value[:, cols]).astype(BF))
        attended_ref[:, wide_at] = jnp.concatenate(heads, 1)

    pairs = KEY_VALUE_HEADS // 2
    for turn in range(max(pairs, half)):
        if turn < half:
            finish_step(1, turn + 1)
            start_chip(1, turn + 1)
        if turn == half - 2:
            start_low(1)
        if turn < pairs:
            heads_pair(turn)
    for copy in keep:
        copy.wait()
    for k in range(1, count):
        for which in range(2):
            across(k, which).wait_recv()
    chip_copies[0].start()
    core_copies[0].start()
    for step in range(1, half + 1):
        pass_step(1, step)
        if step > 1:
            load_step(1, step - 1)
        if step % 2 == 0 and step // 2 < half:
            finish_low(step // 2)
    load_step(1, half)
    for k in range(-(half - 1), half + 1):
        if k:
            load(1, k).wait()

    def branch_tile(j, carry):
        at = pl.ds(pl.multiple_of(j * TILE, TILE), TILE)
        branch = dot(attended_ref[...], out_all[:, at])
        middle_ref[:, at] = tokens_ref[:, at].astype(F32) + branch
        return carry

    lax.fori_loop(0, width // TILE, branch_tile, 0)
    unit, _ = normalize(middle_ref[...])
    normed_two_ref[...] = (unit * gains_all_ref[1:2, :]).astype(BF)

    for step in range(half // 2 + 1, half + 1):
        finish_low(step)
    chip_copies[0].wait_recv()
    core_copies[1].start()
    for copy in core_copies:
        copy.wait_recv()
    for copy in chip_copies + core_copies:
        copy.wait_send()
    for step in range(1, half + 1):
        for direction in range(2):
            low_copy(direction, step).wait_send()
    for i in range(2):
        for step in range(1, half + 1):
            for direction in range(2):
                ring_copy(i, direction, step).wait_send()
            for k in places(step):
                chip_copy(i, k).wait_send()
                for which in range(2):
                    core_copy(i, k, which).wait_send()
    for k in range(1, count):
        gain_copy(k).wait_send()
        for which in range(2):
            across(k, which).wait_send()


def front(count, tokens, gains, cotangent, tables, qkv_own, out_own, gate_own, up_own, wide_k):
    rows, width = tokens.shape
    own_rows, qkv_width = qkv_own.shape
    ff_own = gate_own.shape[1] // count
    half = count // 2
    here = pl.BlockSpec(memory_space=pl.ANY)
    inside = pl.BlockSpec(memory_space=pltpu.VMEM)
    kind = jax.ShapeDtypeStruct
    dma = pltpu.SemaphoreType.DMA
    return pl.pallas_call(
        functools.partial(front_kernel, count),
        in_specs=[inside] * 7 + [here] * 4,
        out_specs=[here] * 4 + [inside] * 7,
        out_shape=[
            kind((count * own_rows, qkv_width), BF),
            kind((count * own_rows, width), BF),
            kind((count, 4, own_rows // 4, 2 * ff_own), BF),
            kind((count * rows, width), BF),
            kind((gains.shape[0], width), F32),
            kind((rows, width), BF),
            kind((rows, wide_k), BF),
            kind((rows, wide_k), BF),
            kind((rows, width), BF),
            kind((rows, width), F32),
            kind((rows, width), BF),
        ],
        scratch_shapes=[
            pltpu.VMEM((rows, width), BF),
            pltpu.VMEM((own_rows // 4, 2 * ff_own), BF),
            pltpu.VMEM((count * own_rows, qkv_width), BF),
            pltpu.VMEM((count * own_rows, width), BF),
            pltpu.VMEM((rows, width), BF),
            pltpu.VMEM((rows, qkv_width), F32),
            dma((6,)),
            dma((2, count)),
            dma((count - 1,)),
            dma((count - 1,)),
            dma((2, 2, half)),
            dma((2, 2, half)),
            dma((2, 2, count)),
            dma((2, 2, count)),
            dma((2, count)),
            dma((2, count)),
            dma((2, count - 1)),
            dma((2, count - 1)),
            dma((3,)),
            dma((3,)),
            dma((2, half)),
            dma((2, half)),
        ],
        compiler_params=pltpu.CompilerParams(
            collective_id=1, has_side_effects=True, vmem_limit_bytes=VMEM_BYTES
        ),
        cost_estimate=pl.CostEstimate(
            flops=2 * rows * width * (qkv_width + width) + 2 * 10**9,
            bytes_accessed=60 * 10**6,
            transcendentals=2 * 10**6,
        ),
    )(tokens, gains, cotangent, *tables, qkv_own, out_own, gate_own, up_own)


def feed_forward_kernel(
    count,
    normed_ref,
    low_ref,
    both_ref,
    down_ref,
    grad_ref,
    branch_ref,
    sums_ref,
    normed,
    low,
    hidden,
    grads,
    w_both,
    w_down,
    turned,
    staged,
    from_core,
    core_sums,
    from_chip,
    group_sums,
    result_tile,
    outgoing,
    incoming,
    local_sem,
    gather_send,
    gather_recv,
    scatter_send,
    scatter_recv,
    credit,
    core_send,
    core_recv,
    chip_send,
    chip_recv,
    group_credit,
    sums_sem,
    result_sem,
):
    half = count // 2
    rows = normed_ref.shape[0]
    cut = rows // 2
    width = normed_ref.shape[1]
    ff = down_ref.shape[0]
    place = ring_place(count, lax.axis_index("shard"))
    neighbours = (ring_shard(count, place + 1), ring_shard(count, place - 1))
    rep = lax.axis_index("rep")
    core, chip = rep % 2, rep // 2
    other_core, other_chip = {"rep": core_partner(rep)}, {"rep": chip_partner(rep)}
    everywhere = pl.ds(0, rows)
    halves = (pl.ds(0, cut), pl.ds(cut, cut))

    def at(slot, part=None):
        start, size = (0, rows) if part is None else (part * cut, cut)
        return pl.ds(pl.multiple_of(slot * rows + start, cut), size)

    def tile(j):
        return pl.ds(pl.multiple_of(j * TILE, TILE), TILE)

    def remote(src, dst, send, recv, direction):
        return remote_copy(src, dst, send, recv, {"shard": neighbours[direction]})

    loads = [
        pltpu.make_async_copy(normed_ref, normed.at[at(0)], local_sem.at[0]),
        pltpu.make_async_copy(low_ref, low, local_sem.at[1]),
        pltpu.make_async_copy(both_ref, w_both, local_sem.at[2]),
        pltpu.make_async_copy(down_ref, w_down, local_sem.at[3]),
    ]
    for load in loads:
        load.start()

    for chain in range(2):
        for direction in range(2):
            blank = halves[1 - direction]
            incoming[chain, direction, 0, blank] = jnp.zeros((cut, width), BF)

    greet([{"shard": neighbour} for neighbour in neighbours] + [other_core, other_chip])

    def gathered(part, direction, step):
        base = 0 if direction == 0 else half
        if isinstance(step, int) and step == 1:
            source = 0
        else:
            source = jnp.where(step == 1, 0, base + step - 1)
        return remote(
            normed.at[at(source, part)],
            normed.at[at(base + step, part)],
            gather_send.at[part, direction, step - 1],
            gather_recv.at[part, direction, step - 1],
            direction,
        )

    def gathered_last(direction):
        source = half - 1 if direction == 0 else 2 * half - 1
        return remote(
            normed.at[at(source, direction)],
            normed.at[at(half, direction)],
            gather_send.at[0, direction, half - 1],
            gather_recv.at[0, direction, half - 1],
            direction,
        )

    def products(slot):
        mine = at(slot)

        def body(j, carry):
            gate_at, up_at = tile(j), tile(j + ff // TILE)
            own = normed[mine, :]
            gate = dot(own, w_both[:, gate_at])
            up = dot(own, w_both[:, up_at])
            grad_hidden = contract_last(low[mine, :], w_down[gate_at, :])
            sigmoid = jax.nn.sigmoid(gate)
            silu = gate * sigmoid
            hidden[mine, gate_at] = (silu * up).astype(BF)
            grads[mine, gate_at] = (
                grad_hidden * up * sigmoid * (1.0 + gate * (1.0 - sigmoid))
            ).astype(BF)
            grads[mine, up_at] = (grad_hidden * silu).astype(BF)
            return carry

        lax.fori_loop(0, ff // TILE, body, 0)

    both_ways = ((0, 0), (0, 1), (1, 0), (1, 1))
    loads[0].wait()
    for part, direction in both_ways:
        gathered(part, direction, 1).start()
    for load in loads[1:]:
        load.wait()
    products(0)

    def gather_step(step, carry):
        for part, direction in both_ways:
            gathered(part, direction, step).wait_recv()

            @pl.when(step < half - 1)
            def _():
                gathered(part, direction, step + 1).start()

            if part == direction:

                @pl.when(step == half - 1)
                def _():
                    gathered_last(direction).start()

        products(step)
        products(half + step)
        return carry

    lax.fori_loop(1, half, gather_step, 0)
    for direction in range(2):
        gathered_last(direction).wait_recv()
    products(half)

    def term(chain, rows_at, j):
        if chain == 0:
            return contract_last(grads[rows_at, :], w_both[tile(j), :])
        return dot(hidden[rows_at, :], w_down[:, tile(j)])

    def scattered(chain, direction, step):
        if isinstance(step, int) and step == 0:
            own, there = halves[direction], 0
        else:
            own, there = everywhere, step % 2
        return remote(
            outgoing.at[chain, direction, own],
            incoming.at[chain, direction, there, own],
            scatter_send.at[chain, direction, step],
            scatter_recv.at[chain, direction, step],
            direction,
        )

    units = (width + ff) // TILE
    per_step = -(-(units + 2) // (half - 1))
    quarter = TILE // 4

    def core_copy(unit):
        spot = unit % 2
        return remote_copy(
            staged.at[spot, :, 1 - core],
            from_core.at[spot],
            core_send.at[spot],
            core_recv.at[spot],
            other_core,
        )

    def chip_copy(unit):
        spot = unit % 2
        return remote_copy(
            core_sums.at[spot, 1 - chip],
            from_chip.at[spot],
            chip_send.at[spot],
            chip_recv.at[spot],
            other_chip,
        )

    def sums_copy(unit):
        spot = unit % 2
        return pltpu.make_async_copy(group_sums.at[spot], sums_ref.at[unit], sums_sem.at[spot])

    def give_credit(which, device):
        pl.semaphore_signal(
            group_credit.at[which], inc=1, device_id=device, device_id_type=pl.DeviceIdType.MESH
        )

    def weight_unit(unit):
        spot = unit % 2

        def from_arrays(left, right, block):
            def turn(c, carry):
                turned[:, at(c)] = left[at(c), tile(block)].T
                return carry

            lax.fori_loop(0, count, turn, 0)

            def body(j, carry):
                value = dot(turned[...], right[:, tile(j)]).astype(BF)
                staged[spot, :, :, :, tile(j)] = value.reshape(2, 2, quarter, TILE)
                return carry

            lax.fori_loop(0, width // TILE, body, 0)

        @pl.when(unit < width // TILE)
        def _():
            from_arrays(normed, grads, unit)

        @pl.when(unit >= width // TILE)
        def _():
            from_arrays(hidden, low, unit - width // TILE)

        @pl.when(unit >= 2)
        def _():
            pl.semaphore_wait(group_credit.at[0], 1)

        core_copy(unit).start()

    def sum_over_cores(unit):
        spot = unit % 2
        core_copy(unit).wait()
        for y in range(2):
            total = staged[spot, y, core].astype(F32) + from_core[spot, y].astype(F32)
            core_sums[spot, y] = total.astype(BF)

        @pl.when(unit < units - 2)
        def _():
            give_credit(0, other_core)

        @pl.when(unit >= 2)
        def _():
            pl.semaphore_wait(group_credit.at[1], 1)

        chip_copy(unit).start()

    def sum_over_chips(unit):
        spot = unit % 2
        chip_copy(unit).wait()

        @pl.when(unit >= 2)
        def _():
            sums_copy(unit - 2).wait()

        total = core_sums[spot, chip].astype(F32) + from_chip[spot].astype(F32)
        group_sums[spot] = total.astype(BF)

        @pl.when(unit < units - 2)
        def _():
            give_credit(1, other_chip)

        sums_copy(unit).start()

    def weight_step(turn):
        @pl.when(turn < units)
        def _():
            weight_unit(turn)

        @pl.when((turn >= 1) & (turn <= units))
        def _():
            sum_over_cores(turn - 1)

        @pl.when(turn >= 2)
        def _():
            sum_over_chips(turn - 2)

    for chain in range(2):

        def first(j, carry):
            value = term(chain, at(half), j).astype(BF)
            outgoing[chain, 0, halves[0], tile(j)] = value[:cut]
            outgoing[chain, 1, halves[1], tile(j)] = value[cut:]
            return carry

        lax.fori_loop(0, width // TILE, first, 0)
        for direction in range(2):
            scattered(chain, direction, 0).start()

    def scatter_step(step, carry):
        k = half - step
        for chain in range(2):
            for direction in range(2):
                slot = half + k if direction == 0 else k

                @pl.when(step == 1)
                def _():
                    scattered(chain, direction, 0).wait()

                @pl.when(step > 1)
                def _():
                    scattered(chain, direction, step - 1).wait()
                    pl.semaphore_wait(credit.at[chain, direction], 1)

                def add(j, carry):
                    value = term(chain, at(slot), j)
                    value += incoming[chain, direction, (step - 1) % 2, :, tile(j)].astype(F32)
                    outgoing[chain, direction, :, tile(j)] = value.astype(BF)
                    return carry

                lax.fori_loop(0, width // TILE, add, 0)
                scattered(chain, direction, step).start()

                @pl.when(step < half - 1)
                def _():
                    pl.semaphore_signal(
                        credit.at[chain, direction],
                        inc=1,
                        device_id={"shard": neighbours[1 - direction]},
                        device_id_type=pl.DeviceIdType.MESH,
                    )

        lax.fori_loop(
            (step - 1) * per_step,
            jnp.minimum(step * per_step, units + 2),
            lambda turn, c: (weight_step(turn), c)[1],
            0,
        )
        return carry

    lax.fori_loop(1, half, scatter_step, 0)

    for chain, result in enumerate((grad_ref, branch_ref)):
        for direction in range(2):
            scattered(chain, direction, half - 1).wait()

        def result_copy(j):
            return pltpu.make_async_copy(
                result_tile.at[j % 2], result.at[:, tile(j)], result_sem.at[j % 2]
            )

        def last(j, carry):
            @pl.when(j >= 2)
            def _():
                result_copy(j - 2).wait()

            value = term(chain, at(0), j)
            for direction in range(2):
                value += incoming[chain, direction, (half - 1) % 2, :, tile(j)].astype(F32)
            result_tile[j % 2] = value
            result_copy(j).start()
            return carry

        lax.fori_loop(0, width // TILE, last, 0)
        for j in (width // TILE - 2, width // TILE - 1):
            result_copy(j).wait()

    for unit in (units - 2, units - 1):
        sums_copy(unit).wait()
    for part, direction in both_ways:
        lax.fori_loop(
            1,
            half,
            lambda step, c: (gathered(part, direction, step).wait_send(), c)[1],
            0,
        )
    for direction in range(2):
        gathered_last(direction).wait_send()


def feed_forward_bytes(count, rows, width, ff):
    tokens = count * rows
    return 2 * (
        tokens * (2 * width + 3 * ff)
        + 3 * width * ff
        + TILE * tokens
        + 5 * TILE * width
        + 12 * rows * width
        + 4 * TILE * rows
    )


def feed_forward(count, normed, low, w_both, w_down):
    rows, width = normed.shape
    ff = w_down.shape[0]
    tokens = count * rows
    half = count // 2
    quarter = TILE // 4
    here = pl.BlockSpec(memory_space=pl.ANY)
    dma = pltpu.SemaphoreType.DMA
    return pl.pallas_call(
        functools.partial(feed_forward_kernel, count),
        in_specs=[here] * 4,
        out_specs=[here] * 3,
        out_shape=[
            jax.ShapeDtypeStruct((rows, width), F32),
            jax.ShapeDtypeStruct((rows, width), F32),
            jax.ShapeDtypeStruct(((width + ff) // TILE, quarter, width), BF),
        ],
        scratch_shapes=[
            pltpu.VMEM((tokens, width), BF),
            pltpu.VMEM((tokens, width), BF),
            pltpu.VMEM((tokens, ff), BF),
            pltpu.VMEM((tokens, 2 * ff), BF),
            pltpu.VMEM((width, 2 * ff), BF),
            pltpu.VMEM((ff, width), BF),
            pltpu.VMEM((TILE, tokens), BF),
            pltpu.VMEM((2, 2, 2, quarter, width), BF),
            pltpu.VMEM((2, 2, quarter, width), BF),
            pltpu.VMEM((2, 2, quarter, width), BF),
            pltpu.VMEM((2, quarter, width), BF),
            pltpu.VMEM((2, quarter, width), BF),
            pltpu.VMEM((2, rows, TILE), F32),
            pltpu.VMEM((2, 2, rows, width), BF),
            pltpu.VMEM((2, 2, 2, rows, width), BF),
            dma((4,)),
            dma((2, 2, half)),
            dma((2, 2, half)),
            dma((2, 2, half)),
            dma((2, 2, half)),
            pltpu.SemaphoreType.REGULAR((2, 2)),
            dma((2,)),
            dma((2,)),
            dma((2,)),
            dma((2,)),
            pltpu.SemaphoreType.REGULAR((2,)),
            dma((2,)),
            dma((2,)),
        ],
        compiler_params=pltpu.CompilerParams(
            collective_id=0, has_side_effects=True, vmem_limit_bytes=VMEM_BYTES
        ),
        cost_estimate=pl.CostEstimate(
            flops=18 * tokens * width * ff, bytes_accessed=50 * 10**6, transcendentals=tokens * ff
        ),
    )(normed, low, w_both, w_down)


def back_kernel(
    count,
    sums_ref,
    mid_low_ref,
    gain_two_ref,
    attended_ref,
    query_ref,
    key_ref,
    value_ref,
    tokens_ref,
    gains_ref,
    cos_ref,
    sin_ref,
    segc_ref,
    segr_ref,
    qkv_all_ref,
    out_all_ref,
    gate_grad_ref,
    up_grad_ref,
    down_grad_ref,
    out_grad_ref,
    qkv_grad_ref,
    grad_input_ref,
    gain_grad_ref,
    both_own,
    down_own,
    turned,
    grad_attended,
    grads,
    weight_tile,
    terms_first,
    terms_second,
    from_core_out,
    from_core_qkv,
    from_chip_out,
    out_sums,
    out_summed,
    outgoing_out,
    outgoing_qkv,
    incoming_out,
    incoming_qkv,
    summed,
    from_chip,
    finished,
    gain_terms,
    gains_in,
    gain_parts,
    gain_swaps,
    own_sem,
    tile_sem,
    across_send,
    across_recv,
    group_send,
    group_recv,
    core_send,
    core_recv,
    ring_send,
    ring_recv,
    chip_send,
    chip_recv,
    last_send,
    last_recv,
    pair_send,
    pair_recv,
    gain_send,
    gain_recv,
    swap_send,
    swap_recv,
):
    half = count // 2
    me, rep = lax.axis_index("shard"), lax.axis_index("rep")
    core, chip = rep % 2, rep // 2
    place = ring_place(count, me)
    others = [ring_shard(count, place + k) for k in range(1, count)]
    near = ({"shard": ring_shard(count, place + 1)}, {"shard": ring_shard(count, place - 1)})
    other_core, other_chip = {"rep": core_partner(rep)}, {"rep": chip_partner(rep)}
    rows, width = tokens_ref.shape
    own_rows = width // count
    strip, quarter = own_rows // 2, own_rows // 4
    ff_own = gate_grad_ref.shape[2] // count
    qkv_half = grads.shape[1] // 2
    wides = (width, qkv_half, qkv_half)
    terms = (terms_first, terms_second, terms_first)
    pieces = (quarter, strip, strip)
    from_core = (from_core_out, from_core_qkv.at[0], from_core_qkv.at[1])
    outgoing = (outgoing_out, outgoing_qkv.at[0], outgoing_qkv.at[1])
    incoming = (incoming_out, incoming_qkv.at[0], incoming_qkv.at[1])
    result_refs = (out_grad_ref, qkv_grad_ref, qkv_grad_ref)
    result_starts = (0, 0, qkv_half)
    chains = range(3)

    def tile(j, size=TILE):
        return pl.ds(pl.multiple_of(j * size, size), size)

    gate_up = (gate_grad_ref, up_grad_ref)

    def own_columns(shard):
        return pl.ds(pl.multiple_of(shard * ff_own, 128), ff_own)

    def across(k, which):
        there = others[k - 1]
        return remote_copy(
            sums_ref.at[there, :, pl.ds(which * ff_own, ff_own)],
            gate_up[which].at[rep, :, own_columns(me)],
            across_send.at[which, k - 1],
            across_recv.at[which, k - 1],
            {"shard": there},
        )

    own_loads = (
        pltpu.make_async_copy(
            sums_ref.at[pl.ds(count, down_grad_ref.shape[0])], down_own, own_sem.at[0]
        ),
        pltpu.make_async_copy(sums_ref.at[me], both_own, own_sem.at[1]),
    )
    keep = [
        pltpu.make_async_copy(
            both_own.at[:, pl.ds(which * ff_own, ff_own)],
            gate_up[which].at[rep, :, own_columns(me)],
            own_sem.at[which],
        )
        for which in range(2)
    ]
    keep.append(pltpu.make_async_copy(down_own, down_grad_ref.at[:, rep], own_sem.at[2]))

    def group_copy(which, index):
        member = chip_partner(rep) if index == 2 else rep
        if which == 2:
            dst = down_grad_ref.at[:, member]
            src = dst if index == 2 else down_own
        else:
            dst = src = gate_up[which].at[member]
        return remote_copy(
            src,
            dst,
            group_send.at[which, index],
            group_recv.at[which, index],
            other_chip if index == 0 else other_core,
        )

    def shard_of(k):
        return ring_shard(count, place + k)

    def core_copy(i, k):
        slot = k + half - 1
        return remote_copy(
            terms[i].at[shard_of(k), 1 - core, :, pl.ds(0, wides[i])],
            from_core[i].at[slot],
            core_send.at[i, slot],
            core_recv.at[i, slot],
            other_core,
        )

    def all_terms(i):
        def body(j, carry):
            if i == 0:
                right = mid_low_ref[:, tile(j)]
            else:
                right = grads[:, tile(j + result_starts[i] // TILE)]
            value = dot(turned[...], right).astype(BF)
            terms[i][:, :, :, tile(j)] = value.reshape(count, 2, strip, TILE)
            return carry

        lax.fori_loop(0, wides[i] // TILE, body, 0)
        for k in [half] + [s * j for j in range(half - 1, 0, -1) for s in (1, -1)] + [0]:
            core_copy(i, k).start()

    def pair_copy(k):
        slot = k + half - 1
        return remote_copy(
            out_sums.at[slot, 1 - chip],
            from_chip_out.at[slot],
            pair_send.at[slot],
            pair_recv.at[slot],
            other_chip,
        )

    def sum_pair(k):
        core_copy(0, k).wait_recv()

        def body(j, carry):
            at = tile(j, WIDE_TILE)
            value = terms[0][shard_of(k), core, :, at].astype(F32)
            value += from_core[0][k + half - 1, :, at].astype(F32)
            out_sums[k + half - 1, :, :, at] = value.astype(BF).reshape(2, quarter, WIDE_TILE)
            return carry

        lax.fori_loop(0, wides[0] // WIDE_TILE, body, 0)
        pair_copy(k).start()

    def piece_sum(i, k, extra, store):
        slot = k + half - 1
        if i == 0:
            pair_copy(k).wait_recv()
            received = from_chip_out
        else:
            core_copy(i, k).wait_recv()
            received = from_core[i]

        def body(j, carry):
            at = tile(j, WIDE_TILE)
            own = out_sums[slot, chip, :, at] if i == 0 else terms[i][shard_of(k), core, :, at]
            value = own.astype(F32)
            value += received[slot, :, at].astype(F32)
            for direction, step in extra:
                value += incoming[i][direction, step, :, at].astype(F32)
            store(at, value.astype(BF))
            return carry

        lax.fori_loop(0, wides[i] // WIDE_TILE, body, 0)

    def ring_copy(i, direction, step):
        cut = pieces[i] // 2
        at = pl.ds(direction * cut, cut) if step == 0 else pl.ds(0, pieces[i])
        return remote_copy(
            outgoing[i].at[direction, at],
            incoming[i].at[direction, step, at],
            ring_send.at[i, direction, step],
            ring_recv.at[i, direction, step],
            near[direction],
        )

    def ring_step(i, step):
        if step == 0:

            cut = pieces[i] // 2

            def store(at, value):
                outgoing[i][0, pl.ds(0, cut), at] = value[:cut]
                outgoing[i][1, pl.ds(cut, cut), at] = value[cut:]

            piece_sum(i, half, (), store)
            for direction in range(2):
                ring_copy(i, direction, 0).start()
            return
        for direction in range(2):
            ring_copy(i, direction, step - 1).wait()

            def store(at, value):
                outgoing[i][direction, :, at] = value

            k = half - step if direction == 0 else step - half
            piece_sum(i, k, ((direction, step - 1),), store)
            ring_copy(i, direction, step).start()

    def chip_copy(i):
        return remote_copy(
            summed.at[i - 1],
            from_chip.at[i - 1],
            chip_send.at[i],
            chip_recv.at[i],
            other_chip,
        )

    def ring_end(i):
        for direction in range(2):
            ring_copy(i, direction, half - 1).wait()

        def store(at, value):
            if i == 0:
                out_summed[:, at] = value
            else:
                summed[i - 1, :, at] = value

        piece_sum(i, 0, tuple((d, half - 1) for d in range(2)), store)
        if i > 0:
            chip_copy(i).start()
        else:
            for copy in out_copies()[:3]:
                copy.start()

    own_strip = pl.ds(pl.multiple_of(core * strip, strip), strip)

    def out_copies():
        def at(which_chip):
            return out_grad_ref.at[
                pl.ds(pl.multiple_of(core * strip + which_chip * quarter, quarter), quarter)
            ]

        done = out_summed
        return (
            pltpu.make_async_copy(done, at(chip), own_sem.at[3]),
            remote_copy(done, at(chip), chip_send.at[0], chip_recv.at[0], other_chip),
            remote_copy(done, at(chip), last_send.at[0], last_recv.at[0], other_core),
            remote_copy(at(1 - chip), at(1 - chip), last_send.at[3], last_recv.at[3], other_core),
        )

    def last_copies(i):
        src = finished.at[i - 1]
        dst = result_refs[i].at[own_strip, pl.ds(result_starts[i], wides[i])]
        return (
            pltpu.make_async_copy(src, dst, own_sem.at[3 + i]),
            remote_copy(src, dst, last_send.at[i], last_recv.at[i], other_core),
        )

    def group_end(i):
        chip_copy(i).wait()
        total = summed[i - 1].astype(F32) + from_chip[i - 1].astype(F32)
        finished[i - 1] = total.astype(BF)
        for copy in last_copies(i):
            copy.start()

    def gain_copy(k):
        return remote_copy(
            gain_terms.at[:, tile(others[k - 1], own_rows)],
            gains_in.at[k],
            gain_send.at[k - 1],
            gain_recv.at[k - 1],
            {"shard": others[k - 1]},
        )

    def gain_swap(index):
        return remote_copy(
            gain_parts.at[index],
            gain_swaps.at[index],
            swap_send.at[index],
            swap_recv.at[index],
            (other_core, other_chip)[index],
        )

    def weight_load(ref, j, wide):
        return pltpu.make_async_copy(
            ref.at[tile(j, LOAD_TILE)], weight_tile.at[j % 2, :, pl.ds(0, wide)], tile_sem.at[j % 2]
        )

    def times_transposed(left, ref, wide, store):
        blocks = width // LOAD_TILE

        def body(j, carry):
            @pl.when(j + 1 < blocks)
            def _():
                weight_load(ref, j + 1, wide).start()

            weight_load(ref, j, wide).wait()
            store(tile(j, LOAD_TILE), contract_last(left[...], weight_tile[j % 2, :, pl.ds(0, wide)]))
            return carry

        lax.fori_loop(0, blocks, body, 0)

    def turn(array):
        def body(j, carry):
            turned[tile(j), :] = array[:, tile(j)].T
            return carry

        lax.fori_loop(0, width // TILE, body, 0)

    cosine, sine = cos_ref[...], -sin_ref[...]
    wide, thin = 2 * GROUP * HEAD_SIZE, 2 * HEAD_SIZE
    key_at, value_at = width, width + key_ref.shape[1]

    def heads_pair(pair):
        allowed = allowed_rows(segc_ref[...], segr_ref[...])
        wide_at, thin_at = pl.ds(pair * wide, wide), pl.ds(pair * thin, thin)
        query, grad = query_ref[:, wide_at], grad_attended[:, wide_at]
        key, value = key_ref[:, thin_at], value_ref[:, thin_at]
        heads, keys, values = [], [], []
        for j in range(2):
            cols = slice(j * HEAD_SIZE, (j + 1) * HEAD_SIZE)
            query_rows, grad_rows = stack_heads(query, j), stack_heads(grad, j)
            probs = softmax_rows(query_rows, key[:, cols], allowed)
            grad_probs = contract_last(grad_rows, value[:, cols])
            grad_scores = (
                probs * (grad_probs - jnp.sum(probs * grad_probs, -1, keepdims=True))
            ).astype(BF)
            heads += unstack_heads(dot(grad_scores, key[:, cols]) * HEAD_SIZE ** (-0.5))
            keys.append(contract_first(grad_scores, query_rows) * HEAD_SIZE ** (-0.5))
            values.append(contract_first(probs.astype(BF), grad_rows))
        grads[:, wide_at] = rotate(jnp.concatenate(heads, 1), cosine, sine).astype(BF)
        grads[:, pl.ds(key_at + pair * thin, thin)] = rotate(
            jnp.concatenate(keys, 1), cosine, sine
        ).astype(BF)
        grads[:, pl.ds(value_at + pair * thin, thin)] = jnp.concatenate(values, 1).astype(BF)

    load_attended = pltpu.make_async_copy(attended_ref, grad_attended, own_sem.at[3])
    load_attended.start()
    for copy in own_loads:
        copy.start()
    for i in chains:
        for direction in range(2):
            cut = pieces[i] // 2
            blank = pl.ds((1 - direction) * cut, cut)
            incoming[i][direction, 0, blank] = jnp.zeros((cut, wides[i]), BF)

    for copy in own_loads:
        copy.wait()
    for copy in keep:
        copy.start()
    greet([{"shard": shard} for shard in others] + [other_core, other_chip])

    for k in range(1, count):
        for which in range(2):
            across(k, which).start()
    weight_load(out_all_ref, 0, width).start()
    load_attended.wait()
    turn(grad_attended)
    all_terms(0)
    for k in [half] + [s * j for j in range(half - 1, 0, -1) for s in (1, -1)] + [0]:
        sum_pair(k)
    group_copy(2, 0).start()
    group_copy(2, 1).start()

    def store_attended(at, value):
        grad_attended[:, at] = value.astype(BF)

    times_transposed(mid_low_ref, out_all_ref, width, store_attended)
    weight_load(qkv_all_ref, 0, grads.shape[1]).start()
    ring_step(0, 0)
    for pair in range(KEY_VALUE_HEADS // 2):
        heads_pair(pair)

    unit, scale_row = normalize(tokens_ref[...].astype(F32))
    gain = gains_ref[0:1, :]
    grad_attended[...] = (unit * gain).astype(BF)
    turn(grad_attended)
    all_terms(1)
    ring_step(1, 0)
    for k in range(-(half - 1), half + 1):
        core_copy(0, k).wait_send()
    all_terms(2)
    ring_step(2, 0)
    for i in chains:
        ring_step(i, 1)

    for copy in keep:
        copy.wait()
    for k in range(1, count):
        for which in range(2):
            across(k, which).wait_recv()
    for which in range(2):
        for index in range(2):
            group_copy(which, index).start()
    group_copy(2, 0).wait_recv()
    group_copy(2, 2).start()

    def store_input(at, value):
        grad_input_ref[:, at] = value

    times_transposed(grads, qkv_all_ref, grads.shape[1], store_input)
    if half > 2:
        for i in chains:
            ring_step(i, 2)
    unit, scale_row = normalize(tokens_ref[...].astype(F32))
    grad_normed = grad_input_ref[...]
    gain_terms[...] = jnp.zeros_like(gain_terms)
    gain_terms[0:1, :] = jnp.sum(grad_normed * unit, 0, keepdims=True)
    gain_terms[1:2, :] = gain_two_ref[...]
    for k in range(1, count):
        gain_copy(k).start()
    grad_input_ref[...] = norm_back(grad_normed * gain, unit, scale_row)
    for step in range(3, half):
        for i in chains:
            ring_step(i, step)
    ring_end(0)
    for which in range(2):
        group_copy(which, 0).wait_recv()
        group_copy(which, 2).start()
    total = gain_terms[:, tile(me, own_rows)]
    for k in range(1, count):
        gain_copy(k).wait_recv()
        total += gains_in[k]
    gain_parts[0] = total
    gain_swap(0).start()
    out_copies()[1].wait_recv()
    out_copies()[3].start()
    for i in (1, 2):
        ring_end(i)
    gain_swap(0).wait()
    gain_parts[1] = gain_parts[0] + gain_swaps[0]
    gain_swap(1).start()
    for i in (1, 2):
        group_end(i)
    gain_swap(1).wait()
    gain_grad_ref[...] = gain_parts[1] + gain_swaps[1]

    for k in range(-(half - 1), half + 1):
        pair_copy(k).wait_send()
    kept, over, passed, again = out_copies()
    kept.wait()
    over.wait_send()
    passed.wait()
    again.wait()
    for i in (1, 2):
        kept, passed = last_copies(i)
        kept.wait()
        passed.wait()
    for i in (1, 2):
        for k in range(-(half - 1), half + 1):
            core_copy(i, k).wait_send()
    for which in range(3):
        for index in range(3):
            if index > 0:
                group_copy(which, index).wait_recv()
            group_copy(which, index).wait_send()
    for k in range(1, count):
        gain_copy(k).wait_send()
        for which in range(2):
            across(k, which).wait_send()


def back(
    count,
    sums,
    mid_low,
    gain_two_term,
    attended,
    query,
    key,
    value,
    tokens,
    gains,
    tables,
    qkv_all,
    out_all,
):
    rows, width = tokens.shape
    qkv_width = qkv_all.shape[1]
    own_rows = width // count
    strip, quarter = own_rows // 2, own_rows // 4
    ff_own = sums.shape[2] // 2
    half = count // 2
    here = pl.BlockSpec(memory_space=pl.ANY)
    inside = pl.BlockSpec(memory_space=pltpu.VMEM)
    kind = jax.ShapeDtypeStruct
    dma = pltpu.SemaphoreType.DMA
    vmem = pltpu.VMEM
    return pl.pallas_call(
        functools.partial(back_kernel, count),
        in_specs=[here] + [inside] * 2 + [here] + [inside] * 9 + [here] * 2,
        out_specs=[here] * 5 + [inside] * 2,
        out_shape=[
            kind((4, quarter, count * ff_own), BF),
            kind((4, quarter, count * ff_own), BF),
            kind((ff_own // own_rows, 4, quarter, width), BF),
            kind((own_rows, width), BF),
            kind((own_rows, qkv_width), BF),
            kind((rows, width), F32),
            kind((8, own_rows), F32),
        ],
        scratch_shapes=[
            vmem((quarter, 2 * ff_own), BF),
            vmem((ff_own // own_rows, quarter, width), BF),
            vmem((width, rows), BF),
            vmem((rows, width), BF),
            vmem((rows, qkv_width), BF),
            vmem((2, LOAD_TILE, qkv_width), BF),
            vmem((count, 2, strip, width), BF),
            vmem((count, 2, strip, qkv_width // 2), BF),
            vmem((count, strip, width), BF),
            vmem((2, count, strip, qkv_width // 2), BF),
            vmem((count, quarter, width), BF),
            vmem((count, 2, quarter, width), BF),
            vmem((quarter, width), BF),
            vmem((2, quarter, width), BF),
            vmem((2, 2, strip, qkv_width // 2), BF),
            vmem((2, half, quarter, width), BF),
            vmem((2, 2, half, strip, qkv_width // 2), BF),
            vmem((2, strip, qkv_width // 2), BF),
            vmem((2, strip, qkv_width // 2), BF),
            vmem((2, strip, qkv_width // 2), BF),
            vmem((8, width), F32),
            vmem((count, 8, own_rows), F32),
            vmem((2, 8, own_rows), F32),
            vmem((2, 8, own_rows), F32),
            dma((6,)),
            dma((2,)),
            dma((2, count - 1)),
            dma((2, count - 1)),
            dma((3, 3)),
            dma((3, 3)),
            dma((3, count)),
            dma((3, count)),
            dma((3, 2, half)),
            dma((3, 2, half)),
            dma((3,)),
            dma((3,)),
            dma((4,)),
            dma((4,)),
            dma((count,)),
            dma((count,)),
            dma((count - 1,)),
            dma((count - 1,)),
            dma((2,)),
            dma((2,)),
        ],
        compiler_params=pltpu.CompilerParams(
            collective_id=2, has_side_effects=True, vmem_limit_bytes=VMEM_BYTES
        ),
        cost_estimate=pl.CostEstimate(
            flops=4 * rows * width * (qkv_width + width) + 4 * 10**9,
            bytes_accessed=60 * 10**6,
            transcendentals=2 * 10**6,
        ),
    )(
        sums,
        mid_low,
        gain_two_term,
        attended,
        query,
        key,
        value,
        tokens,
        gains,
        *tables,
        qkv_all,
        out_all,
    )


def feed_forward_parts(ring, normed_two, grad_low, w_both, w_down):
    sequence, ff_own = normed_two.shape[0], w_down.shape[0]
    low_all, normed_all = run(ring.gather(grad_low), ring.gather(normed_two))
    hidden, grad_both = {}, {}
    for k in normed_all:
        both = dot(normed_all[k], w_both)
        gate, up = both[:, :ff_own], both[:, ff_own:]
        grad_hidden = contract_last(low_all[k], w_down)
        sigmoid = jax.nn.sigmoid(gate)
        silu = gate * sigmoid
        hidden[k] = (silu * up).astype(BF)
        grad_gate = (grad_hidden * up * sigmoid * (1.0 + gate * (1.0 - sigmoid))).astype(BF)
        grad_up = (grad_hidden * silu).astype(BF)
        grad_both[k] = jnp.concatenate([grad_gate, grad_up], 1)

    def terms_of(chunks, product):
        def terms(ks):
            sources = [k if k == ring.half else -k for k in ks]
            whole = product(jnp.concatenate([chunks[k] for k in sources], 0))
            return [whole[i * sequence : (i + 1) * sequence] for i in range(len(ks))]

        return terms

    (grad_normed_two,) = run(ring.scatter(terms_of(grad_both, lambda a: contract_last(a, w_both))))
    (branch_two,) = run(ring.scatter(terms_of(hidden, lambda a: dot(a, w_down))))
    keys = list(normed_all)
    together = lambda parts: jnp.concatenate([parts[k] for k in keys], 0)
    both_term = contract_first(together(normed_all), together(grad_both))
    down_term = contract_first(together(hidden), together(low_all))
    return grad_normed_two, branch_two, both_term, down_term


def swap(array, bit):
    return lax.ppermute(array, "rep", [(i, i ^ bit) for i in range(4)])


def cols(array, start, width):
    return lax.dynamic_slice_in_dim(array, start, width, 1)


def rows_of(array, start, height):
    return lax.dynamic_slice_in_dim(array, start, height, 0)


def put(array, piece, start, axis):
    return lax.dynamic_update_slice_in_dim(array, piece, start, axis)


def gather_rows(ring, array):
    rows = array.shape[0]
    (parts,) = run(ring.gather(array))
    full = jnp.zeros((ring.count * rows, array.shape[1]), array.dtype)
    for k, part in parts.items():
        full = put(full, part, ring.at(-k) * rows, 0)
    return full


def front_parts(ring, tokens, gains_own, cotangent, tables, qkv_own, w_out, w_gate, w_up, wide_k):
    count, own_rows = ring.count, qkv_own.shape[0]
    rep = lax.axis_index("rep")
    ff_own = w_gate.shape[1] // count
    width = tokens.shape[1]
    gains = jnp.zeros((gains_own.shape[0], width), F32)
    for k in range(count):
        piece = ring.send(gains_own, k) if k else gains_own
        gains = put(gains, piece, ring.at(-k) * own_rows, 1)
    qkv_all, out_all = gather_rows(ring, qkv_own), gather_rows(ring, w_out)
    quarter = own_rows // 4
    gate_rows = rows_of(w_gate, rep * quarter, quarter)
    up_rows = rows_of(w_up, rep * quarter, quarter)
    sends = []
    for k in range(count):
        dest = ring.at(k) * ff_own
        piece = jnp.concatenate([cols(gate_rows, dest, ff_own), cols(up_rows, dest, ff_own)], 1)
        sends.append((piece, k))
    fetched = jnp.zeros((count, quarter, 2 * ff_own), BF)
    for k, piece in enumerate([sends[0][0]] + ring.queue(*sends[1:])):
        fetched = put(fetched, piece[None], ring.at(-k), 0)
    pieces = [fetched, swap(fetched, 2)]
    pieces += [swap(piece, 1) for piece in pieces]
    w_both = jnp.zeros((count, 4, quarter, 2 * ff_own), BF)
    for bits, piece in zip((0, 2, 1, 3), pieces):
        w_both = put(w_both, piece[:, None], rep ^ bits, 1)
    resid = tokens.astype(F32)
    unit, _ = normalize(resid)
    linear = dot((unit * gains[:1]).astype(BF), qkv_all)
    query, key, value, attended = attend(
        linear[:, :width], linear[:, width : width + wide_k], linear[:, width + wide_k :], tables
    )
    middle = resid + dot(attended, out_all)
    unit, _ = normalize(middle)
    normed_two = (unit * gains[1:2]).astype(BF)
    low = cotangent.astype(BF)
    return qkv_all, out_all, w_both, low, gains, query, key, value, attended, middle, normed_two


def back_parts(
    ring,
    both_term,
    down_term,
    mid_low,
    gain_two_term,
    attended,
    query,
    key,
    value,
    tokens,
    gains,
    tables,
    qkv_all,
    out_all,
):
    count = ring.count
    rep = lax.axis_index("rep")
    core, chip = rep % 2, rep // 2
    width = tokens.shape[1]
    own_rows = width // count
    quarter = own_rows // 4
    ff_own = both_term.shape[1] // 2
    ff = ff_own * count

    def order_halves(mine, other):
        first = core == 0
        return jnp.where(first, mine, other), jnp.where(first, other, mine)

    def sum_cores(array, half_of):
        keep, pass_on = half_of(array, core), half_of(array, 1 - core)
        return keep.astype(F32) + swap(pass_on.astype(BF), 1).astype(F32)

    both_term = both_term.reshape(count, 2, 2, quarter, 2 * ff_own)
    both_half = sum_cores(
        both_term, lambda a, c: lax.dynamic_index_in_dim(a, c, 2, keepdims=False)
    )
    keep = lax.dynamic_index_in_dim(both_half, chip, 1, keepdims=False)
    pass_on = lax.dynamic_index_in_dim(both_half, 1 - chip, 1, keepdims=False)
    both_quarter = (keep + swap(pass_on.astype(BF), 2).astype(F32)).astype(BF)
    gate_quarter = jnp.zeros((quarter, ff), BF)
    up_quarter = jnp.zeros((quarter, ff), BF)
    sends = [
        (lax.dynamic_index_in_dim(both_quarter, ring.at(k), 0, keepdims=False), k)
        for k in range(count)
    ]
    for k, piece in enumerate([sends[0][0]] + ring.queue(*sends[1:])):
        start = ring.at(-k) * ff_own
        gate_quarter = put(gate_quarter, piece[:, :ff_own], start, 1)
        up_quarter = put(up_quarter, piece[:, ff_own:], start, 1)

    def collect(quarter_rows):
        parts = [quarter_rows, swap(quarter_rows, 2)]
        parts += [swap(part, 1) for part in parts]
        full = jnp.zeros((4 * quarter, ff), BF)
        for bits, part in zip((0, 2, 1, 3), parts):
            full = put(full, part, (rep ^ bits) * quarter, 0)
        return full

    gate_grad, up_grad = collect(gate_quarter), collect(up_quarter)

    down_half = sum_cores(
        down_term, lambda a, c: rows_of(a, c * (a.shape[0] // 2), a.shape[0] // 2)
    ).astype(BF)
    down_half = (down_half.astype(F32) + swap(down_half, 2).astype(F32)).astype(BF)
    down_grad = jnp.concatenate(order_halves(down_half, swap(down_half, 1)), 0)

    def part_sums(left, grads):
        wide = grads.shape[1] // 2
        grads_mine, grads_other = cols(grads, core * wide, wide), cols(grads, (1 - core) * wide, wide)

        def terms(ks):
            blocks = [cols(left, ring.at(k) * own_rows, own_rows) for k in ks]
            block = blocks[0] if len(ks) == 1 else jnp.concatenate(blocks, 1)
            other = swap(contract_first(block, grads_other).astype(BF), 1)
            whole = contract_first(block, grads_mine) + other.astype(F32)
            return [whole[i * own_rows : (i + 1) * own_rows] for i in range(len(ks))]

        mine = run(ring.scatter(terms))[0].astype(BF)
        mine = (mine.astype(F32) + swap(mine, 2).astype(F32)).astype(BF)
        return jnp.concatenate(order_halves(mine, swap(mine, 1)), 1)

    out_grad = part_sums(attended, mid_low)
    grad_attended = contract_last(mid_low, out_all).astype(BF)
    grads = jnp.concatenate(attend_back(query, key, value, grad_attended, tables), 1)
    unit_one, scale_one = normalize(tokens.astype(F32))
    gain_one = gains[:1]
    qkv_grad = part_sums((unit_one * gain_one).astype(BF), grads)
    grad_normed_one = contract_last(grads, qkv_all)
    gain_one_term = jnp.sum(grad_normed_one * unit_one, 0, keepdims=True)
    grad_input = norm_back(grad_normed_one * gain_one, unit_one, scale_one)

    gain_terms = jnp.concatenate([gain_one_term, gain_two_term], 0)
    gain_sums = cols(gain_terms, ring.at(0) * own_rows, own_rows)
    for k in range(1, count):
        gain_sums = gain_sums + ring.send(cols(gain_terms, ring.at(k) * own_rows, own_rows), k)
    gain_sums = gain_sums + swap(gain_sums, 1)
    gain_sums = gain_sums + swap(gain_sums, 2)
    return gate_grad, up_grad, down_grad, out_grad, qkv_grad, grad_input, gain_sums


def on_device(
    count,
    tokens,
    segments,
    norm_attn,
    w_query,
    key_weight,
    value_weight,
    w_out,
    norm_mlp,
    w_gate,
    w_up,
    w_down,
    cotangent,
):
    ring = Ring(count)
    sequence, width = tokens.shape[1], tokens.shape[2]
    own_rows = w_query.shape[0]
    ff = w_gate.shape[1]
    ff_own = ff // count
    wide_k = key_weight.shape[1]
    fits = feed_forward_bytes(count, sequence, width, ff_own) <= VMEM_BYTES
    kernels = fits and sequence == own_rows == TILE

    grad_output = cotangent.reshape(sequence, width)
    cosine, sine = rope_tables(segments)
    seg_row = segments.reshape(1, sequence)
    tables = (cosine, sine, seg_row.reshape(sequence, 1), seg_row)
    own = tokens.reshape(sequence, width)
    qkv_own = jnp.concatenate([w_query, key_weight, value_weight], 1)
    gains_own = jnp.zeros((8, own_rows), F32)
    gains_own = gains_own.at[0].set(norm_attn.astype(F32)).at[1].set(norm_mlp.astype(F32))
    bring = functools.partial(front, count) if kernels else functools.partial(front_parts, ring)
    qkv_all, out_all, w_both, low, gains, query, key, value, attended, middle, normed_two = bring(
        own, gains_own, grad_output, tables, qkv_own, w_out, w_gate, w_up, wide_k
    )
    w_both = w_both.reshape(width, 2 * ff_own)
    gain_one, gain_two = gains[:1], gains[1:2]

    if kernels:
        grad_normed_two, branch_two, sums = feed_forward(count, normed_two, low, w_both, w_down)
    else:
        grad_normed_two, branch_two, both_term, down_term = feed_forward_parts(
            ring, normed_two, low, w_both, w_down
        )
    output = middle + branch_two

    unit_two, scale_two = normalize(middle)
    gain_two_term = jnp.sum(grad_normed_two * unit_two, 0, keepdims=True)
    grad_middle = grad_output + norm_back(grad_normed_two * gain_two, unit_two, scale_two)
    grad_mid_low = grad_middle.astype(BF)

    if kernels:
        gate_grad, up_grad, down_grad, out_grad, qkv_grad, grad_input, gain_sums = back(
            count,
            sums,
            grad_mid_low,
            gain_two_term,
            attended,
            query,
            key,
            value,
            own,
            gains,
            tables,
            qkv_all,
            out_all,
        )
    else:
        gate_grad, up_grad, down_grad, out_grad, qkv_grad, grad_input, gain_sums = back_parts(
            ring,
            both_term,
            down_term,
            grad_mid_low,
            gain_two_term,
            attended,
            query,
            key,
            value,
            own,
            gains,
            tables,
            qkv_all,
            out_all,
        )
    grad_input = grad_middle + grad_input
    qkv_grad = qkv_grad.astype(F32)

    return (
        output.reshape(tokens.shape),
        grad_input.reshape(tokens.shape),
        gain_sums[0],
        qkv_grad[:, :width],
        qkv_grad[:, width : width + wide_k],
        qkv_grad[:, width + wide_k :],
        out_grad.astype(F32),
        gain_sums[1],
        gate_grad.reshape(own_rows, ff).astype(F32),
        up_grad.reshape(own_rows, ff).astype(F32),
        down_grad.reshape(ff_own, width).astype(F32),
    )


def solution(mesh):
    row, vector, matrix = P(("shard", "rep"), None, None), P("shard"), P("shard", None)
    in_specs = (row, P(("shard", "rep"), None), vector, matrix, matrix, matrix, matrix, vector)
    in_specs += (matrix, matrix, matrix, row)
    out_specs = (row, row, vector, matrix, matrix, matrix, matrix, vector, matrix, matrix, matrix)
    return jax.shard_map(
        functools.partial(on_device, mesh.shape["shard"]),
        mesh=mesh,
        in_specs=in_specs,
        out_specs=out_specs,
        check_vma=False,
    )
```

```python
import functools

import jax
import jax.numpy as jnp
from jax import lax
from jax.experimental import pallas as pl
from jax.experimental.pallas import tpu as pltpu
from jax.sharding import PartitionSpec as P

QUERY_HEADS = 32
KEY_VALUE_HEADS = 8
HEAD_SIZE = 64
GROUP = QUERY_HEADS // KEY_VALUE_HEADS

epsilon = 1e-05
masked_score = -1000000000.0
rope_base = 500000.0
WINDOW = 2
TILE = 256
WIDE_TILE = 512
LOAD_TILE = 128
VMEM_BYTES = 62 * 2**20
BF = jnp.bfloat16
F32 = jnp.float32


def dot(left, right):
    return jnp.dot(left, right, preferred_element_type=F32)


def contract_last(left, right):
    return lax.dot_general(left, right, (((1,), (1,)), ((), ())), preferred_element_type=F32)


def contract_first(left, right):
    return lax.dot_general(left, right, (((0,), (0,)), ((), ())), preferred_element_type=F32)


def positions(segment_ids):
    index = lax.broadcasted_iota(jnp.int32, segment_ids.shape, 1)
    first = jnp.concatenate(
        [
            jnp.ones_like(segment_ids[:, :1]),
            (segment_ids[:, 1:] != segment_ids[:, :-1]).astype(jnp.int32),
        ],
        1,
    )
    starts = lax.cummax(jnp.where(first > 0, index, 0), axis=1)
    return (index - starts).astype(F32)


def rope_tables(segment_ids):
    half = HEAD_SIZE // 2
    inverse = rope_base ** (-(2.0 * jnp.arange(half, dtype=F32)) / HEAD_SIZE)
    angle = positions(segment_ids)[0, :, None] * inverse
    cosine, sine = jnp.cos(angle), jnp.sin(angle)
    return jnp.concatenate([cosine] * 4, 1), jnp.concatenate([-sine, sine] * 2, 1)


def normalize(rows):
    scale_row = lax.rsqrt(jnp.mean(rows * rows, -1, keepdims=True) + epsilon)
    return rows * scale_row, scale_row


def norm_back(grad_unit, unit, scale_row):
    return scale_row * (grad_unit - unit * jnp.mean(grad_unit * unit, -1, keepdims=True))


def rotate(block, cosine, sine):
    lane = lax.broadcasted_iota(jnp.int32, cosine.shape, 1)
    lower = lane % HEAD_SIZE < HEAD_SIZE // 2
    parts = []
    for at in range(0, block.shape[1], 128):
        part = block[:, at : at + 128]
        other = jnp.where(
            lower, pltpu.roll(part, 128 - HEAD_SIZE // 2, 1), pltpu.roll(part, HEAD_SIZE // 2, 1)
        )
        parts.append(part * cosine + other * sine)
    return parts[0] if len(parts) == 1 else jnp.concatenate(parts, 1)


def stack_heads(block, key_head):
    first = key_head * GROUP
    return jnp.concatenate(
        [block[:, (first + i) * HEAD_SIZE : (first + i + 1) * HEAD_SIZE] for i in range(GROUP)], 0
    )


def unstack_heads(rows):
    count = rows.shape[0] // GROUP
    return [rows[i * count : (i + 1) * count] for i in range(GROUP)]


def softmax_rows(query, key, allowed):
    raw = contract_last(query, key) * HEAD_SIZE ** (-0.5)
    scores = jnp.where(allowed, raw, masked_score)
    exponent = jnp.exp(scores - jnp.max(scores, -1, keepdims=True))
    return exponent / jnp.sum(exponent, -1, keepdims=True)


def allowed_rows(seg_column, seg_row):
    count = seg_row.shape[1]
    shape = (count, count)
    causal = lax.broadcasted_iota(jnp.int32, shape, 0) >= lax.broadcasted_iota(jnp.int32, shape, 1)
    one = ((seg_column == seg_row) & causal).astype(jnp.int32)
    return jnp.concatenate([one] * GROUP, 0) > 0


def attend_kernel(q_ref, k_ref, v_ref, cos_ref, sin_ref, segc_ref, segr_ref, qo, ko, vo, ao):
    cosine, sine = cos_ref[...], sin_ref[...]
    allowed = allowed_rows(segc_ref[...], segr_ref[...])
    query = rotate(q_ref[...], cosine, sine).astype(BF)
    key = rotate(k_ref[...], cosine, sine).astype(BF)
    value = v_ref[...].astype(BF)
    qo[...] = query
    ko[...] = key
    vo[...] = value
    heads = []
    for j in range(2):
        cols = slice(j * HEAD_SIZE, (j + 1) * HEAD_SIZE)
        probs = softmax_rows(stack_heads(query, j), key[:, cols], allowed).astype(BF)
        heads += unstack_heads(dot(probs, value[:, cols]).astype(BF))
    ao[...] = jnp.concatenate(heads, 1)


def attend_back_kernel(q_ref, k_ref, v_ref, g_ref, cos_ref, sin_ref, segc_ref, segr_ref, gq, gk, gv):
    cosine, sine = cos_ref[...], -sin_ref[...]
    allowed = allowed_rows(segc_ref[...], segr_ref[...])
    query, key, value, grad = q_ref[...], k_ref[...], v_ref[...], g_ref[...]
    heads, keys, values = [], [], []
    for j in range(2):
        cols = slice(j * HEAD_SIZE, (j + 1) * HEAD_SIZE)
        rows, grad_rows = stack_heads(query, j), stack_heads(grad, j)
        probs = softmax_rows(rows, key[:, cols], allowed)
        grad_probs = contract_last(grad_rows, value[:, cols])
        grad_scores = (
            probs * (grad_probs - jnp.sum(probs * grad_probs, -1, keepdims=True))
        ).astype(BF)
        heads += unstack_heads(dot(grad_scores, key[:, cols]) * HEAD_SIZE ** (-0.5))
        keys.append(contract_first(grad_scores, rows) * HEAD_SIZE ** (-0.5))
        values.append(contract_first(probs.astype(BF), grad_rows))
    gq[...] = rotate(jnp.concatenate(heads, 1), cosine, sine).astype(BF)
    gk[...] = rotate(jnp.concatenate(keys, 1), cosine, sine).astype(BF)
    gv[...] = jnp.concatenate(values, 1).astype(BF)


def attention_specs(count):
    wide = pl.BlockSpec((count, 2 * GROUP * HEAD_SIZE), lambda i: (0, i))
    thin = pl.BlockSpec((count, 2 * HEAD_SIZE), lambda i: (0, i))
    whole = lambda shape: pl.BlockSpec(shape, lambda i: (0, 0))
    fixed = [whole((count, 128)), whole((count, 128)), whole((count, 1)), whole((1, count))]
    return wide, thin, fixed


def attend(query_lin, key_lin, value_lin, tables):
    count = query_lin.shape[0]
    wide, thin, fixed = attention_specs(count)
    kinds = [jax.ShapeDtypeStruct(a.shape, BF) for a in (query_lin, key_lin, value_lin, query_lin)]
    return pl.pallas_call(
        attend_kernel,
        grid=(KEY_VALUE_HEADS // 2,),
        in_specs=[wide, thin, thin] + fixed,
        out_specs=[wide, thin, thin, wide],
        out_shape=kinds,
        compiler_params=pltpu.CompilerParams(vmem_limit_bytes=48 * 2**20),
        cost_estimate=pl.CostEstimate(
            flops=2 * 10**9, bytes_accessed=6 * 10**6, transcendentals=2 * 10**6
        ),
    )(query_lin, key_lin, value_lin, *tables)


def attend_back(query, key, value, grad, tables):
    count = query.shape[0]
    wide, thin, fixed = attention_specs(count)
    kinds = [jax.ShapeDtypeStruct(a.shape, BF) for a in (query, key, value)]
    return pl.pallas_call(
        attend_back_kernel,
        grid=(KEY_VALUE_HEADS // 2,),
        in_specs=[wide, thin, thin, wide] + fixed,
        out_specs=[wide, thin, thin],
        out_shape=kinds,
        compiler_params=pltpu.CompilerParams(vmem_limit_bytes=48 * 2**20),
        cost_estimate=pl.CostEstimate(
            flops=4 * 10**9, bytes_accessed=6 * 10**6, transcendentals=2 * 10**6
        ),
    )(query, key, value, grad, *tables)


def ring_order(count):
    return list(range(0, count, 2)) + list(range(count - 1, 0, -2)) if count % 2 == 0 else list(range(count))


class Ring:
    def __init__(self, count):
        self.count = count
        self.half = count // 2
        self.order = ring_order(count)
        inverse = [self.order.index(i) for i in range(count)]
        self.table = jnp.asarray(self.order, jnp.int32)
        self.turns = []
        self.place = jnp.asarray(inverse, jnp.int32)[lax.axis_index("shard")]

    def at(self, offset):
        return self.table[(self.place + offset + self.count) % self.count]

    def send(self, array, offset):
        n, order = self.count, self.order
        pairs = [(order[i], order[(i + offset) % n]) for i in range(n)]
        return lax.ppermute(array, "shard", pairs)

    def queue(self, *sends):
        arrays = [array for array, _ in sends]
        if len(self.turns) >= WINDOW:
            arrays, _ = lax.optimization_barrier((arrays, self.turns[-WINDOW]))
        got = [self.send(array, offset) for array, (_, offset) in zip(arrays, sends)]
        self.turns.append(got[:2])
        return got

    def gather(self, array):
        cut = array.shape[0] // 2
        ahead = back = array
        out = {0: array}
        for k in range(1, self.half):
            ahead, back = self.queue((ahead, 1), (back, -1))
            out[k], out[-k] = ahead, back
            yield out
        out[self.half] = jnp.concatenate(self.queue((ahead[:cut], 1), (back[cut:], -1)), 0)
        yield out

    def scatter(self, terms):
        (far,) = terms((self.half,))
        far = far.astype(BF)
        cut = far.shape[0] // 2
        ahead, back = self.queue((far[:cut], 1), (far[cut:], -1))
        yield None
        for k in range(self.half - 1, 0, -1):
            up, down = terms((k, -k))
            if k == self.half - 1:
                up = jnp.concatenate([up[:cut] + ahead.astype(F32), up[cut:]], 0)
                down = jnp.concatenate([down[:cut], down[cut:] + back.astype(F32)], 0)
            else:
                up, down = up + ahead.astype(F32), down + back.astype(F32)
            ahead, back = self.queue((up.astype(BF), 1), (down.astype(BF), -1))
            if k > 1:
                yield None
        (own,) = terms((0,))
        yield own + ahead.astype(F32) + back.astype(F32)


def run(*flows):
    flows = list(flows)
    last = [None] * len(flows)
    live = list(range(len(flows)))
    while live:
        for i in list(live):
            try:
                last[i] = next(flows[i])
            except StopIteration:
                live.remove(i)
    return last


def ring_place(count, shard):
    return jnp.where(shard % 2 == 0, shard // 2, count - 1 - shard // 2)


def ring_shard(count, place):
    place = (place + count) % count
    return jnp.where(place < count // 2, 2 * place, 2 * (count - 1 - place) + 1)


def core_partner(rep):
    return rep + 1 - 2 * (rep % 2)


def chip_partner(rep):
    return (rep + 2) % 4


def greet(devices):
    barrier = pltpu.get_barrier_semaphore()
    for device in devices:
        pl.semaphore_signal(
            barrier, inc=1, device_id=device, device_id_type=pl.DeviceIdType.MESH
        )
    pl.semaphore_wait(barrier, len(devices))


def remote_copy(src, dst, send, recv, device):
    return pltpu.make_async_remote_copy(
        src_ref=src,
        dst_ref=dst,
        send_sem=send,
        recv_sem=recv,
        device_id=device,
        device_id_type=pl.DeviceIdType.MESH,
    )


def front_kernel(
    count,
    tokens_ref,
    gains_ref,
    cotangent_ref,
    cos_ref,
    sin_ref,
    segc_ref,
    segr_ref,
    query_own_ref,
    key_own_ref,
    value_own_ref,
    out_own_ref,
    gate_ref,
    up_ref,
    qkv_all_ref,
    out_all_ref,
    both_ref,
    low_all_ref,
    gains_all_ref,
    query_ref,
    key_ref,
    value_ref,
    attended_ref,
    middle_ref,
    normed_two_ref,
    low_own,
    both_own,
    qkv_all,
    out_all,
    normed,
    linear,
    own_sem,
    load_sem,
    gain_send,
    gain_recv,
    ring_send,
    ring_recv,
    core_send,
    core_recv,
    chip_send,
    chip_recv,
    across_send,
    across_recv,
    group_send,
    group_recv,
    low_send,
    low_recv,
):
    half = count // 2
    me, rep = lax.axis_index("shard"), lax.axis_index("rep")
    core, chip = rep % 2, rep // 2
    place = ring_place(count, me)
    others = [ring_shard(count, place + k) for k in range(1, count)]
    near = ({"shard": ring_shard(count, place + 1)}, {"shard": ring_shard(count, place - 1)})
    other_core, other_chip = {"rep": core_partner(rep)}, {"rep": chip_partner(rep)}
    own_rows = query_own_ref.shape[0]
    quarter = own_rows // 4
    cut = quarter // 2
    ff_own = gate_ref.shape[1] // count
    rows, width = tokens_ref.shape
    full_refs = (qkv_all_ref, out_all_ref)
    inside = (qkv_all, out_all)

    def rows_at(start, size):
        return pl.ds(pl.multiple_of(start, cut), size)

    def shard_rows(shard):
        return rows_at(shard * own_rows, own_rows)

    def piece_of(shard, which_core, which_chip, part=None):
        start = shard * own_rows + (2 * which_core + which_chip) * quarter
        if part is None:
            return rows_at(start, quarter)
        return rows_at(start + part * cut, cut)

    own_loads = [
        pltpu.make_async_copy(out_own_ref, out_all.at[shard_rows(me)], own_sem.at[6])
    ]
    start = 0
    for index, ref in enumerate((query_own_ref, key_own_ref, value_own_ref)):
        columns = pl.ds(start, ref.shape[1])
        own_loads.append(
            pltpu.make_async_copy(ref, qkv_all.at[shard_rows(me), columns], own_sem.at[7 + index])
        )
        start += ref.shape[1]
    keep = [
        pltpu.make_async_copy(
            inside[i].at[shard_rows(me)], full_refs[i].at[shard_rows(me)], own_sem.at[i]
        )
        for i in range(2)
    ]
    for i, ref in enumerate((gate_ref, up_ref)):
        block = (rows_at(rep * quarter, quarter), pl.ds(pl.multiple_of(me * ff_own, 128), ff_own))
        own_loads.append(
            pltpu.make_async_copy(
                ref.at[block], both_own.at[:, pl.ds(i * ff_own, ff_own)], own_sem.at[2 + i]
            )
        )
    for copy in own_loads:
        copy.start()
    gains_all_ref[:, pl.ds(pl.multiple_of(me * own_rows, 128), own_rows)] = gains_ref[...]
    low_own[...] = cotangent_ref[...].astype(BF)
    for copy in own_loads:
        copy.wait()
    keep.append(pltpu.make_async_copy(low_own, low_all_ref.at[pl.ds(0, rows)], own_sem.at[4]))
    keep.append(pltpu.make_async_copy(both_own, both_ref.at[me, rep], own_sem.at[5]))
    for copy in keep:
        copy.start()

    greet([{"shard": shard} for shard in others] + [other_core, other_chip])

    def gain_copy(k):
        columns = pl.ds(pl.multiple_of(me * own_rows, 128), own_rows)
        return remote_copy(
            gains_ref,
            gains_all_ref.at[:, columns],
            gain_send.at[k - 1],
            gain_recv.at[k - 1],
            {"shard": others[k - 1]},
        )

    def across(k, which):
        ref = (gate_ref, up_ref)[which]
        there = others[k - 1]
        columns = pl.ds(pl.multiple_of(there * ff_own, 128), ff_own)
        return remote_copy(
            ref.at[rows_at(rep * quarter, quarter), columns],
            both_ref.at[me, rep, :, pl.ds(which * ff_own, ff_own)],
            across_send.at[which, k - 1],
            across_recv.at[which, k - 1],
            {"shard": there},
        )

    def ring_copy(i, direction, step):
        sign = 1 if direction == 0 else -1
        shard = ring_shard(count, place - sign * (step - 1))
        if step < half:
            at = piece_of(shard, core, chip)
        else:
            at = piece_of(shard, core, chip, direction)
        src = full_refs[i].at[at]
        if step == 1:
            src = inside[i].at[at]
        return remote_copy(
            src,
            full_refs[i].at[at],
            ring_send.at[i, direction, step - 1],
            ring_recv.at[i, direction, step - 1],
            near[direction],
        )

    def chip_copy(i, k):
        at = piece_of(ring_shard(count, place - k), core, chip)
        slot = k + half - 1
        return remote_copy(
            full_refs[i].at[at],
            full_refs[i].at[at],
            chip_send.at[i, slot],
            chip_recv.at[i, slot],
            other_chip,
        )

    def core_copy(i, k, which):
        from_chip = chip if which == 0 else 1 - chip
        at = piece_of(ring_shard(count, place - k), core, from_chip)
        slot = k + half - 1
        return remote_copy(
            full_refs[i].at[at],
            full_refs[i].at[at],
            core_send.at[i, which, slot],
            core_recv.at[i, which, slot],
            other_core,
        )

    def load(i, k):
        at = shard_rows(ring_shard(count, place - k))
        return pltpu.make_async_copy(
            full_refs[i].at[at], inside[i].at[at], load_sem.at[i, k + half - 1]
        )

    def low_copy(direction, step):
        base = 0 if direction == 0 else half
        to, size = (base + step) * rows, rows
        source = to - rows
        if step == half:
            size = rows // 2
            to = half * rows + direction * size
            source = (base + half - 1) * rows + direction * size
        src = low_all_ref.at[pl.ds(source, size)] if step > 1 else low_own
        return remote_copy(
            src,
            low_all_ref.at[pl.ds(to, size)],
            low_send.at[direction, step - 1],
            low_recv.at[direction, step - 1],
            near[direction],
        )

    def start_low(step):
        for direction in range(2):
            low_copy(direction, step).start()

    def finish_low(step):
        for direction in range(2):
            low_copy(direction, step).wait_recv()
        if step < half:
            start_low(step + 1)

    def start_step(i, step):
        for direction in range(2):
            ring_copy(i, direction, step).start()

    def places(step):
        return (step, -step) if step < half else (half,)

    def finish_step(i, step):
        for direction in range(2):
            ring_copy(i, direction, step).wait_recv()
        if step < half:
            start_step(i, step + 1)
        for k in places(step):
            core_copy(i, k, 0).start()

    def start_chip(i, step):
        for k in places(step):
            chip_copy(i, k).start()

    def pass_step(i, step):
        for k in places(step):
            chip_copy(i, k).wait_recv()
            core_copy(i, k, 1).start()

    def load_step(i, step):
        for k in places(step):
            for which in range(2):
                core_copy(i, k, which).wait_recv()
            load(i, k).start()

    for k in range(1, count):
        gain_copy(k).start()
    start_step(0, 1)
    resid = tokens_ref[...].astype(F32)
    unit, _ = normalize(resid)
    for k in range(1, count):
        gain_copy(k).wait_recv()
    normed[...] = (unit * gains_all_ref[0:1, :]).astype(BF)

    for step in range(1, half + 1):
        finish_step(0, step)
        start_chip(0, step)
        if step == half - 1:
            for k in range(1, count):
                for which in range(2):
                    across(k, which).start()
    start_step(1, 1)
    for step in range(1, half + 1):
        pass_step(0, step)
        if step > 1:
            load_step(0, step - 1)

    def group_copy(index, quarter_at, device):
        at = both_ref.at[:, quarter_at]
        return remote_copy(at, at, group_send.at[index], group_recv.at[index], device)

    chip_copies = [group_copy(0, rep, other_chip)]
    core_copies = [
        group_copy(1, rep, other_core),
        group_copy(2, chip_partner(rep), other_core),
    ]
    load_step(0, half)
    for k in range(-(half - 1), half + 1):
        if k:
            load(0, k).wait()

    def linear_tile(j, carry):
        at = pl.ds(pl.multiple_of(j * TILE, TILE), TILE)
        linear[:, at] = dot(normed[...], qkv_all[:, at])
        return carry

    lax.fori_loop(0, linear.shape[1] // TILE, linear_tile, 0)

    cosine, sine = cos_ref[...], sin_ref[...]
    wide, thin = 2 * GROUP * HEAD_SIZE, 2 * HEAD_SIZE
    key_at, value_at = width, width + key_ref.shape[1]

    def heads_pair(pair):
        allowed = allowed_rows(segc_ref[...], segr_ref[...])
        wide_at = pl.ds(pair * wide, wide)
        thin_at = pl.ds(pair * thin, thin)
        query = rotate(linear[:, wide_at], cosine, sine).astype(BF)
        key = rotate(linear[:, pl.ds(key_at + pair * thin, thin)], cosine, sine).astype(BF)
        value = linear[:, pl.ds(value_at + pair * thin, thin)].astype(BF)
        query_ref[:, wide_at] = query
        key_ref[:, thin_at] = key
        value_ref[:, thin_at] = value
        heads = []
        for j in range(2):
            cols = slice(j * HEAD_SIZE, (j + 1) * HEAD_SIZE)
            probs = softmax_rows(stack_heads(query, j), key[:, cols], allowed).astype(BF)
            heads += unstack_heads(dot(probs, value[:, cols]).astype(BF))
        attended_ref[:, wide_at] = jnp.concatenate(heads, 1)

    pairs = KEY_VALUE_HEADS // 2
    for turn in range(max(pairs, half)):
        if turn < half:
            finish_step(1, turn + 1)
            start_chip(1, turn + 1)
        if turn == half - 2:
            start_low(1)
        if turn < pairs:
            heads_pair(turn)
    for copy in keep:
        copy.wait()
    for k in range(1, count):
        for which in range(2):
            across(k, which).wait_recv()
    chip_copies[0].start()
    core_copies[0].start()
    for step in range(1, half + 1):
        pass_step(1, step)
        if step > 1:
            load_step(1, step - 1)
        if step % 2 == 0 and step // 2 < half:
            finish_low(step // 2)
    load_step(1, half)
    for k in range(-(half - 1), half + 1):
        if k:
            load(1, k).wait()

    def branch_tile(j, carry):
        at = pl.ds(pl.multiple_of(j * TILE, TILE), TILE)
        branch = dot(attended_ref[...], out_all[:, at])
        middle_ref[:, at] = tokens_ref[:, at].astype(F32) + branch
        return carry

    lax.fori_loop(0, width // TILE, branch_tile, 0)
    unit, _ = normalize(middle_ref[...])
    normed_two_ref[...] = (unit * gains_all_ref[1:2, :]).astype(BF)

    for step in range(half // 2 + 1, half + 1):
        finish_low(step)
    chip_copies[0].wait_recv()
    core_copies[1].start()
    for copy in core_copies:
        copy.wait_recv()
    for copy in chip_copies + core_copies:
        copy.wait_send()
    for step in range(1, half + 1):
        for direction in range(2):
            low_copy(direction, step).wait_send()
    for i in range(2):
        for step in range(1, half + 1):
            for direction in range(2):
                ring_copy(i, direction, step).wait_send()
            for k in places(step):
                chip_copy(i, k).wait_send()
                for which in range(2):
                    core_copy(i, k, which).wait_send()
    for k in range(1, count):
        gain_copy(k).wait_send()
        for which in range(2):
            across(k, which).wait_send()


def front(count, tokens, gains, cotangent, tables, own, gate_own, up_own):
    rows, width = tokens.shape
    own_rows, wide_k = own[1].shape
    qkv_width = width + 2 * wide_k
    ff_own = gate_own.shape[1] // count
    half = count // 2
    here = pl.BlockSpec(memory_space=pl.ANY)
    inside = pl.BlockSpec(memory_space=pltpu.VMEM)
    kind = jax.ShapeDtypeStruct
    dma = pltpu.SemaphoreType.DMA
    return pl.pallas_call(
        functools.partial(front_kernel, count),
        in_specs=[inside] * 7 + [here] * 6,
        out_specs=[here] * 4 + [inside] * 7,
        out_shape=[
            kind((count * own_rows, qkv_width), BF),
            kind((count * own_rows, width), BF),
            kind((count, 4, own_rows // 4, 2 * ff_own), BF),
            kind((count * rows, width), BF),
            kind((gains.shape[0], width), F32),
            kind((rows, width), BF),
            kind((rows, wide_k), BF),
            kind((rows, wide_k), BF),
            kind((rows, width), BF),
            kind((rows, width), F32),
            kind((rows, width), BF),
        ],
        scratch_shapes=[
            pltpu.VMEM((rows, width), BF),
            pltpu.VMEM((own_rows // 4, 2 * ff_own), BF),
            pltpu.VMEM((count * own_rows, qkv_width), BF),
            pltpu.VMEM((count * own_rows, width), BF),
            pltpu.VMEM((rows, width), BF),
            pltpu.VMEM((rows, qkv_width), F32),
            dma((10,)),
            dma((2, count)),
            dma((count - 1,)),
            dma((count - 1,)),
            dma((2, 2, half)),
            dma((2, 2, half)),
            dma((2, 2, count)),
            dma((2, 2, count)),
            dma((2, count)),
            dma((2, count)),
            dma((2, count - 1)),
            dma((2, count - 1)),
            dma((3,)),
            dma((3,)),
            dma((2, half)),
            dma((2, half)),
        ],
        compiler_params=pltpu.CompilerParams(
            collective_id=1, has_side_effects=True, vmem_limit_bytes=VMEM_BYTES
        ),
        cost_estimate=pl.CostEstimate(
            flops=2 * rows * width * (qkv_width + width) + 2 * 10**9,
            bytes_accessed=60 * 10**6,
            transcendentals=2 * 10**6,
        ),
    )(tokens, gains, cotangent, *tables, *own, gate_own, up_own)


def feed_forward_kernel(
    count,
    normed_ref,
    low_ref,
    both_ref,
    down_ref,
    grad_ref,
    branch_ref,
    sums_ref,
    down_grad_ref,
    normed,
    low,
    hidden,
    grads,
    w_both,
    w_down,
    turned,
    staged,
    from_core,
    core_sums,
    from_chip,
    group_sums,
    result_tile,
    outgoing,
    incoming,
    local_sem,
    gather_send,
    gather_recv,
    scatter_send,
    scatter_recv,
    credit,
    core_send,
    core_recv,
    chip_send,
    chip_recv,
    group_credit,
    sums_sem,
    result_sem,
    down_send,
    down_recv,
):
    half = count // 2
    rows = normed_ref.shape[0]
    cut = rows // 2
    width = normed_ref.shape[1]
    ff = down_ref.shape[0]
    place = ring_place(count, lax.axis_index("shard"))
    neighbours = (ring_shard(count, place + 1), ring_shard(count, place - 1))
    rep = lax.axis_index("rep")
    core, chip = rep % 2, rep // 2
    other_core, other_chip = {"rep": core_partner(rep)}, {"rep": chip_partner(rep)}
    everywhere = pl.ds(0, rows)
    halves = (pl.ds(0, cut), pl.ds(cut, cut))

    def at(slot, part=None):
        start, size = (0, rows) if part is None else (part * cut, cut)
        return pl.ds(pl.multiple_of(slot * rows + start, cut), size)

    def tile(j):
        return pl.ds(pl.multiple_of(j * TILE, TILE), TILE)

    def remote(src, dst, send, recv, direction):
        return remote_copy(src, dst, send, recv, {"shard": neighbours[direction]})

    loads = [
        pltpu.make_async_copy(normed_ref, normed.at[at(0)], local_sem.at[0]),
        pltpu.make_async_copy(low_ref, low, local_sem.at[1]),
        pltpu.make_async_copy(both_ref, w_both, local_sem.at[2]),
        pltpu.make_async_copy(down_ref, w_down, local_sem.at[3]),
    ]
    for load in loads:
        load.start()

    for chain in range(2):
        for direction in range(2):
            blank = halves[1 - direction]
            incoming[chain, direction, 0, blank] = jnp.zeros((cut, width), BF)

    greet([{"shard": neighbour} for neighbour in neighbours] + [other_core, other_chip])

    def gathered(part, direction, step):
        base = 0 if direction == 0 else half
        if isinstance(step, int) and step == 1:
            source = 0
        else:
            source = jnp.where(step == 1, 0, base + step - 1)
        return remote(
            normed.at[at(source, part)],
            normed.at[at(base + step, part)],
            gather_send.at[part, direction, step - 1],
            gather_recv.at[part, direction, step - 1],
            direction,
        )

    def gathered_last(direction):
        source = half - 1 if direction == 0 else 2 * half - 1
        return remote(
            normed.at[at(source, direction)],
            normed.at[at(half, direction)],
            gather_send.at[0, direction, half - 1],
            gather_recv.at[0, direction, half - 1],
            direction,
        )

    def products(slot):
        mine = at(slot)

        def body(j, carry):
            gate_at, up_at = tile(j), tile(j + ff // TILE)
            own = normed[mine, :]
            gate = dot(own, w_both[:, gate_at])
            up = dot(own, w_both[:, up_at])
            grad_hidden = contract_last(low[mine, :], w_down[gate_at, :])
            sigmoid = jax.nn.sigmoid(gate)
            silu = gate * sigmoid
            hidden[mine, gate_at] = (silu * up).astype(BF)
            grads[mine, gate_at] = (
                grad_hidden * up * sigmoid * (1.0 + gate * (1.0 - sigmoid))
            ).astype(BF)
            grads[mine, up_at] = (grad_hidden * silu).astype(BF)
            return carry

        lax.fori_loop(0, ff // TILE, body, 0)

    both_ways = ((0, 0), (0, 1), (1, 0), (1, 1))
    loads[0].wait()
    for part, direction in both_ways:
        gathered(part, direction, 1).start()
    for load in loads[1:]:
        load.wait()
    products(0)

    def gather_step(step, carry):
        for part, direction in both_ways:
            gathered(part, direction, step).wait_recv()

            @pl.when(step < half - 1)
            def _():
                gathered(part, direction, step + 1).start()

            if part == direction:

                @pl.when(step == half - 1)
                def _():
                    gathered_last(direction).start()

        products(step)

        @pl.when(step < half - 1)
        def _():
            products(half + step)

        return carry

    lax.fori_loop(1, half, gather_step, 0)
    for direction in range(2):
        gathered_last(direction).wait_recv()
    products(half)

    def term(chain, rows_at, j):
        if chain == 0:
            return contract_last(grads[rows_at, :], w_both[tile(j), :])
        return dot(hidden[rows_at, :], w_down[:, tile(j)])

    def scattered(chain, direction, step):
        if isinstance(step, int) and step == 0:
            own, there = halves[direction], 0
        else:
            own, there = everywhere, step % 2
        return remote(
            outgoing.at[chain, direction, own],
            incoming.at[chain, direction, there, own],
            scatter_send.at[chain, direction, step],
            scatter_recv.at[chain, direction, step],
            direction,
        )

    units = (width + ff) // TILE
    per_step = -(-(units + 3) // (half - 1))
    quarter = TILE // 4

    def core_copy(unit):
        spot = unit % 2
        return remote_copy(
            staged.at[spot, :, 1 - core],
            from_core.at[spot],
            core_send.at[spot],
            core_recv.at[spot],
            other_core,
        )

    def chip_copy(unit):
        spot = unit % 3
        return remote_copy(
            core_sums.at[spot, 1 - chip],
            from_chip.at[spot],
            chip_send.at[spot],
            chip_recv.at[spot],
            other_chip,
        )

    down_units = ff // TILE

    def sums_copy(unit, down):
        spot = unit % 2
        target = down_grad_ref.at[unit, rep] if down else sums_ref.at[unit - down_units]
        return pltpu.make_async_copy(group_sums.at[spot], target, sums_sem.at[spot])

    def for_sums(unit, act):
        @pl.when(unit < down_units)
        def _():
            act(sums_copy(unit, True))

        @pl.when(unit >= down_units)
        def _():
            act(sums_copy(unit, False))

    def down_copy(index):
        at = down_grad_ref.at[:, chip_partner(rep) if index == 2 else rep]
        return remote_copy(
            at,
            at,
            down_send.at[index],
            down_recv.at[index],
            other_chip if index == 0 else other_core,
        )

    def give_credit(which, device):
        pl.semaphore_signal(
            group_credit.at[which], inc=1, device_id=device, device_id_type=pl.DeviceIdType.MESH
        )

    def weight_unit(unit):
        spot = unit % 2

        def from_arrays(left, right, block):
            def turn(c, carry):
                turned[:, at(c)] = left[at(c), tile(block)].T
                return carry

            lax.fori_loop(0, count, turn, 0)

            def body(j, carry):
                value = dot(turned[...], right[:, tile(j)]).astype(BF)
                staged[spot, :, :, :, tile(j)] = value.reshape(2, 2, quarter, TILE)
                return carry

            lax.fori_loop(0, width // TILE, body, 0)

        @pl.when(unit < down_units)
        def _():
            from_arrays(hidden, low, unit)

        @pl.when(unit >= down_units)
        def _():
            from_arrays(normed, grads, unit - down_units)

        @pl.when(unit >= 2)
        def _():
            pl.semaphore_wait(group_credit.at[0], 1)

        core_copy(unit).start()

    def sum_over_cores(unit):
        spot, place_of = unit % 2, unit % 3
        core_copy(unit).wait()
        for y in range(2):
            total = staged[spot, y, core].astype(F32) + from_core[spot, y].astype(F32)
            core_sums[place_of, y] = total.astype(BF)

        @pl.when(unit < units - 2)
        def _():
            give_credit(0, other_core)

        @pl.when(unit >= 3)
        def _():
            pl.semaphore_wait(group_credit.at[1], 1)

        chip_copy(unit).start()

    def sum_over_chips(unit):
        spot, place_of = unit % 2, unit % 3
        chip_copy(unit).wait()

        @pl.when(unit >= 2)
        def _():
            for_sums(unit - 2, lambda copy: copy.wait())

        total = core_sums[place_of, chip].astype(F32) + from_chip[place_of].astype(F32)
        group_sums[spot] = total.astype(BF)

        @pl.when(unit < units - 3)
        def _():
            give_credit(1, other_chip)

        for_sums(unit, lambda copy: copy.start())

    def weight_step(turn):
        @pl.when(turn < units)
        def _():
            weight_unit(turn)

        @pl.when((turn >= 1) & (turn <= units))
        def _():
            sum_over_cores(turn - 1)

        @pl.when(turn == units)
        def _():
            for index in range(2):
                down_copy(index).start()

        @pl.when(turn >= 3)
        def _():
            sum_over_chips(turn - 3)

    for chain in range(2):

        def first(j, carry):
            value = term(chain, at(half), j).astype(BF)
            outgoing[chain, 0, halves[0], tile(j)] = value[:cut]
            outgoing[chain, 1, halves[1], tile(j)] = value[cut:]
            return carry

        lax.fori_loop(0, width // TILE, first, 0)
        for direction in range(2):
            scattered(chain, direction, 0).start()

    products(2 * half - 1)

    def scatter_step(step, carry):
        k = half - step
        for chain in range(2):
            for direction in range(2):
                slot = half + k if direction == 0 else k

                @pl.when(step == 1)
                def _():
                    scattered(chain, direction, 0).wait()

                @pl.when(step > 1)
                def _():
                    scattered(chain, direction, step - 1).wait()
                    pl.semaphore_wait(credit.at[chain, direction], 1)

                def add(j, carry):
                    value = term(chain, at(slot), j)
                    value += incoming[chain, direction, (step - 1) % 2, :, tile(j)].astype(F32)
                    outgoing[chain, direction, :, tile(j)] = value.astype(BF)
                    return carry

                lax.fori_loop(0, width // TILE, add, 0)
                scattered(chain, direction, step).start()

                @pl.when(step < half - 1)
                def _():
                    pl.semaphore_signal(
                        credit.at[chain, direction],
                        inc=1,
                        device_id={"shard": neighbours[1 - direction]},
                        device_id_type=pl.DeviceIdType.MESH,
                    )

        lax.fori_loop(
            (step - 1) * per_step,
            jnp.minimum(step * per_step, units + 3),
            lambda turn, c: (weight_step(turn), c)[1],
            0,
        )
        return carry

    lax.fori_loop(1, half, scatter_step, 0)

    for chain, result in enumerate((grad_ref, branch_ref)):
        for direction in range(2):
            scattered(chain, direction, half - 1).wait()

        def result_copy(j):
            return pltpu.make_async_copy(
                result_tile.at[j % 2], result.at[:, tile(j)], result_sem.at[j % 2]
            )

        def last(j, carry):
            @pl.when(j >= 2)
            def _():
                result_copy(j - 2).wait()

            value = term(chain, at(0), j)
            for direction in range(2):
                value += incoming[chain, direction, (half - 1) % 2, :, tile(j)].astype(F32)
            result_tile[j % 2] = value
            result_copy(j).start()
            return carry

        lax.fori_loop(0, width // TILE, last, 0)
        for j in (width // TILE - 2, width // TILE - 1):
            result_copy(j).wait()

    down_copy(0).wait_recv()
    down_copy(2).start()
    for unit in (units - 2, units - 1):
        sums_copy(unit, False).wait()
    down_copy(0).wait_send()
    for index in (1, 2):
        down_copy(index).wait()
    for part, direction in both_ways:
        lax.fori_loop(
            1,
            half,
            lambda step, c: (gathered(part, direction, step).wait_send(), c)[1],
            0,
        )
    for direction in range(2):
        gathered_last(direction).wait_send()


def feed_forward_bytes(count, rows, width, ff):
    tokens = count * rows
    return 2 * (
        tokens * (2 * width + 3 * ff)
        + 3 * width * ff
        + TILE * tokens
        + 6 * TILE * width
        + 12 * rows * width
        + 4 * TILE * rows
    )


def feed_forward(count, normed, low, w_both, w_down):
    rows, width = normed.shape
    ff = w_down.shape[0]
    tokens = count * rows
    half = count // 2
    quarter = TILE // 4
    here = pl.BlockSpec(memory_space=pl.ANY)
    dma = pltpu.SemaphoreType.DMA
    return pl.pallas_call(
        functools.partial(feed_forward_kernel, count),
        in_specs=[here] * 4,
        out_specs=[here] * 4,
        out_shape=[
            jax.ShapeDtypeStruct((rows, width), F32),
            jax.ShapeDtypeStruct((rows, width), F32),
            jax.ShapeDtypeStruct((width // TILE, quarter, width), BF),
            jax.ShapeDtypeStruct((ff // TILE, 4, quarter, width), BF),
        ],
        scratch_shapes=[
            pltpu.VMEM((tokens, width), BF),
            pltpu.VMEM((tokens, width), BF),
            pltpu.VMEM((tokens, ff), BF),
            pltpu.VMEM((tokens, 2 * ff), BF),
            pltpu.VMEM((width, 2 * ff), BF),
            pltpu.VMEM((ff, width), BF),
            pltpu.VMEM((TILE, tokens), BF),
            pltpu.VMEM((2, 2, 2, quarter, width), BF),
            pltpu.VMEM((2, 2, quarter, width), BF),
            pltpu.VMEM((3, 2, quarter, width), BF),
            pltpu.VMEM((3, quarter, width), BF),
            pltpu.VMEM((2, quarter, width), BF),
            pltpu.VMEM((2, rows, TILE), F32),
            pltpu.VMEM((2, 2, rows, width), BF),
            pltpu.VMEM((2, 2, 2, rows, width), BF),
            dma((4,)),
            dma((2, 2, half)),
            dma((2, 2, half)),
            dma((2, 2, half)),
            dma((2, 2, half)),
            pltpu.SemaphoreType.REGULAR((2, 2)),
            dma((2,)),
            dma((2,)),
            dma((3,)),
            dma((3,)),
            pltpu.SemaphoreType.REGULAR((2,)),
            dma((2,)),
            dma((2,)),
            dma((3,)),
            dma((3,)),
        ],
        compiler_params=pltpu.CompilerParams(
            collective_id=0, has_side_effects=True, vmem_limit_bytes=VMEM_BYTES
        ),
        cost_estimate=pl.CostEstimate(
            flops=18 * tokens * width * ff, bytes_accessed=50 * 10**6, transcendentals=tokens * ff
        ),
    )(normed, low, w_both, w_down)


def middle_back_kernel(middle_ref, grad_ref, cotangent_ref, gain_ref, out_ref, low_ref, term_ref):
    unit, scale_row = normalize(middle_ref[...])
    grad = grad_ref[...]
    total = cotangent_ref[...] + norm_back(grad * gain_ref[...], unit, scale_row)
    out_ref[...] = total
    low_ref[...] = total.astype(BF)
    term = jnp.sum(grad * unit, 0, keepdims=True)

    @pl.when(pl.program_id(0) == 0)
    def _():
        term_ref[...] = term

    @pl.when(pl.program_id(0) > 0)
    def _():
        term_ref[...] += term


def middle_back(middle, grad, cotangent, gain):
    rows, width = middle.shape
    block = pl.BlockSpec((rows // 8, width), lambda i: (i, 0))
    fixed = pl.BlockSpec((1, width), lambda i: (0, 0))
    kind = jax.ShapeDtypeStruct
    return pl.pallas_call(
        middle_back_kernel,
        grid=(8,),
        in_specs=[block, block, block, fixed],
        out_specs=[block, block, fixed],
        out_shape=[kind((rows, width), F32), kind((rows, width), BF), kind((1, width), F32)],
    )(middle, grad, cotangent, gain)


def back_kernel(
    count,
    sums_ref,
    mid_low_ref,
    gain_two_ref,
    attended_ref,
    query_ref,
    key_ref,
    value_ref,
    tokens_ref,
    gains_ref,
    cos_ref,
    sin_ref,
    segc_ref,
    segr_ref,
    qkv_all_ref,
    out_all_ref,
    gate_grad_ref,
    up_grad_ref,
    out_grad_ref,
    qkv_grad_ref,
    grad_input_ref,
    gain_grad_ref,
    both_own,
    turned,
    grad_attended,
    grads,
    weight_tile,
    terms_first,
    terms_second,
    from_core_out,
    from_core_qkv,
    from_chip_out,
    out_sums,
    out_summed,
    outgoing_out,
    outgoing_qkv,
    incoming_out,
    incoming_qkv,
    summed,
    from_chip,
    finished,
    gain_terms,
    gains_in,
    gain_parts,
    gain_swaps,
    own_sem,
    tile_sem,
    across_send,
    across_recv,
    group_send,
    group_recv,
    core_send,
    core_recv,
    ring_send,
    ring_recv,
    chip_send,
    chip_recv,
    last_send,
    last_recv,
    pair_send,
    pair_recv,
    gain_send,
    gain_recv,
    swap_send,
    swap_recv,
):
    half = count // 2
    me, rep = lax.axis_index("shard"), lax.axis_index("rep")
    core, chip = rep % 2, rep // 2
    place = ring_place(count, me)
    others = [ring_shard(count, place + k) for k in range(1, count)]
    near = ({"shard": ring_shard(count, place + 1)}, {"shard": ring_shard(count, place - 1)})
    other_core, other_chip = {"rep": core_partner(rep)}, {"rep": chip_partner(rep)}
    rows, width = tokens_ref.shape
    own_rows = width // count
    strip, quarter = own_rows // 2, own_rows // 4
    ff_own = gate_grad_ref.shape[2] // count
    qkv_half = grads.shape[1] // 2
    wides = (width, qkv_half, qkv_half)
    terms = (terms_first, terms_second, terms_first)
    pieces = (quarter, strip, strip)
    from_core = (from_core_out, from_core_qkv.at[0], from_core_qkv.at[1])
    outgoing = (outgoing_out, outgoing_qkv.at[0], outgoing_qkv.at[1])
    incoming = (incoming_out, incoming_qkv.at[0], incoming_qkv.at[1])
    result_refs = (out_grad_ref, qkv_grad_ref, qkv_grad_ref)
    result_starts = (0, 0, qkv_half)
    chains, in_turn = range(3), (1, 2, 0)

    def tile(j, size=TILE):
        return pl.ds(pl.multiple_of(j * size, size), size)

    gate_up = (gate_grad_ref, up_grad_ref)

    def own_columns(shard):
        return pl.ds(pl.multiple_of(shard * ff_own, 128), ff_own)

    def across(k, which):
        there = others[k - 1]
        return remote_copy(
            sums_ref.at[there, :, pl.ds(which * ff_own, ff_own)],
            gate_up[which].at[rep, :, own_columns(me)],
            across_send.at[which, k - 1],
            across_recv.at[which, k - 1],
            {"shard": there},
        )

    own_load = pltpu.make_async_copy(sums_ref.at[me], both_own, own_sem.at[0])
    keep = [
        pltpu.make_async_copy(
            both_own.at[:, pl.ds(which * ff_own, ff_own)],
            gate_up[which].at[rep, :, own_columns(me)],
            own_sem.at[which],
        )
        for which in range(2)
    ]

    def group_copy(which, index):
        member = chip_partner(rep) if index == 2 else rep
        dst = src = gate_up[which].at[member]
        return remote_copy(
            src,
            dst,
            group_send.at[which, index],
            group_recv.at[which, index],
            other_chip if index == 0 else other_core,
        )

    def shard_of(k):
        return ring_shard(count, place + k)

    def core_copy(i, k):
        slot = k + half - 1
        return remote_copy(
            terms[i].at[shard_of(k), 1 - core, :, pl.ds(0, wides[i])],
            from_core[i].at[slot],
            core_send.at[i, slot],
            core_recv.at[i, slot],
            other_core,
        )

    def all_terms(i):
        def body(j, carry):
            if i == 0:
                right = mid_low_ref[:, tile(j)]
            else:
                right = grads[:, tile(j + result_starts[i] // TILE)]
            value = dot(turned[...], right).astype(BF)
            terms[i][:, :, :, tile(j)] = value.reshape(count, 2, strip, TILE)
            return carry

        lax.fori_loop(0, wides[i] // TILE, body, 0)
        for k in [half] + [s * j for j in range(half - 1, 0, -1) for s in (1, -1)] + [0]:
            core_copy(i, k).start()

    def pair_copy(k):
        slot = k + half - 1
        return remote_copy(
            out_sums.at[slot, 1 - chip],
            from_chip_out.at[slot],
            pair_send.at[slot],
            pair_recv.at[slot],
            other_chip,
        )

    def sum_pair(k):
        core_copy(0, k).wait_recv()

        def body(j, carry):
            at = tile(j, WIDE_TILE)
            value = terms[0][shard_of(k), core, :, at].astype(F32)
            value += from_core[0][k + half - 1, :, at].astype(F32)
            out_sums[k + half - 1, :, :, at] = value.astype(BF).reshape(2, quarter, WIDE_TILE)
            return carry

        lax.fori_loop(0, wides[0] // WIDE_TILE, body, 0)
        pair_copy(k).start()

    def piece_sum(i, k, extra, store):
        slot = k + half - 1
        if i == 0:
            pair_copy(k).wait_recv()
            received = from_chip_out
        else:
            core_copy(i, k).wait_recv()
            received = from_core[i]

        def body(j, carry):
            at = tile(j, WIDE_TILE)
            own = out_sums[slot, chip, :, at] if i == 0 else terms[i][shard_of(k), core, :, at]
            value = own.astype(F32)
            value += received[slot, :, at].astype(F32)
            for direction, step in extra:
                value += incoming[i][direction, step, :, at].astype(F32)
            store(at, value.astype(BF))
            return carry

        lax.fori_loop(0, wides[i] // WIDE_TILE, body, 0)

    def ring_copy(i, direction, step):
        cut = pieces[i] // 2
        at = pl.ds(direction * cut, cut) if step == 0 else pl.ds(0, pieces[i])
        return remote_copy(
            outgoing[i].at[direction, at],
            incoming[i].at[direction, step, at],
            ring_send.at[i, direction, step],
            ring_recv.at[i, direction, step],
            near[direction],
        )

    def ring_step(i, step):
        if step == 0:

            cut = pieces[i] // 2

            def store(at, value):
                outgoing[i][0, pl.ds(0, cut), at] = value[:cut]
                outgoing[i][1, pl.ds(cut, cut), at] = value[cut:]

            piece_sum(i, half, (), store)
            for direction in range(2):
                ring_copy(i, direction, 0).start()
            return
        for direction in range(2):
            ring_copy(i, direction, step - 1).wait()

            def store(at, value):
                outgoing[i][direction, :, at] = value

            k = half - step if direction == 0 else step - half
            piece_sum(i, k, ((direction, step - 1),), store)
            ring_copy(i, direction, step).start()

    def chip_copy(i):
        return remote_copy(
            summed.at[i - 1],
            from_chip.at[i - 1],
            chip_send.at[i],
            chip_recv.at[i],
            other_chip,
        )

    def ring_end(i):
        for direction in range(2):
            ring_copy(i, direction, half - 1).wait()

        def store(at, value):
            if i == 0:
                out_summed[:, at] = value
            else:
                summed[i - 1, :, at] = value

        piece_sum(i, 0, tuple((d, half - 1) for d in range(2)), store)
        if i > 0:
            chip_copy(i).start()
        else:
            for copy in out_copies()[:3]:
                copy.start()

    own_strip = pl.ds(pl.multiple_of(core * strip, strip), strip)

    def out_copies():
        def at(which_chip):
            return out_grad_ref.at[
                pl.ds(pl.multiple_of(core * strip + which_chip * quarter, quarter), quarter)
            ]

        done = out_summed
        return (
            pltpu.make_async_copy(done, at(chip), own_sem.at[3]),
            remote_copy(done, at(chip), chip_send.at[0], chip_recv.at[0], other_chip),
            remote_copy(done, at(chip), last_send.at[0], last_recv.at[0], other_core),
            remote_copy(at(1 - chip), at(1 - chip), last_send.at[3], last_recv.at[3], other_core),
        )

    def last_copies(i):
        src = finished.at[i - 1]
        dst = result_refs[i].at[own_strip, pl.ds(result_starts[i], wides[i])]
        return (
            pltpu.make_async_copy(src, dst, own_sem.at[3 + i]),
            remote_copy(src, dst, last_send.at[i], last_recv.at[i], other_core),
        )

    def group_end(i):
        chip_copy(i).wait()
        total = summed[i - 1].astype(F32) + from_chip[i - 1].astype(F32)
        finished[i - 1] = total.astype(BF)
        for copy in last_copies(i):
            copy.start()

    def gain_copy(k):
        return remote_copy(
            gain_terms.at[:, tile(others[k - 1], own_rows)],
            gains_in.at[k],
            gain_send.at[k - 1],
            gain_recv.at[k - 1],
            {"shard": others[k - 1]},
        )

    def gain_swap(index):
        return remote_copy(
            gain_parts.at[index],
            gain_swaps.at[index],
            swap_send.at[index],
            swap_recv.at[index],
            (other_core, other_chip)[index],
        )

    def weight_load(ref, j, wide):
        return pltpu.make_async_copy(
            ref.at[tile(j, LOAD_TILE)], weight_tile.at[j % 2, :, pl.ds(0, wide)], tile_sem.at[j % 2]
        )

    def times_transposed(left, ref, wide, store):
        blocks = width // LOAD_TILE

        def body(j, carry):
            @pl.when(j + 1 < blocks)
            def _():
                weight_load(ref, j + 1, wide).start()

            weight_load(ref, j, wide).wait()
            store(tile(j, LOAD_TILE), contract_last(left[...], weight_tile[j % 2, :, pl.ds(0, wide)]))
            return carry

        lax.fori_loop(0, blocks, body, 0)

    def turn(array):
        def body(j, carry):
            turned[tile(j), :] = array[:, tile(j)].T
            return carry

        lax.fori_loop(0, width // TILE, body, 0)

    cosine, sine = cos_ref[...], -sin_ref[...]
    wide, thin = 2 * GROUP * HEAD_SIZE, 2 * HEAD_SIZE
    key_at, value_at = width, width + key_ref.shape[1]

    def heads_pair(pair):
        allowed = allowed_rows(segc_ref[...], segr_ref[...])
        wide_at, thin_at = pl.ds(pair * wide, wide), pl.ds(pair * thin, thin)
        query, grad = query_ref[:, wide_at], grad_attended[:, wide_at]
        key, value = key_ref[:, thin_at], value_ref[:, thin_at]
        heads, keys, values = [], [], []
        for j in range(2):
            cols = slice(j * HEAD_SIZE, (j + 1) * HEAD_SIZE)
            query_rows, grad_rows = stack_heads(query, j), stack_heads(grad, j)
            probs = softmax_rows(query_rows, key[:, cols], allowed)
            grad_probs = contract_last(grad_rows, value[:, cols])
            grad_scores = (
                probs * (grad_probs - jnp.sum(probs * grad_probs, -1, keepdims=True))
            ).astype(BF)
            heads += unstack_heads(dot(grad_scores, key[:, cols]) * HEAD_SIZE ** (-0.5))
            keys.append(contract_first(grad_scores, query_rows) * HEAD_SIZE ** (-0.5))
            values.append(contract_first(probs.astype(BF), grad_rows))
        grads[:, wide_at] = rotate(jnp.concatenate(heads, 1), cosine, sine).astype(BF)
        grads[:, pl.ds(key_at + pair * thin, thin)] = rotate(
            jnp.concatenate(keys, 1), cosine, sine
        ).astype(BF)
        grads[:, pl.ds(value_at + pair * thin, thin)] = jnp.concatenate(values, 1).astype(BF)

    load_attended = pltpu.make_async_copy(attended_ref, grad_attended, own_sem.at[3])
    load_attended.start()
    own_load.start()
    for i in chains:
        for direction in range(2):
            cut = pieces[i] // 2
            blank = pl.ds((1 - direction) * cut, cut)
            incoming[i][direction, 0, blank] = jnp.zeros((cut, wides[i]), BF)

    own_load.wait()
    for copy in keep:
        copy.start()
    greet([{"shard": shard} for shard in others] + [other_core, other_chip])

    for k in range(1, count):
        for which in range(2):
            across(k, which).start()
    weight_load(out_all_ref, 0, width).start()
    load_attended.wait()
    turn(grad_attended)
    all_terms(0)
    for k in [half] + [s * j for j in range(half - 1, 0, -1) for s in (1, -1)] + [0]:
        sum_pair(k)

    def store_attended(at, value):
        grad_attended[:, at] = value.astype(BF)

    times_transposed(mid_low_ref, out_all_ref, width, store_attended)
    weight_load(qkv_all_ref, 0, grads.shape[1]).start()
    ring_step(0, 0)
    for pair in range(KEY_VALUE_HEADS // 2):
        heads_pair(pair)

    unit, scale_row = normalize(tokens_ref[...].astype(F32))
    gain = gains_ref[0:1, :]
    grad_attended[...] = (unit * gain).astype(BF)
    turn(grad_attended)
    all_terms(1)
    ring_step(1, 0)
    for copy in keep:
        copy.wait()
    for k in range(1, count):
        for which in range(2):
            across(k, which).wait_recv()
    for which in range(2):
        for index in range(2):
            group_copy(which, index).start()
    for k in range(-(half - 1), half + 1):
        core_copy(0, k).wait_send()
    all_terms(2)
    ring_step(2, 0)
    for i in in_turn:
        ring_step(i, 1)

    def store_input(at, value):
        grad_input_ref[:, at] = value

    times_transposed(grads, qkv_all_ref, grads.shape[1], store_input)
    if half > 2:
        for i in in_turn:
            ring_step(i, 2)
    unit, scale_row = normalize(tokens_ref[...].astype(F32))
    grad_normed = grad_input_ref[...]
    gain_terms[...] = jnp.zeros_like(gain_terms)
    gain_terms[0:1, :] = jnp.sum(grad_normed * unit, 0, keepdims=True)
    gain_terms[1:2, :] = gain_two_ref[...]
    for k in range(1, count):
        gain_copy(k).start()
    grad_input_ref[...] = norm_back(grad_normed * gain, unit, scale_row)
    for step in range(3, half):
        for i in in_turn:
            ring_step(i, step)
    for which in range(2):
        group_copy(which, 0).wait_recv()
        group_copy(which, 2).start()
    total = gain_terms[:, tile(me, own_rows)]
    for k in range(1, count):
        gain_copy(k).wait_recv()
        total += gains_in[k]
    gain_parts[0] = total
    gain_swap(0).start()
    for i in in_turn:
        ring_end(i)
    gain_swap(0).wait()
    gain_parts[1] = gain_parts[0] + gain_swaps[0]
    gain_swap(1).start()
    for i in (1, 2):
        group_end(i)
    out_copies()[1].wait_recv()
    out_copies()[3].start()
    gain_swap(1).wait()
    gain_grad_ref[...] = gain_parts[1] + gain_swaps[1]

    for k in range(-(half - 1), half + 1):
        pair_copy(k).wait_send()
    kept, over, passed, again = out_copies()
    kept.wait()
    over.wait_send()
    passed.wait()
    again.wait()
    for i in (1, 2):
        kept, passed = last_copies(i)
        kept.wait()
        passed.wait()
    for i in (1, 2):
        for k in range(-(half - 1), half + 1):
            core_copy(i, k).wait_send()
    for which in range(2):
        for index in range(3):
            if index > 0:
                group_copy(which, index).wait_recv()
            group_copy(which, index).wait_send()
    for k in range(1, count):
        gain_copy(k).wait_send()
        for which in range(2):
            across(k, which).wait_send()


def back(
    count,
    sums,
    mid_low,
    gain_two_term,
    attended,
    query,
    key,
    value,
    tokens,
    gains,
    tables,
    qkv_all,
    out_all,
):
    rows, width = tokens.shape
    qkv_width = qkv_all.shape[1]
    own_rows = width // count
    strip, quarter = own_rows // 2, own_rows // 4
    ff_own = sums.shape[2] // 2
    half = count // 2
    here = pl.BlockSpec(memory_space=pl.ANY)
    inside = pl.BlockSpec(memory_space=pltpu.VMEM)
    kind = jax.ShapeDtypeStruct
    dma = pltpu.SemaphoreType.DMA
    vmem = pltpu.VMEM
    return pl.pallas_call(
        functools.partial(back_kernel, count),
        in_specs=[here] + [inside] * 2 + [here] + [inside] * 9 + [here] * 2,
        out_specs=[here] * 4 + [inside] * 2,
        out_shape=[
            kind((4, quarter, count * ff_own), BF),
            kind((4, quarter, count * ff_own), BF),
            kind((own_rows, width), BF),
            kind((own_rows, qkv_width), BF),
            kind((rows, width), F32),
            kind((8, own_rows), F32),
        ],
        scratch_shapes=[
            vmem((quarter, 2 * ff_own), BF),
            vmem((width, rows), BF),
            vmem((rows, width), BF),
            vmem((rows, qkv_width), BF),
            vmem((2, LOAD_TILE, qkv_width), BF),
            vmem((count, 2, strip, width), BF),
            vmem((count, 2, strip, qkv_width // 2), BF),
            vmem((count, strip, width), BF),
            vmem((2, count, strip, qkv_width // 2), BF),
            vmem((count, quarter, width), BF),
            vmem((count, 2, quarter, width), BF),
            vmem((quarter, width), BF),
            vmem((2, quarter, width), BF),
            vmem((2, 2, strip, qkv_width // 2), BF),
            vmem((2, half, quarter, width), BF),
            vmem((2, 2, half, strip, qkv_width // 2), BF),
            vmem((2, strip, qkv_width // 2), BF),
            vmem((2, strip, qkv_width // 2), BF),
            vmem((2, strip, qkv_width // 2), BF),
            vmem((8, width), F32),
            vmem((count, 8, own_rows), F32),
            vmem((2, 8, own_rows), F32),
            vmem((2, 8, own_rows), F32),
            dma((6,)),
            dma((2,)),
            dma((2, count - 1)),
            dma((2, count - 1)),
            dma((2, 3)),
            dma((2, 3)),
            dma((3, count)),
            dma((3, count)),
            dma((3, 2, half)),
            dma((3, 2, half)),
            dma((3,)),
            dma((3,)),
            dma((4,)),
            dma((4,)),
            dma((count,)),
            dma((count,)),
            dma((count - 1,)),
            dma((count - 1,)),
            dma((2,)),
            dma((2,)),
        ],
        compiler_params=pltpu.CompilerParams(
            collective_id=2, has_side_effects=True, vmem_limit_bytes=VMEM_BYTES
        ),
        cost_estimate=pl.CostEstimate(
            flops=4 * rows * width * (qkv_width + width) + 4 * 10**9,
            bytes_accessed=60 * 10**6,
            transcendentals=2 * 10**6,
        ),
    )(
        sums,
        mid_low,
        gain_two_term,
        attended,
        query,
        key,
        value,
        tokens,
        gains,
        *tables,
        qkv_all,
        out_all,
    )


def feed_forward_parts(ring, normed_two, grad_low, w_both, w_down):
    sequence, ff_own = normed_two.shape[0], w_down.shape[0]
    low_all, normed_all = run(ring.gather(grad_low), ring.gather(normed_two))
    hidden, grad_both = {}, {}
    for k in normed_all:
        both = dot(normed_all[k], w_both)
        gate, up = both[:, :ff_own], both[:, ff_own:]
        grad_hidden = contract_last(low_all[k], w_down)
        sigmoid = jax.nn.sigmoid(gate)
        silu = gate * sigmoid
        hidden[k] = (silu * up).astype(BF)
        grad_gate = (grad_hidden * up * sigmoid * (1.0 + gate * (1.0 - sigmoid))).astype(BF)
        grad_up = (grad_hidden * silu).astype(BF)
        grad_both[k] = jnp.concatenate([grad_gate, grad_up], 1)

    def terms_of(chunks, product):
        def terms(ks):
            sources = [k if k == ring.half else -k for k in ks]
            whole = product(jnp.concatenate([chunks[k] for k in sources], 0))
            return [whole[i * sequence : (i + 1) * sequence] for i in range(len(ks))]

        return terms

    (grad_normed_two,) = run(ring.scatter(terms_of(grad_both, lambda a: contract_last(a, w_both))))
    (branch_two,) = run(ring.scatter(terms_of(hidden, lambda a: dot(a, w_down))))
    keys = list(normed_all)
    together = lambda parts: jnp.concatenate([parts[k] for k in keys], 0)
    both_term = contract_first(together(normed_all), together(grad_both))
    down_term = contract_first(together(hidden), together(low_all))
    return grad_normed_two, branch_two, both_term, down_term


def swap(array, bit):
    return lax.ppermute(array, "rep", [(i, i ^ bit) for i in range(4)])


def cols(array, start, width):
    return lax.dynamic_slice_in_dim(array, start, width, 1)


def rows_of(array, start, height):
    return lax.dynamic_slice_in_dim(array, start, height, 0)


def put(array, piece, start, axis):
    return lax.dynamic_update_slice_in_dim(array, piece, start, axis)


def gather_rows(ring, array):
    rows = array.shape[0]
    (parts,) = run(ring.gather(array))
    full = jnp.zeros((ring.count * rows, array.shape[1]), array.dtype)
    for k, part in parts.items():
        full = put(full, part, ring.at(-k) * rows, 0)
    return full


def front_parts(ring, tokens, gains_own, cotangent, tables, own, w_gate, w_up):
    count, (own_rows, wide_k) = ring.count, own[1].shape
    rep = lax.axis_index("rep")
    ff_own = w_gate.shape[1] // count
    width = tokens.shape[1]
    gains = jnp.zeros((gains_own.shape[0], width), F32)
    for k in range(count):
        piece = ring.send(gains_own, k) if k else gains_own
        gains = put(gains, piece, ring.at(-k) * own_rows, 1)
    qkv_all = gather_rows(ring, jnp.concatenate(own[:3], 1))
    out_all = gather_rows(ring, own[3])
    quarter = own_rows // 4
    gate_rows = rows_of(w_gate, rep * quarter, quarter)
    up_rows = rows_of(w_up, rep * quarter, quarter)
    sends = []
    for k in range(count):
        dest = ring.at(k) * ff_own
        piece = jnp.concatenate([cols(gate_rows, dest, ff_own), cols(up_rows, dest, ff_own)], 1)
        sends.append((piece, k))
    fetched = jnp.zeros((count, quarter, 2 * ff_own), BF)
    for k, piece in enumerate([sends[0][0]] + ring.queue(*sends[1:])):
        fetched = put(fetched, piece[None], ring.at(-k), 0)
    pieces = [fetched, swap(fetched, 2)]
    pieces += [swap(piece, 1) for piece in pieces]
    w_both = jnp.zeros((count, 4, quarter, 2 * ff_own), BF)
    for bits, piece in zip((0, 2, 1, 3), pieces):
        w_both = put(w_both, piece[:, None], rep ^ bits, 1)
    resid = tokens.astype(F32)
    unit, _ = normalize(resid)
    linear = dot((unit * gains[:1]).astype(BF), qkv_all)
    query, key, value, attended = attend(
        linear[:, :width], linear[:, width : width + wide_k], linear[:, width + wide_k :], tables
    )
    middle = resid + dot(attended, out_all)
    unit, _ = normalize(middle)
    normed_two = (unit * gains[1:2]).astype(BF)
    low = cotangent.astype(BF)
    return qkv_all, out_all, w_both, low, gains, query, key, value, attended, middle, normed_two


def back_parts(
    ring,
    both_term,
    down_term,
    mid_low,
    gain_two_term,
    attended,
    query,
    key,
    value,
    tokens,
    gains,
    tables,
    qkv_all,
    out_all,
):
    count = ring.count
    rep = lax.axis_index("rep")
    core, chip = rep % 2, rep // 2
    width = tokens.shape[1]
    own_rows = width // count
    quarter = own_rows // 4
    ff_own = both_term.shape[1] // 2
    ff = ff_own * count

    def order_halves(mine, other):
        first = core == 0
        return jnp.where(first, mine, other), jnp.where(first, other, mine)

    def sum_cores(array, half_of):
        keep, pass_on = half_of(array, core), half_of(array, 1 - core)
        return keep.astype(F32) + swap(pass_on.astype(BF), 1).astype(F32)

    both_term = both_term.reshape(count, 2, 2, quarter, 2 * ff_own)
    both_half = sum_cores(
        both_term, lambda a, c: lax.dynamic_index_in_dim(a, c, 2, keepdims=False)
    )
    keep = lax.dynamic_index_in_dim(both_half, chip, 1, keepdims=False)
    pass_on = lax.dynamic_index_in_dim(both_half, 1 - chip, 1, keepdims=False)
    both_quarter = (keep + swap(pass_on.astype(BF), 2).astype(F32)).astype(BF)
    gate_quarter = jnp.zeros((quarter, ff), BF)
    up_quarter = jnp.zeros((quarter, ff), BF)
    sends = [
        (lax.dynamic_index_in_dim(both_quarter, ring.at(k), 0, keepdims=False), k)
        for k in range(count)
    ]
    for k, piece in enumerate([sends[0][0]] + ring.queue(*sends[1:])):
        start = ring.at(-k) * ff_own
        gate_quarter = put(gate_quarter, piece[:, :ff_own], start, 1)
        up_quarter = put(up_quarter, piece[:, ff_own:], start, 1)

    def collect(quarter_rows):
        parts = [quarter_rows, swap(quarter_rows, 2)]
        parts += [swap(part, 1) for part in parts]
        full = jnp.zeros((4 * quarter, ff), BF)
        for bits, part in zip((0, 2, 1, 3), parts):
            full = put(full, part, (rep ^ bits) * quarter, 0)
        return full

    gate_grad, up_grad = collect(gate_quarter), collect(up_quarter)

    down_half = sum_cores(
        down_term, lambda a, c: rows_of(a, c * (a.shape[0] // 2), a.shape[0] // 2)
    ).astype(BF)
    down_half = (down_half.astype(F32) + swap(down_half, 2).astype(F32)).astype(BF)
    down_grad = jnp.concatenate(order_halves(down_half, swap(down_half, 1)), 0)

    def part_sums(left, grads):
        wide = grads.shape[1] // 2
        grads_mine, grads_other = cols(grads, core * wide, wide), cols(grads, (1 - core) * wide, wide)

        def terms(ks):
            blocks = [cols(left, ring.at(k) * own_rows, own_rows) for k in ks]
            block = blocks[0] if len(ks) == 1 else jnp.concatenate(blocks, 1)
            other = swap(contract_first(block, grads_other).astype(BF), 1)
            whole = contract_first(block, grads_mine) + other.astype(F32)
            return [whole[i * own_rows : (i + 1) * own_rows] for i in range(len(ks))]

        mine = run(ring.scatter(terms))[0].astype(BF)
        mine = (mine.astype(F32) + swap(mine, 2).astype(F32)).astype(BF)
        return jnp.concatenate(order_halves(mine, swap(mine, 1)), 1)

    out_grad = part_sums(attended, mid_low)
    grad_attended = contract_last(mid_low, out_all).astype(BF)
    grads = jnp.concatenate(attend_back(query, key, value, grad_attended, tables), 1)
    unit_one, scale_one = normalize(tokens.astype(F32))
    gain_one = gains[:1]
    qkv_grad = part_sums((unit_one * gain_one).astype(BF), grads)
    grad_normed_one = contract_last(grads, qkv_all)
    gain_one_term = jnp.sum(grad_normed_one * unit_one, 0, keepdims=True)
    grad_input = norm_back(grad_normed_one * gain_one, unit_one, scale_one)

    gain_terms = jnp.concatenate([gain_one_term, gain_two_term], 0)
    gain_sums = cols(gain_terms, ring.at(0) * own_rows, own_rows)
    for k in range(1, count):
        gain_sums = gain_sums + ring.send(cols(gain_terms, ring.at(k) * own_rows, own_rows), k)
    gain_sums = gain_sums + swap(gain_sums, 1)
    gain_sums = gain_sums + swap(gain_sums, 2)
    return gate_grad, up_grad, down_grad, out_grad, qkv_grad, grad_input, gain_sums


def on_device(
    count,
    tokens,
    segments,
    norm_attn,
    w_query,
    key_weight,
    value_weight,
    w_out,
    norm_mlp,
    w_gate,
    w_up,
    w_down,
    cotangent,
):
    ring = Ring(count)
    sequence, width = tokens.shape[1], tokens.shape[2]
    own_rows = w_query.shape[0]
    ff = w_gate.shape[1]
    ff_own = ff // count
    wide_k = key_weight.shape[1]
    fits = feed_forward_bytes(count, sequence, width, ff_own) <= VMEM_BYTES
    kernels = fits and sequence == own_rows == TILE

    grad_output = cotangent.reshape(sequence, width)
    cosine, sine = rope_tables(segments)
    seg_row = segments.reshape(1, sequence)
    tables = (cosine, sine, seg_row.reshape(sequence, 1), seg_row)
    own = tokens.reshape(sequence, width)
    own_weights = (w_query, key_weight, value_weight, w_out)
    gains_own = jnp.zeros((8, own_rows), F32)
    gains_own = gains_own.at[0].set(norm_attn.astype(F32)).at[1].set(norm_mlp.astype(F32))
    bring = functools.partial(front, count) if kernels else functools.partial(front_parts, ring)
    qkv_all, out_all, w_both, low, gains, query, key, value, attended, middle, normed_two = bring(
        own, gains_own, grad_output, tables, own_weights, w_gate, w_up
    )
    w_both = w_both.reshape(width, 2 * ff_own)
    gain_one, gain_two = gains[:1], gains[1:2]

    if kernels:
        grad_normed_two, branch_two, sums, down_grad = feed_forward(
            count, normed_two, low, w_both, w_down
        )
    else:
        grad_normed_two, branch_two, both_term, down_term = feed_forward_parts(
            ring, normed_two, low, w_both, w_down
        )
    output = middle + branch_two

    grad_middle, grad_mid_low, gain_two_term = middle_back(
        middle, grad_normed_two, grad_output, gain_two
    )

    if kernels:
        gate_grad, up_grad, out_grad, qkv_grad, grad_input, gain_sums = back(
            count,
            sums,
            grad_mid_low,
            gain_two_term,
            attended,
            query,
            key,
            value,
            own,
            gains,
            tables,
            qkv_all,
            out_all,
        )
    else:
        gate_grad, up_grad, down_grad, out_grad, qkv_grad, grad_input, gain_sums = back_parts(
            ring,
            both_term,
            down_term,
            grad_mid_low,
            gain_two_term,
            attended,
            query,
            key,
            value,
            own,
            gains,
            tables,
            qkv_all,
            out_all,
        )
    grad_input = grad_middle + grad_input
    qkv_grad = qkv_grad.astype(F32)

    return (
        output.reshape(tokens.shape),
        grad_input.reshape(tokens.shape),
        gain_sums[0],
        qkv_grad[:, :width],
        qkv_grad[:, width : width + wide_k],
        qkv_grad[:, width + wide_k :],
        out_grad.astype(F32),
        gain_sums[1],
        gate_grad.reshape(own_rows, ff).astype(F32),
        up_grad.reshape(own_rows, ff).astype(F32),
        down_grad.reshape(ff_own, width).astype(F32),
    )


def solution(mesh):
    row, vector, matrix = P(("shard", "rep"), None, None), P("shard"), P("shard", None)
    in_specs = (row, P(("shard", "rep"), None), vector, matrix, matrix, matrix, matrix, vector)
    in_specs += (matrix, matrix, matrix, row)
    out_specs = (row, row, vector, matrix, matrix, matrix, matrix, vector, matrix, matrix, matrix)
    return jax.shard_map(
        functools.partial(on_device, mesh.shape["shard"]),
        mesh=mesh,
        in_specs=in_specs,
        out_specs=out_specs,
        check_vma=False,
    )
```

```python
import functools

import jax
import jax.numpy as jnp
from jax import lax
from jax.experimental import pallas as pl
from jax.experimental.pallas import tpu as pltpu
from jax.sharding import PartitionSpec as P

QUERY_HEADS = 32
KEY_VALUE_HEADS = 8
HEAD_SIZE = 64
GROUP = QUERY_HEADS // KEY_VALUE_HEADS

epsilon = 1e-05
masked_score = -1000000000.0
rope_base = 500000.0
WINDOW = 2
TILE = 256
WIDE_TILE = 512
LOAD_TILE = 128
VMEM_BYTES = 62 * 2**20
BF = jnp.bfloat16
F32 = jnp.float32


def dot(left, right):
    return jnp.dot(left, right, preferred_element_type=F32)


def contract_last(left, right):
    return lax.dot_general(left, right, (((1,), (1,)), ((), ())), preferred_element_type=F32)


def contract_first(left, right):
    return lax.dot_general(left, right, (((0,), (0,)), ((), ())), preferred_element_type=F32)


def positions(segment_ids):
    index = lax.broadcasted_iota(jnp.int32, segment_ids.shape, 1)
    first = jnp.concatenate(
        [
            jnp.ones_like(segment_ids[:, :1]),
            (segment_ids[:, 1:] != segment_ids[:, :-1]).astype(jnp.int32),
        ],
        1,
    )
    starts = lax.cummax(jnp.where(first > 0, index, 0), axis=1)
    return (index - starts).astype(F32)


def rope_tables(segment_ids):
    half = HEAD_SIZE // 2
    inverse = rope_base ** (-(2.0 * jnp.arange(half, dtype=F32)) / HEAD_SIZE)
    angle = positions(segment_ids)[0, :, None] * inverse
    cosine, sine = jnp.cos(angle), jnp.sin(angle)
    return jnp.concatenate([cosine] * 4, 1), jnp.concatenate([-sine, sine] * 2, 1)


def normalize(rows):
    scale_row = lax.rsqrt(jnp.mean(rows * rows, -1, keepdims=True) + epsilon)
    return rows * scale_row, scale_row


def norm_back(grad_unit, unit, scale_row):
    return scale_row * (grad_unit - unit * jnp.mean(grad_unit * unit, -1, keepdims=True))


def rotate(block, cosine, sine):
    lane = lax.broadcasted_iota(jnp.int32, cosine.shape, 1)
    lower = lane % HEAD_SIZE < HEAD_SIZE // 2
    parts = []
    for at in range(0, block.shape[1], 128):
        part = block[:, at : at + 128]
        other = jnp.where(
            lower, pltpu.roll(part, 128 - HEAD_SIZE // 2, 1), pltpu.roll(part, HEAD_SIZE // 2, 1)
        )
        parts.append(part * cosine + other * sine)
    return parts[0] if len(parts) == 1 else jnp.concatenate(parts, 1)


def stack_heads(block, key_head):
    first = key_head * GROUP
    return jnp.concatenate(
        [block[:, (first + i) * HEAD_SIZE : (first + i + 1) * HEAD_SIZE] for i in range(GROUP)], 0
    )


def unstack_heads(rows):
    count = rows.shape[0] // GROUP
    return [rows[i * count : (i + 1) * count] for i in range(GROUP)]


def softmax_rows(query, key, allowed):
    raw = contract_last(query, key) * HEAD_SIZE ** (-0.5)
    scores = jnp.where(allowed, raw, masked_score)
    exponent = jnp.exp(scores - jnp.max(scores, -1, keepdims=True))
    return exponent / jnp.sum(exponent, -1, keepdims=True)


def allowed_rows(seg_row):
    count = seg_row.shape[1]
    shape = (count, count)
    at_row = lax.broadcasted_iota(jnp.int32, shape, 0)
    at_column = lax.broadcasted_iota(jnp.int32, shape, 1)
    causal = at_row >= at_column
    seg_column = jnp.sum(
        jnp.where(at_row == at_column, jnp.broadcast_to(seg_row, shape), 0), 1, keepdims=True
    )
    one = ((seg_column == seg_row) & causal).astype(jnp.int32)
    return jnp.concatenate([one] * GROUP, 0) > 0


def attend_kernel(q_ref, k_ref, v_ref, cos_ref, sin_ref, segr_ref, qo, ko, vo, ao):
    cosine, sine = cos_ref[...], sin_ref[...]
    allowed = allowed_rows(segr_ref[...])
    query = rotate(q_ref[...], cosine, sine).astype(BF)
    key = rotate(k_ref[...], cosine, sine).astype(BF)
    value = v_ref[...].astype(BF)
    qo[...] = query
    ko[...] = key
    vo[...] = value
    heads = []
    for j in range(2):
        cols = slice(j * HEAD_SIZE, (j + 1) * HEAD_SIZE)
        probs = softmax_rows(stack_heads(query, j), key[:, cols], allowed).astype(BF)
        heads += unstack_heads(dot(probs, value[:, cols]).astype(BF))
    ao[...] = jnp.concatenate(heads, 1)


def attend_back_kernel(q_ref, k_ref, v_ref, g_ref, cos_ref, sin_ref, segr_ref, gq, gk, gv):
    cosine, sine = cos_ref[...], -sin_ref[...]
    allowed = allowed_rows(segr_ref[...])
    query, key, value, grad = q_ref[...], k_ref[...], v_ref[...], g_ref[...]
    heads, keys, values = [], [], []
    for j in range(2):
        cols = slice(j * HEAD_SIZE, (j + 1) * HEAD_SIZE)
        rows, grad_rows = stack_heads(query, j), stack_heads(grad, j)
        probs = softmax_rows(rows, key[:, cols], allowed)
        grad_probs = contract_last(grad_rows, value[:, cols])
        grad_scores = (
            probs * (grad_probs - jnp.sum(probs * grad_probs, -1, keepdims=True))
        ).astype(BF)
        heads += unstack_heads(dot(grad_scores, key[:, cols]) * HEAD_SIZE ** (-0.5))
        keys.append(contract_first(grad_scores, rows) * HEAD_SIZE ** (-0.5))
        values.append(contract_first(probs.astype(BF), grad_rows))
    gq[...] = rotate(jnp.concatenate(heads, 1), cosine, sine).astype(BF)
    gk[...] = rotate(jnp.concatenate(keys, 1), cosine, sine).astype(BF)
    gv[...] = jnp.concatenate(values, 1).astype(BF)


def attention_specs(count):
    wide = pl.BlockSpec((count, 2 * GROUP * HEAD_SIZE), lambda i: (0, i))
    thin = pl.BlockSpec((count, 2 * HEAD_SIZE), lambda i: (0, i))
    whole = lambda shape: pl.BlockSpec(shape, lambda i: (0, 0))
    fixed = [whole((count, 128)), whole((count, 128)), whole((1, count))]
    return wide, thin, fixed


def attend(query_lin, key_lin, value_lin, tables):
    count = query_lin.shape[0]
    wide, thin, fixed = attention_specs(count)
    kinds = [jax.ShapeDtypeStruct(a.shape, BF) for a in (query_lin, key_lin, value_lin, query_lin)]
    return pl.pallas_call(
        attend_kernel,
        grid=(KEY_VALUE_HEADS // 2,),
        in_specs=[wide, thin, thin] + fixed,
        out_specs=[wide, thin, thin, wide],
        out_shape=kinds,
        compiler_params=pltpu.CompilerParams(vmem_limit_bytes=48 * 2**20),
        cost_estimate=pl.CostEstimate(
            flops=2 * 10**9, bytes_accessed=6 * 10**6, transcendentals=2 * 10**6
        ),
    )(query_lin, key_lin, value_lin, *tables)


def attend_back(query, key, value, grad, tables):
    count = query.shape[0]
    wide, thin, fixed = attention_specs(count)
    kinds = [jax.ShapeDtypeStruct(a.shape, BF) for a in (query, key, value)]
    return pl.pallas_call(
        attend_back_kernel,
        grid=(KEY_VALUE_HEADS // 2,),
        in_specs=[wide, thin, thin, wide] + fixed,
        out_specs=[wide, thin, thin],
        out_shape=kinds,
        compiler_params=pltpu.CompilerParams(vmem_limit_bytes=48 * 2**20),
        cost_estimate=pl.CostEstimate(
            flops=4 * 10**9, bytes_accessed=6 * 10**6, transcendentals=2 * 10**6
        ),
    )(query, key, value, grad, *tables)


def ring_order(count):
    return list(range(0, count, 2)) + list(range(count - 1, 0, -2)) if count % 2 == 0 else list(range(count))


class Ring:
    def __init__(self, count):
        self.count = count
        self.half = count // 2
        self.order = ring_order(count)
        inverse = [self.order.index(i) for i in range(count)]
        self.table = jnp.asarray(self.order, jnp.int32)
        self.turns = []
        self.place = jnp.asarray(inverse, jnp.int32)[lax.axis_index("shard")]

    def at(self, offset):
        return self.table[(self.place + offset + self.count) % self.count]

    def send(self, array, offset):
        n, order = self.count, self.order
        pairs = [(order[i], order[(i + offset) % n]) for i in range(n)]
        return lax.ppermute(array, "shard", pairs)

    def queue(self, *sends):
        arrays = [array for array, _ in sends]
        if len(self.turns) >= WINDOW:
            arrays, _ = lax.optimization_barrier((arrays, self.turns[-WINDOW]))
        got = [self.send(array, offset) for array, (_, offset) in zip(arrays, sends)]
        self.turns.append(got[:2])
        return got

    def gather(self, array):
        cut = array.shape[0] // 2
        ahead = back = array
        out = {0: array}
        for k in range(1, self.half):
            ahead, back = self.queue((ahead, 1), (back, -1))
            out[k], out[-k] = ahead, back
            yield out
        out[self.half] = jnp.concatenate(self.queue((ahead[:cut], 1), (back[cut:], -1)), 0)
        yield out

    def scatter(self, terms):
        (far,) = terms((self.half,))
        far = far.astype(BF)
        cut = far.shape[0] // 2
        ahead, back = self.queue((far[:cut], 1), (far[cut:], -1))
        yield None
        for k in range(self.half - 1, 0, -1):
            up, down = terms((k, -k))
            if k == self.half - 1:
                up = jnp.concatenate([up[:cut] + ahead.astype(F32), up[cut:]], 0)
                down = jnp.concatenate([down[:cut], down[cut:] + back.astype(F32)], 0)
            else:
                up, down = up + ahead.astype(F32), down + back.astype(F32)
            ahead, back = self.queue((up.astype(BF), 1), (down.astype(BF), -1))
            if k > 1:
                yield None
        (own,) = terms((0,))
        yield own + ahead.astype(F32) + back.astype(F32)


def run(*flows):
    flows = list(flows)
    last = [None] * len(flows)
    live = list(range(len(flows)))
    while live:
        for i in list(live):
            try:
                last[i] = next(flows[i])
            except StopIteration:
                live.remove(i)
    return last


def ring_place(count, shard):
    return jnp.where(shard % 2 == 0, shard // 2, count - 1 - shard // 2)


def ring_shard(count, place):
    place = (place + count) % count
    return jnp.where(place < count // 2, 2 * place, 2 * (count - 1 - place) + 1)


def core_partner(rep):
    return rep + 1 - 2 * (rep % 2)


def chip_partner(rep):
    return (rep + 2) % 4


def greet(devices):
    barrier = pltpu.get_barrier_semaphore()
    for device in devices:
        pl.semaphore_signal(
            barrier, inc=1, device_id=device, device_id_type=pl.DeviceIdType.MESH
        )
    pl.semaphore_wait(barrier, len(devices))


def remote_copy(src, dst, send, recv, device):
    return pltpu.make_async_remote_copy(
        src_ref=src,
        dst_ref=dst,
        send_sem=send,
        recv_sem=recv,
        device_id=device,
        device_id_type=pl.DeviceIdType.MESH,
    )


def front_kernel(
    count,
    tokens_ref,
    gains_ref,
    cotangent_ref,
    cos_ref,
    sin_ref,
    segr_ref,
    query_own_ref,
    key_own_ref,
    value_own_ref,
    out_own_ref,
    gate_ref,
    up_ref,
    qkv_all_ref,
    out_all_ref,
    both_ref,
    low_all_ref,
    gains_all_ref,
    query_ref,
    key_ref,
    value_ref,
    attended_ref,
    middle_ref,
    normed_two_ref,
    low_own,
    both_own,
    qkv_all,
    out_all,
    normed,
    linear,
    own_sem,
    load_sem,
    gain_send,
    gain_recv,
    ring_send,
    ring_recv,
    core_send,
    core_recv,
    chip_send,
    chip_recv,
    across_send,
    across_recv,
    group_send,
    group_recv,
    low_send,
    low_recv,
):
    half = count // 2
    me, rep = lax.axis_index("shard"), lax.axis_index("rep")
    core, chip = rep % 2, rep // 2
    place = ring_place(count, me)
    others = [ring_shard(count, place + k) for k in range(1, count)]
    near = ({"shard": ring_shard(count, place + 1)}, {"shard": ring_shard(count, place - 1)})
    other_core, other_chip = {"rep": core_partner(rep)}, {"rep": chip_partner(rep)}
    own_rows = query_own_ref.shape[0]
    quarter = own_rows // 4
    cut = quarter // 2
    ff_own = gate_ref.shape[1] // count
    rows, width = tokens_ref.shape
    full_refs = (qkv_all_ref, out_all_ref)
    inside = (qkv_all, out_all)

    def rows_at(start, size):
        return pl.ds(pl.multiple_of(start, cut), size)

    def shard_rows(shard):
        return rows_at(shard * own_rows, own_rows)

    def piece_of(shard, which_core, which_chip, part=None):
        start = shard * own_rows + (2 * which_core + which_chip) * quarter
        if part is None:
            return rows_at(start, quarter)
        return rows_at(start + part * cut, cut)

    own_loads = [
        pltpu.make_async_copy(out_own_ref, out_all.at[shard_rows(me)], own_sem.at[6])
    ]
    start = 0
    for index, ref in enumerate((query_own_ref, key_own_ref, value_own_ref)):
        columns = pl.ds(start, ref.shape[1])
        own_loads.append(
            pltpu.make_async_copy(ref, qkv_all.at[shard_rows(me), columns], own_sem.at[7 + index])
        )
        start += ref.shape[1]
    keep = [
        pltpu.make_async_copy(
            inside[i].at[shard_rows(me)], full_refs[i].at[shard_rows(me)], own_sem.at[i]
        )
        for i in range(2)
    ]
    for i, ref in enumerate((gate_ref, up_ref)):
        block = (rows_at(rep * quarter, quarter), pl.ds(pl.multiple_of(me * ff_own, 128), ff_own))
        own_loads.append(
            pltpu.make_async_copy(
                ref.at[block], both_own.at[:, pl.ds(i * ff_own, ff_own)], own_sem.at[2 + i]
            )
        )
    for copy in own_loads:
        copy.start()
    gains_all_ref[:, pl.ds(pl.multiple_of(me * own_rows, 128), own_rows)] = gains_ref[...]
    low_own[...] = cotangent_ref[...].astype(BF)
    for copy in own_loads:
        copy.wait()
    keep.append(pltpu.make_async_copy(low_own, low_all_ref.at[pl.ds(0, rows)], own_sem.at[4]))
    keep.append(pltpu.make_async_copy(both_own, both_ref.at[me, rep], own_sem.at[5]))
    for copy in keep:
        copy.start()

    greet([{"shard": shard} for shard in others] + [other_core, other_chip])

    def gain_copy(k):
        columns = pl.ds(pl.multiple_of(me * own_rows, 128), own_rows)
        return remote_copy(
            gains_ref,
            gains_all_ref.at[:, columns],
            gain_send.at[k - 1],
            gain_recv.at[k - 1],
            {"shard": others[k - 1]},
        )

    def across(k, which):
        ref = (gate_ref, up_ref)[which]
        there = others[k - 1]
        columns = pl.ds(pl.multiple_of(there * ff_own, 128), ff_own)
        return remote_copy(
            ref.at[rows_at(rep * quarter, quarter), columns],
            both_ref.at[me, rep, :, pl.ds(which * ff_own, ff_own)],
            across_send.at[which, k - 1],
            across_recv.at[which, k - 1],
            {"shard": there},
        )

    def hops(step):
        return ((0, 0), (0, 1), (1, 0), (1, 1)) if step < half else ((0, 0), (1, 1))

    def ring_copy(i, direction, step, part):
        sign = 1 if direction == 0 else -1
        at = piece_of(ring_shard(count, place - sign * (step - 1)), core, chip, part)
        src = inside[i].at[at] if step == 1 else full_refs[i].at[at]
        return remote_copy(
            src,
            full_refs[i].at[at],
            ring_send.at[i, direction, step - 1, part],
            ring_recv.at[i, direction, step - 1, part],
            near[direction],
        )

    def chip_copy(i, k):
        at = piece_of(ring_shard(count, place - k), core, chip)
        slot = k + half - 1
        return remote_copy(
            full_refs[i].at[at],
            full_refs[i].at[at],
            chip_send.at[i, slot],
            chip_recv.at[i, slot],
            other_chip,
        )

    def core_copy(i, k, which):
        from_chip = chip if which == 0 else 1 - chip
        at = piece_of(ring_shard(count, place - k), core, from_chip)
        slot = k + half - 1
        return remote_copy(
            full_refs[i].at[at],
            full_refs[i].at[at],
            core_send.at[i, which, slot],
            core_recv.at[i, which, slot],
            other_core,
        )

    def load(i, k):
        at = shard_rows(ring_shard(count, place - k))
        return pltpu.make_async_copy(
            full_refs[i].at[at], inside[i].at[at], load_sem.at[i, k + half - 1]
        )

    def low_copy(direction, step, part):
        base = 0 if direction == 0 else half
        source = (base + step - 1) * rows if step > 1 else 0
        to = (base + step if step < half else half) * rows
        size = rows // 2
        src = (low_all_ref if step > 1 else low_own).at[pl.ds(source + part * size, size)]
        return remote_copy(
            src,
            low_all_ref.at[pl.ds(to + part * size, size)],
            low_send.at[direction, step - 1, part],
            low_recv.at[direction, step - 1, part],
            near[direction],
        )

    def pass_on(copy_of, step):
        for part, direction in hops(step):
            copy_of(direction, step, part).wait_recv()
            if step < half - 1 or (step == half - 1 and part == direction):
                copy_of(direction, step + 1, part).start()

    def start_low():
        for part, direction in hops(1):
            low_copy(direction, 1, part).start()

    def finish_low(step):
        pass_on(low_copy, step)

    def start_ring(i):
        for part, direction in hops(1):
            ring_copy(i, direction, 1, part).start()

    def places(step):
        return (step, -step) if step < half else (half,)

    def finish_step(i, step):
        pass_on(functools.partial(ring_copy, i), step)
        for k in places(step):
            core_copy(i, k, 0).start()

    def start_chip(i, step):
        for k in places(step):
            chip_copy(i, k).start()

    def pass_step(i, step):
        for k in places(step):
            chip_copy(i, k).wait_recv()
            core_copy(i, k, 1).start()

    def load_step(i, step):
        for k in places(step):
            for which in range(2):
                core_copy(i, k, which).wait_recv()
            load(i, k).start()

    for k in range(1, count):
        gain_copy(k).start()
    start_ring(0)
    resid = tokens_ref[...].astype(F32)
    unit, _ = normalize(resid)
    for k in range(1, count):
        gain_copy(k).wait_recv()
    normed[...] = (unit * gains_all_ref[0:1, :]).astype(BF)

    for step in range(1, half + 1):
        finish_step(0, step)
        start_chip(0, step)
        if step == half - 1:
            for k in range(1, count):
                for which in range(2):
                    across(k, which).start()
    start_ring(1)
    for step in range(1, half + 1):
        pass_step(0, step)
        if step > 1:
            load_step(0, step - 1)

    def group_copy(index, quarter_at, device):
        at = both_ref.at[:, quarter_at]
        return remote_copy(at, at, group_send.at[index], group_recv.at[index], device)

    chip_copies = [group_copy(0, rep, other_chip)]
    core_copies = [
        group_copy(1, rep, other_core),
        group_copy(2, chip_partner(rep), other_core),
    ]
    load_step(0, half)
    for k in range(-(half - 1), half + 1):
        if k:
            load(0, k).wait()

    def linear_tile(j, carry):
        at = pl.ds(pl.multiple_of(j * TILE, TILE), TILE)
        linear[:, at] = dot(normed[...], qkv_all[:, at])
        return carry

    lax.fori_loop(0, linear.shape[1] // TILE, linear_tile, 0)

    cosine, sine = cos_ref[...], sin_ref[...]
    wide, thin = 2 * GROUP * HEAD_SIZE, 2 * HEAD_SIZE
    key_at, value_at = width, width + key_ref.shape[1]

    def heads_pair(pair):
        allowed = allowed_rows(segr_ref[...])
        wide_at = pl.ds(pair * wide, wide)
        thin_at = pl.ds(pair * thin, thin)
        query = rotate(linear[:, wide_at], cosine, sine).astype(BF)
        key = rotate(linear[:, pl.ds(key_at + pair * thin, thin)], cosine, sine).astype(BF)
        value = linear[:, pl.ds(value_at + pair * thin, thin)].astype(BF)
        query_ref[:, wide_at] = query
        key_ref[:, thin_at] = key
        value_ref[:, thin_at] = value
        heads = []
        for j in range(2):
            cols = slice(j * HEAD_SIZE, (j + 1) * HEAD_SIZE)
            probs = softmax_rows(stack_heads(query, j), key[:, cols], allowed).astype(BF)
            heads += unstack_heads(dot(probs, value[:, cols]).astype(BF))
        attended_ref[:, wide_at] = jnp.concatenate(heads, 1)

    pairs = KEY_VALUE_HEADS // 2
    for turn in range(max(pairs, half)):
        if turn < half:
            finish_step(1, turn + 1)
            start_chip(1, turn + 1)
        if turn == half - 2:
            start_low()
        if turn < pairs:
            heads_pair(turn)
    for copy in keep:
        copy.wait()
    for k in range(1, count):
        for which in range(2):
            across(k, which).wait_recv()
    chip_copies[0].start()
    core_copies[0].start()
    for step in range(1, half + 1):
        pass_step(1, step)
        if step > 1:
            load_step(1, step - 1)
        if step % 2 == 0 and step // 2 < half:
            finish_low(step // 2)
    load_step(1, half)
    for k in range(-(half - 1), half + 1):
        if k:
            load(1, k).wait()

    def branch_tile(j, carry):
        at = pl.ds(pl.multiple_of(j * TILE, TILE), TILE)
        branch = dot(attended_ref[...], out_all[:, at])
        middle_ref[:, at] = tokens_ref[:, at].astype(F32) + branch
        return carry

    lax.fori_loop(0, width // TILE, branch_tile, 0)
    unit, _ = normalize(middle_ref[...])
    normed_two_ref[...] = (unit * gains_all_ref[1:2, :]).astype(BF)

    for step in range(half // 2 + 1, half + 1):
        finish_low(step)
    chip_copies[0].wait_recv()
    core_copies[1].start()
    for copy in core_copies:
        copy.wait_recv()
    for copy in chip_copies + core_copies:
        copy.wait_send()
    for step in range(1, half + 1):
        for part, direction in hops(step):
            low_copy(direction, step, part).wait_send()
    for i in range(2):
        for step in range(1, half + 1):
            for part, direction in hops(step):
                ring_copy(i, direction, step, part).wait_send()
            for k in places(step):
                chip_copy(i, k).wait_send()
                for which in range(2):
                    core_copy(i, k, which).wait_send()
    for k in range(1, count):
        gain_copy(k).wait_send()
        for which in range(2):
            across(k, which).wait_send()


def front(count, tokens, gains, cotangent, tables, own, gate_own, up_own):
    rows, width = tokens.shape
    own_rows, wide_k = own[1].shape
    qkv_width = width + 2 * wide_k
    ff_own = gate_own.shape[1] // count
    half = count // 2
    here = pl.BlockSpec(memory_space=pl.ANY)
    inside = pl.BlockSpec(memory_space=pltpu.VMEM)
    kind = jax.ShapeDtypeStruct
    dma = pltpu.SemaphoreType.DMA
    return pl.pallas_call(
        functools.partial(front_kernel, count),
        in_specs=[inside] * 6 + [here] * 6,
        out_specs=[here] * 4 + [inside] * 7,
        out_shape=[
            kind((count * own_rows, qkv_width), BF),
            kind((count * own_rows, width), BF),
            kind((count, 4, own_rows // 4, 2 * ff_own), BF),
            kind((count * rows, width), BF),
            kind((gains.shape[0], width), F32),
            kind((rows, width), BF),
            kind((rows, wide_k), BF),
            kind((rows, wide_k), BF),
            kind((rows, width), BF),
            kind((rows, width), F32),
            kind((rows, width), BF),
        ],
        scratch_shapes=[
            pltpu.VMEM((rows, width), BF),
            pltpu.VMEM((own_rows // 4, 2 * ff_own), BF),
            pltpu.VMEM((count * own_rows, qkv_width), BF),
            pltpu.VMEM((count * own_rows, width), BF),
            pltpu.VMEM((rows, width), BF),
            pltpu.VMEM((rows, qkv_width), F32),
            dma((10,)),
            dma((2, count)),
            dma((count - 1,)),
            dma((count - 1,)),
            dma((2, 2, half, 2)),
            dma((2, 2, half, 2)),
            dma((2, 2, count)),
            dma((2, 2, count)),
            dma((2, count)),
            dma((2, count)),
            dma((2, count - 1)),
            dma((2, count - 1)),
            dma((3,)),
            dma((3,)),
            dma((2, half, 2)),
            dma((2, half, 2)),
        ],
        compiler_params=pltpu.CompilerParams(
            collective_id=1, has_side_effects=True, vmem_limit_bytes=VMEM_BYTES
        ),
        cost_estimate=pl.CostEstimate(
            flops=2 * rows * width * (qkv_width + width) + 2 * 10**9,
            bytes_accessed=60 * 10**6,
            transcendentals=2 * 10**6,
        ),
    )(tokens, gains, cotangent, *tables, *own, gate_own, up_own)


def feed_forward_kernel(
    count,
    normed_ref,
    low_ref,
    both_ref,
    down_ref,
    grad_ref,
    branch_ref,
    sums_ref,
    down_grad_ref,
    normed,
    low,
    hidden,
    grads,
    w_both,
    w_down,
    turned,
    staged,
    from_core,
    core_sums,
    from_chip,
    group_sums,
    result_tile,
    outgoing,
    incoming,
    local_sem,
    gather_send,
    gather_recv,
    scatter_send,
    scatter_recv,
    credit,
    core_send,
    core_recv,
    chip_send,
    chip_recv,
    group_credit,
    sums_sem,
    result_sem,
    down_send,
    down_recv,
):
    half = count // 2
    rows = normed_ref.shape[0]
    cut = rows // 2
    width = normed_ref.shape[1]
    ff = down_ref.shape[0]
    place = ring_place(count, lax.axis_index("shard"))
    neighbours = (ring_shard(count, place + 1), ring_shard(count, place - 1))
    rep = lax.axis_index("rep")
    core, chip = rep % 2, rep // 2
    other_core, other_chip = {"rep": core_partner(rep)}, {"rep": chip_partner(rep)}
    everywhere = pl.ds(0, rows)
    halves = (pl.ds(0, cut), pl.ds(cut, cut))

    def at(slot, part=None):
        start, size = (0, rows) if part is None else (part * cut, cut)
        return pl.ds(pl.multiple_of(slot * rows + start, cut), size)

    def tile(j):
        return pl.ds(pl.multiple_of(j * TILE, TILE), TILE)

    def remote(src, dst, send, recv, direction):
        return remote_copy(src, dst, send, recv, {"shard": neighbours[direction]})

    loads = [
        pltpu.make_async_copy(normed_ref, normed.at[at(0)], local_sem.at[0]),
        pltpu.make_async_copy(low_ref, low, local_sem.at[1]),
        pltpu.make_async_copy(both_ref, w_both, local_sem.at[2]),
        pltpu.make_async_copy(down_ref, w_down, local_sem.at[3]),
    ]
    for load in loads:
        load.start()

    for chain in range(2):
        for direction in range(2):
            blank = halves[1 - direction]
            incoming[chain, direction, 0, blank] = jnp.zeros((cut, width), BF)

    greet([{"shard": neighbour} for neighbour in neighbours] + [other_core, other_chip])

    def gathered(part, direction, step):
        base = 0 if direction == 0 else half
        if isinstance(step, int) and step == 1:
            source = 0
        else:
            source = jnp.where(step == 1, 0, base + step - 1)
        return remote(
            normed.at[at(source, part)],
            normed.at[at(base + step, part)],
            gather_send.at[part, direction, step - 1],
            gather_recv.at[part, direction, step - 1],
            direction,
        )

    def gathered_last(direction):
        source = half - 1 if direction == 0 else 2 * half - 1
        return remote(
            normed.at[at(source, direction)],
            normed.at[at(half, direction)],
            gather_send.at[0, direction, half - 1],
            gather_recv.at[0, direction, half - 1],
            direction,
        )

    def products(slot):
        mine = at(slot)

        def body(j, carry):
            gate_at, up_at = tile(j), tile(j + ff // TILE)
            own = normed[mine, :]
            gate = dot(own, w_both[:, gate_at])
            up = dot(own, w_both[:, up_at])
            grad_hidden = contract_last(low[mine, :], w_down[gate_at, :])
            sigmoid = jax.nn.sigmoid(gate)
            silu = gate * sigmoid
            hidden[mine, gate_at] = (silu * up).astype(BF)
            grads[mine, gate_at] = (
                grad_hidden * up * sigmoid * (1.0 + gate * (1.0 - sigmoid))
            ).astype(BF)
            grads[mine, up_at] = (grad_hidden * silu).astype(BF)
            return carry

        lax.fori_loop(0, ff // TILE, body, 0)

    both_ways = ((0, 0), (0, 1), (1, 0), (1, 1))
    loads[0].wait()
    for part, direction in both_ways:
        gathered(part, direction, 1).start()
    for load in loads[1:]:
        load.wait()
    products(0)

    def gather_step(step, carry):
        for part, direction in both_ways:
            gathered(part, direction, step).wait_recv()

            @pl.when(step < half - 1)
            def _():
                gathered(part, direction, step + 1).start()

            if part == direction:

                @pl.when(step == half - 1)
                def _():
                    gathered_last(direction).start()

        products(step)

        @pl.when(step < half - 1)
        def _():
            products(half + step)

        return carry

    lax.fori_loop(1, half, gather_step, 0)
    for direction in range(2):
        gathered_last(direction).wait_recv()
    products(half)

    def term(chain, rows_at, j):
        if chain == 0:
            return contract_last(grads[rows_at, :], w_both[tile(j), :])
        return dot(hidden[rows_at, :], w_down[:, tile(j)])

    def scattered(chain, direction, step):
        if isinstance(step, int) and step == 0:
            own, there = halves[direction], 0
        else:
            own, there = everywhere, step % 2
        return remote(
            outgoing.at[chain, direction, own],
            incoming.at[chain, direction, there, own],
            scatter_send.at[chain, direction, step],
            scatter_recv.at[chain, direction, step],
            direction,
        )

    units = (width + ff) // TILE
    per_step = -(-(units + 3) // (half - 1))
    quarter = TILE // 4

    def core_copy(unit):
        spot = unit % 2
        return remote_copy(
            staged.at[spot, :, 1 - core],
            from_core.at[spot],
            core_send.at[spot],
            core_recv.at[spot],
            other_core,
        )

    def chip_copy(unit):
        spot = unit % 3
        return remote_copy(
            core_sums.at[spot, 1 - chip],
            from_chip.at[spot],
            chip_send.at[spot],
            chip_recv.at[spot],
            other_chip,
        )

    down_units = ff // TILE

    def sums_copy(unit, down):
        spot = unit % 2
        target = down_grad_ref.at[unit, rep] if down else sums_ref.at[unit - down_units]
        return pltpu.make_async_copy(group_sums.at[spot], target, sums_sem.at[spot])

    def for_sums(unit, act):
        @pl.when(unit < down_units)
        def _():
            act(sums_copy(unit, True))

        @pl.when(unit >= down_units)
        def _():
            act(sums_copy(unit, False))

    def down_copy(index):
        at = down_grad_ref.at[:, chip_partner(rep) if index == 2 else rep]
        return remote_copy(
            at,
            at,
            down_send.at[index],
            down_recv.at[index],
            other_chip if index == 0 else other_core,
        )

    def give_credit(which, device):
        pl.semaphore_signal(
            group_credit.at[which], inc=1, device_id=device, device_id_type=pl.DeviceIdType.MESH
        )

    def weight_unit(unit):
        spot = unit % 2

        def from_arrays(left, right, block):
            def turn(c, carry):
                turned[:, at(c)] = left[at(c), tile(block)].T
                return carry

            lax.fori_loop(0, count, turn, 0)

            def body(j, carry):
                value = dot(turned[...], right[:, tile(j)]).astype(BF)
                staged[spot, :, :, :, tile(j)] = value.reshape(2, 2, quarter, TILE)
                return carry

            lax.fori_loop(0, width // TILE, body, 0)

        @pl.when(unit < down_units)
        def _():
            from_arrays(hidden, low, unit)

        @pl.when(unit >= down_units)
        def _():
            from_arrays(normed, grads, unit - down_units)

        @pl.when(unit >= 2)
        def _():
            pl.semaphore_wait(group_credit.at[0], 1)

        core_copy(unit).start()

    def sum_over_cores(unit):
        spot, place_of = unit % 2, unit % 3
        core_copy(unit).wait()
        for y in range(2):
            total = staged[spot, y, core].astype(F32) + from_core[spot, y].astype(F32)
            core_sums[place_of, y] = total.astype(BF)

        @pl.when(unit < units - 2)
        def _():
            give_credit(0, other_core)

        @pl.when(unit >= 3)
        def _():
            pl.semaphore_wait(group_credit.at[1], 1)

        chip_copy(unit).start()

    def sum_over_chips(unit):
        spot, place_of = unit % 2, unit % 3
        chip_copy(unit).wait()

        @pl.when(unit >= 2)
        def _():
            for_sums(unit - 2, lambda copy: copy.wait())

        total = core_sums[place_of, chip].astype(F32) + from_chip[place_of].astype(F32)
        group_sums[spot] = total.astype(BF)

        @pl.when(unit < units - 3)
        def _():
            give_credit(1, other_chip)

        for_sums(unit, lambda copy: copy.start())

    def weight_step(turn):
        @pl.when(turn < units)
        def _():
            weight_unit(turn)

        @pl.when((turn >= 1) & (turn <= units))
        def _():
            sum_over_cores(turn - 1)

        @pl.when(turn == units)
        def _():
            for index in range(2):
                down_copy(index).start()

        @pl.when(turn >= 3)
        def _():
            sum_over_chips(turn - 3)

    for chain in range(2):

        def first(j, carry):
            value = term(chain, at(half), j).astype(BF)
            outgoing[chain, 0, halves[0], tile(j)] = value[:cut]
            outgoing[chain, 1, halves[1], tile(j)] = value[cut:]
            return carry

        lax.fori_loop(0, width // TILE, first, 0)
        for direction in range(2):
            scattered(chain, direction, 0).start()

    products(2 * half - 1)

    def scatter_step(step, carry):
        k = half - step
        for chain in range(2):
            for direction in range(2):
                slot = half + k if direction == 0 else k

                @pl.when(step == 1)
                def _():
                    scattered(chain, direction, 0).wait()

                @pl.when(step > 1)
                def _():
                    scattered(chain, direction, step - 1).wait()
                    pl.semaphore_wait(credit.at[chain, direction], 1)

                def add(j, carry):
                    value = term(chain, at(slot), j)
                    value += incoming[chain, direction, (step - 1) % 2, :, tile(j)].astype(F32)
                    outgoing[chain, direction, :, tile(j)] = value.astype(BF)
                    return carry

                lax.fori_loop(0, width // TILE, add, 0)
                scattered(chain, direction, step).start()

                @pl.when(step < half - 1)
                def _():
                    pl.semaphore_signal(
                        credit.at[chain, direction],
                        inc=1,
                        device_id={"shard": neighbours[1 - direction]},
                        device_id_type=pl.DeviceIdType.MESH,
                    )

        lax.fori_loop(
            (step - 1) * per_step,
            jnp.minimum(step * per_step, units + 3),
            lambda turn, c: (weight_step(turn), c)[1],
            0,
        )
        return carry

    lax.fori_loop(1, half, scatter_step, 0)

    for chain, result in enumerate((grad_ref, branch_ref)):
        for direction in range(2):
            scattered(chain, direction, half - 1).wait()

        def result_copy(j):
            return pltpu.make_async_copy(
                result_tile.at[j % 2], result.at[:, tile(j)], result_sem.at[j % 2]
            )

        def last(j, carry):
            @pl.when(j >= 2)
            def _():
                result_copy(j - 2).wait()

            value = term(chain, at(0), j)
            for direction in range(2):
                value += incoming[chain, direction, (half - 1) % 2, :, tile(j)].astype(F32)
            result_tile[j % 2] = value
            result_copy(j).start()
            return carry

        lax.fori_loop(0, width // TILE, last, 0)
        for j in (width // TILE - 2, width // TILE - 1):
            result_copy(j).wait()

    down_copy(0).wait_recv()
    down_copy(2).start()
    for unit in (units - 2, units - 1):
        sums_copy(unit, False).wait()
    down_copy(0).wait_send()
    for index in (1, 2):
        down_copy(index).wait()
    for part, direction in both_ways:
        lax.fori_loop(
            1,
            half,
            lambda step, c: (gathered(part, direction, step).wait_send(), c)[1],
            0,
        )
    for direction in range(2):
        gathered_last(direction).wait_send()


def feed_forward_bytes(count, rows, width, ff):
    tokens = count * rows
    return 2 * (
        tokens * (2 * width + 3 * ff)
        + 3 * width * ff
        + TILE * tokens
        + 6 * TILE * width
        + 12 * rows * width
        + 4 * TILE * rows
    )


def feed_forward(count, normed, low, w_both, w_down):
    rows, width = normed.shape
    ff = w_down.shape[0]
    tokens = count * rows
    half = count // 2
    quarter = TILE // 4
    here = pl.BlockSpec(memory_space=pl.ANY)
    dma = pltpu.SemaphoreType.DMA
    return pl.pallas_call(
        functools.partial(feed_forward_kernel, count),
        in_specs=[here] * 4,
        out_specs=[here] * 4,
        out_shape=[
            jax.ShapeDtypeStruct((rows, width), F32),
            jax.ShapeDtypeStruct((rows, width), F32),
            jax.ShapeDtypeStruct((width // TILE, quarter, width), BF),
            jax.ShapeDtypeStruct((ff // TILE, 4, quarter, width), BF),
        ],
        scratch_shapes=[
            pltpu.VMEM((tokens, width), BF),
            pltpu.VMEM((tokens, width), BF),
            pltpu.VMEM((tokens, ff), BF),
            pltpu.VMEM((tokens, 2 * ff), BF),
            pltpu.VMEM((width, 2 * ff), BF),
            pltpu.VMEM((ff, width), BF),
            pltpu.VMEM((TILE, tokens), BF),
            pltpu.VMEM((2, 2, 2, quarter, width), BF),
            pltpu.VMEM((2, 2, quarter, width), BF),
            pltpu.VMEM((3, 2, quarter, width), BF),
            pltpu.VMEM((3, quarter, width), BF),
            pltpu.VMEM((2, quarter, width), BF),
            pltpu.VMEM((2, rows, TILE), F32),
            pltpu.VMEM((2, 2, rows, width), BF),
            pltpu.VMEM((2, 2, 2, rows, width), BF),
            dma((4,)),
            dma((2, 2, half)),
            dma((2, 2, half)),
            dma((2, 2, half)),
            dma((2, 2, half)),
            pltpu.SemaphoreType.REGULAR((2, 2)),
            dma((2,)),
            dma((2,)),
            dma((3,)),
            dma((3,)),
            pltpu.SemaphoreType.REGULAR((2,)),
            dma((2,)),
            dma((2,)),
            dma((3,)),
            dma((3,)),
        ],
        compiler_params=pltpu.CompilerParams(
            collective_id=0, has_side_effects=True, vmem_limit_bytes=VMEM_BYTES
        ),
        cost_estimate=pl.CostEstimate(
            flops=18 * tokens * width * ff, bytes_accessed=50 * 10**6, transcendentals=tokens * ff
        ),
    )(normed, low, w_both, w_down)


def middle_back_kernel(
    middle_ref, branch_ref, grad_ref, cotangent_ref, gains_ref, result_ref, out_ref, low_ref, term_ref
):
    middle = middle_ref[...]
    result_ref[...] = middle + branch_ref[...]
    unit, scale_row = normalize(middle)
    grad = grad_ref[...]
    total = cotangent_ref[...] + norm_back(grad * gains_ref[1:2, :], unit, scale_row)
    out_ref[...] = total
    low_ref[...] = total.astype(BF)
    term = jnp.sum(grad * unit, 0, keepdims=True)

    @pl.when(pl.program_id(0) == 0)
    def _():
        term_ref[...] = term

    @pl.when(pl.program_id(0) > 0)
    def _():
        term_ref[...] += term


def middle_back(middle, branch, grad, cotangent, gains):
    rows, width = middle.shape
    block = pl.BlockSpec((rows // 4, width), lambda i: (i, 0))
    fixed = pl.BlockSpec((1, width), lambda i: (0, 0))
    kind = jax.ShapeDtypeStruct
    full = kind((rows, width), F32)
    return pl.pallas_call(
        middle_back_kernel,
        grid=(4,),
        in_specs=[block] * 4 + [pl.BlockSpec(gains.shape, lambda i: (0, 0))],
        out_specs=[block] * 3 + [fixed],
        out_shape=[full, full, kind((rows, width), BF), kind((1, width), F32)],
        compiler_params=pltpu.CompilerParams(vmem_limit_bytes=VMEM_BYTES),
    )(middle, branch, grad, cotangent, gains)


def back_kernel(
    count,
    sums_ref,
    mid_low_ref,
    gain_two_ref,
    attended_ref,
    query_ref,
    key_ref,
    value_ref,
    tokens_ref,
    gains_ref,
    cos_ref,
    sin_ref,
    segr_ref,
    qkv_all_ref,
    out_all_ref,
    gate_grad_ref,
    up_grad_ref,
    out_grad_ref,
    qkv_grad_ref,
    grad_input_ref,
    gain_grad_ref,
    both_own,
    turned,
    grad_attended,
    grads,
    weight_tile,
    terms_first,
    terms_second,
    from_core_out,
    from_core_qkv,
    from_chip_out,
    out_sums,
    out_summed,
    outgoing_out,
    outgoing_qkv,
    incoming_out,
    incoming_qkv,
    summed,
    from_chip,
    finished,
    gain_terms,
    gains_in,
    gain_parts,
    gain_swaps,
    own_sem,
    tile_sem,
    across_send,
    across_recv,
    group_send,
    group_recv,
    core_send,
    core_recv,
    ring_send,
    ring_recv,
    chip_send,
    chip_recv,
    last_send,
    last_recv,
    pair_send,
    pair_recv,
    gain_send,
    gain_recv,
    swap_send,
    swap_recv,
):
    half = count // 2
    me, rep = lax.axis_index("shard"), lax.axis_index("rep")
    core, chip = rep % 2, rep // 2
    place = ring_place(count, me)
    others = [ring_shard(count, place + k) for k in range(1, count)]
    near = ({"shard": ring_shard(count, place + 1)}, {"shard": ring_shard(count, place - 1)})
    other_core, other_chip = {"rep": core_partner(rep)}, {"rep": chip_partner(rep)}
    rows, width = tokens_ref.shape
    own_rows = width // count
    strip, quarter = own_rows // 2, own_rows // 4
    ff_own = gate_grad_ref.shape[2] // count
    qkv_half = grads.shape[1] // 2
    wides = (width, qkv_half, qkv_half)
    terms = (terms_first, terms_second, terms_first)
    pieces = (quarter, strip, strip)
    from_core = (from_core_out, from_core_qkv.at[0], from_core_qkv.at[1])
    outgoing = (outgoing_out, outgoing_qkv.at[0], outgoing_qkv.at[1])
    incoming = (incoming_out, incoming_qkv.at[0], incoming_qkv.at[1])
    result_refs = (out_grad_ref, qkv_grad_ref, qkv_grad_ref)
    result_starts = (0, 0, qkv_half)
    chains, in_turn = range(3), (1, 2, 0)

    def tile(j, size=TILE):
        return pl.ds(pl.multiple_of(j * size, size), size)

    gate_up = (gate_grad_ref, up_grad_ref)

    def own_columns(shard):
        return pl.ds(pl.multiple_of(shard * ff_own, 128), ff_own)

    def across(k, which):
        there = others[k - 1]
        return remote_copy(
            sums_ref.at[there, :, pl.ds(which * ff_own, ff_own)],
            gate_up[which].at[rep, :, own_columns(me)],
            across_send.at[which, k - 1],
            across_recv.at[which, k - 1],
            {"shard": there},
        )

    own_load = pltpu.make_async_copy(sums_ref.at[me], both_own, own_sem.at[0])
    keep = [
        pltpu.make_async_copy(
            both_own.at[:, pl.ds(which * ff_own, ff_own)],
            gate_up[which].at[rep, :, own_columns(me)],
            own_sem.at[which],
        )
        for which in range(2)
    ]

    def group_copy(which, index):
        member = chip_partner(rep) if index == 2 else rep
        dst = src = gate_up[which].at[member]
        return remote_copy(
            src,
            dst,
            group_send.at[which, index],
            group_recv.at[which, index],
            other_chip if index == 0 else other_core,
        )

    def shard_of(k):
        return ring_shard(count, place + k)

    def core_copy(i, k):
        slot = k + half - 1
        return remote_copy(
            terms[i].at[shard_of(k), 1 - core, :, pl.ds(0, wides[i])],
            from_core[i].at[slot],
            core_send.at[i, slot],
            core_recv.at[i, slot],
            other_core,
        )

    def all_terms(i):
        def body(j, carry):
            if i == 0:
                right = mid_low_ref[:, tile(j)]
            else:
                right = grads[:, tile(j + result_starts[i] // TILE)]
            value = dot(turned[...], right).astype(BF)
            terms[i][:, :, :, tile(j)] = value.reshape(count, 2, strip, TILE)
            return carry

        lax.fori_loop(0, wides[i] // TILE, body, 0)
        for k in [half] + [s * j for j in range(half - 1, 0, -1) for s in (1, -1)] + [0]:
            core_copy(i, k).start()

    def pair_copy(k):
        slot = k + half - 1
        return remote_copy(
            out_sums.at[slot, 1 - chip],
            from_chip_out.at[slot],
            pair_send.at[slot],
            pair_recv.at[slot],
            other_chip,
        )

    def sum_pair(k):
        core_copy(0, k).wait_recv()

        def body(j, carry):
            at = tile(j, WIDE_TILE)
            value = terms[0][shard_of(k), core, :, at].astype(F32)
            value += from_core[0][k + half - 1, :, at].astype(F32)
            out_sums[k + half - 1, :, :, at] = value.astype(BF).reshape(2, quarter, WIDE_TILE)
            return carry

        lax.fori_loop(0, wides[0] // WIDE_TILE, body, 0)
        pair_copy(k).start()

    def piece_sum(i, k, extra, store):
        slot = k + half - 1
        if i == 0:
            pair_copy(k).wait_recv()
            received = from_chip_out
        else:
            core_copy(i, k).wait_recv()
            received = from_core[i]

        def body(j, carry):
            at = tile(j, WIDE_TILE)
            own = out_sums[slot, chip, :, at] if i == 0 else terms[i][shard_of(k), core, :, at]
            value = own.astype(F32)
            value += received[slot, :, at].astype(F32)
            for direction, step in extra:
                value += incoming[i][direction, step, :, at].astype(F32)
            store(at, value.astype(BF))
            return carry

        lax.fori_loop(0, wides[i] // WIDE_TILE, body, 0)

    def ring_copy(i, direction, step):
        cut = pieces[i] // 2
        at = pl.ds(direction * cut, cut) if step == 0 else pl.ds(0, pieces[i])
        return remote_copy(
            outgoing[i].at[direction, at],
            incoming[i].at[direction, step, at],
            ring_send.at[i, direction, step],
            ring_recv.at[i, direction, step],
            near[direction],
        )

    def ring_step(i, step):
        if step == 0:

            cut = pieces[i] // 2

            def store(at, value):
                outgoing[i][0, pl.ds(0, cut), at] = value[:cut]
                outgoing[i][1, pl.ds(cut, cut), at] = value[cut:]

            piece_sum(i, half, (), store)
            for direction in range(2):
                ring_copy(i, direction, 0).start()
            return
        for direction in range(2):
            ring_copy(i, direction, step - 1).wait()

            def store(at, value):
                outgoing[i][direction, :, at] = value

            k = half - step if direction == 0 else step - half
            piece_sum(i, k, ((direction, step - 1),), store)
            ring_copy(i, direction, step).start()

    def chip_copy(i):
        return remote_copy(
            summed.at[i - 1],
            from_chip.at[i - 1],
            chip_send.at[i],
            chip_recv.at[i],
            other_chip,
        )

    def ring_end(i):
        for direction in range(2):
            ring_copy(i, direction, half - 1).wait()

        def store(at, value):
            if i == 0:
                out_summed[:, at] = value
            else:
                summed[i - 1, :, at] = value

        piece_sum(i, 0, tuple((d, half - 1) for d in range(2)), store)
        if i > 0:
            chip_copy(i).start()
        else:
            for copy in out_copies()[:3]:
                copy.start()

    own_strip = pl.ds(pl.multiple_of(core * strip, strip), strip)

    def out_copies():
        def at(which_chip):
            return out_grad_ref.at[
                pl.ds(pl.multiple_of(core * strip + which_chip * quarter, quarter), quarter)
            ]

        done = out_summed
        return (
            pltpu.make_async_copy(done, at(chip), own_sem.at[3]),
            remote_copy(done, at(chip), chip_send.at[0], chip_recv.at[0], other_chip),
            remote_copy(done, at(chip), last_send.at[0], last_recv.at[0], other_core),
            remote_copy(at(1 - chip), at(1 - chip), last_send.at[3], last_recv.at[3], other_core),
        )

    def last_copies(i):
        src = finished.at[i - 1]
        dst = result_refs[i].at[own_strip, pl.ds(result_starts[i], wides[i])]
        return (
            pltpu.make_async_copy(src, dst, own_sem.at[3 + i]),
            remote_copy(src, dst, last_send.at[i], last_recv.at[i], other_core),
        )

    def group_end(i):
        chip_copy(i).wait()
        total = summed[i - 1].astype(F32) + from_chip[i - 1].astype(F32)
        finished[i - 1] = total.astype(BF)
        for copy in last_copies(i):
            copy.start()

    def gain_copy(k):
        return remote_copy(
            gain_terms.at[:, tile(others[k - 1], own_rows)],
            gains_in.at[k],
            gain_send.at[k - 1],
            gain_recv.at[k - 1],
            {"shard": others[k - 1]},
        )

    def gain_swap(index):
        return remote_copy(
            gain_parts.at[index],
            gain_swaps.at[index],
            swap_send.at[index],
            swap_recv.at[index],
            (other_core, other_chip)[index],
        )

    def weight_load(ref, j, wide):
        return pltpu.make_async_copy(
            ref.at[tile(j, LOAD_TILE)], weight_tile.at[j % 2, :, pl.ds(0, wide)], tile_sem.at[j % 2]
        )

    def times_transposed(left, ref, wide, store):
        blocks = width // LOAD_TILE

        def body(j, carry):
            @pl.when(j + 1 < blocks)
            def _():
                weight_load(ref, j + 1, wide).start()

            weight_load(ref, j, wide).wait()
            store(tile(j, LOAD_TILE), contract_last(left[...], weight_tile[j % 2, :, pl.ds(0, wide)]))
            return carry

        lax.fori_loop(0, blocks, body, 0)

    def turn(array):
        def body(j, carry):
            turned[tile(j), :] = array[:, tile(j)].T
            return carry

        lax.fori_loop(0, width // TILE, body, 0)

    cosine, sine = cos_ref[...], -sin_ref[...]
    wide, thin = 2 * GROUP * HEAD_SIZE, 2 * HEAD_SIZE
    key_at, value_at = width, width + key_ref.shape[1]

    def heads_pair(pair):
        allowed = allowed_rows(segr_ref[...])
        wide_at, thin_at = pl.ds(pair * wide, wide), pl.ds(pair * thin, thin)
        query, grad = query_ref[:, wide_at], grad_attended[:, wide_at]
        key, value = key_ref[:, thin_at], value_ref[:, thin_at]
        heads, keys, values = [], [], []
        for j in range(2):
            cols = slice(j * HEAD_SIZE, (j + 1) * HEAD_SIZE)
            query_rows, grad_rows = stack_heads(query, j), stack_heads(grad, j)
            probs = softmax_rows(query_rows, key[:, cols], allowed)
            grad_probs = contract_last(grad_rows, value[:, cols])
            grad_scores = (
                probs * (grad_probs - jnp.sum(probs * grad_probs, -1, keepdims=True))
            ).astype(BF)
            heads += unstack_heads(dot(grad_scores, key[:, cols]) * HEAD_SIZE ** (-0.5))
            keys.append(contract_first(grad_scores, query_rows) * HEAD_SIZE ** (-0.5))
            values.append(contract_first(probs.astype(BF), grad_rows))
        grads[:, wide_at] = rotate(jnp.concatenate(heads, 1), cosine, sine).astype(BF)
        grads[:, pl.ds(key_at + pair * thin, thin)] = rotate(
            jnp.concatenate(keys, 1), cosine, sine
        ).astype(BF)
        grads[:, pl.ds(value_at + pair * thin, thin)] = jnp.concatenate(values, 1).astype(BF)

    load_attended = pltpu.make_async_copy(attended_ref, grad_attended, own_sem.at[3])
    load_attended.start()
    own_load.start()
    for i in chains:
        for direction in range(2):
            cut = pieces[i] // 2
            blank = pl.ds((1 - direction) * cut, cut)
            incoming[i][direction, 0, blank] = jnp.zeros((cut, wides[i]), BF)

    own_load.wait()
    for copy in keep:
        copy.start()
    greet([{"shard": shard} for shard in others] + [other_core, other_chip])

    for k in range(1, count):
        for which in range(2):
            across(k, which).start()
    weight_load(out_all_ref, 0, width).start()
    load_attended.wait()
    turn(grad_attended)
    all_terms(0)
    for k in [half] + [s * j for j in range(half - 1, 0, -1) for s in (1, -1)] + [0]:
        sum_pair(k)

    def store_attended(at, value):
        grad_attended[:, at] = value.astype(BF)

    times_transposed(mid_low_ref, out_all_ref, width, store_attended)
    weight_load(qkv_all_ref, 0, grads.shape[1]).start()
    ring_step(0, 0)
    for pair in range(KEY_VALUE_HEADS // 2):
        heads_pair(pair)

    unit, scale_row = normalize(tokens_ref[...].astype(F32))
    gain = gains_ref[0:1, :]
    grad_attended[...] = (unit * gain).astype(BF)
    turn(grad_attended)
    all_terms(1)
    ring_step(1, 0)
    for copy in keep:
        copy.wait()
    for k in range(1, count):
        for which in range(2):
            across(k, which).wait_recv()
    for which in range(2):
        for index in range(2):
            group_copy(which, index).start()
    for k in range(-(half - 1), half + 1):
        core_copy(0, k).wait_send()
    all_terms(2)
    ring_step(2, 0)
    for i in in_turn:
        ring_step(i, 1)

    def store_input(at, value):
        grad_input_ref[:, at] = value

    times_transposed(grads, qkv_all_ref, grads.shape[1], store_input)
    if half > 2:
        for i in in_turn:
            ring_step(i, 2)
    unit, scale_row = normalize(tokens_ref[...].astype(F32))
    grad_normed = grad_input_ref[...]
    gain_terms[...] = jnp.zeros_like(gain_terms)
    gain_terms[0:1, :] = jnp.sum(grad_normed * unit, 0, keepdims=True)
    gain_terms[1:2, :] = gain_two_ref[...]
    for k in range(1, count):
        gain_copy(k).start()
    grad_input_ref[...] = norm_back(grad_normed * gain, unit, scale_row)
    for step in range(3, half):
        for i in in_turn:
            ring_step(i, step)
    for which in range(2):
        group_copy(which, 0).wait_recv()
        group_copy(which, 2).start()
    total = gain_terms[:, tile(me, own_rows)]
    for k in range(1, count):
        gain_copy(k).wait_recv()
        total += gains_in[k]
    gain_parts[0] = total
    gain_swap(0).start()
    for i in in_turn:
        ring_end(i)
    gain_swap(0).wait()
    gain_parts[1] = gain_parts[0] + gain_swaps[0]
    gain_swap(1).start()
    for i in (1, 2):
        group_end(i)
    out_copies()[1].wait_recv()
    out_copies()[3].start()
    gain_swap(1).wait()
    gain_grad_ref[...] = gain_parts[1] + gain_swaps[1]

    for k in range(-(half - 1), half + 1):
        pair_copy(k).wait_send()
    kept, over, passed, again = out_copies()
    kept.wait()
    over.wait_send()
    passed.wait()
    again.wait()
    for i in (1, 2):
        kept, passed = last_copies(i)
        kept.wait()
        passed.wait()
    for i in (1, 2):
        for k in range(-(half - 1), half + 1):
            core_copy(i, k).wait_send()
    for which in range(2):
        for index in range(3):
            if index > 0:
                group_copy(which, index).wait_recv()
            group_copy(which, index).wait_send()
    for k in range(1, count):
        gain_copy(k).wait_send()
        for which in range(2):
            across(k, which).wait_send()


def back(
    count,
    sums,
    mid_low,
    gain_two_term,
    attended,
    query,
    key,
    value,
    tokens,
    gains,
    tables,
    qkv_all,
    out_all,
):
    rows, width = tokens.shape
    qkv_width = qkv_all.shape[1]
    own_rows = width // count
    strip, quarter = own_rows // 2, own_rows // 4
    ff_own = sums.shape[2] // 2
    half = count // 2
    here = pl.BlockSpec(memory_space=pl.ANY)
    inside = pl.BlockSpec(memory_space=pltpu.VMEM)
    kind = jax.ShapeDtypeStruct
    dma = pltpu.SemaphoreType.DMA
    vmem = pltpu.VMEM
    return pl.pallas_call(
        functools.partial(back_kernel, count),
        in_specs=[here] + [inside] * 2 + [here] + [inside] * 8 + [here] * 2,
        out_specs=[here] * 4 + [inside] * 2,
        out_shape=[
            kind((4, quarter, count * ff_own), BF),
            kind((4, quarter, count * ff_own), BF),
            kind((own_rows, width), BF),
            kind((own_rows, qkv_width), BF),
            kind((rows, width), F32),
            kind((8, own_rows), F32),
        ],
        scratch_shapes=[
            vmem((quarter, 2 * ff_own), BF),
            vmem((width, rows), BF),
            vmem((rows, width), BF),
            vmem((rows, qkv_width), BF),
            vmem((2, LOAD_TILE, qkv_width), BF),
            vmem((count, 2, strip, width), BF),
            vmem((count, 2, strip, qkv_width // 2), BF),
            vmem((count, strip, width), BF),
            vmem((2, count, strip, qkv_width // 2), BF),
            vmem((count, quarter, width), BF),
            vmem((count, 2, quarter, width), BF),
            vmem((quarter, width), BF),
            vmem((2, quarter, width), BF),
            vmem((2, 2, strip, qkv_width // 2), BF),
            vmem((2, half, quarter, width), BF),
            vmem((2, 2, half, strip, qkv_width // 2), BF),
            vmem((2, strip, qkv_width // 2), BF),
            vmem((2, strip, qkv_width // 2), BF),
            vmem((2, strip, qkv_width // 2), BF),
            vmem((8, width), F32),
            vmem((count, 8, own_rows), F32),
            vmem((2, 8, own_rows), F32),
            vmem((2, 8, own_rows), F32),
            dma((6,)),
            dma((2,)),
            dma((2, count - 1)),
            dma((2, count - 1)),
            dma((2, 3)),
            dma((2, 3)),
            dma((3, count)),
            dma((3, count)),
            dma((3, 2, half)),
            dma((3, 2, half)),
            dma((3,)),
            dma((3,)),
            dma((4,)),
            dma((4,)),
            dma((count,)),
            dma((count,)),
            dma((count - 1,)),
            dma((count - 1,)),
            dma((2,)),
            dma((2,)),
        ],
        compiler_params=pltpu.CompilerParams(
            collective_id=2, has_side_effects=True, vmem_limit_bytes=VMEM_BYTES
        ),
        cost_estimate=pl.CostEstimate(
            flops=4 * rows * width * (qkv_width + width) + 4 * 10**9,
            bytes_accessed=60 * 10**6,
            transcendentals=2 * 10**6,
        ),
    )(
        sums,
        mid_low,
        gain_two_term,
        attended,
        query,
        key,
        value,
        tokens,
        gains,
        *tables,
        qkv_all,
        out_all,
    )


def results_kernel(*refs):
    gate, up, down, out, qkv, middle, change = refs[:7]
    gate_to, up_to, down_to, out_to, query_to, key_to, value_to, input_to = refs[7:]
    for source, result in ((gate, gate_to), (up, up_to), (down, down_to), (out, out_to)):
        result[...] = source[...].astype(F32)
    start = 0
    for result in (query_to, key_to, value_to):
        result[...] = qkv[:, start : start + result.shape[1]].astype(F32)
        start += result.shape[1]
    input_to[...] = middle[...] + change[...]


def results(gate, up, down, out, qkv, wide_k, grad_middle, change):
    steps = 8
    kind = jax.ShapeDtypeStruct
    sources = (gate, up, down, out, qkv, grad_middle, change)
    width = out.shape[1]
    shapes = [a.shape for a in (gate, up, down, out)]
    shapes += [(qkv.shape[0], w) for w in (width, wide_k, wide_k)] + [change.shape]
    block = lambda shape: pl.BlockSpec((shape[0] // steps, shape[1]), lambda i: (i, 0))
    return pl.pallas_call(
        results_kernel,
        grid=(steps,),
        in_specs=[block(a.shape) for a in sources],
        out_specs=[block(shape) for shape in shapes],
        out_shape=[kind(shape, F32) for shape in shapes],
        compiler_params=pltpu.CompilerParams(vmem_limit_bytes=VMEM_BYTES),
    )(*sources)


def feed_forward_parts(ring, normed_two, grad_low, w_both, w_down):
    sequence, ff_own = normed_two.shape[0], w_down.shape[0]
    low_all, normed_all = run(ring.gather(grad_low), ring.gather(normed_two))
    hidden, grad_both = {}, {}
    for k in normed_all:
        both = dot(normed_all[k], w_both)
        gate, up = both[:, :ff_own], both[:, ff_own:]
        grad_hidden = contract_last(low_all[k], w_down)
        sigmoid = jax.nn.sigmoid(gate)
        silu = gate * sigmoid
        hidden[k] = (silu * up).astype(BF)
        grad_gate = (grad_hidden * up * sigmoid * (1.0 + gate * (1.0 - sigmoid))).astype(BF)
        grad_up = (grad_hidden * silu).astype(BF)
        grad_both[k] = jnp.concatenate([grad_gate, grad_up], 1)

    def terms_of(chunks, product):
        def terms(ks):
            sources = [k if k == ring.half else -k for k in ks]
            whole = product(jnp.concatenate([chunks[k] for k in sources], 0))
            return [whole[i * sequence : (i + 1) * sequence] for i in range(len(ks))]

        return terms

    (grad_normed_two,) = run(ring.scatter(terms_of(grad_both, lambda a: contract_last(a, w_both))))
    (branch_two,) = run(ring.scatter(terms_of(hidden, lambda a: dot(a, w_down))))
    keys = list(normed_all)
    together = lambda parts: jnp.concatenate([parts[k] for k in keys], 0)
    both_term = contract_first(together(normed_all), together(grad_both))
    down_term = contract_first(together(hidden), together(low_all))
    return grad_normed_two, branch_two, both_term, down_term


def swap(array, bit):
    return lax.ppermute(array, "rep", [(i, i ^ bit) for i in range(4)])


def cols(array, start, width):
    return lax.dynamic_slice_in_dim(array, start, width, 1)


def rows_of(array, start, height):
    return lax.dynamic_slice_in_dim(array, start, height, 0)


def put(array, piece, start, axis):
    return lax.dynamic_update_slice_in_dim(array, piece, start, axis)


def gather_rows(ring, array):
    rows = array.shape[0]
    (parts,) = run(ring.gather(array))
    full = jnp.zeros((ring.count * rows, array.shape[1]), array.dtype)
    for k, part in parts.items():
        full = put(full, part, ring.at(-k) * rows, 0)
    return full


def front_parts(ring, tokens, gains_own, cotangent, tables, own, w_gate, w_up):
    count, (own_rows, wide_k) = ring.count, own[1].shape
    rep = lax.axis_index("rep")
    ff_own = w_gate.shape[1] // count
    width = tokens.shape[1]
    gains = jnp.zeros((gains_own.shape[0], width), F32)
    for k in range(count):
        piece = ring.send(gains_own, k) if k else gains_own
        gains = put(gains, piece, ring.at(-k) * own_rows, 1)
    qkv_all = gather_rows(ring, jnp.concatenate(own[:3], 1))
    out_all = gather_rows(ring, own[3])
    quarter = own_rows // 4
    gate_rows = rows_of(w_gate, rep * quarter, quarter)
    up_rows = rows_of(w_up, rep * quarter, quarter)
    sends = []
    for k in range(count):
        dest = ring.at(k) * ff_own
        piece = jnp.concatenate([cols(gate_rows, dest, ff_own), cols(up_rows, dest, ff_own)], 1)
        sends.append((piece, k))
    fetched = jnp.zeros((count, quarter, 2 * ff_own), BF)
    for k, piece in enumerate([sends[0][0]] + ring.queue(*sends[1:])):
        fetched = put(fetched, piece[None], ring.at(-k), 0)
    pieces = [fetched, swap(fetched, 2)]
    pieces += [swap(piece, 1) for piece in pieces]
    w_both = jnp.zeros((count, 4, quarter, 2 * ff_own), BF)
    for bits, piece in zip((0, 2, 1, 3), pieces):
        w_both = put(w_both, piece[:, None], rep ^ bits, 1)
    resid = tokens.astype(F32)
    unit, _ = normalize(resid)
    linear = dot((unit * gains[:1]).astype(BF), qkv_all)
    query, key, value, attended = attend(
        linear[:, :width], linear[:, width : width + wide_k], linear[:, width + wide_k :], tables
    )
    middle = resid + dot(attended, out_all)
    unit, _ = normalize(middle)
    normed_two = (unit * gains[1:2]).astype(BF)
    low = cotangent.astype(BF)
    return qkv_all, out_all, w_both, low, gains, query, key, value, attended, middle, normed_two


def back_parts(
    ring,
    both_term,
    down_term,
    mid_low,
    gain_two_term,
    attended,
    query,
    key,
    value,
    tokens,
    gains,
    tables,
    qkv_all,
    out_all,
):
    count = ring.count
    rep = lax.axis_index("rep")
    core, chip = rep % 2, rep // 2
    width = tokens.shape[1]
    own_rows = width // count
    quarter = own_rows // 4
    ff_own = both_term.shape[1] // 2
    ff = ff_own * count

    def order_halves(mine, other):
        first = core == 0
        return jnp.where(first, mine, other), jnp.where(first, other, mine)

    def sum_cores(array, half_of):
        keep, pass_on = half_of(array, core), half_of(array, 1 - core)
        return keep.astype(F32) + swap(pass_on.astype(BF), 1).astype(F32)

    both_term = both_term.reshape(count, 2, 2, quarter, 2 * ff_own)
    both_half = sum_cores(
        both_term, lambda a, c: lax.dynamic_index_in_dim(a, c, 2, keepdims=False)
    )
    keep = lax.dynamic_index_in_dim(both_half, chip, 1, keepdims=False)
    pass_on = lax.dynamic_index_in_dim(both_half, 1 - chip, 1, keepdims=False)
    both_quarter = (keep + swap(pass_on.astype(BF), 2).astype(F32)).astype(BF)
    gate_quarter = jnp.zeros((quarter, ff), BF)
    up_quarter = jnp.zeros((quarter, ff), BF)
    sends = [
        (lax.dynamic_index_in_dim(both_quarter, ring.at(k), 0, keepdims=False), k)
        for k in range(count)
    ]
    for k, piece in enumerate([sends[0][0]] + ring.queue(*sends[1:])):
        start = ring.at(-k) * ff_own
        gate_quarter = put(gate_quarter, piece[:, :ff_own], start, 1)
        up_quarter = put(up_quarter, piece[:, ff_own:], start, 1)

    def collect(quarter_rows):
        parts = [quarter_rows, swap(quarter_rows, 2)]
        parts += [swap(part, 1) for part in parts]
        full = jnp.zeros((4 * quarter, ff), BF)
        for bits, part in zip((0, 2, 1, 3), parts):
            full = put(full, part, (rep ^ bits) * quarter, 0)
        return full

    gate_grad, up_grad = collect(gate_quarter), collect(up_quarter)

    down_half = sum_cores(
        down_term, lambda a, c: rows_of(a, c * (a.shape[0] // 2), a.shape[0] // 2)
    ).astype(BF)
    down_half = (down_half.astype(F32) + swap(down_half, 2).astype(F32)).astype(BF)
    down_grad = jnp.concatenate(order_halves(down_half, swap(down_half, 1)), 0)

    def part_sums(left, grads):
        wide = grads.shape[1] // 2
        grads_mine, grads_other = cols(grads, core * wide, wide), cols(grads, (1 - core) * wide, wide)

        def terms(ks):
            blocks = [cols(left, ring.at(k) * own_rows, own_rows) for k in ks]
            block = blocks[0] if len(ks) == 1 else jnp.concatenate(blocks, 1)
            other = swap(contract_first(block, grads_other).astype(BF), 1)
            whole = contract_first(block, grads_mine) + other.astype(F32)
            return [whole[i * own_rows : (i + 1) * own_rows] for i in range(len(ks))]

        mine = run(ring.scatter(terms))[0].astype(BF)
        mine = (mine.astype(F32) + swap(mine, 2).astype(F32)).astype(BF)
        return jnp.concatenate(order_halves(mine, swap(mine, 1)), 1)

    out_grad = part_sums(attended, mid_low)
    grad_attended = contract_last(mid_low, out_all).astype(BF)
    grads = jnp.concatenate(attend_back(query, key, value, grad_attended, tables), 1)
    unit_one, scale_one = normalize(tokens.astype(F32))
    gain_one = gains[:1]
    qkv_grad = part_sums((unit_one * gain_one).astype(BF), grads)
    grad_normed_one = contract_last(grads, qkv_all)
    gain_one_term = jnp.sum(grad_normed_one * unit_one, 0, keepdims=True)
    grad_input = norm_back(grad_normed_one * gain_one, unit_one, scale_one)

    gain_terms = jnp.concatenate([gain_one_term, gain_two_term], 0)
    gain_sums = cols(gain_terms, ring.at(0) * own_rows, own_rows)
    for k in range(1, count):
        gain_sums = gain_sums + ring.send(cols(gain_terms, ring.at(k) * own_rows, own_rows), k)
    gain_sums = gain_sums + swap(gain_sums, 1)
    gain_sums = gain_sums + swap(gain_sums, 2)
    return gate_grad, up_grad, down_grad, out_grad, qkv_grad, grad_input, gain_sums


def on_device(
    count,
    tokens,
    segments,
    norm_attn,
    w_query,
    key_weight,
    value_weight,
    w_out,
    norm_mlp,
    w_gate,
    w_up,
    w_down,
    cotangent,
):
    ring = Ring(count)
    sequence, width = tokens.shape[1], tokens.shape[2]
    own_rows = w_query.shape[0]
    ff = w_gate.shape[1]
    ff_own = ff // count
    wide_k = key_weight.shape[1]
    fits = feed_forward_bytes(count, sequence, width, ff_own) <= VMEM_BYTES
    kernels = fits and sequence == own_rows == TILE

    grad_output = cotangent.reshape(sequence, width)
    cosine, sine = rope_tables(segments)
    tables = (cosine, sine, segments.reshape(1, sequence))
    own = tokens.reshape(sequence, width)
    own_weights = (w_query, key_weight, value_weight, w_out)
    gains_own = jnp.zeros((8, own_rows), F32)
    gains_own = gains_own.at[0].set(norm_attn.astype(F32)).at[1].set(norm_mlp.astype(F32))
    bring = functools.partial(front, count) if kernels else functools.partial(front_parts, ring)
    qkv_all, out_all, w_both, low, gains, query, key, value, attended, middle, normed_two = bring(
        own, gains_own, grad_output, tables, own_weights, w_gate, w_up
    )
    w_both = w_both.reshape(width, 2 * ff_own)

    if kernels:
        grad_normed_two, branch_two, sums, down_grad = feed_forward(
            count, normed_two, low, w_both, w_down
        )
    else:
        grad_normed_two, branch_two, both_term, down_term = feed_forward_parts(
            ring, normed_two, low, w_both, w_down
        )
    output, grad_middle, grad_mid_low, gain_two_term = middle_back(
        middle, branch_two, grad_normed_two, grad_output, gains
    )

    if kernels:
        gate_grad, up_grad, out_grad, qkv_grad, grad_input, gain_sums = back(
            count,
            sums,
            grad_mid_low,
            gain_two_term,
            attended,
            query,
            key,
            value,
            own,
            gains,
            tables,
            qkv_all,
            out_all,
        )
    else:
        gate_grad, up_grad, down_grad, out_grad, qkv_grad, grad_input, gain_sums = back_parts(
            ring,
            both_term,
            down_term,
            grad_mid_low,
            gain_two_term,
            attended,
            query,
            key,
            value,
            own,
            gains,
            tables,
            qkv_all,
            out_all,
        )
    gate_grad, up_grad, down_grad, out_grad, query_grad, key_grad, value_grad, grad_input = results(
        gate_grad.reshape(own_rows, ff),
        up_grad.reshape(own_rows, ff),
        down_grad.reshape(ff_own, width),
        out_grad,
        qkv_grad,
        wide_k,
        grad_middle,
        grad_input,
    )

    return (
        output.reshape(tokens.shape),
        grad_input.reshape(tokens.shape),
        gain_sums[0],
        query_grad,
        key_grad,
        value_grad,
        out_grad,
        gain_sums[1],
        gate_grad,
        up_grad,
        down_grad,
    )


def solution(mesh):
    row, vector, matrix = P(("shard", "rep"), None, None), P("shard"), P("shard", None)
    in_specs = (row, P(("shard", "rep"), None), vector, matrix, matrix, matrix, matrix, vector)
    in_specs += (matrix, matrix, matrix, row)
    out_specs = (row, row, vector, matrix, matrix, matrix, matrix, vector, matrix, matrix, matrix)
    return jax.shard_map(
        functools.partial(on_device, mesh.shape["shard"]),
        mesh=mesh,
        in_specs=in_specs,
        out_specs=out_specs,
        check_vma=False,
    )
```

```python
import functools

import jax
import jax.numpy as jnp
from jax import lax
from jax.experimental import pallas as pl
from jax.experimental.pallas import tpu as pltpu
from jax.sharding import PartitionSpec as P

QUERY_HEADS = 32
KEY_VALUE_HEADS = 8
HEAD_SIZE = 64
GROUP = QUERY_HEADS // KEY_VALUE_HEADS

epsilon = 1e-05
masked_score = -1000000000.0
rope_base = 500000.0
WINDOW = 2
TILE = 256
WIDE_TILE = 512
LOAD_TILE = 128
VMEM_BYTES = 62 * 2**20
BF = jnp.bfloat16
F32 = jnp.float32


def dot(left, right):
    return jnp.dot(left, right, preferred_element_type=F32)


def contract_last(left, right):
    return lax.dot_general(left, right, (((1,), (1,)), ((), ())), preferred_element_type=F32)


def contract_first(left, right):
    return lax.dot_general(left, right, (((0,), (0,)), ((), ())), preferred_element_type=F32)


def positions(segment_ids):
    index = lax.broadcasted_iota(jnp.int32, segment_ids.shape, 1)
    first = jnp.concatenate(
        [
            jnp.ones_like(segment_ids[:, :1]),
            (segment_ids[:, 1:] != segment_ids[:, :-1]).astype(jnp.int32),
        ],
        1,
    )
    starts = lax.cummax(jnp.where(first > 0, index, 0), axis=1)
    return (index - starts).astype(F32)


def rope_tables(segment_ids):
    half = HEAD_SIZE // 2
    inverse = rope_base ** (-(2.0 * jnp.arange(half, dtype=F32)) / HEAD_SIZE)
    angle = positions(segment_ids)[0, :, None] * inverse
    cosine, sine = jnp.cos(angle), jnp.sin(angle)
    return jnp.concatenate([cosine] * 4, 1), jnp.concatenate([-sine, sine] * 2, 1)


def normalize(rows):
    scale_row = lax.rsqrt(jnp.mean(rows * rows, -1, keepdims=True) + epsilon)
    return rows * scale_row, scale_row


def norm_back(grad_unit, unit, scale_row):
    return scale_row * (grad_unit - unit * jnp.mean(grad_unit * unit, -1, keepdims=True))


def rotate(block, cosine, sine):
    lane = lax.broadcasted_iota(jnp.int32, cosine.shape, 1)
    lower = lane % HEAD_SIZE < HEAD_SIZE // 2
    parts = []
    for at in range(0, block.shape[1], 128):
        part = block[:, at : at + 128]
        other = jnp.where(
            lower, pltpu.roll(part, 128 - HEAD_SIZE // 2, 1), pltpu.roll(part, HEAD_SIZE // 2, 1)
        )
        parts.append(part * cosine + other * sine)
    return parts[0] if len(parts) == 1 else jnp.concatenate(parts, 1)


def stack_heads(block, key_head):
    first = key_head * GROUP
    return jnp.concatenate(
        [block[:, (first + i) * HEAD_SIZE : (first + i + 1) * HEAD_SIZE] for i in range(GROUP)], 0
    )


def unstack_heads(rows):
    count = rows.shape[0] // GROUP
    return [rows[i * count : (i + 1) * count] for i in range(GROUP)]


def softmax_rows(query, key, allowed):
    raw = contract_last(query, key) * HEAD_SIZE ** (-0.5)
    scores = jnp.where(allowed, raw, masked_score)
    exponent = jnp.exp(scores - jnp.max(scores, -1, keepdims=True))
    return exponent / jnp.sum(exponent, -1, keepdims=True)


def allowed_rows(seg_row):
    count = seg_row.shape[1]
    shape = (count, count)
    at_row = lax.broadcasted_iota(jnp.int32, shape, 0)
    at_column = lax.broadcasted_iota(jnp.int32, shape, 1)
    causal = at_row >= at_column
    seg_column = jnp.sum(
        jnp.where(at_row == at_column, jnp.broadcast_to(seg_row, shape), 0), 1, keepdims=True
    )
    one = ((seg_column == seg_row) & causal).astype(jnp.int32)
    return jnp.concatenate([one] * GROUP, 0) > 0


def attend_kernel(q_ref, k_ref, v_ref, cos_ref, sin_ref, segr_ref, qo, ko, vo, ao):
    cosine, sine = cos_ref[...], sin_ref[...]
    allowed = allowed_rows(segr_ref[...])
    query = rotate(q_ref[...], cosine, sine).astype(BF)
    key = rotate(k_ref[...], cosine, sine).astype(BF)
    value = v_ref[...].astype(BF)
    qo[...] = query
    ko[...] = key
    vo[...] = value
    heads = []
    for j in range(2):
        cols = slice(j * HEAD_SIZE, (j + 1) * HEAD_SIZE)
        probs = softmax_rows(stack_heads(query, j), key[:, cols], allowed).astype(BF)
        heads += unstack_heads(dot(probs, value[:, cols]).astype(BF))
    ao[...] = jnp.concatenate(heads, 1)


def attend_back_kernel(q_ref, k_ref, v_ref, g_ref, cos_ref, sin_ref, segr_ref, gq, gk, gv):
    cosine, sine = cos_ref[...], -sin_ref[...]
    allowed = allowed_rows(segr_ref[...])
    query, key, value, grad = q_ref[...], k_ref[...], v_ref[...], g_ref[...]
    heads, keys, values = [], [], []
    for j in range(2):
        cols = slice(j * HEAD_SIZE, (j + 1) * HEAD_SIZE)
        rows, grad_rows = stack_heads(query, j), stack_heads(grad, j)
        probs = softmax_rows(rows, key[:, cols], allowed)
        grad_probs = contract_last(grad_rows, value[:, cols])
        grad_scores = (
            probs * (grad_probs - jnp.sum(probs * grad_probs, -1, keepdims=True))
        ).astype(BF)
        heads += unstack_heads(dot(grad_scores, key[:, cols]) * HEAD_SIZE ** (-0.5))
        keys.append(contract_first(grad_scores, rows) * HEAD_SIZE ** (-0.5))
        values.append(contract_first(probs.astype(BF), grad_rows))
    gq[...] = rotate(jnp.concatenate(heads, 1), cosine, sine).astype(BF)
    gk[...] = rotate(jnp.concatenate(keys, 1), cosine, sine).astype(BF)
    gv[...] = jnp.concatenate(values, 1).astype(BF)


def attention_specs(count):
    wide = pl.BlockSpec((count, 2 * GROUP * HEAD_SIZE), lambda i: (0, i))
    thin = pl.BlockSpec((count, 2 * HEAD_SIZE), lambda i: (0, i))
    whole = lambda shape: pl.BlockSpec(shape, lambda i: (0, 0))
    fixed = [whole((count, 128)), whole((count, 128)), whole((1, count))]
    return wide, thin, fixed


def attend(query_lin, key_lin, value_lin, tables):
    count = query_lin.shape[0]
    wide, thin, fixed = attention_specs(count)
    kinds = [jax.ShapeDtypeStruct(a.shape, BF) for a in (query_lin, key_lin, value_lin, query_lin)]
    return pl.pallas_call(
        attend_kernel,
        grid=(KEY_VALUE_HEADS // 2,),
        in_specs=[wide, thin, thin] + fixed,
        out_specs=[wide, thin, thin, wide],
        out_shape=kinds,
        compiler_params=pltpu.CompilerParams(vmem_limit_bytes=48 * 2**20),
        cost_estimate=pl.CostEstimate(
            flops=2 * 10**9, bytes_accessed=6 * 10**6, transcendentals=2 * 10**6
        ),
    )(query_lin, key_lin, value_lin, *tables)


def attend_back(query, key, value, grad, tables):
    count = query.shape[0]
    wide, thin, fixed = attention_specs(count)
    kinds = [jax.ShapeDtypeStruct(a.shape, BF) for a in (query, key, value)]
    return pl.pallas_call(
        attend_back_kernel,
        grid=(KEY_VALUE_HEADS // 2,),
        in_specs=[wide, thin, thin, wide] + fixed,
        out_specs=[wide, thin, thin],
        out_shape=kinds,
        compiler_params=pltpu.CompilerParams(vmem_limit_bytes=48 * 2**20),
        cost_estimate=pl.CostEstimate(
            flops=4 * 10**9, bytes_accessed=6 * 10**6, transcendentals=2 * 10**6
        ),
    )(query, key, value, grad, *tables)


def ring_order(count):
    return list(range(0, count, 2)) + list(range(count - 1, 0, -2)) if count % 2 == 0 else list(range(count))


class Ring:
    def __init__(self, count):
        self.count = count
        self.half = count // 2
        self.order = ring_order(count)
        inverse = [self.order.index(i) for i in range(count)]
        self.table = jnp.asarray(self.order, jnp.int32)
        self.turns = []
        self.place = jnp.asarray(inverse, jnp.int32)[lax.axis_index("shard")]

    def at(self, offset):
        return self.table[(self.place + offset + self.count) % self.count]

    def send(self, array, offset):
        n, order = self.count, self.order
        pairs = [(order[i], order[(i + offset) % n]) for i in range(n)]
        return lax.ppermute(array, "shard", pairs)

    def queue(self, *sends):
        arrays = [array for array, _ in sends]
        if len(self.turns) >= WINDOW:
            arrays, _ = lax.optimization_barrier((arrays, self.turns[-WINDOW]))
        got = [self.send(array, offset) for array, (_, offset) in zip(arrays, sends)]
        self.turns.append(got[:2])
        return got

    def gather(self, array):
        cut = array.shape[0] // 2
        ahead = back = array
        out = {0: array}
        for k in range(1, self.half):
            ahead, back = self.queue((ahead, 1), (back, -1))
            out[k], out[-k] = ahead, back
            yield out
        out[self.half] = jnp.concatenate(self.queue((ahead[:cut], 1), (back[cut:], -1)), 0)
        yield out

    def scatter(self, terms):
        (far,) = terms((self.half,))
        far = far.astype(BF)
        cut = far.shape[0] // 2
        ahead, back = self.queue((far[:cut], 1), (far[cut:], -1))
        yield None
        for k in range(self.half - 1, 0, -1):
            up, down = terms((k, -k))
            if k == self.half - 1:
                up = jnp.concatenate([up[:cut] + ahead.astype(F32), up[cut:]], 0)
                down = jnp.concatenate([down[:cut], down[cut:] + back.astype(F32)], 0)
            else:
                up, down = up + ahead.astype(F32), down + back.astype(F32)
            ahead, back = self.queue((up.astype(BF), 1), (down.astype(BF), -1))
            if k > 1:
                yield None
        (own,) = terms((0,))
        yield own + ahead.astype(F32) + back.astype(F32)


def run(*flows):
    flows = list(flows)
    last = [None] * len(flows)
    live = list(range(len(flows)))
    while live:
        for i in list(live):
            try:
                last[i] = next(flows[i])
            except StopIteration:
                live.remove(i)
    return last


def ring_place(count, shard):
    return jnp.where(shard % 2 == 0, shard // 2, count - 1 - shard // 2)


def ring_shard(count, place):
    place = (place + count) % count
    return jnp.where(place < count // 2, 2 * place, 2 * (count - 1 - place) + 1)


def core_partner(rep):
    return rep + 1 - 2 * (rep % 2)


def chip_partner(rep):
    return (rep + 2) % 4


def greet(devices):
    barrier = pltpu.get_barrier_semaphore()
    for device in devices:
        pl.semaphore_signal(
            barrier, inc=1, device_id=device, device_id_type=pl.DeviceIdType.MESH
        )
    pl.semaphore_wait(barrier, len(devices))


def remote_copy(src, dst, send, recv, device):
    return pltpu.make_async_remote_copy(
        src_ref=src,
        dst_ref=dst,
        send_sem=send,
        recv_sem=recv,
        device_id=device,
        device_id_type=pl.DeviceIdType.MESH,
    )


def front_kernel(
    count,
    tokens_ref,
    gains_ref,
    cotangent_ref,
    cos_ref,
    sin_ref,
    segr_ref,
    query_own_ref,
    key_own_ref,
    value_own_ref,
    out_own_ref,
    gate_ref,
    up_ref,
    qkv_all_ref,
    out_all_ref,
    both_ref,
    low_all_ref,
    gains_all_ref,
    query_ref,
    key_ref,
    value_ref,
    attended_ref,
    middle_ref,
    normed_two_ref,
    low_own,
    both_own,
    qkv_all,
    out_all,
    normed,
    linear,
    own_sem,
    load_sem,
    gain_send,
    gain_recv,
    ring_send,
    ring_recv,
    core_send,
    core_recv,
    chip_send,
    chip_recv,
    across_send,
    across_recv,
    group_send,
    group_recv,
    low_send,
    low_recv,
):
    half = count // 2
    me, rep = lax.axis_index("shard"), lax.axis_index("rep")
    core, chip = rep % 2, rep // 2
    place = ring_place(count, me)
    others = [ring_shard(count, place + k) for k in range(1, count)]
    near = ({"shard": ring_shard(count, place + 1)}, {"shard": ring_shard(count, place - 1)})
    other_core, other_chip = {"rep": core_partner(rep)}, {"rep": chip_partner(rep)}
    own_rows = query_own_ref.shape[0]
    quarter = own_rows // 4
    cut = quarter // 2
    ff_own = gate_ref.shape[1] // count
    rows, width = tokens_ref.shape
    full_refs = (qkv_all_ref, out_all_ref)
    inside = (qkv_all, out_all)

    def rows_at(start, size):
        return pl.ds(pl.multiple_of(start, cut), size)

    def shard_rows(shard):
        return rows_at(shard * own_rows, own_rows)

    def piece_of(shard, which_core, which_chip, part=None):
        start = shard * own_rows + (2 * which_core + which_chip) * quarter
        if part is None:
            return rows_at(start, quarter)
        return rows_at(start + part * cut, cut)

    own_loads = [
        pltpu.make_async_copy(out_own_ref, out_all.at[shard_rows(me)], own_sem.at[6])
    ]
    start = 0
    for index, ref in enumerate((query_own_ref, key_own_ref, value_own_ref)):
        columns = pl.ds(start, ref.shape[1])
        own_loads.append(
            pltpu.make_async_copy(ref, qkv_all.at[shard_rows(me), columns], own_sem.at[7 + index])
        )
        start += ref.shape[1]
    keep = [
        pltpu.make_async_copy(
            inside[i].at[shard_rows(me)], full_refs[i].at[shard_rows(me)], own_sem.at[i]
        )
        for i in range(2)
    ]
    for i, ref in enumerate((gate_ref, up_ref)):
        block = (rows_at(rep * quarter, quarter), pl.ds(pl.multiple_of(me * ff_own, 128), ff_own))
        own_loads.append(
            pltpu.make_async_copy(
                ref.at[block], both_own.at[:, pl.ds(i * ff_own, ff_own)], own_sem.at[2 + i]
            )
        )
    for copy in own_loads:
        copy.start()
    gains_all_ref[:, pl.ds(pl.multiple_of(me * own_rows, 128), own_rows)] = gains_ref[...]
    low_own[...] = cotangent_ref[...].astype(BF)
    for copy in own_loads:
        copy.wait()
    keep.append(pltpu.make_async_copy(low_own, low_all_ref.at[pl.ds(0, rows)], own_sem.at[4]))
    keep.append(pltpu.make_async_copy(both_own, both_ref.at[me, rep], own_sem.at[5]))
    for copy in keep:
        copy.start()

    greet([{"shard": shard} for shard in others] + [other_core, other_chip])

    def gain_copy(k):
        columns = pl.ds(pl.multiple_of(me * own_rows, 128), own_rows)
        return remote_copy(
            gains_ref,
            gains_all_ref.at[:, columns],
            gain_send.at[k - 1],
            gain_recv.at[k - 1],
            {"shard": others[k - 1]},
        )

    def across(k, which):
        ref = (gate_ref, up_ref)[which]
        there = others[k - 1]
        columns = pl.ds(pl.multiple_of(there * ff_own, 128), ff_own)
        return remote_copy(
            ref.at[rows_at(rep * quarter, quarter), columns],
            both_ref.at[me, rep, :, pl.ds(which * ff_own, ff_own)],
            across_send.at[which, k - 1],
            across_recv.at[which, k - 1],
            {"shard": there},
        )

    def hops(step):
        return ((0, 0), (0, 1), (1, 0), (1, 1)) if step < half else ((0, 0), (1, 1))

    def ring_copy(i, direction, step, part):
        sign = 1 if direction == 0 else -1
        at = piece_of(ring_shard(count, place - sign * (step - 1)), core, chip, part)
        src = inside[i].at[at] if step == 1 else full_refs[i].at[at]
        return remote_copy(
            src,
            full_refs[i].at[at],
            ring_send.at[i, direction, step - 1, part],
            ring_recv.at[i, direction, step - 1, part],
            near[direction],
        )

    def chip_copy(i, k):
        at = piece_of(ring_shard(count, place - k), core, chip)
        slot = k + half - 1
        return remote_copy(
            full_refs[i].at[at],
            full_refs[i].at[at],
            chip_send.at[i, slot],
            chip_recv.at[i, slot],
            other_chip,
        )

    def core_copy(i, k, which):
        from_chip = chip if which == 0 else 1 - chip
        at = piece_of(ring_shard(count, place - k), core, from_chip)
        slot = k + half - 1
        return remote_copy(
            full_refs[i].at[at],
            full_refs[i].at[at],
            core_send.at[i, which, slot],
            core_recv.at[i, which, slot],
            other_core,
        )

    def load(i, k):
        at = shard_rows(ring_shard(count, place - k))
        return pltpu.make_async_copy(
            full_refs[i].at[at], inside[i].at[at], load_sem.at[i, k + half - 1]
        )

    def low_copy(direction, step, part):
        base = 0 if direction == 0 else half
        source = (base + step - 1) * rows if step > 1 else 0
        to = (base + step if step < half else half) * rows
        size = rows // 2
        src = (low_all_ref if step > 1 else low_own).at[pl.ds(source + part * size, size)]
        return remote_copy(
            src,
            low_all_ref.at[pl.ds(to + part * size, size)],
            low_send.at[direction, step - 1, part],
            low_recv.at[direction, step - 1, part],
            near[direction],
        )

    def pass_on(copy_of, step):
        for part, direction in hops(step):
            copy_of(direction, step, part).wait_recv()
            if step < half - 1 or (step == half - 1 and part == direction):
                copy_of(direction, step + 1, part).start()

    def start_low():
        for part, direction in hops(1):
            low_copy(direction, 1, part).start()

    def finish_low(step):
        pass_on(low_copy, step)

    def start_ring(i):
        for part, direction in hops(1):
            ring_copy(i, direction, 1, part).start()

    def places(step):
        return (step, -step) if step < half else (half,)

    def finish_step(i, step):
        pass_on(functools.partial(ring_copy, i), step)
        for k in places(step):
            core_copy(i, k, 0).start()

    def start_chip(i, step):
        for k in places(step):
            chip_copy(i, k).start()

    def pass_step(i, step):
        for k in places(step):
            chip_copy(i, k).wait_recv()
            core_copy(i, k, 1).start()

    def load_step(i, step):
        for k in places(step):
            for which in range(2):
                core_copy(i, k, which).wait_recv()
            load(i, k).start()

    for k in range(1, count):
        gain_copy(k).start()
    start_ring(0)
    resid = tokens_ref[...].astype(F32)
    unit, _ = normalize(resid)
    for k in range(1, count):
        gain_copy(k).wait_recv()
    normed[...] = (unit * gains_all_ref[0:1, :]).astype(BF)

    for step in range(1, half + 1):
        finish_step(0, step)
        start_chip(0, step)
        if step == half - 1:
            for k in range(1, count):
                for which in range(2):
                    across(k, which).start()
    start_ring(1)
    for step in range(1, half + 1):
        pass_step(0, step)
        if step > 1:
            load_step(0, step - 1)

    def group_copy(index, quarter_at, device):
        at = both_ref.at[:, quarter_at]
        return remote_copy(at, at, group_send.at[index], group_recv.at[index], device)

    chip_copies = [group_copy(0, rep, other_chip)]
    core_copies = [
        group_copy(1, rep, other_core),
        group_copy(2, chip_partner(rep), other_core),
    ]
    load_step(0, half)
    for k in range(-(half - 1), half + 1):
        if k:
            load(0, k).wait()

    def linear_tile(j, carry):
        at = pl.ds(pl.multiple_of(j * TILE, TILE), TILE)
        linear[:, at] = dot(normed[...], qkv_all[:, at])
        return carry

    lax.fori_loop(0, linear.shape[1] // TILE, linear_tile, 0)

    cosine, sine = cos_ref[...], sin_ref[...]
    wide, thin = 2 * GROUP * HEAD_SIZE, 2 * HEAD_SIZE
    key_at, value_at = width, width + key_ref.shape[1]

    def heads_pair(pair):
        allowed = allowed_rows(segr_ref[...])
        wide_at = pl.ds(pair * wide, wide)
        thin_at = pl.ds(pair * thin, thin)
        query = rotate(linear[:, wide_at], cosine, sine).astype(BF)
        key = rotate(linear[:, pl.ds(key_at + pair * thin, thin)], cosine, sine).astype(BF)
        value = linear[:, pl.ds(value_at + pair * thin, thin)].astype(BF)
        query_ref[:, wide_at] = query
        key_ref[:, thin_at] = key
        value_ref[:, thin_at] = value
        heads = []
        for j in range(2):
            cols = slice(j * HEAD_SIZE, (j + 1) * HEAD_SIZE)
            probs = softmax_rows(stack_heads(query, j), key[:, cols], allowed).astype(BF)
            heads += unstack_heads(dot(probs, value[:, cols]).astype(BF))
        attended_ref[:, wide_at] = jnp.concatenate(heads, 1)

    pairs = KEY_VALUE_HEADS // 2
    for turn in range(max(pairs, half)):
        if turn < half:
            finish_step(1, turn + 1)
            start_chip(1, turn + 1)
        if turn == half - 2:
            start_low()
        if turn < pairs:
            heads_pair(turn)
    for copy in keep:
        copy.wait()
    for k in range(1, count):
        for which in range(2):
            across(k, which).wait_recv()
    chip_copies[0].start()
    core_copies[0].start()
    for step in range(1, half + 1):
        pass_step(1, step)
        if step > 1:
            load_step(1, step - 1)
        if step % 2 == 0 and step // 2 < half:
            finish_low(step // 2)
    load_step(1, half)
    for k in range(-(half - 1), half + 1):
        if k:
            load(1, k).wait()

    def branch_tile(j, carry):
        at = pl.ds(pl.multiple_of(j * TILE, TILE), TILE)
        branch = dot(attended_ref[...], out_all[:, at])
        middle_ref[:, at] = tokens_ref[:, at].astype(F32) + branch
        return carry

    lax.fori_loop(0, width // TILE, branch_tile, 0)
    unit, _ = normalize(middle_ref[...])
    normed_two_ref[...] = (unit * gains_all_ref[1:2, :]).astype(BF)

    for step in range(half // 2 + 1, half + 1):
        finish_low(step)
    chip_copies[0].wait_recv()
    core_copies[1].start()
    for copy in core_copies:
        copy.wait_recv()
    for copy in chip_copies + core_copies:
        copy.wait_send()
    for step in range(1, half + 1):
        for part, direction in hops(step):
            low_copy(direction, step, part).wait_send()
    for i in range(2):
        for step in range(1, half + 1):
            for part, direction in hops(step):
                ring_copy(i, direction, step, part).wait_send()
            for k in places(step):
                chip_copy(i, k).wait_send()
                for which in range(2):
                    core_copy(i, k, which).wait_send()
    for k in range(1, count):
        gain_copy(k).wait_send()
        for which in range(2):
            across(k, which).wait_send()


def front(count, tokens, gains, cotangent, tables, own, gate_own, up_own):
    rows, width = tokens.shape
    own_rows, wide_k = own[1].shape
    qkv_width = width + 2 * wide_k
    ff_own = gate_own.shape[1] // count
    half = count // 2
    here = pl.BlockSpec(memory_space=pl.ANY)
    inside = pl.BlockSpec(memory_space=pltpu.VMEM)
    kind = jax.ShapeDtypeStruct
    dma = pltpu.SemaphoreType.DMA
    return pl.pallas_call(
        functools.partial(front_kernel, count),
        in_specs=[inside] * 6 + [here] * 6,
        out_specs=[here] * 4 + [inside] * 7,
        out_shape=[
            kind((count * own_rows, qkv_width), BF),
            kind((count * own_rows, width), BF),
            kind((count, 4, own_rows // 4, 2 * ff_own), BF),
            kind((count * rows, width), BF),
            kind((gains.shape[0], width), F32),
            kind((rows, width), BF),
            kind((rows, wide_k), BF),
            kind((rows, wide_k), BF),
            kind((rows, width), BF),
            kind((rows, width), F32),
            kind((rows, width), BF),
        ],
        scratch_shapes=[
            pltpu.VMEM((rows, width), BF),
            pltpu.VMEM((own_rows // 4, 2 * ff_own), BF),
            pltpu.VMEM((count * own_rows, qkv_width), BF),
            pltpu.VMEM((count * own_rows, width), BF),
            pltpu.VMEM((rows, width), BF),
            pltpu.VMEM((rows, qkv_width), F32),
            dma((10,)),
            dma((2, count)),
            dma((count - 1,)),
            dma((count - 1,)),
            dma((2, 2, half, 2)),
            dma((2, 2, half, 2)),
            dma((2, 2, count)),
            dma((2, 2, count)),
            dma((2, count)),
            dma((2, count)),
            dma((2, count - 1)),
            dma((2, count - 1)),
            dma((3,)),
            dma((3,)),
            dma((2, half, 2)),
            dma((2, half, 2)),
        ],
        compiler_params=pltpu.CompilerParams(
            collective_id=1, has_side_effects=True, vmem_limit_bytes=VMEM_BYTES
        ),
        cost_estimate=pl.CostEstimate(
            flops=2 * rows * width * (qkv_width + width) + 2 * 10**9,
            bytes_accessed=60 * 10**6,
            transcendentals=2 * 10**6,
        ),
    )(tokens, gains, cotangent, *tables, *own, gate_own, up_own)


def feed_forward_kernel(
    count,
    normed_ref,
    low_ref,
    both_ref,
    down_ref,
    grad_ref,
    branch_ref,
    sums_ref,
    down_grad_ref,
    normed,
    low,
    hidden,
    grads,
    w_both,
    w_down,
    turned,
    staged,
    from_core,
    core_sums,
    from_chip,
    group_sums,
    result_tile,
    outgoing,
    incoming,
    local_sem,
    gather_send,
    gather_recv,
    scatter_send,
    scatter_recv,
    credit,
    core_send,
    core_recv,
    chip_send,
    chip_recv,
    group_credit,
    sums_sem,
    result_sem,
    down_send,
    down_recv,
):
    half = count // 2
    rows = normed_ref.shape[0]
    cut = rows // 2
    width = normed_ref.shape[1]
    ff = down_ref.shape[0]
    place = ring_place(count, lax.axis_index("shard"))
    neighbours = (ring_shard(count, place + 1), ring_shard(count, place - 1))
    rep = lax.axis_index("rep")
    core, chip = rep % 2, rep // 2
    other_core, other_chip = {"rep": core_partner(rep)}, {"rep": chip_partner(rep)}
    everywhere = pl.ds(0, rows)
    halves = (pl.ds(0, cut), pl.ds(cut, cut))

    def at(slot, part=None):
        start, size = (0, rows) if part is None else (part * cut, cut)
        return pl.ds(pl.multiple_of(slot * rows + start, cut), size)

    def tile(j):
        return pl.ds(pl.multiple_of(j * TILE, TILE), TILE)

    def remote(src, dst, send, recv, direction):
        return remote_copy(src, dst, send, recv, {"shard": neighbours[direction]})

    loads = [
        pltpu.make_async_copy(normed_ref, normed.at[at(0)], local_sem.at[0]),
        pltpu.make_async_copy(low_ref, low, local_sem.at[1]),
        pltpu.make_async_copy(both_ref, w_both, local_sem.at[2]),
        pltpu.make_async_copy(down_ref, w_down, local_sem.at[3]),
    ]
    for load in loads:
        load.start()

    for chain in range(2):
        for direction in range(2):
            blank = halves[1 - direction]
            incoming[chain, direction, 0, blank] = jnp.zeros((cut, width), BF)

    greet([{"shard": neighbour} for neighbour in neighbours] + [other_core, other_chip])

    def gathered(part, direction, step):
        base = 0 if direction == 0 else half
        if isinstance(step, int) and step == 1:
            source = 0
        else:
            source = jnp.where(step == 1, 0, base + step - 1)
        return remote(
            normed.at[at(source, part)],
            normed.at[at(base + step, part)],
            gather_send.at[part, direction, step - 1],
            gather_recv.at[part, direction, step - 1],
            direction,
        )

    def gathered_last(direction):
        source = half - 1 if direction == 0 else 2 * half - 1
        return remote(
            normed.at[at(source, direction)],
            normed.at[at(half, direction)],
            gather_send.at[0, direction, half - 1],
            gather_recv.at[0, direction, half - 1],
            direction,
        )

    def products(slot):
        mine = at(slot)

        def body(j, carry):
            gate_at, up_at = tile(j), tile(j + ff // TILE)
            own = normed[mine, :]
            gate = dot(own, w_both[:, gate_at])
            up = dot(own, w_both[:, up_at])
            grad_hidden = contract_last(low[mine, :], w_down[gate_at, :])
            sigmoid = jax.nn.sigmoid(gate)
            silu = gate * sigmoid
            hidden[mine, gate_at] = (silu * up).astype(BF)
            grads[mine, gate_at] = (
                grad_hidden * up * sigmoid * (1.0 + gate * (1.0 - sigmoid))
            ).astype(BF)
            grads[mine, up_at] = (grad_hidden * silu).astype(BF)
            return carry

        lax.fori_loop(0, ff // TILE, body, 0)

    both_ways = ((0, 0), (0, 1), (1, 0), (1, 1))
    loads[0].wait()
    for part, direction in both_ways:
        gathered(part, direction, 1).start()
    for load in loads[1:]:
        load.wait()
    products(0)

    def gather_step(step, carry):
        for part, direction in both_ways:
            gathered(part, direction, step).wait_recv()

            @pl.when(step < half - 1)
            def _():
                gathered(part, direction, step + 1).start()

            if part == direction:

                @pl.when(step == half - 1)
                def _():
                    gathered_last(direction).start()

        products(step)

        @pl.when(step < half - 1)
        def _():
            products(half + step)

        return carry

    lax.fori_loop(1, half, gather_step, 0)
    for direction in range(2):
        gathered_last(direction).wait_recv()
    products(half)

    def term(chain, rows_at, j):
        if chain == 0:
            return contract_last(grads[rows_at, :], w_both[tile(j), :])
        return dot(hidden[rows_at, :], w_down[:, tile(j)])

    def scattered(chain, direction, step):
        if isinstance(step, int) and step == 0:
            own, there = halves[direction], 0
        else:
            own, there = everywhere, step % 2
        return remote(
            outgoing.at[chain, direction, own],
            incoming.at[chain, direction, there, own],
            scatter_send.at[chain, direction, step],
            scatter_recv.at[chain, direction, step],
            direction,
        )

    units = (width + ff) // TILE
    per_step = -(-(units + 3) // (half - 1)) + 1
    quarter = TILE // 4

    def core_copy(unit):
        spot = unit % 2
        return remote_copy(
            staged.at[spot, :, 1 - core],
            from_core.at[spot],
            core_send.at[spot],
            core_recv.at[spot],
            other_core,
        )

    def chip_copy(unit):
        spot = unit % 3
        return remote_copy(
            core_sums.at[spot, 1 - chip],
            from_chip.at[spot],
            chip_send.at[spot],
            chip_recv.at[spot],
            other_chip,
        )

    down_units = ff // TILE

    def sums_copy(unit, down):
        spot = unit % 2
        target = down_grad_ref.at[unit, rep] if down else sums_ref.at[unit - down_units]
        return pltpu.make_async_copy(group_sums.at[spot], target, sums_sem.at[spot])

    def for_sums(unit, act):
        @pl.when(unit < down_units)
        def _():
            act(sums_copy(unit, True))

        @pl.when(unit >= down_units)
        def _():
            act(sums_copy(unit, False))

    def down_copy(index):
        at = down_grad_ref.at[:, chip_partner(rep) if index == 2 else rep]
        return remote_copy(
            at,
            at,
            down_send.at[index],
            down_recv.at[index],
            other_chip if index == 0 else other_core,
        )

    def give_credit(which, device):
        pl.semaphore_signal(
            group_credit.at[which], inc=1, device_id=device, device_id_type=pl.DeviceIdType.MESH
        )

    def weight_unit(unit):
        spot = unit % 2

        def from_arrays(left, right, block):
            def turn(c, carry):
                turned[:, at(c)] = left[at(c), tile(block)].T
                return carry

            lax.fori_loop(0, count, turn, 0)

            def body(j, carry):
                value = dot(turned[...], right[:, tile(j)]).astype(BF)
                staged[spot, :, :, :, tile(j)] = value.reshape(2, 2, quarter, TILE)
                return carry

            lax.fori_loop(0, width // TILE, body, 0)

        @pl.when(unit < down_units)
        def _():
            from_arrays(hidden, low, unit)

        @pl.when(unit >= down_units)
        def _():
            from_arrays(normed, grads, unit - down_units)

        @pl.when(unit >= 2)
        def _():
            pl.semaphore_wait(group_credit.at[0], 1)

        core_copy(unit).start()

    def sum_over_cores(unit):
        spot, place_of = unit % 2, unit % 3
        core_copy(unit).wait()
        for y in range(2):
            total = staged[spot, y, core].astype(F32) + from_core[spot, y].astype(F32)
            core_sums[place_of, y] = total.astype(BF)

        @pl.when(unit < units - 2)
        def _():
            give_credit(0, other_core)

        @pl.when(unit >= 3)
        def _():
            pl.semaphore_wait(group_credit.at[1], 1)

        chip_copy(unit).start()

    def sum_over_chips(unit):
        spot, place_of = unit % 2, unit % 3
        chip_copy(unit).wait()

        @pl.when(unit >= 2)
        def _():
            for_sums(unit - 2, lambda copy: copy.wait())

        total = core_sums[place_of, chip].astype(F32) + from_chip[place_of].astype(F32)
        group_sums[spot] = total.astype(BF)

        @pl.when(unit < units - 3)
        def _():
            give_credit(1, other_chip)

        for_sums(unit, lambda copy: copy.start())

    def weight_step(turn):
        @pl.when(turn < units)
        def _():
            weight_unit(turn)

        @pl.when((turn >= 1) & (turn <= units))
        def _():
            sum_over_cores(turn - 1)

        @pl.when(turn == units)
        def _():
            for index in range(2):
                down_copy(index).start()

        @pl.when(turn >= 3)
        def _():
            sum_over_chips(turn - 3)

    for chain in range(2):

        def first(j, carry):
            value = term(chain, at(half), j).astype(BF)
            outgoing[chain, 0, halves[0], tile(j)] = value[:cut]
            outgoing[chain, 1, halves[1], tile(j)] = value[cut:]
            return carry

        lax.fori_loop(0, width // TILE, first, 0)
        for direction in range(2):
            scattered(chain, direction, 0).start()

    products(2 * half - 1)

    def scatter_step(step, carry):
        k = half - step
        for chain in range(2):
            for direction in range(2):
                slot = half + k if direction == 0 else k

                @pl.when(step == 1)
                def _():
                    scattered(chain, direction, 0).wait()

                @pl.when(step > 1)
                def _():
                    scattered(chain, direction, step - 1).wait()
                    pl.semaphore_wait(credit.at[chain, direction], 1)

                def add(j, carry):
                    value = term(chain, at(slot), j)
                    value += incoming[chain, direction, (step - 1) % 2, :, tile(j)].astype(F32)
                    outgoing[chain, direction, :, tile(j)] = value.astype(BF)
                    return carry

                lax.fori_loop(0, width // TILE, add, 0)
                scattered(chain, direction, step).start()

                @pl.when(step < half - 1)
                def _():
                    pl.semaphore_signal(
                        credit.at[chain, direction],
                        inc=1,
                        device_id={"shard": neighbours[1 - direction]},
                        device_id_type=pl.DeviceIdType.MESH,
                    )

        lax.fori_loop(
            (step - 1) * per_step,
            jnp.minimum(step * per_step, units + 3),
            lambda turn, c: (weight_step(turn), c)[1],
            0,
        )
        return carry

    lax.fori_loop(1, half, scatter_step, 0)

    for chain, result in enumerate((grad_ref, branch_ref)):
        for direction in range(2):
            scattered(chain, direction, half - 1).wait()

        def result_copy(j):
            return pltpu.make_async_copy(
                result_tile.at[j % 2], result.at[:, tile(j)], result_sem.at[j % 2]
            )

        def last(j, carry):
            @pl.when(j >= 2)
            def _():
                result_copy(j - 2).wait()

            value = term(chain, at(0), j)
            for direction in range(2):
                value += incoming[chain, direction, (half - 1) % 2, :, tile(j)].astype(F32)
            result_tile[j % 2] = value
            result_copy(j).start()
            return carry

        lax.fori_loop(0, width // TILE, last, 0)
        for j in (width // TILE - 2, width // TILE - 1):
            result_copy(j).wait()

    down_copy(0).wait_recv()
    down_copy(2).start()
    for unit in (units - 2, units - 1):
        sums_copy(unit, False).wait()
    down_copy(0).wait_send()
    for index in (1, 2):
        down_copy(index).wait()
    for part, direction in both_ways:
        lax.fori_loop(
            1,
            half,
            lambda step, c: (gathered(part, direction, step).wait_send(), c)[1],
            0,
        )
    for direction in range(2):
        gathered_last(direction).wait_send()


def feed_forward_bytes(count, rows, width, ff):
    tokens = count * rows
    return 2 * (
        tokens * (2 * width + 3 * ff)
        + 3 * width * ff
        + TILE * tokens
        + 6 * TILE * width
        + 12 * rows * width
        + 4 * TILE * rows
    )


def feed_forward(count, normed, low, w_both, w_down):
    rows, width = normed.shape
    ff = w_down.shape[0]
    tokens = count * rows
    half = count // 2
    quarter = TILE // 4
    here = pl.BlockSpec(memory_space=pl.ANY)
    dma = pltpu.SemaphoreType.DMA
    return pl.pallas_call(
        functools.partial(feed_forward_kernel, count),
        in_specs=[here] * 4,
        out_specs=[here] * 4,
        out_shape=[
            jax.ShapeDtypeStruct((rows, width), F32),
            jax.ShapeDtypeStruct((rows, width), F32),
            jax.ShapeDtypeStruct((width // TILE, quarter, width), BF),
            jax.ShapeDtypeStruct((ff // TILE, 4, quarter, width), BF),
        ],
        scratch_shapes=[
            pltpu.VMEM((tokens, width), BF),
            pltpu.VMEM((tokens, width), BF),
            pltpu.VMEM((tokens, ff), BF),
            pltpu.VMEM((tokens, 2 * ff), BF),
            pltpu.VMEM((width, 2 * ff), BF),
            pltpu.VMEM((ff, width), BF),
            pltpu.VMEM((TILE, tokens), BF),
            pltpu.VMEM((2, 2, 2, quarter, width), BF),
            pltpu.VMEM((2, 2, quarter, width), BF),
            pltpu.VMEM((3, 2, quarter, width), BF),
            pltpu.VMEM((3, quarter, width), BF),
            pltpu.VMEM((2, quarter, width), BF),
            pltpu.VMEM((2, rows, TILE), F32),
            pltpu.VMEM((2, 2, rows, width), BF),
            pltpu.VMEM((2, 2, 2, rows, width), BF),
            dma((4,)),
            dma((2, 2, half)),
            dma((2, 2, half)),
            dma((2, 2, half)),
            dma((2, 2, half)),
            pltpu.SemaphoreType.REGULAR((2, 2)),
            dma((2,)),
            dma((2,)),
            dma((3,)),
            dma((3,)),
            pltpu.SemaphoreType.REGULAR((2,)),
            dma((2,)),
            dma((2,)),
            dma((3,)),
            dma((3,)),
        ],
        compiler_params=pltpu.CompilerParams(
            collective_id=0, has_side_effects=True, vmem_limit_bytes=VMEM_BYTES
        ),
        cost_estimate=pl.CostEstimate(
            flops=18 * tokens * width * ff, bytes_accessed=50 * 10**6, transcendentals=tokens * ff
        ),
    )(normed, low, w_both, w_down)


def middle_back_kernel(
    middle_ref, branch_ref, grad_ref, cotangent_ref, gains_ref, result_ref, out_ref, low_ref, term_ref
):
    middle = middle_ref[...]
    result_ref[...] = middle + branch_ref[...]
    unit, scale_row = normalize(middle)
    grad = grad_ref[...]
    total = cotangent_ref[...] + norm_back(grad * gains_ref[1:2, :], unit, scale_row)
    out_ref[...] = total
    low_ref[...] = total.astype(BF)
    term = jnp.sum(grad * unit, 0, keepdims=True)

    @pl.when(pl.program_id(0) == 0)
    def _():
        term_ref[...] = term

    @pl.when(pl.program_id(0) > 0)
    def _():
        term_ref[...] += term


def middle_back(middle, branch, grad, cotangent, gains):
    rows, width = middle.shape
    block = pl.BlockSpec((rows // 4, width), lambda i: (i, 0))
    fixed = pl.BlockSpec((1, width), lambda i: (0, 0))
    kind = jax.ShapeDtypeStruct
    full = kind((rows, width), F32)
    return pl.pallas_call(
        middle_back_kernel,
        grid=(4,),
        in_specs=[block] * 4 + [pl.BlockSpec(gains.shape, lambda i: (0, 0))],
        out_specs=[block] * 3 + [fixed],
        out_shape=[full, full, kind((rows, width), BF), kind((1, width), F32)],
        compiler_params=pltpu.CompilerParams(vmem_limit_bytes=VMEM_BYTES),
    )(middle, branch, grad, cotangent, gains)


def back_kernel(
    count,
    sums_ref,
    mid_low_ref,
    gain_two_ref,
    attended_ref,
    query_ref,
    key_ref,
    value_ref,
    tokens_ref,
    gains_ref,
    cos_ref,
    sin_ref,
    segr_ref,
    qkv_all_ref,
    out_all_ref,
    gate_grad_ref,
    up_grad_ref,
    out_grad_ref,
    qkv_grad_ref,
    grad_input_ref,
    gain_grad_ref,
    both_own,
    turned,
    grad_attended,
    grads,
    weight_tile,
    terms_first,
    terms_second,
    from_core_out,
    from_core_qkv,
    from_chip_out,
    out_sums,
    out_summed,
    outgoing_out,
    outgoing_qkv,
    incoming_out,
    incoming_qkv,
    summed,
    from_chip,
    finished,
    gain_terms,
    gains_in,
    gain_parts,
    gain_swaps,
    own_sem,
    tile_sem,
    across_send,
    across_recv,
    group_send,
    group_recv,
    core_send,
    core_recv,
    ring_send,
    ring_recv,
    chip_send,
    chip_recv,
    last_send,
    last_recv,
    pair_send,
    pair_recv,
    gain_send,
    gain_recv,
    swap_send,
    swap_recv,
):
    half = count // 2
    me, rep = lax.axis_index("shard"), lax.axis_index("rep")
    core, chip = rep % 2, rep // 2
    place = ring_place(count, me)
    others = [ring_shard(count, place + k) for k in range(1, count)]
    near = ({"shard": ring_shard(count, place + 1)}, {"shard": ring_shard(count, place - 1)})
    other_core, other_chip = {"rep": core_partner(rep)}, {"rep": chip_partner(rep)}
    rows, width = tokens_ref.shape
    own_rows = width // count
    strip, quarter = own_rows // 2, own_rows // 4
    ff_own = gate_grad_ref.shape[2] // count
    qkv_half = grads.shape[1] // 2
    wides = (width, qkv_half, qkv_half)
    terms = (terms_first, terms_second, terms_first)
    pieces = (quarter, strip, strip)
    from_core = (from_core_out, from_core_qkv.at[0], from_core_qkv.at[1])
    outgoing = (outgoing_out, outgoing_qkv.at[0], outgoing_qkv.at[1])
    incoming = (incoming_out, incoming_qkv.at[0], incoming_qkv.at[1])
    result_refs = (out_grad_ref, qkv_grad_ref, qkv_grad_ref)
    result_starts = (0, 0, qkv_half)
    chains, in_turn = range(3), (1, 2, 0)

    def tile(j, size=TILE):
        return pl.ds(pl.multiple_of(j * size, size), size)

    gate_up = (gate_grad_ref, up_grad_ref)

    def own_columns(shard):
        return pl.ds(pl.multiple_of(shard * ff_own, 128), ff_own)

    def across(k, which):
        there = others[k - 1]
        return remote_copy(
            sums_ref.at[there, :, pl.ds(which * ff_own, ff_own)],
            gate_up[which].at[rep, :, own_columns(me)],
            across_send.at[which, k - 1],
            across_recv.at[which, k - 1],
            {"shard": there},
        )

    own_load = pltpu.make_async_copy(sums_ref.at[me], both_own, own_sem.at[0])
    keep = [
        pltpu.make_async_copy(
            both_own.at[:, pl.ds(which * ff_own, ff_own)],
            gate_up[which].at[rep, :, own_columns(me)],
            own_sem.at[which],
        )
        for which in range(2)
    ]

    def group_copy(which, index):
        member = chip_partner(rep) if index == 2 else rep
        dst = src = gate_up[which].at[member]
        return remote_copy(
            src,
            dst,
            group_send.at[which, index],
            group_recv.at[which, index],
            other_chip if index == 0 else other_core,
        )

    def shard_of(k):
        return ring_shard(count, place + k)

    def core_copy(i, k):
        slot = k + half - 1
        return remote_copy(
            terms[i].at[shard_of(k), 1 - core, :, pl.ds(0, wides[i])],
            from_core[i].at[slot],
            core_send.at[i, slot],
            core_recv.at[i, slot],
            other_core,
        )

    def all_terms(i):
        def body(j, carry):
            if i == 0:
                right = mid_low_ref[:, tile(j)]
            else:
                right = grads[:, tile(j + result_starts[i] // TILE)]
            value = dot(turned[...], right).astype(BF)
            terms[i][:, :, :, tile(j)] = value.reshape(count, 2, strip, TILE)
            return carry

        lax.fori_loop(0, wides[i] // TILE, body, 0)
        for k in [half] + [s * j for j in range(half - 1, 0, -1) for s in (1, -1)] + [0]:
            core_copy(i, k).start()

    def pair_copy(k):
        slot = k + half - 1
        return remote_copy(
            out_sums.at[slot, 1 - chip],
            from_chip_out.at[slot],
            pair_send.at[slot],
            pair_recv.at[slot],
            other_chip,
        )

    def sum_pair(k):
        core_copy(0, k).wait_recv()

        def body(j, carry):
            at = tile(j, WIDE_TILE)
            value = terms[0][shard_of(k), core, :, at].astype(F32)
            value += from_core[0][k + half - 1, :, at].astype(F32)
            out_sums[k + half - 1, :, :, at] = value.astype(BF).reshape(2, quarter, WIDE_TILE)
            return carry

        lax.fori_loop(0, wides[0] // WIDE_TILE, body, 0)
        pair_copy(k).start()

    def piece_sum(i, k, extra, store):
        slot = k + half - 1
        if i == 0:
            pair_copy(k).wait_recv()
            received = from_chip_out
        else:
            core_copy(i, k).wait_recv()
            received = from_core[i]

        def body(j, carry):
            at = tile(j, WIDE_TILE)
            own = out_sums[slot, chip, :, at] if i == 0 else terms[i][shard_of(k), core, :, at]
            value = own.astype(F32)
            value += received[slot, :, at].astype(F32)
            for direction, step in extra:
                value += incoming[i][direction, step, :, at].astype(F32)
            store(at, value.astype(BF))
            return carry

        lax.fori_loop(0, wides[i] // WIDE_TILE, body, 0)

    def ring_copy(i, direction, step):
        cut = pieces[i] // 2
        at = pl.ds(direction * cut, cut) if step == 0 else pl.ds(0, pieces[i])
        return remote_copy(
            outgoing[i].at[direction, at],
            incoming[i].at[direction, step, at],
            ring_send.at[i, direction, step],
            ring_recv.at[i, direction, step],
            near[direction],
        )

    def ring_step(i, step):
        if step == 0:

            cut = pieces[i] // 2

            def store(at, value):
                outgoing[i][0, pl.ds(0, cut), at] = value[:cut]
                outgoing[i][1, pl.ds(cut, cut), at] = value[cut:]

            piece_sum(i, half, (), store)
            for direction in range(2):
                ring_copy(i, direction, 0).start()
            return
        for direction in range(2):
            ring_copy(i, direction, step - 1).wait()

            def store(at, value):
                outgoing[i][direction, :, at] = value

            k = half - step if direction == 0 else step - half
            piece_sum(i, k, ((direction, step - 1),), store)
            ring_copy(i, direction, step).start()

    def chip_copy(i):
        return remote_copy(
            summed.at[i - 1],
            from_chip.at[i - 1],
            chip_send.at[i],
            chip_recv.at[i],
            other_chip,
        )

    def ring_end(i):
        for direction in range(2):
            ring_copy(i, direction, half - 1).wait()

        def store(at, value):
            if i == 0:
                out_summed[:, at] = value
            else:
                summed[i - 1, :, at] = value

        piece_sum(i, 0, tuple((d, half - 1) for d in range(2)), store)
        if i > 0:
            chip_copy(i).start()
        else:
            for copy in out_copies()[:3]:
                copy.start()

    own_strip = pl.ds(pl.multiple_of(core * strip, strip), strip)

    def out_copies():
        def at(which_chip):
            return out_grad_ref.at[
                pl.ds(pl.multiple_of(core * strip + which_chip * quarter, quarter), quarter)
            ]

        done = out_summed
        return (
            pltpu.make_async_copy(done, at(chip), own_sem.at[3]),
            remote_copy(done, at(chip), chip_send.at[0], chip_recv.at[0], other_chip),
            remote_copy(done, at(chip), last_send.at[0], last_recv.at[0], other_core),
            remote_copy(at(1 - chip), at(1 - chip), last_send.at[3], last_recv.at[3], other_core),
        )

    def last_copies(i):
        src = finished.at[i - 1]
        dst = result_refs[i].at[own_strip, pl.ds(result_starts[i], wides[i])]
        return (
            pltpu.make_async_copy(src, dst, own_sem.at[3 + i]),
            remote_copy(src, dst, last_send.at[i], last_recv.at[i], other_core),
        )

    def group_end(i):
        chip_copy(i).wait()
        total = summed[i - 1].astype(F32) + from_chip[i - 1].astype(F32)
        finished[i - 1] = total.astype(BF)
        for copy in last_copies(i):
            copy.start()

    def gain_copy(k):
        return remote_copy(
            gain_terms.at[:, tile(others[k - 1], own_rows)],
            gains_in.at[k],
            gain_send.at[k - 1],
            gain_recv.at[k - 1],
            {"shard": others[k - 1]},
        )

    def gain_swap(index):
        return remote_copy(
            gain_parts.at[index],
            gain_swaps.at[index],
            swap_send.at[index],
            swap_recv.at[index],
            (other_core, other_chip)[index],
        )

    def weight_load(ref, j, wide):
        return pltpu.make_async_copy(
            ref.at[tile(j, LOAD_TILE)], weight_tile.at[j % 2, :, pl.ds(0, wide)], tile_sem.at[j % 2]
        )

    def times_transposed(left, ref, wide, store):
        blocks = width // LOAD_TILE

        def body(j, carry):
            @pl.when(j + 1 < blocks)
            def _():
                weight_load(ref, j + 1, wide).start()

            weight_load(ref, j, wide).wait()
            store(tile(j, LOAD_TILE), contract_last(left[...], weight_tile[j % 2, :, pl.ds(0, wide)]))
            return carry

        lax.fori_loop(0, blocks, body, 0)

    def turn(array):
        def body(j, carry):
            turned[tile(j), :] = array[:, tile(j)].T
            return carry

        lax.fori_loop(0, width // TILE, body, 0)

    cosine, sine = cos_ref[...], -sin_ref[...]
    wide, thin = 2 * GROUP * HEAD_SIZE, 2 * HEAD_SIZE
    key_at, value_at = width, width + key_ref.shape[1]

    def heads_pair(pair):
        allowed = allowed_rows(segr_ref[...])
        wide_at, thin_at = pl.ds(pair * wide, wide), pl.ds(pair * thin, thin)
        query, grad = query_ref[:, wide_at], grad_attended[:, wide_at]
        key, value = key_ref[:, thin_at], value_ref[:, thin_at]
        heads, keys, values = [], [], []
        for j in range(2):
            cols = slice(j * HEAD_SIZE, (j + 1) * HEAD_SIZE)
            query_rows, grad_rows = stack_heads(query, j), stack_heads(grad, j)
            probs = softmax_rows(query_rows, key[:, cols], allowed)
            grad_probs = contract_last(grad_rows, value[:, cols])
            grad_scores = (
                probs * (grad_probs - jnp.sum(probs * grad_probs, -1, keepdims=True))
            ).astype(BF)
            heads += unstack_heads(dot(grad_scores, key[:, cols]) * HEAD_SIZE ** (-0.5))
            keys.append(contract_first(grad_scores, query_rows) * HEAD_SIZE ** (-0.5))
            values.append(contract_first(probs.astype(BF), grad_rows))
        grads[:, wide_at] = rotate(jnp.concatenate(heads, 1), cosine, sine).astype(BF)
        grads[:, pl.ds(key_at + pair * thin, thin)] = rotate(
            jnp.concatenate(keys, 1), cosine, sine
        ).astype(BF)
        grads[:, pl.ds(value_at + pair * thin, thin)] = jnp.concatenate(values, 1).astype(BF)

    load_attended = pltpu.make_async_copy(attended_ref, grad_attended, own_sem.at[3])
    load_attended.start()
    own_load.start()
    for i in chains:
        for direction in range(2):
            cut = pieces[i] // 2
            blank = pl.ds((1 - direction) * cut, cut)
            incoming[i][direction, 0, blank] = jnp.zeros((cut, wides[i]), BF)

    own_load.wait()
    for copy in keep:
        copy.start()
    greet([{"shard": shard} for shard in others] + [other_core, other_chip])

    for k in range(1, count):
        for which in range(2):
            across(k, which).start()
    weight_load(out_all_ref, 0, width).start()
    load_attended.wait()
    turn(grad_attended)
    all_terms(0)
    for k in [half] + [s * j for j in range(half - 1, 0, -1) for s in (1, -1)] + [0]:
        sum_pair(k)

    def store_attended(at, value):
        grad_attended[:, at] = value.astype(BF)

    times_transposed(mid_low_ref, out_all_ref, width, store_attended)
    weight_load(qkv_all_ref, 0, grads.shape[1]).start()
    ring_step(0, 0)
    for pair in range(KEY_VALUE_HEADS // 2):
        heads_pair(pair)

    unit, scale_row = normalize(tokens_ref[...].astype(F32))
    gain = gains_ref[0:1, :]
    grad_attended[...] = (unit * gain).astype(BF)
    turn(grad_attended)
    all_terms(1)
    ring_step(1, 0)
    for copy in keep:
        copy.wait()
    for k in range(1, count):
        for which in range(2):
            across(k, which).wait_recv()
    for which in range(2):
        for index in range(2):
            group_copy(which, index).start()
    for k in range(-(half - 1), half + 1):
        core_copy(0, k).wait_send()
    all_terms(2)
    ring_step(2, 0)
    for i in in_turn:
        ring_step(i, 1)

    def store_input(at, value):
        grad_input_ref[:, at] = value

    times_transposed(grads, qkv_all_ref, grads.shape[1], store_input)
    if half > 2:
        for i in in_turn:
            ring_step(i, 2)
    unit, scale_row = normalize(tokens_ref[...].astype(F32))
    grad_normed = grad_input_ref[...]
    gain_terms[...] = jnp.zeros_like(gain_terms)
    gain_terms[0:1, :] = jnp.sum(grad_normed * unit, 0, keepdims=True)
    gain_terms[1:2, :] = gain_two_ref[...]
    for k in range(1, count):
        gain_copy(k).start()
    grad_input_ref[...] = norm_back(grad_normed * gain, unit, scale_row)
    for step in range(3, half):
        for i in in_turn:
            ring_step(i, step)
    for which in range(2):
        group_copy(which, 0).wait_recv()
        group_copy(which, 2).start()
    total = gain_terms[:, tile(me, own_rows)]
    for k in range(1, count):
        gain_copy(k).wait_recv()
        total += gains_in[k]
    gain_parts[0] = total
    gain_swap(0).start()
    for i in in_turn:
        ring_end(i)
    gain_swap(0).wait()
    gain_parts[1] = gain_parts[0] + gain_swaps[0]
    gain_swap(1).start()
    for i in (1, 2):
        group_end(i)
    out_copies()[1].wait_recv()
    out_copies()[3].start()
    gain_swap(1).wait()
    gain_grad_ref[...] = gain_parts[1] + gain_swaps[1]

    for k in range(-(half - 1), half + 1):
        pair_copy(k).wait_send()
    kept, over, passed, again = out_copies()
    kept.wait()
    over.wait_send()
    passed.wait()
    again.wait()
    for i in (1, 2):
        kept, passed = last_copies(i)
        kept.wait()
        passed.wait()
    for i in (1, 2):
        for k in range(-(half - 1), half + 1):
            core_copy(i, k).wait_send()
    for which in range(2):
        for index in range(3):
            if index > 0:
                group_copy(which, index).wait_recv()
            group_copy(which, index).wait_send()
    for k in range(1, count):
        gain_copy(k).wait_send()
        for which in range(2):
            across(k, which).wait_send()


def back(
    count,
    sums,
    mid_low,
    gain_two_term,
    attended,
    query,
    key,
    value,
    tokens,
    gains,
    tables,
    qkv_all,
    out_all,
):
    rows, width = tokens.shape
    qkv_width = qkv_all.shape[1]
    own_rows = width // count
    strip, quarter = own_rows // 2, own_rows // 4
    ff_own = sums.shape[2] // 2
    half = count // 2
    here = pl.BlockSpec(memory_space=pl.ANY)
    inside = pl.BlockSpec(memory_space=pltpu.VMEM)
    kind = jax.ShapeDtypeStruct
    dma = pltpu.SemaphoreType.DMA
    vmem = pltpu.VMEM
    return pl.pallas_call(
        functools.partial(back_kernel, count),
        in_specs=[here] + [inside] * 2 + [here] + [inside] * 8 + [here] * 2,
        out_specs=[here] * 4 + [inside] * 2,
        out_shape=[
            kind((4, quarter, count * ff_own), BF),
            kind((4, quarter, count * ff_own), BF),
            kind((own_rows, width), BF),
            kind((own_rows, qkv_width), BF),
            kind((rows, width), F32),
            kind((8, own_rows), F32),
        ],
        scratch_shapes=[
            vmem((quarter, 2 * ff_own), BF),
            vmem((width, rows), BF),
            vmem((rows, width), BF),
            vmem((rows, qkv_width), BF),
            vmem((2, LOAD_TILE, qkv_width), BF),
            vmem((count, 2, strip, width), BF),
            vmem((count, 2, strip, qkv_width // 2), BF),
            vmem((count, strip, width), BF),
            vmem((2, count, strip, qkv_width // 2), BF),
            vmem((count, quarter, width), BF),
            vmem((count, 2, quarter, width), BF),
            vmem((quarter, width), BF),
            vmem((2, quarter, width), BF),
            vmem((2, 2, strip, qkv_width // 2), BF),
            vmem((2, half, quarter, width), BF),
            vmem((2, 2, half, strip, qkv_width // 2), BF),
            vmem((2, strip, qkv_width // 2), BF),
            vmem((2, strip, qkv_width // 2), BF),
            vmem((2, strip, qkv_width // 2), BF),
            vmem((8, width), F32),
            vmem((count, 8, own_rows), F32),
            vmem((2, 8, own_rows), F32),
            vmem((2, 8, own_rows), F32),
            dma((6,)),
            dma((2,)),
            dma((2, count - 1)),
            dma((2, count - 1)),
            dma((2, 3)),
            dma((2, 3)),
            dma((3, count)),
            dma((3, count)),
            dma((3, 2, half)),
            dma((3, 2, half)),
            dma((3,)),
            dma((3,)),
            dma((4,)),
            dma((4,)),
            dma((count,)),
            dma((count,)),
            dma((count - 1,)),
            dma((count - 1,)),
            dma((2,)),
            dma((2,)),
        ],
        compiler_params=pltpu.CompilerParams(
            collective_id=2, has_side_effects=True, vmem_limit_bytes=VMEM_BYTES
        ),
        cost_estimate=pl.CostEstimate(
            flops=4 * rows * width * (qkv_width + width) + 4 * 10**9,
            bytes_accessed=60 * 10**6,
            transcendentals=2 * 10**6,
        ),
    )(
        sums,
        mid_low,
        gain_two_term,
        attended,
        query,
        key,
        value,
        tokens,
        gains,
        *tables,
        qkv_all,
        out_all,
    )


def results_kernel(*refs):
    gate, up, down, out, qkv, middle, change = refs[:7]
    gate_to, up_to, down_to, out_to, query_to, key_to, value_to, input_to = refs[7:]
    for source, result in ((gate, gate_to), (up, up_to), (down, down_to), (out, out_to)):
        result[...] = source[...].astype(F32)
    start = 0
    for result in (query_to, key_to, value_to):
        result[...] = qkv[:, start : start + result.shape[1]].astype(F32)
        start += result.shape[1]
    input_to[...] = middle[...] + change[...]


def results(gate, up, down, out, qkv, wide_k, grad_middle, change):
    steps = 8
    kind = jax.ShapeDtypeStruct
    sources = (gate, up, down, out, qkv, grad_middle, change)
    width = out.shape[1]
    shapes = [a.shape for a in (gate, up, down, out)]
    shapes += [(qkv.shape[0], w) for w in (width, wide_k, wide_k)] + [change.shape]
    block = lambda shape: pl.BlockSpec((shape[0] // steps, shape[1]), lambda i: (i, 0))
    return pl.pallas_call(
        results_kernel,
        grid=(steps,),
        in_specs=[block(a.shape) for a in sources],
        out_specs=[block(shape) for shape in shapes],
        out_shape=[kind(shape, F32) for shape in shapes],
        compiler_params=pltpu.CompilerParams(vmem_limit_bytes=VMEM_BYTES),
    )(*sources)


def feed_forward_parts(ring, normed_two, grad_low, w_both, w_down):
    sequence, ff_own = normed_two.shape[0], w_down.shape[0]
    low_all, normed_all = run(ring.gather(grad_low), ring.gather(normed_two))
    hidden, grad_both = {}, {}
    for k in normed_all:
        both = dot(normed_all[k], w_both)
        gate, up = both[:, :ff_own], both[:, ff_own:]
        grad_hidden = contract_last(low_all[k], w_down)
        sigmoid = jax.nn.sigmoid(gate)
        silu = gate * sigmoid
        hidden[k] = (silu * up).astype(BF)
        grad_gate = (grad_hidden * up * sigmoid * (1.0 + gate * (1.0 - sigmoid))).astype(BF)
        grad_up = (grad_hidden * silu).astype(BF)
        grad_both[k] = jnp.concatenate([grad_gate, grad_up], 1)

    def terms_of(chunks, product):
        def terms(ks):
            sources = [k if k == ring.half else -k for k in ks]
            whole = product(jnp.concatenate([chunks[k] for k in sources], 0))
            return [whole[i * sequence : (i + 1) * sequence] for i in range(len(ks))]

        return terms

    (grad_normed_two,) = run(ring.scatter(terms_of(grad_both, lambda a: contract_last(a, w_both))))
    (branch_two,) = run(ring.scatter(terms_of(hidden, lambda a: dot(a, w_down))))
    keys = list(normed_all)
    together = lambda parts: jnp.concatenate([parts[k] for k in keys], 0)
    both_term = contract_first(together(normed_all), together(grad_both))
    down_term = contract_first(together(hidden), together(low_all))
    return grad_normed_two, branch_two, both_term, down_term


def swap(array, bit):
    return lax.ppermute(array, "rep", [(i, i ^ bit) for i in range(4)])


def cols(array, start, width):
    return lax.dynamic_slice_in_dim(array, start, width, 1)


def rows_of(array, start, height):
    return lax.dynamic_slice_in_dim(array, start, height, 0)


def put(array, piece, start, axis):
    return lax.dynamic_update_slice_in_dim(array, piece, start, axis)


def gather_rows(ring, array):
    rows = array.shape[0]
    (parts,) = run(ring.gather(array))
    full = jnp.zeros((ring.count * rows, array.shape[1]), array.dtype)
    for k, part in parts.items():
        full = put(full, part, ring.at(-k) * rows, 0)
    return full


def front_parts(ring, tokens, gains_own, cotangent, tables, own, w_gate, w_up):
    count, (own_rows, wide_k) = ring.count, own[1].shape
    rep = lax.axis_index("rep")
    ff_own = w_gate.shape[1] // count
    width = tokens.shape[1]
    gains = jnp.zeros((gains_own.shape[0], width), F32)
    for k in range(count):
        piece = ring.send(gains_own, k) if k else gains_own
        gains = put(gains, piece, ring.at(-k) * own_rows, 1)
    qkv_all = gather_rows(ring, jnp.concatenate(own[:3], 1))
    out_all = gather_rows(ring, own[3])
    quarter = own_rows // 4
    gate_rows = rows_of(w_gate, rep * quarter, quarter)
    up_rows = rows_of(w_up, rep * quarter, quarter)
    sends = []
    for k in range(count):
        dest = ring.at(k) * ff_own
        piece = jnp.concatenate([cols(gate_rows, dest, ff_own), cols(up_rows, dest, ff_own)], 1)
        sends.append((piece, k))
    fetched = jnp.zeros((count, quarter, 2 * ff_own), BF)
    for k, piece in enumerate([sends[0][0]] + ring.queue(*sends[1:])):
        fetched = put(fetched, piece[None], ring.at(-k), 0)
    pieces = [fetched, swap(fetched, 2)]
    pieces += [swap(piece, 1) for piece in pieces]
    w_both = jnp.zeros((count, 4, quarter, 2 * ff_own), BF)
    for bits, piece in zip((0, 2, 1, 3), pieces):
        w_both = put(w_both, piece[:, None], rep ^ bits, 1)
    resid = tokens.astype(F32)
    unit, _ = normalize(resid)
    linear = dot((unit * gains[:1]).astype(BF), qkv_all)
    query, key, value, attended = attend(
        linear[:, :width], linear[:, width : width + wide_k], linear[:, width + wide_k :], tables
    )
    middle = resid + dot(attended, out_all)
    unit, _ = normalize(middle)
    normed_two = (unit * gains[1:2]).astype(BF)
    low = cotangent.astype(BF)
    return qkv_all, out_all, w_both, low, gains, query, key, value, attended, middle, normed_two


def back_parts(
    ring,
    both_term,
    down_term,
    mid_low,
    gain_two_term,
    attended,
    query,
    key,
    value,
    tokens,
    gains,
    tables,
    qkv_all,
    out_all,
):
    count = ring.count
    rep = lax.axis_index("rep")
    core, chip = rep % 2, rep // 2
    width = tokens.shape[1]
    own_rows = width // count
    quarter = own_rows // 4
    ff_own = both_term.shape[1] // 2
    ff = ff_own * count

    def order_halves(mine, other):
        first = core == 0
        return jnp.where(first, mine, other), jnp.where(first, other, mine)

    def sum_cores(array, half_of):
        keep, pass_on = half_of(array, core), half_of(array, 1 - core)
        return keep.astype(F32) + swap(pass_on.astype(BF), 1).astype(F32)

    both_term = both_term.reshape(count, 2, 2, quarter, 2 * ff_own)
    both_half = sum_cores(
        both_term, lambda a, c: lax.dynamic_index_in_dim(a, c, 2, keepdims=False)
    )
    keep = lax.dynamic_index_in_dim(both_half, chip, 1, keepdims=False)
    pass_on = lax.dynamic_index_in_dim(both_half, 1 - chip, 1, keepdims=False)
    both_quarter = (keep + swap(pass_on.astype(BF), 2).astype(F32)).astype(BF)
    gate_quarter = jnp.zeros((quarter, ff), BF)
    up_quarter = jnp.zeros((quarter, ff), BF)
    sends = [
        (lax.dynamic_index_in_dim(both_quarter, ring.at(k), 0, keepdims=False), k)
        for k in range(count)
    ]
    for k, piece in enumerate([sends[0][0]] + ring.queue(*sends[1:])):
        start = ring.at(-k) * ff_own
        gate_quarter = put(gate_quarter, piece[:, :ff_own], start, 1)
        up_quarter = put(up_quarter, piece[:, ff_own:], start, 1)

    def collect(quarter_rows):
        parts = [quarter_rows, swap(quarter_rows, 2)]
        parts += [swap(part, 1) for part in parts]
        full = jnp.zeros((4 * quarter, ff), BF)
        for bits, part in zip((0, 2, 1, 3), parts):
            full = put(full, part, (rep ^ bits) * quarter, 0)
        return full

    gate_grad, up_grad = collect(gate_quarter), collect(up_quarter)

    down_half = sum_cores(
        down_term, lambda a, c: rows_of(a, c * (a.shape[0] // 2), a.shape[0] // 2)
    ).astype(BF)
    down_half = (down_half.astype(F32) + swap(down_half, 2).astype(F32)).astype(BF)
    down_grad = jnp.concatenate(order_halves(down_half, swap(down_half, 1)), 0)

    def part_sums(left, grads):
        wide = grads.shape[1] // 2
        grads_mine, grads_other = cols(grads, core * wide, wide), cols(grads, (1 - core) * wide, wide)

        def terms(ks):
            blocks = [cols(left, ring.at(k) * own_rows, own_rows) for k in ks]
            block = blocks[0] if len(ks) == 1 else jnp.concatenate(blocks, 1)
            other = swap(contract_first(block, grads_other).astype(BF), 1)
            whole = contract_first(block, grads_mine) + other.astype(F32)
            return [whole[i * own_rows : (i + 1) * own_rows] for i in range(len(ks))]

        mine = run(ring.scatter(terms))[0].astype(BF)
        mine = (mine.astype(F32) + swap(mine, 2).astype(F32)).astype(BF)
        return jnp.concatenate(order_halves(mine, swap(mine, 1)), 1)

    out_grad = part_sums(attended, mid_low)
    grad_attended = contract_last(mid_low, out_all).astype(BF)
    grads = jnp.concatenate(attend_back(query, key, value, grad_attended, tables), 1)
    unit_one, scale_one = normalize(tokens.astype(F32))
    gain_one = gains[:1]
    qkv_grad = part_sums((unit_one * gain_one).astype(BF), grads)
    grad_normed_one = contract_last(grads, qkv_all)
    gain_one_term = jnp.sum(grad_normed_one * unit_one, 0, keepdims=True)
    grad_input = norm_back(grad_normed_one * gain_one, unit_one, scale_one)

    gain_terms = jnp.concatenate([gain_one_term, gain_two_term], 0)
    gain_sums = cols(gain_terms, ring.at(0) * own_rows, own_rows)
    for k in range(1, count):
        gain_sums = gain_sums + ring.send(cols(gain_terms, ring.at(k) * own_rows, own_rows), k)
    gain_sums = gain_sums + swap(gain_sums, 1)
    gain_sums = gain_sums + swap(gain_sums, 2)
    return gate_grad, up_grad, down_grad, out_grad, qkv_grad, grad_input, gain_sums


def on_device(
    count,
    tokens,
    segments,
    norm_attn,
    w_query,
    key_weight,
    value_weight,
    w_out,
    norm_mlp,
    w_gate,
    w_up,
    w_down,
    cotangent,
):
    ring = Ring(count)
    sequence, width = tokens.shape[1], tokens.shape[2]
    own_rows = w_query.shape[0]
    ff = w_gate.shape[1]
    ff_own = ff // count
    wide_k = key_weight.shape[1]
    fits = feed_forward_bytes(count, sequence, width, ff_own) <= VMEM_BYTES
    kernels = fits and sequence == own_rows == TILE

    grad_output = cotangent.reshape(sequence, width)
    cosine, sine = rope_tables(segments)
    tables = (cosine, sine, segments.reshape(1, sequence))
    own = tokens.reshape(sequence, width)
    own_weights = (w_query, key_weight, value_weight, w_out)
    gains_own = jnp.zeros((8, own_rows), F32)
    gains_own = gains_own.at[0].set(norm_attn.astype(F32)).at[1].set(norm_mlp.astype(F32))
    bring = functools.partial(front, count) if kernels else functools.partial(front_parts, ring)
    qkv_all, out_all, w_both, low, gains, query, key, value, attended, middle, normed_two = bring(
        own, gains_own, grad_output, tables, own_weights, w_gate, w_up
    )
    w_both = w_both.reshape(width, 2 * ff_own)

    if kernels:
        grad_normed_two, branch_two, sums, down_grad = feed_forward(
            count, normed_two, low, w_both, w_down
        )
    else:
        grad_normed_two, branch_two, both_term, down_term = feed_forward_parts(
            ring, normed_two, low, w_both, w_down
        )
    output, grad_middle, grad_mid_low, gain_two_term = middle_back(
        middle, branch_two, grad_normed_two, grad_output, gains
    )

    if kernels:
        gate_grad, up_grad, out_grad, qkv_grad, grad_input, gain_sums = back(
            count,
            sums,
            grad_mid_low,
            gain_two_term,
            attended,
            query,
            key,
            value,
            own,
            gains,
            tables,
            qkv_all,
            out_all,
        )
    else:
        gate_grad, up_grad, down_grad, out_grad, qkv_grad, grad_input, gain_sums = back_parts(
            ring,
            both_term,
            down_term,
            grad_mid_low,
            gain_two_term,
            attended,
            query,
            key,
            value,
            own,
            gains,
            tables,
            qkv_all,
            out_all,
        )
    gate_grad, up_grad, down_grad, out_grad, query_grad, key_grad, value_grad, grad_input = results(
        gate_grad.reshape(own_rows, ff),
        up_grad.reshape(own_rows, ff),
        down_grad.reshape(ff_own, width),
        out_grad,
        qkv_grad,
        wide_k,
        grad_middle,
        grad_input,
    )

    return (
        output.reshape(tokens.shape),
        grad_input.reshape(tokens.shape),
        gain_sums[0],
        query_grad,
        key_grad,
        value_grad,
        out_grad,
        gain_sums[1],
        gate_grad,
        up_grad,
        down_grad,
    )


def solution(mesh):
    row, vector, matrix = P(("shard", "rep"), None, None), P("shard"), P("shard", None)
    in_specs = (row, P(("shard", "rep"), None), vector, matrix, matrix, matrix, matrix, vector)
    in_specs += (matrix, matrix, matrix, row)
    out_specs = (row, row, vector, matrix, matrix, matrix, matrix, vector, matrix, matrix, matrix)
    return jax.shard_map(
        functools.partial(on_device, mesh.shape["shard"]),
        mesh=mesh,
        in_specs=in_specs,
        out_specs=out_specs,
        check_vma=False,
    )
```

```python
import functools

import jax
import jax.numpy as jnp
from jax import lax
from jax.experimental import pallas as pl
from jax.experimental.pallas import tpu as pltpu
from jax.sharding import PartitionSpec as P

QUERY_HEADS = 32
KEY_VALUE_HEADS = 8
HEAD_SIZE = 64
GROUP = QUERY_HEADS // KEY_VALUE_HEADS

epsilon = 1e-05
masked_score = -1000000000.0
rope_base = 500000.0
WINDOW = 2
TILE = 256
WIDE_TILE = 512
LOAD_TILE = 128
VMEM_BYTES = 62 * 2**20
BF = jnp.bfloat16
F32 = jnp.float32


def dot(left, right):
    return jnp.dot(left, right, preferred_element_type=F32)


def contract_last(left, right):
    return lax.dot_general(left, right, (((1,), (1,)), ((), ())), preferred_element_type=F32)


def contract_first(left, right):
    return lax.dot_general(left, right, (((0,), (0,)), ((), ())), preferred_element_type=F32)


def positions(segment_ids):
    index = lax.broadcasted_iota(jnp.int32, segment_ids.shape, 1)
    first = jnp.concatenate(
        [
            jnp.ones_like(segment_ids[:, :1]),
            (segment_ids[:, 1:] != segment_ids[:, :-1]).astype(jnp.int32),
        ],
        1,
    )
    starts = lax.cummax(jnp.where(first > 0, index, 0), axis=1)
    return (index - starts).astype(F32)


def rope_tables(segment_ids):
    half = HEAD_SIZE // 2
    inverse = rope_base ** (-(2.0 * jnp.arange(half, dtype=F32)) / HEAD_SIZE)
    angle = positions(segment_ids)[0, :, None] * inverse
    cosine, sine = jnp.cos(angle), jnp.sin(angle)
    return jnp.concatenate([cosine] * 4, 1), jnp.concatenate([-sine, sine] * 2, 1)


def normalize(rows):
    scale_row = lax.rsqrt(jnp.mean(rows * rows, -1, keepdims=True) + epsilon)
    return rows * scale_row, scale_row


def norm_back(grad_unit, unit, scale_row):
    return scale_row * (grad_unit - unit * jnp.mean(grad_unit * unit, -1, keepdims=True))


def rotate(block, cosine, sine):
    lane = lax.broadcasted_iota(jnp.int32, cosine.shape, 1)
    lower = lane % HEAD_SIZE < HEAD_SIZE // 2
    parts = []
    for at in range(0, block.shape[1], 128):
        part = block[:, at : at + 128]
        other = jnp.where(
            lower, pltpu.roll(part, 128 - HEAD_SIZE // 2, 1), pltpu.roll(part, HEAD_SIZE // 2, 1)
        )
        parts.append(part * cosine + other * sine)
    return parts[0] if len(parts) == 1 else jnp.concatenate(parts, 1)


def stack_heads(block, key_head):
    first = key_head * GROUP
    return jnp.concatenate(
        [block[:, (first + i) * HEAD_SIZE : (first + i + 1) * HEAD_SIZE] for i in range(GROUP)], 0
    )


def unstack_heads(rows):
    count = rows.shape[0] // GROUP
    return [rows[i * count : (i + 1) * count] for i in range(GROUP)]


def softmax_rows(query, key, allowed):
    raw = contract_last(query, key) * HEAD_SIZE ** (-0.5)
    scores = jnp.where(allowed, raw, masked_score)
    exponent = jnp.exp(scores - jnp.max(scores, -1, keepdims=True))
    return exponent / jnp.sum(exponent, -1, keepdims=True)


def allowed_rows(seg_row):
    count = seg_row.shape[1]
    shape = (count, count)
    at_row = lax.broadcasted_iota(jnp.int32, shape, 0)
    at_column = lax.broadcasted_iota(jnp.int32, shape, 1)
    causal = at_row >= at_column
    seg_column = jnp.sum(
        jnp.where(at_row == at_column, jnp.broadcast_to(seg_row, shape), 0), 1, keepdims=True
    )
    one = ((seg_column == seg_row) & causal).astype(jnp.int32)
    return jnp.concatenate([one] * GROUP, 0) > 0


def attend_kernel(q_ref, k_ref, v_ref, cos_ref, sin_ref, segr_ref, qo, ko, vo, ao):
    cosine, sine = cos_ref[...], sin_ref[...]
    allowed = allowed_rows(segr_ref[...])
    query = rotate(q_ref[...], cosine, sine).astype(BF)
    key = rotate(k_ref[...], cosine, sine).astype(BF)
    value = v_ref[...].astype(BF)
    qo[...] = query
    ko[...] = key
    vo[...] = value
    heads = []
    for j in range(2):
        cols = slice(j * HEAD_SIZE, (j + 1) * HEAD_SIZE)
        probs = softmax_rows(stack_heads(query, j), key[:, cols], allowed).astype(BF)
        heads += unstack_heads(dot(probs, value[:, cols]).astype(BF))
    ao[...] = jnp.concatenate(heads, 1)


def attend_back_kernel(q_ref, k_ref, v_ref, g_ref, cos_ref, sin_ref, segr_ref, gq, gk, gv):
    cosine, sine = cos_ref[...], -sin_ref[...]
    allowed = allowed_rows(segr_ref[...])
    query, key, value, grad = q_ref[...], k_ref[...], v_ref[...], g_ref[...]
    heads, keys, values = [], [], []
    for j in range(2):
        cols = slice(j * HEAD_SIZE, (j + 1) * HEAD_SIZE)
        rows, grad_rows = stack_heads(query, j), stack_heads(grad, j)
        probs = softmax_rows(rows, key[:, cols], allowed)
        grad_probs = contract_last(grad_rows, value[:, cols])
        grad_scores = (
            probs * (grad_probs - jnp.sum(probs * grad_probs, -1, keepdims=True))
        ).astype(BF)
        heads += unstack_heads(dot(grad_scores, key[:, cols]) * HEAD_SIZE ** (-0.5))
        keys.append(contract_first(grad_scores, rows) * HEAD_SIZE ** (-0.5))
        values.append(contract_first(probs.astype(BF), grad_rows))
    gq[...] = rotate(jnp.concatenate(heads, 1), cosine, sine).astype(BF)
    gk[...] = rotate(jnp.concatenate(keys, 1), cosine, sine).astype(BF)
    gv[...] = jnp.concatenate(values, 1).astype(BF)


def attention_specs(count):
    wide = pl.BlockSpec((count, 2 * GROUP * HEAD_SIZE), lambda i: (0, i))
    thin = pl.BlockSpec((count, 2 * HEAD_SIZE), lambda i: (0, i))
    whole = lambda shape: pl.BlockSpec(shape, lambda i: (0, 0))
    fixed = [whole((count, 128)), whole((count, 128)), whole((1, count))]
    return wide, thin, fixed


def attend(query_lin, key_lin, value_lin, tables):
    count = query_lin.shape[0]
    wide, thin, fixed = attention_specs(count)
    kinds = [jax.ShapeDtypeStruct(a.shape, BF) for a in (query_lin, key_lin, value_lin, query_lin)]
    return pl.pallas_call(
        attend_kernel,
        grid=(KEY_VALUE_HEADS // 2,),
        in_specs=[wide, thin, thin] + fixed,
        out_specs=[wide, thin, thin, wide],
        out_shape=kinds,
        compiler_params=pltpu.CompilerParams(vmem_limit_bytes=48 * 2**20),
        cost_estimate=pl.CostEstimate(
            flops=2 * 10**9, bytes_accessed=6 * 10**6, transcendentals=2 * 10**6
        ),
    )(query_lin, key_lin, value_lin, *tables)


def attend_back(query, key, value, grad, tables):
    count = query.shape[0]
    wide, thin, fixed = attention_specs(count)
    kinds = [jax.ShapeDtypeStruct(a.shape, BF) for a in (query, key, value)]
    return pl.pallas_call(
        attend_back_kernel,
        grid=(KEY_VALUE_HEADS // 2,),
        in_specs=[wide, thin, thin, wide] + fixed,
        out_specs=[wide, thin, thin],
        out_shape=kinds,
        compiler_params=pltpu.CompilerParams(vmem_limit_bytes=48 * 2**20),
        cost_estimate=pl.CostEstimate(
            flops=4 * 10**9, bytes_accessed=6 * 10**6, transcendentals=2 * 10**6
        ),
    )(query, key, value, grad, *tables)


def ring_order(count):
    return list(range(0, count, 2)) + list(range(count - 1, 0, -2)) if count % 2 == 0 else list(range(count))


class Ring:
    def __init__(self, count):
        self.count = count
        self.half = count // 2
        self.order = ring_order(count)
        inverse = [self.order.index(i) for i in range(count)]
        self.table = jnp.asarray(self.order, jnp.int32)
        self.turns = []
        self.place = jnp.asarray(inverse, jnp.int32)[lax.axis_index("shard")]

    def at(self, offset):
        return self.table[(self.place + offset + self.count) % self.count]

    def send(self, array, offset):
        n, order = self.count, self.order
        pairs = [(order[i], order[(i + offset) % n]) for i in range(n)]
        return lax.ppermute(array, "shard", pairs)

    def queue(self, *sends):
        arrays = [array for array, _ in sends]
        if len(self.turns) >= WINDOW:
            arrays, _ = lax.optimization_barrier((arrays, self.turns[-WINDOW]))
        got = [self.send(array, offset) for array, (_, offset) in zip(arrays, sends)]
        self.turns.append(got[:2])
        return got

    def gather(self, array):
        cut = array.shape[0] // 2
        ahead = back = array
        out = {0: array}
        for k in range(1, self.half):
            ahead, back = self.queue((ahead, 1), (back, -1))
            out[k], out[-k] = ahead, back
            yield out
        out[self.half] = jnp.concatenate(self.queue((ahead[:cut], 1), (back[cut:], -1)), 0)
        yield out

    def scatter(self, terms):
        (far,) = terms((self.half,))
        far = far.astype(BF)
        cut = far.shape[0] // 2
        ahead, back = self.queue((far[:cut], 1), (far[cut:], -1))
        yield None
        for k in range(self.half - 1, 0, -1):
            up, down = terms((k, -k))
            if k == self.half - 1:
                up = jnp.concatenate([up[:cut] + ahead.astype(F32), up[cut:]], 0)
                down = jnp.concatenate([down[:cut], down[cut:] + back.astype(F32)], 0)
            else:
                up, down = up + ahead.astype(F32), down + back.astype(F32)
            ahead, back = self.queue((up.astype(BF), 1), (down.astype(BF), -1))
            if k > 1:
                yield None
        (own,) = terms((0,))
        yield own + ahead.astype(F32) + back.astype(F32)


def run(*flows):
    flows = list(flows)
    last = [None] * len(flows)
    live = list(range(len(flows)))
    while live:
        for i in list(live):
            try:
                last[i] = next(flows[i])
            except StopIteration:
                live.remove(i)
    return last


def ring_place(count, shard):
    return jnp.where(shard % 2 == 0, shard // 2, count - 1 - shard // 2)


def ring_shard(count, place):
    place = (place + count) % count
    return jnp.where(place < count // 2, 2 * place, 2 * (count - 1 - place) + 1)


def core_partner(rep):
    return rep + 1 - 2 * (rep % 2)


def chip_partner(rep):
    return (rep + 2) % 4


def greet(devices):
    barrier = pltpu.get_barrier_semaphore()
    for device in devices:
        pl.semaphore_signal(
            barrier, inc=1, device_id=device, device_id_type=pl.DeviceIdType.MESH
        )
    pl.semaphore_wait(barrier, len(devices))


def remote_copy(src, dst, send, recv, device):
    return pltpu.make_async_remote_copy(
        src_ref=src,
        dst_ref=dst,
        send_sem=send,
        recv_sem=recv,
        device_id=device,
        device_id_type=pl.DeviceIdType.MESH,
    )


def front_kernel(
    count,
    tokens_ref,
    gains_ref,
    cotangent_ref,
    cos_ref,
    sin_ref,
    segr_ref,
    query_own_ref,
    key_own_ref,
    value_own_ref,
    out_own_ref,
    gate_ref,
    up_ref,
    qkv_all_ref,
    out_all_ref,
    both_ref,
    low_all_ref,
    gains_all_ref,
    query_ref,
    key_ref,
    value_ref,
    attended_ref,
    middle_ref,
    normed_two_ref,
    low_own,
    both_own,
    qkv_all,
    out_all,
    normed,
    linear,
    own_sem,
    load_sem,
    gain_send,
    gain_recv,
    ring_send,
    ring_recv,
    core_send,
    core_recv,
    chip_send,
    chip_recv,
    across_send,
    across_recv,
    group_send,
    group_recv,
    low_send,
    low_recv,
):
    half = count // 2
    me, rep = lax.axis_index("shard"), lax.axis_index("rep")
    core, chip = rep % 2, rep // 2
    place = ring_place(count, me)
    others = [ring_shard(count, place + k) for k in range(1, count)]
    near = ({"shard": ring_shard(count, place + 1)}, {"shard": ring_shard(count, place - 1)})
    other_core, other_chip = {"rep": core_partner(rep)}, {"rep": chip_partner(rep)}
    own_rows = query_own_ref.shape[0]
    quarter = own_rows // 4
    cut = quarter // 2
    ff_own = gate_ref.shape[1] // count
    rows, width = tokens_ref.shape
    full_refs = (qkv_all_ref, out_all_ref)
    inside = (qkv_all, out_all)

    def rows_at(start, size):
        return pl.ds(pl.multiple_of(start, cut), size)

    def shard_rows(shard):
        return rows_at(shard * own_rows, own_rows)

    def piece_of(shard, which_core, which_chip, part=None):
        start = shard * own_rows + (2 * which_core + which_chip) * quarter
        if part is None:
            return rows_at(start, quarter)
        return rows_at(start + part * cut, cut)

    own_loads = [
        pltpu.make_async_copy(out_own_ref, out_all.at[shard_rows(me)], own_sem.at[6])
    ]
    start = 0
    for index, ref in enumerate((query_own_ref, key_own_ref, value_own_ref)):
        columns = pl.ds(start, ref.shape[1])
        own_loads.append(
            pltpu.make_async_copy(ref, qkv_all.at[shard_rows(me), columns], own_sem.at[7 + index])
        )
        start += ref.shape[1]
    keep = [
        pltpu.make_async_copy(
            inside[i].at[shard_rows(me)], full_refs[i].at[shard_rows(me)], own_sem.at[i]
        )
        for i in range(2)
    ]
    for i, ref in enumerate((gate_ref, up_ref)):
        block = (rows_at(rep * quarter, quarter), pl.ds(pl.multiple_of(me * ff_own, 128), ff_own))
        own_loads.append(
            pltpu.make_async_copy(
                ref.at[block], both_own.at[:, pl.ds(i * ff_own, ff_own)], own_sem.at[2 + i]
            )
        )
    for copy in own_loads:
        copy.start()
    gains_all_ref[:, pl.ds(pl.multiple_of(me * own_rows, 128), own_rows)] = gains_ref[...]
    low_own[...] = cotangent_ref[...].astype(BF)
    for copy in own_loads:
        copy.wait()
    keep.append(pltpu.make_async_copy(low_own, low_all_ref.at[pl.ds(0, rows)], own_sem.at[4]))
    keep.append(pltpu.make_async_copy(both_own, both_ref.at[me, rep], own_sem.at[5]))
    for copy in keep:
        copy.start()

    greet([{"shard": shard} for shard in others] + [other_core, other_chip])

    def gain_copy(k):
        columns = pl.ds(pl.multiple_of(me * own_rows, 128), own_rows)
        return remote_copy(
            gains_ref,
            gains_all_ref.at[:, columns],
            gain_send.at[k - 1],
            gain_recv.at[k - 1],
            {"shard": others[k - 1]},
        )

    def across(k, which):
        ref = (gate_ref, up_ref)[which]
        there = others[k - 1]
        columns = pl.ds(pl.multiple_of(there * ff_own, 128), ff_own)
        return remote_copy(
            ref.at[rows_at(rep * quarter, quarter), columns],
            both_ref.at[me, rep, :, pl.ds(which * ff_own, ff_own)],
            across_send.at[which, k - 1],
            across_recv.at[which, k - 1],
            {"shard": there},
        )

    def hops(step):
        return ((0, 0), (0, 1), (1, 0), (1, 1)) if step < half else ((0, 0), (1, 1))

    def ring_copy(i, direction, step, part):
        sign = 1 if direction == 0 else -1
        at = piece_of(ring_shard(count, place - sign * (step - 1)), core, chip, part)
        src = inside[i].at[at] if step == 1 else full_refs[i].at[at]
        return remote_copy(
            src,
            full_refs[i].at[at],
            ring_send.at[i, direction, step - 1, part],
            ring_recv.at[i, direction, step - 1, part],
            near[direction],
        )

    def chip_copy(i, k):
        at = piece_of(ring_shard(count, place - k), core, chip)
        slot = k + half - 1
        return remote_copy(
            full_refs[i].at[at],
            full_refs[i].at[at],
            chip_send.at[i, slot],
            chip_recv.at[i, slot],
            other_chip,
        )

    def core_copy(i, k, which):
        from_chip = chip if which == 0 else 1 - chip
        at = piece_of(ring_shard(count, place - k), core, from_chip)
        slot = k + half - 1
        return remote_copy(
            full_refs[i].at[at],
            full_refs[i].at[at],
            core_send.at[i, which, slot],
            core_recv.at[i, which, slot],
            other_core,
        )

    def load(i, k):
        at = shard_rows(ring_shard(count, place - k))
        return pltpu.make_async_copy(
            full_refs[i].at[at], inside[i].at[at], load_sem.at[i, k + half - 1]
        )

    def low_copy(direction, step, part):
        base = 0 if direction == 0 else half
        source = (base + step - 1) * rows if step > 1 else 0
        to = (base + step if step < half else half) * rows
        size = rows // 2
        src = (low_all_ref if step > 1 else low_own).at[pl.ds(source + part * size, size)]
        return remote_copy(
            src,
            low_all_ref.at[pl.ds(to + part * size, size)],
            low_send.at[direction, step - 1, part],
            low_recv.at[direction, step - 1, part],
            near[direction],
        )

    def pass_on(copy_of, step):
        for part, direction in hops(step):
            copy_of(direction, step, part).wait_recv()
            if step < half - 1 or (step == half - 1 and part == direction):
                copy_of(direction, step + 1, part).start()

    def start_low():
        for part, direction in hops(1):
            low_copy(direction, 1, part).start()

    def finish_low(step):
        pass_on(low_copy, step)

    def start_ring(i):
        for part, direction in hops(1):
            ring_copy(i, direction, 1, part).start()

    def places(step):
        return (step, -step) if step < half else (half,)

    def finish_step(i, step):
        pass_on(functools.partial(ring_copy, i), step)
        for k in places(step):
            core_copy(i, k, 0).start()

    def start_chip(i, step):
        for k in places(step):
            chip_copy(i, k).start()

    def pass_step(i, step):
        for k in places(step):
            chip_copy(i, k).wait_recv()
            core_copy(i, k, 1).start()

    def load_step(i, step):
        for k in places(step):
            for which in range(2):
                core_copy(i, k, which).wait_recv()
            load(i, k).start()

    for k in range(1, count):
        gain_copy(k).start()
    start_ring(0)
    resid = tokens_ref[...].astype(F32)
    unit, _ = normalize(resid)
    for k in range(1, count):
        gain_copy(k).wait_recv()
    normed[...] = (unit * gains_all_ref[0:1, :]).astype(BF)

    for step in range(1, half + 1):
        finish_step(0, step)
        start_chip(0, step)
        if step == half - 1:
            for k in range(1, count):
                for which in range(2):
                    across(k, which).start()
    start_ring(1)
    for step in range(1, half + 1):
        pass_step(0, step)
        if step > 1:
            load_step(0, step - 1)

    def group_copy(index, quarter_at, device):
        at = both_ref.at[:, quarter_at]
        return remote_copy(at, at, group_send.at[index], group_recv.at[index], device)

    chip_copies = [group_copy(0, rep, other_chip)]
    core_copies = [
        group_copy(1, rep, other_core),
        group_copy(2, chip_partner(rep), other_core),
    ]
    load_step(0, half)
    for k in range(-(half - 1), half + 1):
        if k:
            load(0, k).wait()

    def linear_tile(j, carry):
        at = pl.ds(pl.multiple_of(j * TILE, TILE), TILE)
        linear[:, at] = dot(normed[...], qkv_all[:, at])
        return carry

    lax.fori_loop(0, linear.shape[1] // TILE, linear_tile, 0)

    cosine, sine = cos_ref[...], sin_ref[...]
    wide, thin = 2 * GROUP * HEAD_SIZE, 2 * HEAD_SIZE
    key_at, value_at = width, width + key_ref.shape[1]

    def heads_pair(pair):
        allowed = allowed_rows(segr_ref[...])
        wide_at = pl.ds(pair * wide, wide)
        thin_at = pl.ds(pair * thin, thin)
        query = rotate(linear[:, wide_at], cosine, sine).astype(BF)
        key = rotate(linear[:, pl.ds(key_at + pair * thin, thin)], cosine, sine).astype(BF)
        value = linear[:, pl.ds(value_at + pair * thin, thin)].astype(BF)
        query_ref[:, wide_at] = query
        key_ref[:, thin_at] = key
        value_ref[:, thin_at] = value
        heads = []
        for j in range(2):
            cols = slice(j * HEAD_SIZE, (j + 1) * HEAD_SIZE)
            probs = softmax_rows(stack_heads(query, j), key[:, cols], allowed).astype(BF)
            heads += unstack_heads(dot(probs, value[:, cols]).astype(BF))
        attended_ref[:, wide_at] = jnp.concatenate(heads, 1)

    pairs = KEY_VALUE_HEADS // 2
    for turn in range(max(pairs, half)):
        if turn < half:
            finish_step(1, turn + 1)
            start_chip(1, turn + 1)
        if turn == half - 2:
            start_low()
        if turn < pairs:
            heads_pair(turn)
    for copy in keep:
        copy.wait()
    for k in range(1, count):
        for which in range(2):
            across(k, which).wait_recv()
    chip_copies[0].start()
    core_copies[0].start()
    for step in range(1, half + 1):
        pass_step(1, step)
        if step > 1:
            load_step(1, step - 1)
        if step % 2 == 0 and step // 2 < half:
            finish_low(step // 2)
    load_step(1, half)
    for k in range(-(half - 1), half + 1):
        if k:
            load(1, k).wait()

    def branch_tile(j, carry):
        at = pl.ds(pl.multiple_of(j * TILE, TILE), TILE)
        branch = dot(attended_ref[...], out_all[:, at])
        middle_ref[:, at] = tokens_ref[:, at].astype(F32) + branch
        return carry

    lax.fori_loop(0, width // TILE, branch_tile, 0)
    unit, _ = normalize(middle_ref[...])
    normed_two_ref[...] = (unit * gains_all_ref[1:2, :]).astype(BF)

    for step in range(half // 2 + 1, half + 1):
        finish_low(step)
    chip_copies[0].wait_recv()
    core_copies[1].start()
    for copy in core_copies:
        copy.wait_recv()
    for copy in chip_copies + core_copies:
        copy.wait_send()
    for step in range(1, half + 1):
        for part, direction in hops(step):
            low_copy(direction, step, part).wait_send()
    for i in range(2):
        for step in range(1, half + 1):
            for part, direction in hops(step):
                ring_copy(i, direction, step, part).wait_send()
            for k in places(step):
                chip_copy(i, k).wait_send()
                for which in range(2):
                    core_copy(i, k, which).wait_send()
    for k in range(1, count):
        gain_copy(k).wait_send()
        for which in range(2):
            across(k, which).wait_send()


def front(count, tokens, gains, cotangent, tables, own, gate_own, up_own):
    rows, width = tokens.shape
    own_rows, wide_k = own[1].shape
    qkv_width = width + 2 * wide_k
    ff_own = gate_own.shape[1] // count
    half = count // 2
    here = pl.BlockSpec(memory_space=pl.ANY)
    inside = pl.BlockSpec(memory_space=pltpu.VMEM)
    kind = jax.ShapeDtypeStruct
    dma = pltpu.SemaphoreType.DMA
    return pl.pallas_call(
        functools.partial(front_kernel, count),
        in_specs=[inside] * 6 + [here] * 6,
        out_specs=[here] * 4 + [inside] * 7,
        out_shape=[
            kind((count * own_rows, qkv_width), BF),
            kind((count * own_rows, width), BF),
            kind((count, 4, own_rows // 4, 2 * ff_own), BF),
            kind((count * rows, width), BF),
            kind((gains.shape[0], width), F32),
            kind((rows, width), BF),
            kind((rows, wide_k), BF),
            kind((rows, wide_k), BF),
            kind((rows, width), BF),
            kind((rows, width), F32),
            kind((rows, width), BF),
        ],
        scratch_shapes=[
            pltpu.VMEM((rows, width), BF),
            pltpu.VMEM((own_rows // 4, 2 * ff_own), BF),
            pltpu.VMEM((count * own_rows, qkv_width), BF),
            pltpu.VMEM((count * own_rows, width), BF),
            pltpu.VMEM((rows, width), BF),
            pltpu.VMEM((rows, qkv_width), F32),
            dma((10,)),
            dma((2, count)),
            dma((count - 1,)),
            dma((count - 1,)),
            dma((2, 2, half, 2)),
            dma((2, 2, half, 2)),
            dma((2, 2, count)),
            dma((2, 2, count)),
            dma((2, count)),
            dma((2, count)),
            dma((2, count - 1)),
            dma((2, count - 1)),
            dma((3,)),
            dma((3,)),
            dma((2, half, 2)),
            dma((2, half, 2)),
        ],
        compiler_params=pltpu.CompilerParams(
            collective_id=1, has_side_effects=True, vmem_limit_bytes=VMEM_BYTES
        ),
        cost_estimate=pl.CostEstimate(
            flops=2 * rows * width * (qkv_width + width) + 2 * 10**9,
            bytes_accessed=60 * 10**6,
            transcendentals=2 * 10**6,
        ),
    )(tokens, gains, cotangent, *tables, *own, gate_own, up_own)


def feed_forward_kernel(
    count,
    normed_ref,
    low_ref,
    both_ref,
    down_ref,
    grad_ref,
    branch_ref,
    sums_ref,
    down_grad_ref,
    normed,
    low,
    hidden,
    grads,
    w_both,
    w_down,
    turned,
    staged,
    from_core,
    core_sums,
    from_chip,
    group_sums,
    result_tile,
    outgoing,
    incoming,
    local_sem,
    gather_send,
    gather_recv,
    scatter_send,
    scatter_recv,
    credit,
    core_send,
    core_recv,
    chip_send,
    chip_recv,
    group_credit,
    sums_sem,
    result_sem,
    down_send,
    down_recv,
):
    half = count // 2
    rows = normed_ref.shape[0]
    cut = rows // 2
    width = normed_ref.shape[1]
    ff = down_ref.shape[0]
    place = ring_place(count, lax.axis_index("shard"))
    neighbours = (ring_shard(count, place + 1), ring_shard(count, place - 1))
    rep = lax.axis_index("rep")
    core, chip = rep % 2, rep // 2
    other_core, other_chip = {"rep": core_partner(rep)}, {"rep": chip_partner(rep)}
    everywhere = pl.ds(0, rows)
    halves = (pl.ds(0, cut), pl.ds(cut, cut))

    def at(slot, part=None):
        start, size = (0, rows) if part is None else (part * cut, cut)
        return pl.ds(pl.multiple_of(slot * rows + start, cut), size)

    def tile(j):
        return pl.ds(pl.multiple_of(j * TILE, TILE), TILE)

    def remote(src, dst, send, recv, direction):
        return remote_copy(src, dst, send, recv, {"shard": neighbours[direction]})

    loads = [
        pltpu.make_async_copy(normed_ref, normed.at[at(0)], local_sem.at[0]),
        pltpu.make_async_copy(low_ref, low, local_sem.at[1]),
        pltpu.make_async_copy(both_ref, w_both, local_sem.at[2]),
        pltpu.make_async_copy(down_ref, w_down, local_sem.at[3]),
    ]
    for load in loads:
        load.start()

    for chain in range(2):
        for direction in range(2):
            blank = halves[1 - direction]
            incoming[chain, direction, 0, blank] = jnp.zeros((cut, width), BF)

    greet([{"shard": neighbour} for neighbour in neighbours] + [other_core, other_chip])

    def gathered(part, direction, step):
        base = 0 if direction == 0 else half
        if isinstance(step, int) and step == 1:
            source = 0
        else:
            source = jnp.where(step == 1, 0, base + step - 1)
        return remote(
            normed.at[at(source, part)],
            normed.at[at(base + step, part)],
            gather_send.at[part, direction, step - 1],
            gather_recv.at[part, direction, step - 1],
            direction,
        )

    def gathered_last(direction):
        source = half - 1 if direction == 0 else 2 * half - 1
        return remote(
            normed.at[at(source, direction)],
            normed.at[at(half, direction)],
            gather_send.at[0, direction, half - 1],
            gather_recv.at[0, direction, half - 1],
            direction,
        )

    def products(slot):
        mine = at(slot)

        def body(j, carry):
            gate_at, up_at = tile(j), tile(j + ff // TILE)
            own = normed[mine, :]
            gate = dot(own, w_both[:, gate_at])
            up = dot(own, w_both[:, up_at])
            grad_hidden = contract_last(low[mine, :], w_down[gate_at, :])
            sigmoid = jax.nn.sigmoid(gate)
            silu = gate * sigmoid
            hidden[mine, gate_at] = (silu * up).astype(BF)
            grads[mine, gate_at] = (
                grad_hidden * up * sigmoid * (1.0 + gate * (1.0 - sigmoid))
            ).astype(BF)
            grads[mine, up_at] = (grad_hidden * silu).astype(BF)
            return carry

        lax.fori_loop(0, ff // TILE, body, 0)

    both_ways = ((0, 0), (0, 1), (1, 0), (1, 1))
    loads[0].wait()
    for part, direction in both_ways:
        gathered(part, direction, 1).start()
    for load in loads[1:]:
        load.wait()
    products(0)

    def gather_step(step, carry):
        for part, direction in both_ways:
            gathered(part, direction, step).wait_recv()

            @pl.when(step < half - 1)
            def _():
                gathered(part, direction, step + 1).start()

            if part == direction:

                @pl.when(step == half - 1)
                def _():
                    gathered_last(direction).start()

        products(step)

        @pl.when(step < half - 1)
        def _():
            products(half + step)

        return carry

    lax.fori_loop(1, half, gather_step, 0)
    for direction in range(2):
        gathered_last(direction).wait_recv()
    products(half)

    def term(chain, rows_at, j):
        if chain == 0:
            return contract_last(grads[rows_at, :], w_both[tile(j), :])
        return dot(hidden[rows_at, :], w_down[:, tile(j)])

    def scattered(chain, direction, step):
        if isinstance(step, int) and step == 0:
            own, there = halves[direction], 0
        else:
            own, there = everywhere, step % 2
        return remote(
            outgoing.at[chain, direction, own],
            incoming.at[chain, direction, there, own],
            scatter_send.at[chain, direction, step],
            scatter_recv.at[chain, direction, step],
            direction,
        )

    units = (width + ff) // TILE
    per_step = -(-(units + 3) // (half - 1)) + 2
    quarter = TILE // 4

    def core_copy(unit):
        spot = unit % 2
        return remote_copy(
            staged.at[spot, :, 1 - core],
            from_core.at[spot],
            core_send.at[spot],
            core_recv.at[spot],
            other_core,
        )

    def chip_copy(unit):
        spot = unit % 3
        return remote_copy(
            core_sums.at[spot, 1 - chip],
            from_chip.at[spot],
            chip_send.at[spot],
            chip_recv.at[spot],
            other_chip,
        )

    down_units = ff // TILE

    def sums_copy(unit, down):
        spot = unit % 2
        target = down_grad_ref.at[unit, rep] if down else sums_ref.at[unit - down_units]
        return pltpu.make_async_copy(group_sums.at[spot], target, sums_sem.at[spot])

    def for_sums(unit, act):
        @pl.when(unit < down_units)
        def _():
            act(sums_copy(unit, True))

        @pl.when(unit >= down_units)
        def _():
            act(sums_copy(unit, False))

    def down_copy(index):
        at = down_grad_ref.at[:, chip_partner(rep) if index == 2 else rep]
        return remote_copy(
            at,
            at,
            down_send.at[index],
            down_recv.at[index],
            other_chip if index == 0 else other_core,
        )

    def give_credit(which, device):
        pl.semaphore_signal(
            group_credit.at[which], inc=1, device_id=device, device_id_type=pl.DeviceIdType.MESH
        )

    def weight_unit(unit):
        spot = unit % 2

        def from_arrays(left, right, block):
            def turn(c, carry):
                turned[:, at(c)] = left[at(c), tile(block)].T
                return carry

            lax.fori_loop(0, count, turn, 0)

            def body(j, carry):
                value = dot(turned[...], right[:, tile(j)]).astype(BF)
                staged[spot, :, :, :, tile(j)] = value.reshape(2, 2, quarter, TILE)
                return carry

            lax.fori_loop(0, width // TILE, body, 0)

        @pl.when(unit < down_units)
        def _():
            from_arrays(hidden, low, unit)

        @pl.when(unit >= down_units)
        def _():
            from_arrays(normed, grads, unit - down_units)

        @pl.when(unit >= 2)
        def _():
            pl.semaphore_wait(group_credit.at[0], 1)

        core_copy(unit).start()

    def sum_over_cores(unit):
        spot, place_of = unit % 2, unit % 3
        core_copy(unit).wait()
        for y in range(2):
            total = staged[spot, y, core].astype(F32) + from_core[spot, y].astype(F32)
            core_sums[place_of, y] = total.astype(BF)

        @pl.when(unit < units - 2)
        def _():
            give_credit(0, other_core)

        @pl.when(unit >= 3)
        def _():
            pl.semaphore_wait(group_credit.at[1], 1)

        chip_copy(unit).start()

    def sum_over_chips(unit):
        spot, place_of = unit % 2, unit % 3
        chip_copy(unit).wait()

        @pl.when(unit >= 2)
        def _():
            for_sums(unit - 2, lambda copy: copy.wait())

        total = core_sums[place_of, chip].astype(F32) + from_chip[place_of].astype(F32)
        group_sums[spot] = total.astype(BF)

        @pl.when(unit < units - 3)
        def _():
            give_credit(1, other_chip)

        for_sums(unit, lambda copy: copy.start())

    def weight_step(turn):
        @pl.when(turn < units)
        def _():
            weight_unit(turn)

        @pl.when((turn >= 1) & (turn <= units))
        def _():
            sum_over_cores(turn - 1)

        @pl.when(turn == units)
        def _():
            for index in range(2):
                down_copy(index).start()

        @pl.when(turn >= 3)
        def _():
            sum_over_chips(turn - 3)

    for chain in range(2):

        def first(j, carry):
            value = term(chain, at(half), j).astype(BF)
            outgoing[chain, 0, halves[0], tile(j)] = value[:cut]
            outgoing[chain, 1, halves[1], tile(j)] = value[cut:]
            return carry

        lax.fori_loop(0, width // TILE, first, 0)
        for direction in range(2):
            scattered(chain, direction, 0).start()

    products(2 * half - 1)

    def scatter_step(step, carry):
        k = half - step
        for chain in range(2):
            for direction in range(2):
                slot = half + k if direction == 0 else k

                @pl.when(step == 1)
                def _():
                    scattered(chain, direction, 0).wait()

                @pl.when(step > 1)
                def _():
                    scattered(chain, direction, step - 1).wait()
                    pl.semaphore_wait(credit.at[chain, direction], 1)

                def add(j, carry):
                    value = term(chain, at(slot), j)
                    value += incoming[chain, direction, (step - 1) % 2, :, tile(j)].astype(F32)
                    outgoing[chain, direction, :, tile(j)] = value.astype(BF)
                    return carry

                lax.fori_loop(0, width // TILE, add, 0)
                scattered(chain, direction, step).start()

                @pl.when(step < half - 1)
                def _():
                    pl.semaphore_signal(
                        credit.at[chain, direction],
                        inc=1,
                        device_id={"shard": neighbours[1 - direction]},
                        device_id_type=pl.DeviceIdType.MESH,
                    )

        lax.fori_loop(
            (step - 1) * per_step,
            jnp.minimum(step * per_step, units + 3),
            lambda turn, c: (weight_step(turn), c)[1],
            0,
        )
        return carry

    lax.fori_loop(1, half, scatter_step, 0)

    for chain, result in enumerate((grad_ref, branch_ref)):
        for direction in range(2):
            scattered(chain, direction, half - 1).wait()

        def result_copy(j):
            return pltpu.make_async_copy(
                result_tile.at[j % 2], result.at[:, tile(j)], result_sem.at[j % 2]
            )

        def last(j, carry):
            @pl.when(j >= 2)
            def _():
                result_copy(j - 2).wait()

            value = term(chain, at(0), j)
            for direction in range(2):
                value += incoming[chain, direction, (half - 1) % 2, :, tile(j)].astype(F32)
            result_tile[j % 2] = value
            result_copy(j).start()
            return carry

        lax.fori_loop(0, width // TILE, last, 0)
        for j in (width // TILE - 2, width // TILE - 1):
            result_copy(j).wait()

    down_copy(0).wait_recv()
    down_copy(2).start()
    for unit in (units - 2, units - 1):
        sums_copy(unit, False).wait()
    down_copy(0).wait_send()
    for index in (1, 2):
        down_copy(index).wait()
    for part, direction in both_ways:
        lax.fori_loop(
            1,
            half,
            lambda step, c: (gathered(part, direction, step).wait_send(), c)[1],
            0,
        )
    for direction in range(2):
        gathered_last(direction).wait_send()


def feed_forward_bytes(count, rows, width, ff):
    tokens = count * rows
    return 2 * (
        tokens * (2 * width + 3 * ff)
        + 3 * width * ff
        + TILE * tokens
        + 6 * TILE * width
        + 12 * rows * width
        + 4 * TILE * rows
    )


def feed_forward(count, normed, low, w_both, w_down):
    rows, width = normed.shape
    ff = w_down.shape[0]
    tokens = count * rows
    half = count // 2
    quarter = TILE // 4
    here = pl.BlockSpec(memory_space=pl.ANY)
    dma = pltpu.SemaphoreType.DMA
    return pl.pallas_call(
        functools.partial(feed_forward_kernel, count),
        in_specs=[here] * 4,
        out_specs=[here] * 4,
        out_shape=[
            jax.ShapeDtypeStruct((rows, width), F32),
            jax.ShapeDtypeStruct((rows, width), F32),
            jax.ShapeDtypeStruct((width // TILE, quarter, width), BF),
            jax.ShapeDtypeStruct((ff // TILE, 4, quarter, width), BF),
        ],
        scratch_shapes=[
            pltpu.VMEM((tokens, width), BF),
            pltpu.VMEM((tokens, width), BF),
            pltpu.VMEM((tokens, ff), BF),
            pltpu.VMEM((tokens, 2 * ff), BF),
            pltpu.VMEM((width, 2 * ff), BF),
            pltpu.VMEM((ff, width), BF),
            pltpu.VMEM((TILE, tokens), BF),
            pltpu.VMEM((2, 2, 2, quarter, width), BF),
            pltpu.VMEM((2, 2, quarter, width), BF),
            pltpu.VMEM((3, 2, quarter, width), BF),
            pltpu.VMEM((3, quarter, width), BF),
            pltpu.VMEM((2, quarter, width), BF),
            pltpu.VMEM((2, rows, TILE), F32),
            pltpu.VMEM((2, 2, rows, width), BF),
            pltpu.VMEM((2, 2, 2, rows, width), BF),
            dma((4,)),
            dma((2, 2, half)),
            dma((2, 2, half)),
            dma((2, 2, half)),
            dma((2, 2, half)),
            pltpu.SemaphoreType.REGULAR((2, 2)),
            dma((2,)),
            dma((2,)),
            dma((3,)),
            dma((3,)),
            pltpu.SemaphoreType.REGULAR((2,)),
            dma((2,)),
            dma((2,)),
            dma((3,)),
            dma((3,)),
        ],
        compiler_params=pltpu.CompilerParams(
            collective_id=0, has_side_effects=True, vmem_limit_bytes=VMEM_BYTES
        ),
        cost_estimate=pl.CostEstimate(
            flops=18 * tokens * width * ff, bytes_accessed=50 * 10**6, transcendentals=tokens * ff
        ),
    )(normed, low, w_both, w_down)


def middle_back_kernel(
    middle_ref, branch_ref, grad_ref, cotangent_ref, gains_ref, result_ref, out_ref, low_ref, term_ref
):
    middle = middle_ref[...]
    result_ref[...] = middle + branch_ref[...]
    unit, scale_row = normalize(middle)
    grad = grad_ref[...]
    total = cotangent_ref[...] + norm_back(grad * gains_ref[1:2, :], unit, scale_row)
    out_ref[...] = total
    low_ref[...] = total.astype(BF)
    term = jnp.sum(grad * unit, 0, keepdims=True)

    @pl.when(pl.program_id(0) == 0)
    def _():
        term_ref[...] = term

    @pl.when(pl.program_id(0) > 0)
    def _():
        term_ref[...] += term


def middle_back(middle, branch, grad, cotangent, gains):
    rows, width = middle.shape
    block = pl.BlockSpec((rows // 4, width), lambda i: (i, 0))
    fixed = pl.BlockSpec((1, width), lambda i: (0, 0))
    kind = jax.ShapeDtypeStruct
    full = kind((rows, width), F32)
    return pl.pallas_call(
        middle_back_kernel,
        grid=(4,),
        in_specs=[block] * 4 + [pl.BlockSpec(gains.shape, lambda i: (0, 0))],
        out_specs=[block] * 3 + [fixed],
        out_shape=[full, full, kind((rows, width), BF), kind((1, width), F32)],
        compiler_params=pltpu.CompilerParams(vmem_limit_bytes=VMEM_BYTES),
    )(middle, branch, grad, cotangent, gains)


def back_kernel(
    count,
    sums_ref,
    mid_low_ref,
    gain_two_ref,
    attended_ref,
    query_ref,
    key_ref,
    value_ref,
    tokens_ref,
    gains_ref,
    cos_ref,
    sin_ref,
    segr_ref,
    qkv_all_ref,
    out_all_ref,
    gate_grad_ref,
    up_grad_ref,
    out_grad_ref,
    qkv_grad_ref,
    grad_input_ref,
    gain_grad_ref,
    both_own,
    turned,
    grad_attended,
    grads,
    weight_tile,
    terms_first,
    terms_second,
    from_core_out,
    from_core_qkv,
    from_chip_out,
    out_sums,
    out_summed,
    outgoing_out,
    outgoing_qkv,
    incoming_out,
    incoming_qkv,
    summed,
    from_chip,
    finished,
    gain_terms,
    gains_in,
    gain_parts,
    gain_swaps,
    own_sem,
    tile_sem,
    across_send,
    across_recv,
    group_send,
    group_recv,
    core_send,
    core_recv,
    ring_send,
    ring_recv,
    chip_send,
    chip_recv,
    last_send,
    last_recv,
    pair_send,
    pair_recv,
    gain_send,
    gain_recv,
    swap_send,
    swap_recv,
):
    half = count // 2
    me, rep = lax.axis_index("shard"), lax.axis_index("rep")
    core, chip = rep % 2, rep // 2
    place = ring_place(count, me)
    others = [ring_shard(count, place + k) for k in range(1, count)]
    near = ({"shard": ring_shard(count, place + 1)}, {"shard": ring_shard(count, place - 1)})
    other_core, other_chip = {"rep": core_partner(rep)}, {"rep": chip_partner(rep)}
    rows, width = tokens_ref.shape
    own_rows = width // count
    strip, quarter = own_rows // 2, own_rows // 4
    ff_own = gate_grad_ref.shape[2] // count
    qkv_half = grads.shape[1] // 2
    wides = (width, qkv_half, qkv_half)
    terms = (terms_first, terms_second, terms_first)
    pieces = (quarter, strip, strip)
    from_core = (from_core_out, from_core_qkv.at[0], from_core_qkv.at[1])
    outgoing = (outgoing_out, outgoing_qkv.at[0], outgoing_qkv.at[1])
    incoming = (incoming_out, incoming_qkv.at[0], incoming_qkv.at[1])
    result_refs = (out_grad_ref, qkv_grad_ref, qkv_grad_ref)
    result_starts = (0, 0, qkv_half)
    chains, in_turn = range(3), (1, 2, 0)

    def tile(j, size=TILE):
        return pl.ds(pl.multiple_of(j * size, size), size)

    gate_up = (gate_grad_ref, up_grad_ref)

    def own_columns(shard):
        return pl.ds(pl.multiple_of(shard * ff_own, 128), ff_own)

    def across(k, which):
        there = others[k - 1]
        return remote_copy(
            sums_ref.at[there, :, pl.ds(which * ff_own, ff_own)],
            gate_up[which].at[rep, :, own_columns(me)],
            across_send.at[which, k - 1],
            across_recv.at[which, k - 1],
            {"shard": there},
        )

    own_load = pltpu.make_async_copy(sums_ref.at[me], both_own, own_sem.at[0])
    keep = [
        pltpu.make_async_copy(
            both_own.at[:, pl.ds(which * ff_own, ff_own)],
            gate_up[which].at[rep, :, own_columns(me)],
            own_sem.at[which],
        )
        for which in range(2)
    ]

    def group_copy(which, index):
        member = chip_partner(rep) if index == 2 else rep
        dst = src = gate_up[which].at[member]
        return remote_copy(
            src,
            dst,
            group_send.at[which, index],
            group_recv.at[which, index],
            other_chip if index == 0 else other_core,
        )

    def shard_of(k):
        return ring_shard(count, place + k)

    def core_copy(i, k):
        slot = k + half - 1
        return remote_copy(
            terms[i].at[shard_of(k), 1 - core, :, pl.ds(0, wides[i])],
            from_core[i].at[slot],
            core_send.at[i, slot],
            core_recv.at[i, slot],
            other_core,
        )

    def all_terms(i):
        def body(j, carry):
            if i == 0:
                right = mid_low_ref[:, tile(j)]
            else:
                right = grads[:, tile(j + result_starts[i] // TILE)]
            value = dot(turned[...], right).astype(BF)
            terms[i][:, :, :, tile(j)] = value.reshape(count, 2, strip, TILE)
            return carry

        lax.fori_loop(0, wides[i] // TILE, body, 0)
        for k in [half] + [s * j for j in range(half - 1, 0, -1) for s in (1, -1)] + [0]:
            core_copy(i, k).start()

    def pair_copy(k):
        slot = k + half - 1
        return remote_copy(
            out_sums.at[slot, 1 - chip],
            from_chip_out.at[slot],
            pair_send.at[slot],
            pair_recv.at[slot],
            other_chip,
        )

    def sum_pair(k):
        core_copy(0, k).wait_recv()

        def body(j, carry):
            at = tile(j, WIDE_TILE)
            value = terms[0][shard_of(k), core, :, at].astype(F32)
            value += from_core[0][k + half - 1, :, at].astype(F32)
            out_sums[k + half - 1, :, :, at] = value.astype(BF).reshape(2, quarter, WIDE_TILE)
            return carry

        lax.fori_loop(0, wides[0] // WIDE_TILE, body, 0)
        pair_copy(k).start()

    def piece_sum(i, k, extra, store):
        slot = k + half - 1
        if i == 0:
            pair_copy(k).wait_recv()
            received = from_chip_out
        else:
            core_copy(i, k).wait_recv()
            received = from_core[i]

        def body(j, carry):
            at = tile(j, WIDE_TILE)
            own = out_sums[slot, chip, :, at] if i == 0 else terms[i][shard_of(k), core, :, at]
            value = own.astype(F32)
            value += received[slot, :, at].astype(F32)
            for direction, step in extra:
                value += incoming[i][direction, step, :, at].astype(F32)
            store(at, value.astype(BF))
            return carry

        lax.fori_loop(0, wides[i] // WIDE_TILE, body, 0)

    def ring_copy(i, direction, step):
        cut = pieces[i] // 2
        at = pl.ds(direction * cut, cut) if step == 0 else pl.ds(0, pieces[i])
        return remote_copy(
            outgoing[i].at[direction, at],
            incoming[i].at[direction, step, at],
            ring_send.at[i, direction, step],
            ring_recv.at[i, direction, step],
            near[direction],
        )

    def ring_step(i, step):
        if step == 0:

            cut = pieces[i] // 2

            def store(at, value):
                outgoing[i][0, pl.ds(0, cut), at] = value[:cut]
                outgoing[i][1, pl.ds(cut, cut), at] = value[cut:]

            piece_sum(i, half, (), store)
            for direction in range(2):
                ring_copy(i, direction, 0).start()
            return
        for direction in range(2):
            ring_copy(i, direction, step - 1).wait()

            def store(at, value):
                outgoing[i][direction, :, at] = value

            k = half - step if direction == 0 else step - half
            piece_sum(i, k, ((direction, step - 1),), store)
            ring_copy(i, direction, step).start()

    def chip_copy(i):
        return remote_copy(
            summed.at[i - 1],
            from_chip.at[i - 1],
            chip_send.at[i],
            chip_recv.at[i],
            other_chip,
        )

    def ring_end(i):
        for direction in range(2):
            ring_copy(i, direction, half - 1).wait()

        def store(at, value):
            if i == 0:
                out_summed[:, at] = value
            else:
                summed[i - 1, :, at] = value

        piece_sum(i, 0, tuple((d, half - 1) for d in range(2)), store)
        if i > 0:
            chip_copy(i).start()
        else:
            for copy in out_copies()[:3]:
                copy.start()

    own_strip = pl.ds(pl.multiple_of(core * strip, strip), strip)

    def out_copies():
        def at(which_chip):
            return out_grad_ref.at[
                pl.ds(pl.multiple_of(core * strip + which_chip * quarter, quarter), quarter)
            ]

        done = out_summed
        return (
            pltpu.make_async_copy(done, at(chip), own_sem.at[3]),
            remote_copy(done, at(chip), chip_send.at[0], chip_recv.at[0], other_chip),
            remote_copy(done, at(chip), last_send.at[0], last_recv.at[0], other_core),
            remote_copy(at(1 - chip), at(1 - chip), last_send.at[3], last_recv.at[3], other_core),
        )

    def last_copies(i):
        src = finished.at[i - 1]
        dst = result_refs[i].at[own_strip, pl.ds(result_starts[i], wides[i])]
        return (
            pltpu.make_async_copy(src, dst, own_sem.at[3 + i]),
            remote_copy(src, dst, last_send.at[i], last_recv.at[i], other_core),
        )

    def group_end(i):
        chip_copy(i).wait()
        total = summed[i - 1].astype(F32) + from_chip[i - 1].astype(F32)
        finished[i - 1] = total.astype(BF)
        for copy in last_copies(i):
            copy.start()

    def gain_copy(k):
        return remote_copy(
            gain_terms.at[:, tile(others[k - 1], own_rows)],
            gains_in.at[k],
            gain_send.at[k - 1],
            gain_recv.at[k - 1],
            {"shard": others[k - 1]},
        )

    def gain_swap(index):
        return remote_copy(
            gain_parts.at[index],
            gain_swaps.at[index],
            swap_send.at[index],
            swap_recv.at[index],
            (other_core, other_chip)[index],
        )

    def weight_load(ref, j, wide):
        return pltpu.make_async_copy(
            ref.at[tile(j, LOAD_TILE)], weight_tile.at[j % 2, :, pl.ds(0, wide)], tile_sem.at[j % 2]
        )

    def times_transposed(left, ref, wide, store):
        blocks = width // LOAD_TILE

        def body(j, carry):
            @pl.when(j + 1 < blocks)
            def _():
                weight_load(ref, j + 1, wide).start()

            weight_load(ref, j, wide).wait()
            store(tile(j, LOAD_TILE), contract_last(left[...], weight_tile[j % 2, :, pl.ds(0, wide)]))
            return carry

        lax.fori_loop(0, blocks, body, 0)

    def turn(array):
        def body(j, carry):
            turned[tile(j), :] = array[:, tile(j)].T
            return carry

        lax.fori_loop(0, width // TILE, body, 0)

    cosine, sine = cos_ref[...], -sin_ref[...]
    wide, thin = 2 * GROUP * HEAD_SIZE, 2 * HEAD_SIZE
    key_at, value_at = width, width + key_ref.shape[1]

    def heads_pair(pair):
        allowed = allowed_rows(segr_ref[...])
        wide_at, thin_at = pl.ds(pair * wide, wide), pl.ds(pair * thin, thin)
        query, grad = query_ref[:, wide_at], grad_attended[:, wide_at]
        key, value = key_ref[:, thin_at], value_ref[:, thin_at]
        heads, keys, values = [], [], []
        for j in range(2):
            cols = slice(j * HEAD_SIZE, (j + 1) * HEAD_SIZE)
            query_rows, grad_rows = stack_heads(query, j), stack_heads(grad, j)
            probs = softmax_rows(query_rows, key[:, cols], allowed)
            grad_probs = contract_last(grad_rows, value[:, cols])
            grad_scores = (
                probs * (grad_probs - jnp.sum(probs * grad_probs, -1, keepdims=True))
            ).astype(BF)
            heads += unstack_heads(dot(grad_scores, key[:, cols]) * HEAD_SIZE ** (-0.5))
            keys.append(contract_first(grad_scores, query_rows) * HEAD_SIZE ** (-0.5))
            values.append(contract_first(probs.astype(BF), grad_rows))
        grads[:, wide_at] = rotate(jnp.concatenate(heads, 1), cosine, sine).astype(BF)
        grads[:, pl.ds(key_at + pair * thin, thin)] = rotate(
            jnp.concatenate(keys, 1), cosine, sine
        ).astype(BF)
        grads[:, pl.ds(value_at + pair * thin, thin)] = jnp.concatenate(values, 1).astype(BF)

    load_attended = pltpu.make_async_copy(attended_ref, grad_attended, own_sem.at[3])
    load_attended.start()
    own_load.start()
    for i in chains:
        for direction in range(2):
            cut = pieces[i] // 2
            blank = pl.ds((1 - direction) * cut, cut)
            incoming[i][direction, 0, blank] = jnp.zeros((cut, wides[i]), BF)

    own_load.wait()
    for copy in keep:
        copy.start()
    greet([{"shard": shard} for shard in others] + [other_core, other_chip])

    for k in range(1, count):
        for which in range(2):
            across(k, which).start()
    weight_load(out_all_ref, 0, width).start()
    load_attended.wait()
    turn(grad_attended)
    all_terms(0)
    for k in [half] + [s * j for j in range(half - 1, 0, -1) for s in (1, -1)] + [0]:
        sum_pair(k)

    def store_attended(at, value):
        grad_attended[:, at] = value.astype(BF)

    times_transposed(mid_low_ref, out_all_ref, width, store_attended)
    weight_load(qkv_all_ref, 0, grads.shape[1]).start()
    ring_step(0, 0)
    for pair in range(KEY_VALUE_HEADS // 2):
        heads_pair(pair)

    unit, scale_row = normalize(tokens_ref[...].astype(F32))
    gain = gains_ref[0:1, :]
    grad_attended[...] = (unit * gain).astype(BF)
    turn(grad_attended)
    all_terms(1)
    ring_step(1, 0)
    for copy in keep:
        copy.wait()
    for k in range(1, count):
        for which in range(2):
            across(k, which).wait_recv()
    for which in range(2):
        for index in range(2):
            group_copy(which, index).start()
    for k in range(-(half - 1), half + 1):
        core_copy(0, k).wait_send()
    all_terms(2)
    ring_step(2, 0)
    for i in in_turn:
        ring_step(i, 1)

    def store_input(at, value):
        grad_input_ref[:, at] = value

    times_transposed(grads, qkv_all_ref, grads.shape[1], store_input)
    if half > 2:
        for i in in_turn:
            ring_step(i, 2)
    unit, scale_row = normalize(tokens_ref[...].astype(F32))
    grad_normed = grad_input_ref[...]
    gain_terms[...] = jnp.zeros_like(gain_terms)
    gain_terms[0:1, :] = jnp.sum(grad_normed * unit, 0, keepdims=True)
    gain_terms[1:2, :] = gain_two_ref[...]
    for k in range(1, count):
        gain_copy(k).start()
    grad_input_ref[...] = norm_back(grad_normed * gain, unit, scale_row)
    for step in range(3, half):
        for i in in_turn:
            ring_step(i, step)
    for which in range(2):
        group_copy(which, 0).wait_recv()
        group_copy(which, 2).start()
    total = gain_terms[:, tile(me, own_rows)]
    for k in range(1, count):
        gain_copy(k).wait_recv()
        total += gains_in[k]
    gain_parts[0] = total
    gain_swap(0).start()
    for i in in_turn:
        ring_end(i)
    gain_swap(0).wait()
    gain_parts[1] = gain_parts[0] + gain_swaps[0]
    gain_swap(1).start()
    for i in (1, 2):
        group_end(i)
    out_copies()[1].wait_recv()
    out_copies()[3].start()
    gain_swap(1).wait()
    gain_grad_ref[...] = gain_parts[1] + gain_swaps[1]

    for k in range(-(half - 1), half + 1):
        pair_copy(k).wait_send()
    kept, over, passed, again = out_copies()
    kept.wait()
    over.wait_send()
    passed.wait()
    again.wait()
    for i in (1, 2):
        kept, passed = last_copies(i)
        kept.wait()
        passed.wait()
    for i in (1, 2):
        for k in range(-(half - 1), half + 1):
            core_copy(i, k).wait_send()
    for which in range(2):
        for index in range(3):
            if index > 0:
                group_copy(which, index).wait_recv()
            group_copy(which, index).wait_send()
    for k in range(1, count):
        gain_copy(k).wait_send()
        for which in range(2):
            across(k, which).wait_send()


def back(
    count,
    sums,
    mid_low,
    gain_two_term,
    attended,
    query,
    key,
    value,
    tokens,
    gains,
    tables,
    qkv_all,
    out_all,
):
    rows, width = tokens.shape
    qkv_width = qkv_all.shape[1]
    own_rows = width // count
    strip, quarter = own_rows // 2, own_rows // 4
    ff_own = sums.shape[2] // 2
    half = count // 2
    here = pl.BlockSpec(memory_space=pl.ANY)
    inside = pl.BlockSpec(memory_space=pltpu.VMEM)
    kind = jax.ShapeDtypeStruct
    dma = pltpu.SemaphoreType.DMA
    vmem = pltpu.VMEM
    return pl.pallas_call(
        functools.partial(back_kernel, count),
        in_specs=[here] + [inside] * 2 + [here] + [inside] * 8 + [here] * 2,
        out_specs=[here] * 4 + [inside] * 2,
        out_shape=[
            kind((4, quarter, count * ff_own), BF),
            kind((4, quarter, count * ff_own), BF),
            kind((own_rows, width), BF),
            kind((own_rows, qkv_width), BF),
            kind((rows, width), F32),
            kind((8, own_rows), F32),
        ],
        scratch_shapes=[
            vmem((quarter, 2 * ff_own), BF),
            vmem((width, rows), BF),
            vmem((rows, width), BF),
            vmem((rows, qkv_width), BF),
            vmem((2, LOAD_TILE, qkv_width), BF),
            vmem((count, 2, strip, width), BF),
            vmem((count, 2, strip, qkv_width // 2), BF),
            vmem((count, strip, width), BF),
            vmem((2, count, strip, qkv_width // 2), BF),
            vmem((count, quarter, width), BF),
            vmem((count, 2, quarter, width), BF),
            vmem((quarter, width), BF),
            vmem((2, quarter, width), BF),
            vmem((2, 2, strip, qkv_width // 2), BF),
            vmem((2, half, quarter, width), BF),
            vmem((2, 2, half, strip, qkv_width // 2), BF),
            vmem((2, strip, qkv_width // 2), BF),
            vmem((2, strip, qkv_width // 2), BF),
            vmem((2, strip, qkv_width // 2), BF),
            vmem((8, width), F32),
            vmem((count, 8, own_rows), F32),
            vmem((2, 8, own_rows), F32),
            vmem((2, 8, own_rows), F32),
            dma((6,)),
            dma((2,)),
            dma((2, count - 1)),
            dma((2, count - 1)),
            dma((2, 3)),
            dma((2, 3)),
            dma((3, count)),
            dma((3, count)),
            dma((3, 2, half)),
            dma((3, 2, half)),
            dma((3,)),
            dma((3,)),
            dma((4,)),
            dma((4,)),
            dma((count,)),
            dma((count,)),
            dma((count - 1,)),
            dma((count - 1,)),
            dma((2,)),
            dma((2,)),
        ],
        compiler_params=pltpu.CompilerParams(
            collective_id=2, has_side_effects=True, vmem_limit_bytes=VMEM_BYTES
        ),
        cost_estimate=pl.CostEstimate(
            flops=4 * rows * width * (qkv_width + width) + 4 * 10**9,
            bytes_accessed=60 * 10**6,
            transcendentals=2 * 10**6,
        ),
    )(
        sums,
        mid_low,
        gain_two_term,
        attended,
        query,
        key,
        value,
        tokens,
        gains,
        *tables,
        qkv_all,
        out_all,
    )


def results_kernel(*refs):
    gate, up, down, out, qkv, middle, change = refs[:7]
    gate_to, up_to, down_to, out_to, query_to, key_to, value_to, input_to = refs[7:]
    for source, result in ((gate, gate_to), (up, up_to), (down, down_to), (out, out_to)):
        result[...] = source[...].astype(F32)
    start = 0
    for result in (query_to, key_to, value_to):
        result[...] = qkv[:, start : start + result.shape[1]].astype(F32)
        start += result.shape[1]
    input_to[...] = middle[...] + change[...]


def results(gate, up, down, out, qkv, wide_k, grad_middle, change):
    steps = 8
    kind = jax.ShapeDtypeStruct
    sources = (gate, up, down, out, qkv, grad_middle, change)
    width = out.shape[1]
    shapes = [a.shape for a in (gate, up, down, out)]
    shapes += [(qkv.shape[0], w) for w in (width, wide_k, wide_k)] + [change.shape]
    block = lambda shape: pl.BlockSpec((shape[0] // steps, shape[1]), lambda i: (i, 0))
    return pl.pallas_call(
        results_kernel,
        grid=(steps,),
        in_specs=[block(a.shape) for a in sources],
        out_specs=[block(shape) for shape in shapes],
        out_shape=[kind(shape, F32) for shape in shapes],
        compiler_params=pltpu.CompilerParams(vmem_limit_bytes=VMEM_BYTES),
    )(*sources)


def feed_forward_parts(ring, normed_two, grad_low, w_both, w_down):
    sequence, ff_own = normed_two.shape[0], w_down.shape[0]
    low_all, normed_all = run(ring.gather(grad_low), ring.gather(normed_two))
    hidden, grad_both = {}, {}
    for k in normed_all:
        both = dot(normed_all[k], w_both)
        gate, up = both[:, :ff_own], both[:, ff_own:]
        grad_hidden = contract_last(low_all[k], w_down)
        sigmoid = jax.nn.sigmoid(gate)
        silu = gate * sigmoid
        hidden[k] = (silu * up).astype(BF)
        grad_gate = (grad_hidden * up * sigmoid * (1.0 + gate * (1.0 - sigmoid))).astype(BF)
        grad_up = (grad_hidden * silu).astype(BF)
        grad_both[k] = jnp.concatenate([grad_gate, grad_up], 1)

    def terms_of(chunks, product):
        def terms(ks):
            sources = [k if k == ring.half else -k for k in ks]
            whole = product(jnp.concatenate([chunks[k] for k in sources], 0))
            return [whole[i * sequence : (i + 1) * sequence] for i in range(len(ks))]

        return terms

    (grad_normed_two,) = run(ring.scatter(terms_of(grad_both, lambda a: contract_last(a, w_both))))
    (branch_two,) = run(ring.scatter(terms_of(hidden, lambda a: dot(a, w_down))))
    keys = list(normed_all)
    together = lambda parts: jnp.concatenate([parts[k] for k in keys], 0)
    both_term = contract_first(together(normed_all), together(grad_both))
    down_term = contract_first(together(hidden), together(low_all))
    return grad_normed_two, branch_two, both_term, down_term


def swap(array, bit):
    return lax.ppermute(array, "rep", [(i, i ^ bit) for i in range(4)])


def cols(array, start, width):
    return lax.dynamic_slice_in_dim(array, start, width, 1)


def rows_of(array, start, height):
    return lax.dynamic_slice_in_dim(array, start, height, 0)


def put(array, piece, start, axis):
    return lax.dynamic_update_slice_in_dim(array, piece, start, axis)


def gather_rows(ring, array):
    rows = array.shape[0]
    (parts,) = run(ring.gather(array))
    full = jnp.zeros((ring.count * rows, array.shape[1]), array.dtype)
    for k, part in parts.items():
        full = put(full, part, ring.at(-k) * rows, 0)
    return full


def front_parts(ring, tokens, gains_own, cotangent, tables, own, w_gate, w_up):
    count, (own_rows, wide_k) = ring.count, own[1].shape
    rep = lax.axis_index("rep")
    ff_own = w_gate.shape[1] // count
    width = tokens.shape[1]
    gains = jnp.zeros((gains_own.shape[0], width), F32)
    for k in range(count):
        piece = ring.send(gains_own, k) if k else gains_own
        gains = put(gains, piece, ring.at(-k) * own_rows, 1)
    qkv_all = gather_rows(ring, jnp.concatenate(own[:3], 1))
    out_all = gather_rows(ring, own[3])
    quarter = own_rows // 4
    gate_rows = rows_of(w_gate, rep * quarter, quarter)
    up_rows = rows_of(w_up, rep * quarter, quarter)
    sends = []
    for k in range(count):
        dest = ring.at(k) * ff_own
        piece = jnp.concatenate([cols(gate_rows, dest, ff_own), cols(up_rows, dest, ff_own)], 1)
        sends.append((piece, k))
    fetched = jnp.zeros((count, quarter, 2 * ff_own), BF)
    for k, piece in enumerate([sends[0][0]] + ring.queue(*sends[1:])):
        fetched = put(fetched, piece[None], ring.at(-k), 0)
    pieces = [fetched, swap(fetched, 2)]
    pieces += [swap(piece, 1) for piece in pieces]
    w_both = jnp.zeros((count, 4, quarter, 2 * ff_own), BF)
    for bits, piece in zip((0, 2, 1, 3), pieces):
        w_both = put(w_both, piece[:, None], rep ^ bits, 1)
    resid = tokens.astype(F32)
    unit, _ = normalize(resid)
    linear = dot((unit * gains[:1]).astype(BF), qkv_all)
    query, key, value, attended = attend(
        linear[:, :width], linear[:, width : width + wide_k], linear[:, width + wide_k :], tables
    )
    middle = resid + dot(attended, out_all)
    unit, _ = normalize(middle)
    normed_two = (unit * gains[1:2]).astype(BF)
    low = cotangent.astype(BF)
    return qkv_all, out_all, w_both, low, gains, query, key, value, attended, middle, normed_two


def back_parts(
    ring,
    both_term,
    down_term,
    mid_low,
    gain_two_term,
    attended,
    query,
    key,
    value,
    tokens,
    gains,
    tables,
    qkv_all,
    out_all,
):
    count = ring.count
    rep = lax.axis_index("rep")
    core, chip = rep % 2, rep // 2
    width = tokens.shape[1]
    own_rows = width // count
    quarter = own_rows // 4
    ff_own = both_term.shape[1] // 2
    ff = ff_own * count

    def order_halves(mine, other):
        first = core == 0
        return jnp.where(first, mine, other), jnp.where(first, other, mine)

    def sum_cores(array, half_of):
        keep, pass_on = half_of(array, core), half_of(array, 1 - core)
        return keep.astype(F32) + swap(pass_on.astype(BF), 1).astype(F32)

    both_term = both_term.reshape(count, 2, 2, quarter, 2 * ff_own)
    both_half = sum_cores(
        both_term, lambda a, c: lax.dynamic_index_in_dim(a, c, 2, keepdims=False)
    )
    keep = lax.dynamic_index_in_dim(both_half, chip, 1, keepdims=False)
    pass_on = lax.dynamic_index_in_dim(both_half, 1 - chip, 1, keepdims=False)
    both_quarter = (keep + swap(pass_on.astype(BF), 2).astype(F32)).astype(BF)
    gate_quarter = jnp.zeros((quarter, ff), BF)
    up_quarter = jnp.zeros((quarter, ff), BF)
    sends = [
        (lax.dynamic_index_in_dim(both_quarter, ring.at(k), 0, keepdims=False), k)
        for k in range(count)
    ]
    for k, piece in enumerate([sends[0][0]] + ring.queue(*sends[1:])):
        start = ring.at(-k) * ff_own
        gate_quarter = put(gate_quarter, piece[:, :ff_own], start, 1)
        up_quarter = put(up_quarter, piece[:, ff_own:], start, 1)

    def collect(quarter_rows):
        parts = [quarter_rows, swap(quarter_rows, 2)]
        parts += [swap(part, 1) for part in parts]
        full = jnp.zeros((4 * quarter, ff), BF)
        for bits, part in zip((0, 2, 1, 3), parts):
            full = put(full, part, (rep ^ bits) * quarter, 0)
        return full

    gate_grad, up_grad = collect(gate_quarter), collect(up_quarter)

    down_half = sum_cores(
        down_term, lambda a, c: rows_of(a, c * (a.shape[0] // 2), a.shape[0] // 2)
    ).astype(BF)
    down_half = (down_half.astype(F32) + swap(down_half, 2).astype(F32)).astype(BF)
    down_grad = jnp.concatenate(order_halves(down_half, swap(down_half, 1)), 0)

    def part_sums(left, grads):
        wide = grads.shape[1] // 2
        grads_mine, grads_other = cols(grads, core * wide, wide), cols(grads, (1 - core) * wide, wide)

        def terms(ks):
            blocks = [cols(left, ring.at(k) * own_rows, own_rows) for k in ks]
            block = blocks[0] if len(ks) == 1 else jnp.concatenate(blocks, 1)
            other = swap(contract_first(block, grads_other).astype(BF), 1)
            whole = contract_first(block, grads_mine) + other.astype(F32)
            return [whole[i * own_rows : (i + 1) * own_rows] for i in range(len(ks))]

        mine = run(ring.scatter(terms))[0].astype(BF)
        mine = (mine.astype(F32) + swap(mine, 2).astype(F32)).astype(BF)
        return jnp.concatenate(order_halves(mine, swap(mine, 1)), 1)

    out_grad = part_sums(attended, mid_low)
    grad_attended = contract_last(mid_low, out_all).astype(BF)
    grads = jnp.concatenate(attend_back(query, key, value, grad_attended, tables), 1)
    unit_one, scale_one = normalize(tokens.astype(F32))
    gain_one = gains[:1]
    qkv_grad = part_sums((unit_one * gain_one).astype(BF), grads)
    grad_normed_one = contract_last(grads, qkv_all)
    gain_one_term = jnp.sum(grad_normed_one * unit_one, 0, keepdims=True)
    grad_input = norm_back(grad_normed_one * gain_one, unit_one, scale_one)

    gain_terms = jnp.concatenate([gain_one_term, gain_two_term], 0)
    gain_sums = cols(gain_terms, ring.at(0) * own_rows, own_rows)
    for k in range(1, count):
        gain_sums = gain_sums + ring.send(cols(gain_terms, ring.at(k) * own_rows, own_rows), k)
    gain_sums = gain_sums + swap(gain_sums, 1)
    gain_sums = gain_sums + swap(gain_sums, 2)
    return gate_grad, up_grad, down_grad, out_grad, qkv_grad, grad_input, gain_sums


def on_device(
    count,
    tokens,
    segments,
    norm_attn,
    w_query,
    key_weight,
    value_weight,
    w_out,
    norm_mlp,
    w_gate,
    w_up,
    w_down,
    cotangent,
):
    ring = Ring(count)
    sequence, width = tokens.shape[1], tokens.shape[2]
    own_rows = w_query.shape[0]
    ff = w_gate.shape[1]
    ff_own = ff // count
    wide_k = key_weight.shape[1]
    fits = feed_forward_bytes(count, sequence, width, ff_own) <= VMEM_BYTES
    kernels = fits and sequence == own_rows == TILE

    grad_output = cotangent.reshape(sequence, width)
    cosine, sine = rope_tables(segments)
    tables = (cosine, sine, segments.reshape(1, sequence))
    own = tokens.reshape(sequence, width)
    own_weights = (w_query, key_weight, value_weight, w_out)
    gains_own = jnp.zeros((8, own_rows), F32)
    gains_own = gains_own.at[0].set(norm_attn.astype(F32)).at[1].set(norm_mlp.astype(F32))
    bring = functools.partial(front, count) if kernels else functools.partial(front_parts, ring)
    qkv_all, out_all, w_both, low, gains, query, key, value, attended, middle, normed_two = bring(
        own, gains_own, grad_output, tables, own_weights, w_gate, w_up
    )
    w_both = w_both.reshape(width, 2 * ff_own)

    if kernels:
        grad_normed_two, branch_two, sums, down_grad = feed_forward(
            count, normed_two, low, w_both, w_down
        )
    else:
        grad_normed_two, branch_two, both_term, down_term = feed_forward_parts(
            ring, normed_two, low, w_both, w_down
        )
    output, grad_middle, grad_mid_low, gain_two_term = middle_back(
        middle, branch_two, grad_normed_two, grad_output, gains
    )

    if kernels:
        gate_grad, up_grad, out_grad, qkv_grad, grad_input, gain_sums = back(
            count,
            sums,
            grad_mid_low,
            gain_two_term,
            attended,
            query,
            key,
            value,
            own,
            gains,
            tables,
            qkv_all,
            out_all,
        )
    else:
        gate_grad, up_grad, down_grad, out_grad, qkv_grad, grad_input, gain_sums = back_parts(
            ring,
            both_term,
            down_term,
            grad_mid_low,
            gain_two_term,
            attended,
            query,
            key,
            value,
            own,
            gains,
            tables,
            qkv_all,
            out_all,
        )
    gate_grad, up_grad, down_grad, out_grad, query_grad, key_grad, value_grad, grad_input = results(
        gate_grad.reshape(own_rows, ff),
        up_grad.reshape(own_rows, ff),
        down_grad.reshape(ff_own, width),
        out_grad,
        qkv_grad,
        wide_k,
        grad_middle,
        grad_input,
    )

    return (
        output.reshape(tokens.shape),
        grad_input.reshape(tokens.shape),
        gain_sums[0],
        query_grad,
        key_grad,
        value_grad,
        out_grad,
        gain_sums[1],
        gate_grad,
        up_grad,
        down_grad,
    )


def solution(mesh):
    row, vector, matrix = P(("shard", "rep"), None, None), P("shard"), P("shard", None)
    in_specs = (row, P(("shard", "rep"), None), vector, matrix, matrix, matrix, matrix, vector)
    in_specs += (matrix, matrix, matrix, row)
    out_specs = (row, row, vector, matrix, matrix, matrix, matrix, vector, matrix, matrix, matrix)
    return jax.shard_map(
        functools.partial(on_device, mesh.shape["shard"]),
        mesh=mesh,
        in_specs=in_specs,
        out_specs=out_specs,
        check_vma=False,
    )
```
